128 devices in a mesh: fsdp: 4 (over z), seq: 8 (over x, core), tensor: 4 (over y).
Axes of the slice: x: 4, y: 4, z: 4, core: 2. Of those that a mesh axis runs over, the one named last changes fastest.
Arguments:
- block_input: bfloat16 [16384, 512], P(('fsdp', 'seq', 'tensor')), may hold values from -6 to 6
- cotangent: bfloat16 [16384, 512], P(('fsdp', 'seq', 'tensor')), may hold values from -6 to 6
- doc_lengths: int32 [4, 4], P('fsdp'), may hold values from 1 to 3840, as said below
- joint_weight: float32 [512, 1536], P(('fsdp', 'seq', 'tensor')), may hold values from -0.375 to 0.375
- output_weight: float32 [512, 512], P(('fsdp', 'seq', 'tensor')), may hold values from -1.5 to 1.5
- expand_weight: float32 [512, 2048], P(('fsdp', 'seq', 'tensor')), may hold values from -0.25 to 0.25
- reduce_weight: float32 [512, 2048], P(('fsdp', 'seq', 'tensor')), may hold values from -0.125 to 0.125
- joint_moment: float32 [512, 1536], P(('fsdp', 'seq', 'tensor')), may hold values from -4096 to 4096
- output_moment: float32 [512, 512], P(('fsdp', 'seq', 'tensor')), may hold values from -224 to 224
- expand_moment: float32 [512, 2048], P(('fsdp', 'seq', 'tensor')), may hold values from -224 to 224
- reduce_moment: float32 [512, 2048], P(('fsdp', 'seq', 'tensor')), may hold values from -448 to 448
- vectors: float32 [11, 512], P(None, ('fsdp', 'seq', 'tensor'))
- first_moment: float32 [11, 512], P(None, ('fsdp', 'seq', 'tensor'))
- second_moment: float32 [11, 512], P(None, ('fsdp', 'seq', 'tensor'))
Outputs:
- block_output: bfloat16 [16384, 512], P(('fsdp', 'seq', 'tensor'))
- input_grad: float32 [16384, 512], P(('fsdp', 'seq', 'tensor'))
- gradient_joint: float32 [512, 1536], P(('fsdp', 'seq', 'tensor'))
- gradient_output: float32 [512, 512], P(('fsdp', 'seq', 'tensor'))
- gradient_expand: float32 [512, 2048], P(('fsdp', 'seq', 'tensor'))
- gradient_reduce: float32 [512, 2048], P(('fsdp', 'seq', 'tensor'))
- momentum_joint: float32 [512, 1536], P(('fsdp', 'seq', 'tensor'))
- momentum_output: float32 [512, 512], P(('fsdp', 'seq', 'tensor'))
- momentum_expand: float32 [512, 2048], P(('fsdp', 'seq', 'tensor'))
- momentum_reduce: float32 [512, 2048], P(('fsdp', 'seq', 'tensor'))
- updated_joint: float32 [512, 1536], P(('fsdp', 'seq', 'tensor'))
- updated_output: float32 [512, 512], P(('fsdp', 'seq', 'tensor'))
- updated_expand: float32 [512, 2048], P(('fsdp', 'seq', 'tensor'))
- updated_reduce: float32 [512, 2048], P(('fsdp', 'seq', 'tensor'))
- vector_grad: float32 [11, 512], P(None, ('fsdp', 'seq', 'tensor'))
- second_next: float32 [11, 512], P(None, ('fsdp', 'seq', 'tensor'))
- vector_next: float32 [11, 512], P(None, ('fsdp', 'seq', 'tensor'))
The draws below stay inside these ranges and needn't reach their ends.
Inputs may be any that keep to these rules, and one draw needn't show every extreme that they name: `doc_lengths`: each row gives the lengths of the 4 documents of one pack in order; they sum to 4096, and exactly one of them, at a place drawn from the seed, is 3840 tokens long.
All inputs are finite; a program needn't handle non-finite values.
Results may differ from the reference program's by a relative error of at most 0.014.
The reference program's roundings to bfloat16 on the way count: a program that leaves them out, or rounds other values in their place, can miss the bound.
Values may be sent and summed in bfloat16 or wider, within the bound.
A program may use at most 128 MiB of HBM per device.

```python
import math
import jax
import jax.numpy as jnp
from jax import lax

D = 512
HEADS = 8
FF = 2048
ROT = 16
HD = 64
TOK_DEV = 128
DOCS = 4
SWEEPS = 5
STEP = 10
GROUP = 4096
TOKENS = 16384
VROWS = 11
N_FSDP = 4
N_SEQ = 8
N_TENSOR = 4


def vector_scales():
    boost = N_SEQ ** 0.5
    row_ids = jnp.arange(VROWS)
    table = jnp.where(row_ids < 2, 2.0 * boost, jnp.where(row_ids < 4, 0.5 * boost, jnp.where(row_ids == 4, 1.5 * boost, jnp.where(row_ids < 7, 1.0, 0.3))))
    return table.astype(jnp.float32) * TOKENS ** 0.5


def draw_doc_lengths(key, part):
    key = jax.random.fold_in(key, 11)
    short_total = N_TENSOR * TOK_DEV // 2
    longest = TOK_DEV * N_SEQ * N_TENSOR - short_total

    def one_row(row_key):
        cut_key, slot_key = jax.random.split(row_key)
        picked = jax.random.permutation(cut_key, short_total - 1)[:DOCS - 2].astype(jnp.int32) + 1
        cut_points = jnp.sort(picked)
        boundaries = jnp.concatenate([jnp.zeros((1,), jnp.int32), cut_points, jnp.full((1,), short_total, jnp.int32)])
        short_lengths = boundaries[1:] - boundaries[:-1]
        longest_slot = jax.random.randint(slot_key, (), 0, DOCS)
        slot_ids = jnp.arange(DOCS, dtype=jnp.int32)
        source_ids = jnp.clip(jnp.where(slot_ids > longest_slot, slot_ids - 1, slot_ids), 0, DOCS - 2)
        return jnp.where(slot_ids == longest_slot, longest, short_lengths[source_ids]).astype(jnp.int32)
    return jax.vmap(one_row)(jax.random.split(key, N_FSDP))


def draw_vectors(key, part):
    key = jax.random.fold_in(key, 21)
    gain_key, shift_key = jax.random.split(key)
    row_ids = jnp.arange(VROWS)[:, None]
    gains = jnp.exp(jax.random.uniform(gain_key, (VROWS, D), minval=-0.35, maxval=0.35))
    biases = 0.3 * jax.random.normal(shift_key, (VROWS, D))
    return jnp.where(row_ids == 0, gains, biases).astype(jnp.float32)


def draw_first_moment(key, part):
    key = jax.random.fold_in(key, 31)
    size_key, sign_key = jax.random.split(key)
    magnitude = jnp.exp(jax.random.uniform(size_key, (VROWS, D), minval=-0.69, maxval=0.69))
    signs = jnp.where(jax.random.bernoulli(sign_key, 0.5, (VROWS, D)), 1.0, -1.0)
    return (signs * magnitude * (0.1 / 0.9) * vector_scales()[:, None]).astype(jnp.float32)


def draw_second_moment(key, part):
    key = jax.random.fold_in(key, 41)
    factor = jnp.exp(jax.random.uniform(key, (VROWS, D), minval=-0.69, maxval=2.08))
    scales = vector_scales()[:, None]
    return (factor * (0.05 / 0.95) * scales * scales).astype(jnp.float32)


def levels(rng, shape, cuts, least, high):
    factor_of, own = 1.0, jax.random.fold_in(rng, 6)
    for dim, blocks in cuts:
        heights = jnp.exp(jax.random.uniform(jax.random.fold_in(own, dim), (blocks,), jnp.float32, least / len(cuts), high / len(cuts)))
        factor_of = factor_of * jnp.repeat(heights, shape[dim] // blocks).reshape([-1 if axis == dim else 1 for axis in range(len(shape))])
    return factor_of


def normal_values(stream_key, extent, scale, reach, cuts=(), kind=jnp.bfloat16):
    values = jax.random.normal(stream_key, extent, jnp.float32) * scale
    if len(cuts) > 0:
        values = levels(stream_key, extent, cuts, -0.22, 0.18) * values
    return jnp.clip(values, min=-reach, max=reach).astype(kind)


def setup_inputs(seed: int = 0) -> dict:
    keys = jax.random.split(jax.random.key(seed), 15)
    block_input = normal_values(keys[0], (TOKENS, D), 1.0, 6.0, ((0, 128),))
    cotangent = normal_values(keys[1], (TOKENS, D), 1.0, 6.0, ((0, 128),))
    doc_lengths = draw_doc_lengths(jax.random.fold_in(keys[14], 71), 0)
    joint_weight = normal_values(keys[3], (D, 3 * D), (D // 2) ** -0.5, 0.375, ((0, 128),), jnp.float32)
    output_weight = normal_values(keys[4], (D, D), (D // (4 * N_SEQ)) ** -0.5, 1.5, ((0, 128),), jnp.float32)
    expand_weight = normal_values(keys[5], (D, FF), D ** -0.5, 0.25, ((0, 128),), jnp.float32)
    reduce_weight = normal_values(keys[6], (D, FF), FF ** -0.5, 0.125, ((0, 128),), jnp.float32)
    joint_moment = normal_values(keys[7], (D, 3 * D), (2.0 * (N_SEQ * TOKENS) ** 0.5), 4096.0, ((0, 128),), jnp.float32)
    output_moment = normal_values(keys[8], (D, D), (0.3 * TOKENS ** 0.5), 224.0, ((0, 128),), jnp.float32)
    expand_moment = normal_values(keys[9], (D, FF), (0.3 * TOKENS ** 0.5), 224.0, ((0, 128),), jnp.float32)
    reduce_moment = normal_values(keys[10], (D, FF), (0.6 * TOKENS ** 0.5), 448.0, ((0, 128),), jnp.float32)
    vectors = draw_vectors(jax.random.fold_in(keys[14], 71), 0)
    first_moment = draw_first_moment(jax.random.fold_in(keys[14], 71), 0)
    second_moment = draw_second_moment(jax.random.fold_in(keys[14], 71), 0)
    return {"block_input": block_input, "cotangent": cotangent, "doc_lengths": doc_lengths, "joint_weight": joint_weight, "output_weight": output_weight, "expand_weight": expand_weight, "reduce_weight": reduce_weight, "joint_moment": joint_moment, "output_moment": output_moment, "expand_moment": expand_moment, "reduce_moment": reduce_moment, "vectors": vectors, "first_moment": first_moment, "second_moment": second_moment}


@jax.custom_vjp
def low(v):
    return lax.optimization_barrier(v.astype(jnp.bfloat16)).astype(jnp.float32)

@jax.custom_vjp
def low_back(v):
    return v

def low_keep(v):
    return (low(v), None)

def low_pass(kept, grad):
    return (grad,)

def back_keep(v):
    return (v, None)

def back_low(kept, grad):
    return (low(grad),)
low.defvjp(low_keep, low_pass)
low_back.defvjp(back_keep, back_low)
highest = lax.Precision.HIGHEST
norm_epsilon = 1e-05
masked_score = -1e+30
newton_first = 3.4445
newton_second = -4.775
newton_third = 2.0315
beta_first = 0.9
beta_second = 0.95
adam_epsilon = 1e-08
vector_rate = 0.2
muon_rate = 0.25
muon_beta = 0.95
muon_decay = 0.01

def doc_positions(row_index, lengths):
    finish = jnp.cumsum(lengths, dtype=jnp.int32)
    passed = row_index[:, None] >= finish[None, :]
    documents = lax.optimization_barrier(jnp.sum(passed.astype(jnp.int32), axis=1, dtype=jnp.int32))
    starts = lax.optimization_barrier(jnp.sum(jnp.where(passed, lengths[None, :], 0), axis=1, dtype=jnp.int32))
    return (documents, (row_index - starts).astype(jnp.int32))

def rotate(tensor, position, rot_dims, direction):
    half_dims = rot_dims // 2
    frequency = 10000.0 ** (-(jnp.arange(half_dims, dtype=jnp.float32) * 2.0) / rot_dims)
    angles = position.astype(jnp.float32)[:, None] * frequency[None, :]
    cosine = jnp.cos(angles)[:, None, :]
    sine = direction * jnp.sin(angles)[:, None, :]
    first = tensor[..., :half_dims]
    second = tensor[..., half_dims:rot_dims]
    return jnp.concatenate([first * cosine - second * sine, second * cosine + first * sine, tensor[..., rot_dims:]], axis=-1)

def layer_norm(values, norm_gain, norm_shift):
    mean_value = lax.optimization_barrier(jnp.mean(values, axis=-1, keepdims=True))
    centred = values - mean_value
    variance = lax.optimization_barrier(jnp.mean(centred * centred, axis=-1, keepdims=True))
    return centred * lax.rsqrt(variance + norm_epsilon) * norm_gain + norm_shift

def orthogonalize(matrix):
    current = matrix / (jnp.sqrt(jnp.sum(matrix * matrix)) + 1e-07)
    for iteration in range(SWEEPS):
        gram_matrix = jnp.dot(current, current.T, precision=highest)
        mixture = newton_second * gram_matrix + newton_third * jnp.dot(gram_matrix, gram_matrix, precision=highest)
        current = newton_first * current + jnp.dot(mixture, current, precision=highest)
    return current

def reference(block_input, cotangent, doc_lengths, joint_weight, output_weight, expand_weight, reduce_weight, joint_moment, output_moment, expand_moment, reduce_moment, vectors, first_moment, second_moment):
    group_rows = jnp.arange(GROUP, dtype=jnp.int32)

    def group_tables(lengths_row):
        return doc_positions(group_rows, lengths_row)
    documents, positions = jax.vmap(group_tables)(doc_lengths)
    flat_positions = positions.reshape(-1)
    block_rows = math.gcd(GROUP, 512)
    block_count = GROUP // block_rows
    scaling = HD ** (-0.5)
    doc_blocks = documents.reshape(N_FSDP * block_count, block_rows)
    index_blocks = jnp.tile(group_rows.reshape(block_count, block_rows), (N_FSDP, 1))
    group_ids = (jnp.arange(N_FSDP * block_count, dtype=jnp.int32) // block_count).astype(jnp.int32)

    def forward(inputs, joint_master, output_master, expand_master, reduce_master, vector_master):
        joint_low = low(joint_master)
        output_low = low(output_master)
        expand_low = low(expand_master)
        reduce_low = low(reduce_master)
        vector_low = low(vector_master)
        norm_gain = vector_low[0]
        norm_shift = vector_low[1]
        query_bias = vector_low[2]
        key_bias = vector_low[3]
        value_bias = vector_low[4]
        output_bias = vector_low[5]
        reduce_bias = vector_low[6]
        expand_bias = vector_low[7:].reshape(FF)
        normed = low(layer_norm(inputs, norm_gain, norm_shift))
        joint_bias = jnp.concatenate([query_bias, key_bias, value_bias])
        projected = low_back(jnp.dot(normed, joint_low, precision=highest) + joint_bias)
        query_rot = low_back(low(rotate(projected[:, :D].reshape(TOKENS, HEADS, HD), flat_positions, ROT, 1.0)))
        key_rot = low_back(low(rotate(projected[:, D:2 * D].reshape(TOKENS, HEADS, HD), flat_positions, ROT, 1.0)))
        value_low = low(projected[:, 2 * D:]).reshape(TOKENS, HEADS, HD)
        key_groups = key_rot.reshape(N_FSDP, GROUP, HEADS, HD)
        value_groups = value_low.reshape(N_FSDP, GROUP, HEADS, HD)
        query_blocks = query_rot.reshape(N_FSDP * block_count, block_rows, HEADS, HD)

        def attend(packed):
            query_block, group_id, doc_block, index_block = packed
            key_group = lax.dynamic_index_in_dim(key_groups, group_id, 0, keepdims=False)
            value_group = lax.dynamic_index_in_dim(value_groups, group_id, 0, keepdims=False)
            doc_group = lax.dynamic_index_in_dim(documents, group_id, 0, keepdims=False)
            scores = low_back(jnp.einsum('qhd,khd->hqk', query_block, key_group, precision=highest) * scaling)
            allowed = (doc_block[:, None] == doc_group[None, :]) & (group_rows[None, :] <= index_block[:, None])
            scores = jnp.where(allowed[None], scores, masked_score)
            row_max = lax.optimization_barrier(jnp.max(scores, axis=-1, keepdims=True))
            exponent = jnp.exp(scores - row_max)
            probability = exponent / lax.optimization_barrier(jnp.sum(exponent, axis=-1, keepdims=True))
            return jnp.einsum('hqk,khd->qhd', low(probability), value_group, precision=highest)
        attended = lax.map(jax.checkpoint(attend), (query_blocks, group_ids, doc_blocks, index_blocks))
        attended = low_back(low(attended.reshape(TOKENS, D)))
        attention = jnp.dot(attended, output_low, precision=highest) + output_bias
        hidden_pre = low_back(jnp.dot(normed, expand_low, precision=highest) + expand_bias)
        hidden = low(jax.nn.gelu(hidden_pre, approximate=True))
        feed_term = jnp.dot(hidden, reduce_low.T, precision=highest) + reduce_bias
        return inputs + attention + feed_term
    result, pullback = jax.vjp(forward, block_input.astype(jnp.float32), joint_weight, output_weight, expand_weight, reduce_weight, vectors)
    input_grad, joint_grad, output_grad, expand_grad, reduce_grad, vector_grad = pullback(cotangent.astype(jnp.float32))

    def muon(master, moment, gradient):
        momentum = muon_beta * moment + gradient
        orthogonal = orthogonalize(momentum)
        factor = muon_rate * 0.2 * math.sqrt(max(master.shape))
        return (momentum, master * (1.0 - muon_rate * muon_decay) - factor * orthogonal)
    momentum_joint, updated_joint = muon(joint_weight, joint_moment, joint_grad)
    momentum_output, updated_output = muon(output_weight, output_moment, output_grad)
    momentum_expand, updated_expand = muon(expand_weight, expand_moment, expand_grad)
    momentum_reduce, updated_reduce = muon(reduce_weight, reduce_moment, reduce_grad)
    first_next = beta_first * first_moment + (1.0 - beta_first) * vector_grad
    second_next = beta_second * second_moment + (1.0 - beta_second) * vector_grad * vector_grad
    first_hat = first_next / (1.0 - beta_first ** STEP)
    second_hat = second_next / (1.0 - beta_second ** STEP)
    vector_next = vectors - vector_rate * first_hat / (jnp.sqrt(second_hat) + adam_epsilon)
    return (result.astype(jnp.bfloat16), input_grad, joint_grad, output_grad, expand_grad, reduce_grad, momentum_joint, momentum_output, momentum_expand, momentum_reduce, updated_joint, updated_output, updated_expand, updated_reduce, vector_grad, second_next, vector_next)
```

```python
import math

import jax
import jax.numpy as jnp
from jax import lax
from jax.experimental import pallas as pl
from jax.experimental.pallas import tpu as pltpu
from jax.sharding import PartitionSpec as P

D = 512
HEADS = 8
FF = 2048
ROT = 16
HD = 64
STEP = 10

norm_epsilon = 1e-05
masked_score = -1e30
newton_first = 3.4445
newton_second = -4.775
newton_third = 2.0315
beta_first = 0.9
beta_second = 0.95
adam_epsilon = 1e-08
vector_rate = 0.2
muon_rate = 0.25
muon_beta = 0.95
muon_decay = 0.01

BF = jnp.bfloat16
F32 = jnp.float32
MESH = pl.DeviceIdType.MESH
VMEM = pl.BlockSpec(memory_space=pltpu.VMEM)
SMEM = pl.BlockSpec(memory_space=pltpu.SMEM)
WIDTHS = (3 * D, D, FF, FF)


def shape(dims, dtype):
    return jax.ShapeDtypeStruct(dims, dtype)


class Place:
    def __init__(self):
        self.z = lax.axis_index("fsdp")
        seq = lax.axis_index("seq")
        self.t = lax.axis_index("tensor")
        self.x = lax.div(seq, 2)
        self.c = lax.rem(seq, 2)
        self.seq = seq
        self.g = 4 * self.c + self.t
        self.b = 4 * self.z + self.x
        self.d = 1 - 2 * self.c

    def at(self, z=None, x=None, c=None, t=None):
        z = self.z if z is None else z
        x = self.x if x is None else x
        c = self.c if c is None else c
        t = self.t if t is None else t
        return (z, 2 * x + c, t)

    def member(self, g):
        return self.at(c=lax.div(g, 4), t=lax.rem(g, 4))

    def sibling(self):
        return self.at(c=1 - self.c)

    def octet(self):
        return [self.member(lax.rem(self.g + k, 8)) for k in range(1, 8)]

    def row_x(self):
        return [self.at(x=lax.rem(self.x + k, 4)) for k in range(1, 4)]

    def row_z(self):
        return [self.at(z=lax.rem(self.z + k, 4)) for k in range(1, 4)]

    def row_t(self):
        return [self.at(t=lax.rem(self.t + k, 4)) for k in range(1, 4)]


def ring(index, step):
    return lax.rem(index + step + 4, 4)


def greet(partners):
    barrier = pltpu.get_barrier_semaphore()
    for partner in partners:
        pl.semaphore_signal(barrier, inc=1, device_id=partner, device_id_type=MESH)
    pl.semaphore_wait(barrier, len(partners))


class Wire:
    def __init__(self, send, recv):
        self.send = send
        self.recv = recv
        self.count = 0
        self.open = []

    def make(self, src, dst, device):
        index = self.count
        self.count += 1
        return pltpu.make_async_remote_copy(
            src_ref=src,
            dst_ref=dst,
            send_sem=self.send.at[index],
            recv_sem=self.recv.at[index],
            device_id=device,
            device_id_type=MESH,
        )

    def push(self, src, dst, device):
        copy = self.make(src, dst, device)
        copy.start()
        self.open.append(copy)
        return copy

    def drain(self):
        for copy in self.open:
            copy.wait_send()


def arrive(copies):
    for copy in copies:
        copy.wait_recv()


def dot(left, right):
    return jnp.dot(left, right, preferred_element_type=F32)


def dot_cols(left, right):
    return lax.dot_general(left, right, (((1,), (1,)), ((), ())), preferred_element_type=F32)


def dot_rows(left, right):
    return lax.dot_general(left, right, (((0,), (0,)), ((), ())), preferred_element_type=F32)


def exchange_octet(wire, place, out_ref, in_ref):
    copies = []
    for k in range(1, 8):
        goal = lax.rem(place.g + k, 8)
        copies.append(wire.push(out_ref.at[goal], in_ref.at[place.g], place.member(goal)))
    return copies


def gather_x(wire, place, ref):
    block = ref.at[place.c, place.b]
    return [wire.push(block, block, partner) for partner in place.row_x()]


def gather_z(wire, place, ref):
    z, c, d = place.z, place.c, place.d

    def part(index):
        return ref.at[c, pl.ds(4 * index, 4)]

    ahead, behind = ring(z, d), ring(z, -d)
    swaps = []
    first = wire.push(part(z), part(z), place.at(z=ahead))
    second = wire.push(part(z), part(z), place.at(z=behind))
    swaps.append(wire.push(part(z), part(z), place.sibling()))
    first.wait_recv()
    third = wire.push(part(behind), part(behind), place.at(z=ahead))
    swaps.append(wire.push(part(behind), part(behind), place.sibling()))
    second.wait_recv()
    swaps.append(wire.push(part(ahead), part(ahead), place.sibling()))
    third.wait_recv()
    opposite = ring(z, 2)
    swaps.append(wire.push(part(opposite), part(opposite), place.sibling()))
    return swaps


def gather_kernel(
    x_ref, c_ref, joint, output, expand, reduce, v_ref,
    w_out, rows_x, rows_c, v_out,
    out_buf, in_buf, whole, v_in, v_x, send, recv,
):
    place = Place()
    wire = Wire(send, recv)
    t, c, z, d = place.t, place.c, place.z, place.d
    greet(place.octet() + place.row_x() + place.row_z())
    for k in range(4):
        out_buf[k, :, 0:128] = joint[:, 128 * k : 128 * k + 128]
        out_buf[k, :, 128:256] = joint[:, 512 + 128 * k : 640 + 128 * k]
        out_buf[k, :, 256:384] = joint[:, 1024 + 128 * k : 1152 + 128 * k]
        out_buf[k, :, 384:896] = output[...]
        out_buf[k, :, 896:1024] = jnp.zeros((4, 128), F32)
        out_buf[4 + k, :, 0:512] = expand[:, 512 * k : 512 * k + 512]
        out_buf[4 + k, :, 512:1024] = reduce[:, 512 * k : 512 * k + 512]
    octet = exchange_octet(wire, place, out_buf, in_buf)
    for k, partner in enumerate(place.octet()):
        octet.append(wire.push(v_ref, v_in.at[place.g], partner))
    ahead, behind = ring(t, d), ring(t, -d)
    first, second = [], []
    for source, rows in ((x_ref, rows_x), (c_ref, rows_c)):
        first.append(wire.push(source, rows.at[t], place.at(t=ahead)))
        second.append(wire.push(source, rows.at[t], place.at(t=behind)))
        rows[t] = source[...]
    in_buf[place.g] = out_buf[place.g]
    v_in[place.g] = v_ref[...]
    arrive(octet)
    for k in range(8):
        whole[4 * k : 4 * k + 4, :] = in_buf[k]

    @pl.when(c == 0)
    def _():
        keys, values = whole[:, 128:256], whole[:, 256:384]
        low = lax.broadcasted_iota(jnp.int32, (32, 128), 1) < 64
        whole[:, 128:256] = jnp.where(low, keys, pltpu.roll(values, 64, 1))
        whole[:, 256:384] = jnp.where(low, pltpu.roll(keys, 64, 1), values)

    w_out[c, place.b] = whole[...].astype(BF)
    total = v_in[0]
    for k in range(1, 8):
        total = total + v_in[k]
    v_x[place.x] = total
    along = gather_x(wire, place, w_out)
    for partner in place.row_x():
        along.append(wire.push(v_x.at[place.x], v_x.at[place.x], partner))
    arrive(along)
    v_out[z] = (v_x[0] + v_x[1]) + (v_x[2] + v_x[3])
    spread = [wire.push(v_out.at[z], v_out.at[z], partner) for partner in place.row_z()]
    arrive(first)
    third = []
    for rows in (rows_x, rows_c):
        third.append(wire.push(rows.at[behind], rows.at[behind], place.at(t=ahead)))
    swaps = gather_z(wire, place, w_out)
    arrive(second)
    arrive(third)
    arrive(spread)
    arrive(swaps)
    wire.drain()


def gather_stage(block_input, cotangent, joint, output, expand, reduce, vec):
    return pl.pallas_call(
        gather_kernel,
        out_shape=(
            shape((2, 16, 32, 1024), BF),
            shape((4, 128, D), BF),
            shape((4, 128, D), BF),
            shape((4, 16, 128), F32),
        ),
        in_specs=[VMEM] * 7,
        out_specs=(VMEM,) * 4,
        scratch_shapes=[
            pltpu.VMEM((8, 4, 1024), F32),
            pltpu.VMEM((8, 4, 1024), F32),
            pltpu.VMEM((32, 1024), F32),
            pltpu.VMEM((8, 16, 128), F32),
            pltpu.VMEM((4, 16, 128), F32),
            pltpu.SemaphoreType.DMA((40,)),
            pltpu.SemaphoreType.DMA((40,)),
        ],
        compiler_params=pltpu.CompilerParams(
            collective_id=1, has_side_effects=True, vmem_limit_bytes=24 << 20
        ),
        name="gather",
    )(block_input, cotangent, joint, output, expand, reduce, vec)


def turn(values, cosine, sine, sign):
    lane = lax.broadcasted_iota(jnp.int32, values.shape, 1)
    lane = lax.rem(lane, 64)
    up = pltpu.roll(values, 120, 1)
    down = pltpu.roll(values, 8, 1)
    crossed = jnp.where(lane < 8, -up, down)
    return values * cosine + crossed * (sine * sign)


def vec_row(v_ref, row):
    return jnp.concatenate([v_ref[k, row : row + 1, :] for k in range(4)], axis=1)


def normalise(rows):
    wide = rows.astype(F32)
    centred = wide - jnp.mean(wide, axis=-1, keepdims=True)
    variance = jnp.mean(centred * centred, axis=-1, keepdims=True)
    rate = lax.rsqrt(variance + norm_epsilon)
    return centred * rate, rate


def project_kernel(
    rows_x, rows_c, w, v, cos, sin,
    normed, qo, kv, feed, row_grad, expand_grad, reduce_grad, hidden_sum,
    q_buf, kv_buf, hidden, pre, send, recv,
):
    place = Place()
    wire = Wire(send, recv)
    x, c, t, d = place.x, place.c, place.t, place.d
    partners = []
    for k in range(1, 8):
        other = lax.rem(place.seq + k, 8)
        partners.append((place.z, other, t))
    greet(partners)
    gain, shift = vec_row(v, 0), vec_row(v, 1)
    q_bias, k_bias, v_bias = v[t, 2:3, :], v[t, 3:4, :], v[t, 4:5, :]
    low_row = lax.broadcasted_iota(jnp.int32, (1, 128), 1) < 64
    pair_bias = (
        jnp.where(low_row, k_bias, pltpu.roll(v_bias, 64, 1)),
        jnp.where(low_row, pltpu.roll(k_bias, 64, 1), v_bias),
    )
    low = lax.broadcasted_iota(jnp.int32, (128, 128), 1) < 64

    def project(i, _):
        normal, _rate = normalise(rows_x[i])
        part = (normal * gain + shift).astype(BF)
        normed[i] = part
        raw = dot(part, w[0, :, :, 0:384].reshape(512, 384))
        out_rows = w[0, pl.ds(4 * t, 4), :, 384:896].reshape(128, 512)
        grad = dot_cols(rows_c[i], out_rows)
        cosine, sine = cos[i], sin[i]
        query = turn(raw[:, 0:128] + q_bias, cosine, sine, 1.0)
        q_buf[0, i] = jnp.where(low, query, pltpu.roll(grad, 64, 1)).astype(BF)
        q_buf[1, i] = jnp.where(low, pltpu.roll(query, 64, 1), grad).astype(BF)
        key_cos = jnp.where(low, cosine, 1.0)
        key_sin = jnp.where(low, sine, 0.0)
        for h in range(2):
            pair = raw[:, 128 + 128 * h : 256 + 128 * h] + pair_bias[h]
            kv_buf[h, i] = turn(pair, key_cos, key_sin, 1.0).astype(BF)
        return 0

    lax.fori_loop(0, 4, project, 0)
    own = place.seq
    swap = wire.push(kv_buf.at[1 - c], kv.at[own], place.sibling())
    first_q = wire.make(q_buf.at[0], qo.at[1], place.at(x=3 - x, c=0))
    second_q = wire.make(q_buf.at[1], qo.at[1], place.at(x=3 - x, c=1))
    near_q = wire.make(q_buf.at[1], qo.at[0], place.at(c=1))

    @pl.when(c == 0)
    def _():
        near_q.start()
        qo[0] = q_buf[0]

    @pl.when(c == 1)
    def _():
        first_q.start()
        second_q.start()

    kv[own] = kv_buf[c]

    def feed_forward(i, sums):
        wide = dot(normed[i], w[1, :, :, 0:512].reshape(512, 512))
        bias = jnp.concatenate([v[k, pl.ds(7 + t, 1), :] for k in range(4)], axis=1)
        wide = wide + bias
        square = wide * wide
        curve = jnp.tanh(0.7978845608 * (wide + 0.044715 * (square * wide)))
        hidden[i] = (0.5 * wide * (1.0 + curve)).astype(BF)
        slope = 0.5 * (1.0 + curve) + (0.5 * 0.7978845608) * wide * (1.0 - curve * curve) * (
            1.0 + (3 * 0.044715) * square
        )
        back = dot(rows_c[i], w[1, :, :, 512:1024].reshape(512, 512))
        grad = (back * slope).astype(BF)
        pre[i] = grad
        return sums + jnp.sum(grad.astype(F32), axis=0, keepdims=True)

    hidden_sum[...] = lax.fori_loop(0, 4, feed_forward, jnp.zeros((1, 512), F32))
    swap.wait_recv()

    def pair(index):
        return kv.at[pl.ds(2 * index, 2)]

    ahead, behind = ring(x, d), ring(x, -d)
    first = wire.push(pair(x), pair(x), place.at(x=ahead))
    second = wire.push(pair(x), pair(x), place.at(x=behind))

    def feed_out(i, _):
        feed[i] = dot_cols(hidden[i], w[1, :, :, 512:1024].reshape(512, 512))
        row_grad[i] = dot_cols(pre[i], w[1, :, :, 0:512].reshape(512, 512))
        return 0

    lax.fori_loop(0, 4, feed_out, 0)
    first.wait_recv()
    third = wire.push(pair(behind), pair(behind), place.at(x=ahead))
    for j in range(4):
        lanes = slice(128 * j, 128 * j + 128)
        reduce_grad[j] = dot_rows(
            rows_c[:, :, lanes].reshape(512, 128), hidden[...].reshape(512, 512)
        ).astype(BF)
        expand_grad[j] = dot_rows(
            normed[:, :, lanes].reshape(512, 128), pre[...].reshape(512, 512)
        ).astype(BF)
    second.wait_recv()
    third.wait_recv()

    @pl.when(c == 0)
    def _():
        near_q.wait_send()
        first_q.wait_recv()

    @pl.when(c == 1)
    def _():
        first_q.wait_send()
        second_q.wait_send()
        near_q.wait_recv()
        second_q.wait_recv()

    wire.drain()


def project_stage(rows_x, rows_c, w, v, cos, sin):
    return pl.pallas_call(
        project_kernel,
        out_shape=(
            shape((4, 128, D), BF),
            shape((2, 4, 128, 128), BF),
            shape((8, 4, 128, 128), BF),
            shape((4, 128, D), F32),
            shape((4, 128, D), F32),
            shape((4, 128, D), BF),
            shape((4, 128, D), BF),
            shape((1, 512), F32),
        ),
        in_specs=[VMEM] * 6,
        out_specs=(VMEM,) * 8,
        scratch_shapes=[
            pltpu.VMEM((2, 4, 128, 128), BF),
            pltpu.VMEM((2, 4, 128, 128), BF),
            pltpu.VMEM((4, 128, D), BF),
            pltpu.VMEM((4, 128, D), BF),
            pltpu.SemaphoreType.DMA((8,)),
            pltpu.SemaphoreType.DMA((8,)),
        ],
        compiler_params=pltpu.CompilerParams(
            collective_id=2, has_side_effects=True, vmem_limit_bytes=32 << 20
        ),
        name="project",
    )(rows_x, rows_c, w, v, cos, sin)


def attention_kernel(lengths, qo, kv, od, dkv, turned, scores, grads, sums):
    x = lax.div(lax.axis_index("seq"), 2)
    low = lax.broadcasted_iota(jnp.int32, (512, 128), 1) < 64
    sums[...] = jnp.zeros_like(sums)
    for k in range(8):
        turned[k] = kv[k].T

    for slot in range(2):
        chunk = 2 * x if slot == 0 else 7 - 2 * x
        packed = qo[slot]
        query = jnp.where(low, packed.astype(F32) * (HD ** -0.5), 0.0).astype(BF)
        out_grad = jnp.where(low, 0.0, packed.astype(F32)).astype(BF)
        index = 512 * chunk + lax.broadcasted_iota(jnp.int32, (1, 512), 1)
        begin = jnp.zeros((1, 512), jnp.int32)
        finish = 0
        for j in range(4):
            finish = finish + lengths[0, j]
            begin = jnp.where(index >= finish, finish, begin)

        def first(k, top):
            raw = dot_cols(kv[k], query)
            key = 512 * k + lax.broadcasted_iota(jnp.int32, (512, 512), 0)
            raw = jnp.where((key <= index) & (key >= begin), raw, masked_score)
            scores[k] = raw
            return jnp.maximum(top, jnp.max(raw, axis=0, keepdims=True))

        top = lax.fori_loop(0, chunk + 1, first, jnp.full((1, 512), masked_score, F32))

        def second(k, total):
            power = jnp.exp(scores[k] - top)
            scores[k] = power
            return total + jnp.sum(power, axis=0, keepdims=True)

        total = lax.fori_loop(0, chunk + 1, second, jnp.zeros((1, 512), F32))
        inverse = 1.0 / total

        def third(k, carry):
            centre, out = carry
            prob = scores[k] * inverse
            scores[k] = prob
            grad = dot_cols(kv[k], out_grad)
            grads[k] = grad
            prob_low = prob.astype(BF)
            out = out + dot(turned[k, 64:128, :], prob_low)
            sums[k] += dot(prob_low, out_grad)
            return centre + jnp.sum(prob * grad, axis=0, keepdims=True), out

        centre, out = lax.fori_loop(
            0, chunk + 1, third, (jnp.zeros((1, 512), F32), jnp.zeros((64, 512), F32))
        )

        def fourth(k, back):
            grad_low = (scores[k] * (grads[k] - centre)).astype(BF)
            sums[k] += dot(grad_low, query)
            return back + dot(turned[k, 0:64, :], grad_low)

        back = lax.fori_loop(0, chunk + 1, fourth, jnp.zeros((64, 512), F32))
        both = jnp.concatenate([out, back * (HD ** -0.5)], axis=0)
        od[slot] = both.T.astype(BF)
    dkv[...] = sums[...].astype(BF)


def attention_stage(lengths, qo, kv):
    return pl.pallas_call(
        attention_kernel,
        out_shape=(shape((2, 512, 128), BF), shape((8, 512, 128), BF)),
        in_specs=[SMEM, VMEM, VMEM],
        out_specs=(VMEM,) * 2,
        scratch_shapes=[
            pltpu.VMEM((8, 128, 512), BF),
            pltpu.VMEM((8, 512, 512), F32),
            pltpu.VMEM((8, 512, 512), F32),
            pltpu.VMEM((8, 512, 128), F32),
        ],
        compiler_params=pltpu.CompilerParams(vmem_limit_bytes=44 << 20),
        name="attention",
    )(lengths, qo, kv)


def backward_kernel(
    od, dkv, normed, rows_x, rows_c, w, v, cos, sin, feed, row_grad, expand_grad, reduce_grad,
    hidden_sum,
    grads, out_part, back_part, vec_part,
    od_in, near, mid, far, keep, give, took, pair_out, joint_out, out_cols, out_in, send, recv,
):
    place = Place()
    wire = Wire(send, recv)
    x, c, t, d = place.x, place.c, place.t, place.d
    partners = []
    for k in range(1, 8):
        partners.append((place.z, lax.rem(place.seq + k, 8), t))
    greet(partners + place.row_t())
    ahead, behind, opposite = ring(x, d), ring(x, -d), ring(x, 2)

    def pair(index):
        return dkv.at[pl.ds(2 * index, 2)]

    first = wire.push(pair(opposite), near, place.at(x=ahead))
    second = wire.push(pair(behind), far, place.at(x=behind))
    near_o = wire.make(od.at[0], od_in.at[1], place.at(c=0))
    first_o = wire.make(od.at[1], od_in.at[0], place.at(x=3 - x, c=1))
    second_o = wire.make(od.at[1], od_in.at[1], place.at(x=3 - x, c=1))

    @pl.when(c == 0)
    def _():
        first_o.start()
        od_in[0] = od[0]

    @pl.when(c == 1)
    def _():
        near_o.start()
        second_o.start()

    first.wait_recv()
    mid[...] = (near[...].astype(F32) + dkv[pl.ds(2 * ahead, 2)].astype(F32)).astype(BF)
    third = wire.push(mid, keep, place.at(x=ahead))

    @pl.when(c == 0)
    def _():
        first_o.wait_send()
        near_o.wait_recv()

    @pl.when(c == 1)
    def _():
        near_o.wait_send()
        second_o.wait_send()
        first_o.wait_recv()
        second_o.wait_recv()

    low = lax.broadcasted_iota(jnp.int32, (128, 128), 1) < 64
    for i in range(4):
        rows = pl.ds(128 * i, 128)
        left = od_in[0, rows, :].astype(F32)
        right = od_in[1, rows, :].astype(F32)
        joined = jnp.where(low, left, pltpu.roll(right, 64, 1)).astype(BF)
        pair_out[rows, :] = joined
        back = jnp.where(low, pltpu.roll(left, 64, 1), right)
        joint_out[rows, 0:128] = turn(back, cos[i], sin[i], -1.0).astype(BF)
        out_rows = w[0, pl.ds(4 * t, 4), :, 384:896].reshape(128, 512)
        out_part[i] = (feed[i] + dot(joined, out_rows)).astype(BF)
    for j in range(4):
        part = rows_c[:, :, 128 * j : 128 * j + 128].reshape(512, 128)
        out_cols[j] = dot_rows(pair_out[...], part).astype(BF)
    out_in[t] = out_cols[t]
    trade = []
    for k in range(1, 4):
        goal = lax.rem(t + k, 4)
        trade.append(wire.push(out_cols.at[goal], out_in.at[t], place.at(t=goal)))
    for j in range(4):
        grads[1, 4 * j : 4 * j + 4, :, 0:512] = expand_grad[j].reshape(4, 32, 512)
        grads[1, 4 * j : 4 * j + 4, :, 512:768] = reduce_grad[j, :, 256:512].reshape(4, 32, 256)
        grads[0, 4 * j : 4 * j + 4, :, 512:768] = reduce_grad[j, :, 0:256].reshape(4, 32, 256)
    second.wait_recv()
    third.wait_recv()
    other = 1 - c
    give[...] = (
        dkv[2 * x + other].astype(F32) + far[other].astype(F32) + keep[other].astype(F32)
    ).astype(BF)
    swap = wire.push(give, took.at[c], place.sibling())
    took[c] = (
        dkv[2 * x + c].astype(F32) + far[c].astype(F32) + keep[c].astype(F32)
    ).astype(BF)
    swap.wait_recv()
    for h in range(2):
        for i in range(4):
            rows = pl.ds(128 * i, 128)
            part = took[h, rows, :].astype(F32)
            key_cos = jnp.where(low, cos[i], 1.0)
            key_sin = jnp.where(low, sin[i], 0.0)
            joint_out[rows, 128 + 128 * h : 256 + 128 * h] = turn(
                part, key_cos, key_sin, -1.0
            ).astype(BF)
    for j in range(4):
        part = normed[:, :, 128 * j : 128 * j + 128].reshape(512, 128)
        grads[0, 4 * j : 4 * j + 4, :, 0:384] = (
            dot_rows(part, joint_out[...]).astype(BF).reshape(4, 32, 384)
        )
    vec_part[...] = jnp.zeros_like(vec_part)
    shift_sum = jnp.zeros((1, 512), F32)
    gain_sum = jnp.zeros((1, 512), F32)
    for i in range(4):
        rows = pl.ds(128 * i, 128)
        part = row_grad[i] + dot_cols(
            joint_out[rows, :], w[0, :, :, 0:384].reshape(512, 384)
        )
        back_part[i] = part.astype(BF)
        normal, _rate = normalise(rows_x[i])
        shift_sum = shift_sum + jnp.sum(part, axis=0, keepdims=True)
        gain_sum = gain_sum + jnp.sum(part * normal, axis=0, keepdims=True)
    out_sum = jnp.sum(rows_c[t].astype(F32), axis=0, keepdims=True)
    joint_sum = jnp.sum(joint_out[...].astype(F32), axis=0, keepdims=True)
    one, two = joint_sum[:, 128:256], joint_sum[:, 256:384]
    low_row = lax.broadcasted_iota(jnp.int32, (1, 128), 1) < 64
    for k in range(4):
        lanes = slice(128 * k, 128 * k + 128)
        vec_part[k, 0:1, :] = gain_sum[:, lanes]
        vec_part[k, 1:2, :] = shift_sum[:, lanes]
        vec_part[k, 5:6, :] = out_sum[:, lanes]
        vec_part[k, 6:7, :] = out_sum[:, lanes]
        vec_part[k, pl.ds(7 + t, 1), :] = hidden_sum[:, lanes]
    vec_part[t, 2:3, :] = joint_sum[:, 0:128]
    vec_part[t, 3:4, :] = jnp.where(low_row, one, pltpu.roll(two, 64, 1))
    vec_part[t, 4:5, :] = jnp.where(low_row, pltpu.roll(one, 64, 1), two)
    arrive(trade)
    for j in range(4):
        grads[0, 4 * j : 4 * j + 4, :, 384:512] = out_in[j].reshape(4, 32, 128)
    wire.drain()


def backward_stage(*arrays):
    return pl.pallas_call(
        backward_kernel,
        out_shape=(
            shape((2, 16, 32, 768), BF),
            shape((4, 128, D), BF),
            shape((4, 128, D), BF),
            shape((4, 16, 128), F32),
        ),
        in_specs=[VMEM] * 14,
        out_specs=(VMEM,) * 4,
        scratch_shapes=[
            pltpu.VMEM((2, 512, 128), BF),
            pltpu.VMEM((2, 512, 128), BF),
            pltpu.VMEM((2, 512, 128), BF),
            pltpu.VMEM((2, 512, 128), BF),
            pltpu.VMEM((2, 512, 128), BF),
            pltpu.VMEM((512, 128), BF),
            pltpu.VMEM((2, 512, 128), BF),
            pltpu.VMEM((512, 128), BF),
            pltpu.VMEM((512, 384), BF),
            pltpu.VMEM((4, 128, 128), BF),
            pltpu.VMEM((4, 128, 128), BF),
            pltpu.SemaphoreType.DMA((12,)),
            pltpu.SemaphoreType.DMA((12,)),
        ],
        compiler_params=pltpu.CompilerParams(
            collective_id=3, has_side_effects=True, vmem_limit_bytes=40 << 20
        ),
        name="backward",
    )(*arrays)


def reduce_kernel(
    grads, out_part, back_part, vec_part, x_ref, c_ref, v, m_joint, m_output, m_expand, m_reduce,
    g_joint, g_output, g_expand, g_reduce, n_joint, n_output, n_expand, n_reduce,
    block_output, input_grad, vec_sum, moments,
    core_in, chip, near, mid, far, keep, x_out, x_in, out_buf, in_buf, out_in, back_in,
    v_core, v_acc, v_z, v_x, v_t, send, recv,
):
    place = Place()
    wire = Wire(send, recv)
    z, x, c, t, d = place.z, place.x, place.c, place.t, place.d
    greet(place.octet() + place.row_x() + place.row_z())
    sibling = place.sibling()
    ahead, behind, opposite = ring(z, d), ring(z, -d), ring(z, 2)

    def part(ref, index):
        return ref.at[pl.ds(4 * index, 4)]

    handed = []
    for index in (opposite, ahead, behind, z):
        handed.append(
            wire.push(grads.at[1 - c, pl.ds(4 * index, 4)], part(core_in, index), sibling)
        )
    v_swap = wire.push(vec_part, v_core, sibling)
    swaps = []
    for k in range(1, 4):
        goal = lax.rem(t + k, 4)
        swaps.append(wire.push(back_part.at[goal], back_in.at[k - 1], place.at(t=goal)))
        swaps.append(wire.push(out_part.at[goal], out_in.at[k - 1], place.at(t=goal)))

    def chip_sum(index):
        rows = pl.ds(4 * index, 4)
        return grads[c, rows].astype(F32) + core_in[rows].astype(F32)

    handed[0].wait_recv()
    chip[0] = chip_sum(opposite).astype(BF)
    first = wire.push(chip.at[0], near, place.at(z=ahead))
    handed[1].wait_recv()
    chip[1] = chip_sum(behind).astype(BF)
    second = wire.push(chip.at[1], far, place.at(z=behind))
    v_swap.wait_recv()
    v_acc[0] = vec_part[...] + v_core[...]
    v_first = [wire.push(v_acc.at[0], v_z.at[k], p) for k, p in enumerate(place.row_z())]
    handed[2].wait_recv()
    first.wait_recv()
    mid[...] = (near[...].astype(F32) + chip_sum(ahead)).astype(BF)
    third = wire.push(mid, keep, place.at(z=ahead))
    arrive(v_first)
    v_acc[1] = (v_acc[0] + v_z[0]) + (v_z[1] + v_z[2])
    v_second = [wire.push(v_acc.at[1], v_x.at[k], p) for k, p in enumerate(place.row_x())]
    handed[3].wait_recv()
    second.wait_recv()
    partial = chip_sum(z) + far[...].astype(F32)
    third.wait_recv()
    x_sum = partial + keep[...].astype(F32)
    x_out[...] = x_sum.astype(BF)
    along = []
    for k in range(1, 4):
        goal = lax.rem(x + k, 4)
        along.append(wire.push(x_out.at[goal], x_in.at[k - 1], place.at(x=goal)))
    arrive(v_second)
    v_acc[2] = (v_acc[1] + v_x[0]) + (v_x[1] + v_x[2])
    v_third = [wire.push(v_acc.at[2], v_t.at[k], p) for k, p in enumerate(place.row_t())]
    arrive(along)
    own = x_out[x].astype(F32)
    for k in range(3):
        own = own + x_in[k].astype(F32)
    for k in range(8):
        out_buf[k] = own[4 * k : 4 * k + 4, :]
    octet = exchange_octet(wire, place, out_buf, in_buf)
    in_buf[place.g] = out_buf[place.g]

    arrive(swaps)
    wide = x_ref[...].astype(F32)
    feed = out_part[t].astype(F32)
    back = back_part[t].astype(F32)
    for k in range(3):
        feed = feed + out_in[k].astype(F32)
        back = back + back_in[k].astype(F32)
    block_output[...] = (wide + feed + vec_row(v, 5) + vec_row(v, 6)).astype(BF)
    normal, rate = normalise(x_ref[...])
    scaled = back * vec_row(v, 0)
    mean_one = jnp.mean(scaled, axis=-1, keepdims=True)
    mean_two = jnp.mean(scaled * normal, axis=-1, keepdims=True)
    input_grad[...] = c_ref[...].astype(F32) + rate * (scaled - mean_one - normal * mean_two)

    arrive(octet)
    for k in range(4):
        lanes = slice(128 * k, 128 * k + 128)
        first_kind, second_kind = in_buf[k], in_buf[4 + k]
        g_joint[:, lanes] = first_kind[:, 0:128]
        one, two = first_kind[:, 128:256], first_kind[:, 256:384]
        g_joint[:, 512 + 128 * k : 640 + 128 * k] = jnp.concatenate(
            [one[:, 0:64], two[:, 0:64]], axis=1
        )
        g_joint[:, 1024 + 128 * k : 1152 + 128 * k] = jnp.concatenate(
            [one[:, 64:128], two[:, 64:128]], axis=1
        )
        g_output[:, lanes] = first_kind[:, 384:512]
        g_expand[:, 512 * k : 512 * k + 512] = second_kind[:, 0:512]
        g_reduce[:, 512 * k : 512 * k + 256] = first_kind[:, 512:768]
        g_reduce[:, 512 * k + 256 : 512 * k + 512] = second_kind[:, 512:768]
    moments[...] = jnp.zeros_like(moments)
    for k, (old, grad, new) in enumerate(
        (
            (m_joint, g_joint, n_joint),
            (m_output, g_output, n_output),
            (m_expand, g_expand, n_expand),
            (m_reduce, g_reduce, n_reduce),
        )
    ):
        value = muon_beta * old[...] + grad[...]
        new[...] = value
        width = min(WIDTHS[k], 1024)
        moments[k, :, 0:width] = value[:, 0:width]
        if WIDTHS[k] > 1024:
            moments[4 + k, :, 0 : WIDTHS[k] - 1024] = value[:, 1024:]
    arrive(v_third)
    vec_sum[...] = (v_acc[2] + v_t[0]) + (v_t[1] + v_t[2])
    wire.drain()


def reduce_stage(*arrays):
    narrow = [shape((4, width), F32) for width in WIDTHS]
    block = pltpu.VMEM((4, 32, 768), BF)
    return pl.pallas_call(
        reduce_kernel,
        out_shape=(
            *narrow,
            *narrow,
            shape((128, D), BF),
            shape((128, D), F32),
            shape((4, 16, 128), F32),
            shape((8, 4, 1024), F32),
        ),
        in_specs=[VMEM] * 11,
        out_specs=(VMEM,) * 12,
        scratch_shapes=[
            pltpu.VMEM((16, 32, 768), BF),
            pltpu.VMEM((2, 4, 32, 768), BF),
            block,
            block,
            block,
            block,
            block,
            pltpu.VMEM((3, 32, 768), BF),
            pltpu.VMEM((8, 4, 768), F32),
            pltpu.VMEM((8, 4, 768), F32),
            pltpu.VMEM((3, 128, D), BF),
            pltpu.VMEM((3, 128, D), BF),
            pltpu.VMEM((4, 16, 128), F32),
            pltpu.VMEM((3, 4, 16, 128), F32),
            pltpu.VMEM((3, 4, 16, 128), F32),
            pltpu.VMEM((3, 4, 16, 128), F32),
            pltpu.VMEM((3, 4, 16, 128), F32),
            pltpu.SemaphoreType.DMA((40,)),
            pltpu.SemaphoreType.DMA((40,)),
        ],
        compiler_params=pltpu.CompilerParams(
            collective_id=4, has_side_effects=True, vmem_limit_bytes=32 << 20
        ),
        name="reduce",
    )(*arrays)


def halves(values):
    high = values.astype(BF)
    return high, (values - high.astype(F32)).astype(BF)


def muon_kernel(
    moments, w_joint, w_output, w_expand, w_reduce,
    u_joint, u_output, u_expand, u_reduce,
    in_buf, whole, momentum, gram, gram_h, gram_l, poly_h, poly_l, temp_h, temp_l, out_buf, back_buf,
    send, recv,
):
    place = Place()
    wire = Wire(send, recv)
    c = place.c
    greet(place.octet() + place.row_x() + place.row_z())
    octet = exchange_octet(wire, place, moments, in_buf)
    in_buf[place.g] = moments[place.g]
    arrive(octet)
    for k in range(8):
        whole[4 * k : 4 * k + 4, :] = in_buf[k]
    momentum[c, place.b] = whole[...].astype(BF)
    arrive(gather_x(wire, place, momentum))
    arrive(gather_z(wire, place, momentum))

    def flat(ref):
        return ref[...].reshape(512, 512)

    def block(ref, i):
        return ref[pl.ds(4 * i, 4)].reshape(128, 512)

    def fill(i, total):
        rows = pl.ds(4 * i, 4)
        value = jnp.zeros((128, 512), F32)
        for k in range(2):
            value = value + dot_cols(
                momentum[k, rows].reshape(128, 1024), momentum[k].reshape(512, 1024)
            )
        gram[rows] = value.reshape(4, 32, 512)
        row = 128 * i + lax.broadcasted_iota(jnp.int32, (128, 512), 0)
        column = lax.broadcasted_iota(jnp.int32, (128, 512), 1)
        return total + jnp.sum(jnp.where(row == column, value, 0.0), keepdims=True)

    total = lax.fori_loop(0, 4, fill, jnp.zeros((1, 1), F32))
    scale = 1.0 / (jnp.sqrt(total) + 1e-07)

    def prepare(i, _):
        rows = pl.ds(4 * i, 4)
        value = block(gram, i) * (scale * scale)
        gram[rows] = value.reshape(4, 32, 512)
        high, small = halves(value)
        gram_h[rows] = high.reshape(4, 32, 512)
        gram_l[rows] = small.reshape(4, 32, 512)
        return 0

    lax.fori_loop(0, 4, prepare, 0)

    def product(left_h, left_l, right_h, right_l):
        return dot(left_h, right_h) + (dot(left_h, right_l) + dot(left_l, right_h))

    def polynomial(i, _):
        rows = pl.ds(4 * i, 4)
        square = product(block(gram_h, i), block(gram_l, i), flat(gram_h), flat(gram_l))
        row = 128 * i + lax.broadcasted_iota(jnp.int32, (128, 512), 0)
        column = lax.broadcasted_iota(jnp.int32, (128, 512), 1)
        value = (
            jnp.where(row == column, newton_first, 0.0)
            + newton_second * block(gram, i)
            + newton_third * square
        )
        high, small = halves(value)
        poly_h[rows] = high.reshape(4, 32, 512)
        poly_l[rows] = small.reshape(4, 32, 512)
        return 0

    def inner(i, _):
        rows = pl.ds(4 * i, 4)
        value = product(block(gram_h, i), block(gram_l, i), flat(poly_h), flat(poly_l))
        high, small = halves(value)
        temp_h[rows] = high.reshape(4, 32, 512)
        temp_l[rows] = small.reshape(4, 32, 512)
        return 0

    def outer(i, _):
        rows = pl.ds(4 * i, 4)
        value = product(block(temp_h, i), block(temp_l, i), flat(poly_h), flat(poly_l))
        gram[rows] = value.reshape(4, 32, 512)
        high, small = halves(value)
        gram_h[rows] = high.reshape(4, 32, 512)
        gram_l[rows] = small.reshape(4, 32, 512)
        return 0

    def times(left, right_h, right_l):
        high, small = halves(left)
        return product(high, small, flat(right_h), flat(right_l))

    own = None
    for sweep in range(4):
        lax.fori_loop(0, 4, polynomial, 0)
        if sweep == 0:
            own = poly_h[place.b].astype(F32) + poly_l[place.b].astype(F32)
        else:
            own = times(own, poly_h, poly_l)
        if sweep < 3:
            lax.fori_loop(0, 4, inner, 0)
            lax.fori_loop(0, 4, outer, 0)

    def last_gram(left):
        left = times(left, gram_h, gram_l)
        left = times(left, poly_h, poly_l)
        return times(left, poly_h, poly_l)

    once = last_gram(own)
    own = newton_first * own + newton_second * once + newton_third * last_gram(once)
    high, small = halves(own * scale)
    columns = momentum[c].reshape(512, 1024)
    result = dot(high, columns) + dot(small, columns)
    for k in range(8):
        out_buf[k] = result[4 * k : 4 * k + 4, :]
    octet = exchange_octet(wire, place, out_buf, back_buf)
    back_buf[place.g] = out_buf[place.g]
    arrive(octet)
    for k, (old, new) in enumerate(
        ((w_joint, u_joint), (w_output, u_output), (w_expand, u_expand), (w_reduce, u_reduce))
    ):
        factor = muon_rate * 0.2 * math.sqrt(max(D, WIDTHS[k]))
        for half in range(2):
            start = 1024 * half
            stop = min(WIDTHS[k], start + 1024)
            if stop > start:
                new[:, start:stop] = (
                    old[:, start:stop] * (1.0 - muon_rate * muon_decay)
                    - factor * back_buf[4 * half + k, :, 0 : stop - start]
                )
    wire.drain()


def muon_stage(*arrays):
    square = pltpu.VMEM((16, 32, 512), BF)
    return pl.pallas_call(
        muon_kernel,
        out_shape=tuple(shape((4, width), F32) for width in WIDTHS),
        in_specs=[VMEM] * 5,
        out_specs=(VMEM,) * 4,
        scratch_shapes=[
            pltpu.VMEM((8, 4, 1024), F32),
            pltpu.VMEM((32, 1024), F32),
            pltpu.VMEM((2, 16, 32, 1024), BF),
            pltpu.VMEM((16, 32, 512), F32),
            square,
            square,
            square,
            square,
            square,
            square,
            pltpu.VMEM((8, 4, 1024), F32),
            pltpu.VMEM((8, 4, 1024), F32),
            pltpu.SemaphoreType.DMA((32,)),
            pltpu.SemaphoreType.DMA((32,)),
        ],
        compiler_params=pltpu.CompilerParams(
            collective_id=5, has_side_effects=True, vmem_limit_bytes=32 << 20
        ),
        name="muon",
    )(*arrays)


def tables(lengths, seq):
    index = 512 * seq + jnp.arange(512, dtype=jnp.int32)
    finish = jnp.cumsum(lengths, dtype=jnp.int32)
    passed = index[:, None] >= finish[None, :]
    starts = jnp.sum(jnp.where(passed, lengths[None, :], 0), axis=1, dtype=jnp.int32)
    position = (index - starts).astype(F32)
    half = ROT // 2
    frequency = 10000.0 ** (-(jnp.arange(half, dtype=F32) * 2.0) / ROT)
    head = jnp.concatenate([frequency, frequency, jnp.zeros((HD - ROT,), F32)])
    angle = position[:, None] * jnp.concatenate([head, head])[None, :]
    return jnp.cos(angle).reshape(4, 128, 128), jnp.sin(angle).reshape(4, 128, 128)


def shards(
    block_input,
    cotangent,
    doc_lengths,
    joint_weight,
    output_weight,
    expand_weight,
    reduce_weight,
    joint_moment,
    output_moment,
    expand_moment,
    reduce_moment,
    vectors,
    first_moment,
    second_moment,
):
    z = lax.axis_index("fsdp")
    seq = lax.axis_index("seq")
    t = lax.axis_index("tensor")
    place = 16 * seq + 4 * t
    cos, sin = tables(doc_lengths[0], seq)
    vec = lax.dynamic_update_slice(
        jnp.zeros((16, 128), F32), vectors.astype(BF).astype(F32), (0, place)
    )
    w, rows_x, rows_c, v = gather_stage(
        block_input, cotangent, joint_weight, output_weight, expand_weight, reduce_weight, vec
    )
    normed, qo, kv, feed, row_grad, expand_grad, reduce_grad, hidden_sum = project_stage(
        rows_x, rows_c, w, v, cos, sin
    )
    od, dkv = attention_stage(doc_lengths, qo.reshape(2, 512, 128), kv.reshape(8, 512, 128))
    grads, out_part, back_part, vec_part = backward_stage(
        od, dkv, normed, rows_x, rows_c, w, v, cos, sin, feed, row_grad, expand_grad, reduce_grad,
        hidden_sum,
    )
    reduced = reduce_stage(
        grads, out_part, back_part, vec_part, block_input, cotangent, v,
        joint_moment, output_moment, expand_moment, reduce_moment,
    )
    gradients, momenta = reduced[0:4], reduced[4:8]
    block_output, input_grad, vec_sum, moments = reduced[8:]
    updated = muon_stage(moments, joint_weight, output_weight, expand_weight, reduce_weight)
    vector_grad = lax.dynamic_slice(vec_sum, (z, 0, place), (1, 11, 4)).reshape(11, 4)
    first_next = beta_first * first_moment + (1.0 - beta_first) * vector_grad
    second_next = beta_second * second_moment + (1.0 - beta_second) * vector_grad * vector_grad
    first_hat = first_next / (1.0 - beta_first**STEP)
    second_hat = second_next / (1.0 - beta_second**STEP)
    vector_next = vectors - vector_rate * first_hat / (jnp.sqrt(second_hat) + adam_epsilon)
    return (
        block_output,
        input_grad,
        *gradients,
        *momenta,
        *updated,
        vector_grad,
        second_next,
        vector_next,
    )


def solution(mesh):
    rows = P(("fsdp", "seq", "tensor"), None)
    columns = P(None, ("fsdp", "seq", "tensor"))
    return jax.shard_map(
        shards,
        mesh=mesh,
        in_specs=(rows, rows, P("fsdp", None)) + (rows,) * 8 + (columns,) * 3,
        out_specs=(rows,) * 14 + (columns,) * 3,
        check_vma=False,
    )
```

```python
import math

import jax
import jax.numpy as jnp
from jax import lax
from jax.experimental import pallas as pl
from jax.experimental.pallas import tpu as pltpu
from jax.sharding import PartitionSpec as P

D = 512
HEADS = 8
FF = 2048
ROT = 16
HD = 64
STEP = 10

norm_epsilon = 1e-05
masked_score = -1e30
newton_first = 3.4445
newton_second = -4.775
newton_third = 2.0315
beta_first = 0.9
beta_second = 0.95
adam_epsilon = 1e-08
vector_rate = 0.2
muon_rate = 0.25
muon_beta = 0.95
muon_decay = 0.01
LOG2_E = 1.4426950408889634

BF = jnp.bfloat16
F32 = jnp.float32
MESH = pl.DeviceIdType.MESH
VMEM = pl.BlockSpec(memory_space=pltpu.VMEM)
SMEM = pl.BlockSpec(memory_space=pltpu.SMEM)
ANY = pl.BlockSpec(memory_space=pl.ANY)
WIDTHS = (3 * D, D, FF, FF)


def shape(dims, dtype):
    return jax.ShapeDtypeStruct(dims, dtype)


class Place:
    def __init__(self):
        self.z = lax.axis_index("fsdp")
        self.seq = lax.axis_index("seq")
        self.t = lax.axis_index("tensor")
        self.x = lax.div(self.seq, 2)
        self.c = lax.rem(self.seq, 2)
        self.d = 1 - 2 * self.c
        self.a = self.c * self.x + (1 - self.c) * self.z
        self.b = self.c * self.z + (1 - self.c) * self.x
        self.mate = self.x + 1 - 2 * lax.rem(self.x, 2)
        self.cross = 3 - self.x
        self.head = lax.div(self.x, 2)

    def at(self, z=None, x=None, c=None, t=None):
        z = self.z if z is None else z
        x = self.x if x is None else x
        c = self.c if c is None else c
        t = self.t if t is None else t
        return (z, 2 * x + c, t)

    def at_a(self, a):
        c = self.c
        return self.at(z=(1 - c) * a + c * self.z, x=c * a + (1 - c) * self.x)

    def at_b(self, b):
        c = self.c
        return self.at(z=c * b + (1 - c) * self.z, x=(1 - c) * b + c * self.x)

    def sibling(self):
        return self.at(c=1 - self.c)

    def octet(self):
        g = 4 * self.c + self.t
        members = [lax.rem(g + k, 8) for k in range(1, 8)]
        return [self.at(c=lax.div(m, 4), t=lax.rem(m, 4)) for m in members]

    def row_x(self):
        return [self.at(x=lax.rem(self.x + k, 4)) for k in range(1, 4)]

    def row_z(self):
        return [self.at(z=lax.rem(self.z + k, 4)) for k in range(1, 4)]

    def row_t(self):
        return [self.at(t=lax.rem(self.t + k, 4)) for k in range(1, 4)]


def ring(index, step):
    return lax.rem(index + step + 4, 4)


def greet(partners):
    barrier = pltpu.get_barrier_semaphore()
    for partner in partners:
        pl.semaphore_signal(barrier, inc=1, device_id=partner, device_id_type=MESH)
    return lambda: pl.semaphore_wait(barrier, len(partners))


class Wire:
    def __init__(self, send, recv, local):
        self.send = send
        self.recv = recv
        self.local = local
        self.count = 0
        self.loads = 0
        self.open = []

    def push(self, src, dst, device):
        index = self.count
        self.count += 1
        copy = pltpu.make_async_remote_copy(
            src_ref=src,
            dst_ref=dst,
            send_sem=self.send.at[index],
            recv_sem=self.recv.at[index],
            device_id=device,
            device_id_type=MESH,
        )
        copy.start()
        self.open.append(copy)
        return copy

    def load(self, src, dst):
        copy = pltpu.make_async_copy(src, dst, self.local.at[self.loads])
        self.loads += 1
        copy.start()
        return copy

    def drain(self):
        for copy in self.open:
            copy.wait_send()


def arrive(copies):
    for copy in copies:
        copy.wait_recv()


def dot(left, right):
    return jnp.dot(left, right, preferred_element_type=F32)


def dot_cols(left, right):
    return lax.dot_general(left, right, (((1,), (1,)), ((), ())), preferred_element_type=F32)


def dot_rows(left, right):
    return lax.dot_general(left, right, (((0,), (0,)), ((), ())), preferred_element_type=F32)


def turn(values, cosine, sine, sign):
    lane = lax.rem(lax.broadcasted_iota(jnp.int32, values.shape, 1), 64)
    crossed = jnp.where(lane < 8, -pltpu.roll(values, 120, 1), pltpu.roll(values, 8, 1))
    return values * cosine + crossed * (sine * sign)


def vec_row(v_ref, row):
    return jnp.concatenate([v_ref[k, row : row + 1, :] for k in range(4)], axis=1)


def normalise(rows):
    wide = rows.astype(F32)
    centred = wide - jnp.mean(wide, axis=-1, keepdims=True)
    variance = jnp.mean(centred * centred, axis=-1, keepdims=True)
    rate = lax.rsqrt(variance + norm_epsilon)
    return centred * rate, rate


def halves(values):
    high = values.astype(BF)
    return high, (values - high.astype(F32)).astype(BF)


def product(left_h, left_l, right_h, right_l):
    return dot(left_h, right_h) + (dot(left_h, right_l) + dot(left_l, right_h))


def spread_b(wire, place, ref):
    block = ref.at[place.c, place.a, place.b]
    return [wire.push(block, block, place.at_b(ring(place.b, k))) for k in range(1, 4)]


def spread_a(wire, place, ref):
    block = ref.at[place.c, place.a]
    return [wire.push(block, block, place.at_a(ring(place.a, k))) for k in range(1, 4)]


def ring_open(wire, place, ref):
    ups, downs = {}, {}
    for p, q in ((0, 2), (1, 3), (2, 0), (3, 1)):
        block = ref.at[place.c, place.a, p]
        ups[p] = wire.push(block, block, place.at_a(ring(place.a, 1)))
        block = ref.at[place.c, place.a, q]
        downs[q] = wire.push(block, block, place.at_a(ring(place.a, -1)))
    return ups, downs


def ring_pass(wire, place, ref, ups, downs):
    more = []
    for p, q in ((0, 2), (1, 3)):
        ups[p].wait_recv()
        block = ref.at[place.c, ring(place.a, -1), p]
        more.append(wire.push(block, block, place.at_a(ring(place.a, 1))))
        downs[q].wait_recv()
        block = ref.at[place.c, ring(place.a, 1), q]
        more.append(wire.push(block, block, place.at_a(ring(place.a, -1))))
    return more


def swap_part(wire, place, ref, step):
    block = ref.at[place.c, ring(place.a, step)]
    return wire.push(block, block, place.sibling())


def ring_close(wire, place, ref, ups, downs, more):
    arrive([ups[2], ups[3]])
    swaps = [swap_part(wire, place, ref, -1)]
    arrive([downs[0], downs[1]])
    swaps.append(swap_part(wire, place, ref, 1))
    arrive(more)
    swaps.append(swap_part(wire, place, ref, 2))
    return swaps


def swap_cores(wire, place, ref):
    return wire.push(ref.at[place.c], ref.at[place.c], place.sibling())


def natural(source, target, start, stop):
    for z in range(4):
        for x in range(4):
            target[8 * z + 2 * x] = source[0, z, x, :, start:stop]
            target[8 * z + 2 * x + 1] = source[1, x, z, :, start:stop]


def by_owner(target, z, rows, start, stop):
    for x in range(4):
        target[0, z, x, :, start:stop] = rows[32 * x : 32 * x + 16, :]
        target[1, x, z, :, start:stop] = rows[32 * x + 16 : 32 * x + 32, :]


def sum_cores(wire, place, ref, target):
    return wire.push(ref.at[1 - place.c], target, place.sibling())


def scatter_a(wire, place, ref, target):
    copies = []
    for k in range(1, 4):
        goal = ring(place.a, k)
        copies.append(wire.push(ref.at[goal], target.at[k - 1], place.at_a(goal)))
    return copies


def scatter_b(wire, place, ref, target):
    copies = []
    for k in range(1, 4):
        goal = ring(place.b, k)
        copies.append(wire.push(ref.at[goal], target.at[k - 1], place.at_b(goal)))
    return copies


def trade_t(wire, place, source, target):
    copies = []
    for k in range(1, 4):
        goal = ring(place.t, k)
        copies.append(wire.push(source.at[goal], target.at[place.t], place.at(t=goal)))
    return copies


def total(first, parts):
    value = first.astype(F32)
    for k in range(3):
        value = value + parts[k].astype(F32)
    return value


def unpair(target, part, k):
    one, two = part[:, 128:256], part[:, 256:384]
    target[:, 128 * k : 128 * k + 128] = part[:, 0:128]
    target[:, 512 + 128 * k : 640 + 128 * k] = jnp.concatenate(
        [one[:, 0:64], two[:, 0:64]], axis=1
    )
    target[:, 1024 + 128 * k : 1152 + 128 * k] = jnp.concatenate(
        [one[:, 64:128], two[:, 64:128]], axis=1
    )


INPUTS = (
    "lengths",
    "x",
    "c",
    "joint",
    "output",
    "expand",
    "reduce",
    "vectors",
    "m_joint",
    "m_output",
    "m_expand",
    "m_reduce",
    "first",
    "second",
)

OUTPUTS = (
    ("g_joint", (4, 1536), F32),
    ("g_output", (4, 512), F32),
    ("g_expand", (4, 2048), F32),
    ("g_reduce", (4, 2048), F32),
    ("n_joint", (4, 1536), F32),
    ("n_output", (4, 512), F32),
    ("n_expand", (4, 2048), F32),
    ("n_reduce", (4, 2048), F32),
    ("u_joint", (4, 1536), F32),
    ("u_output", (4, 512), F32),
    ("u_expand", (4, 2048), F32),
    ("u_reduce", (4, 2048), F32),
    ("block_output", (128, 512), BF),
    ("input_grad", (128, 512), F32),
    ("vector_grad", (4, 11), F32),
    ("second_next", (4, 11), F32),
    ("vector_next", (4, 11), F32),
)

SCRATCH = (
    ("joint_v", (4, 1536), F32),
    ("output_v", (4, 512), F32),
    ("expand_v", (4, 2048), F32),
    ("reduce_v", (4, 2048), F32),
    ("vectors_v", (4, 11), F32),
    ("first_v", (4, 11), F32),
    ("second_v", (4, 11), F32),
    ("table", (128, 128), F32),
    ("vec_sum", (4, 16, 128), F32),
    ("m_joint_v", (4, 1536), F32),
    ("m_output_v", (4, 512), F32),
    ("m_expand_v", (4, 2048), F32),
    ("m_reduce_v", (4, 2048), F32),
    ("w_out", (4, 4, 1920), F32),
    ("w_in", (4, 4, 1920), F32),
    ("w_rows", (16, 1920), F32),
    ("wj", (2, 4, 4, 16, 384), BF),
    ("wr", (2, 4, 4, 16, 1536), BF),
    ("w_joint", (32, 16, 384), BF),
    ("w_output", (32, 16, 512), BF),
    ("w_expand", (32, 16, 512), BF),
    ("w_reduce", (32, 16, 512), BF),
    ("v_own", (16, 128), F32),
    ("m_own", (4, 4, 2048), F32),
    ("m_early", (4, 4, 2048), F32),
    ("m_old", (16, 2048), F32),
    ("v_in", (8, 16, 128), F32),
    ("v_x", (4, 16, 128), F32),
    ("v", (4, 16, 128), F32),
    ("rows_x", (4, 128, 512), BF),
    ("rows_c", (4, 128, 512), BF),
    ("cos", (4, 128, 128), F32),
    ("sin", (4, 128, 128), F32),
    ("normed", (4, 128, 512), BF),
    ("query", (512, 128), F32),
    ("q_buf", (2, 512, 128), BF),
    ("kv_buf", (2, 512, 128), BF),
    ("qo", (2, 512, 128), BF),
    ("kv", (8, 512, 128), BF),
    ("hidden", (4, 128, 512), BF),
    ("pre", (4, 128, 512), BF),
    ("feed", (4, 128, 512), F32),
    ("row_grad", (4, 128, 512), F32),
    ("gf", (2, 4, 4, 16, 1024), BF),
    ("gf_core", (4, 4, 16, 1024), BF),
    ("gf_chip", (4, 4, 16, 1024), BF),
    ("gf_a", (3, 4, 16, 1024), BF),
    ("gf_line", (4, 16, 1024), BF),
    ("gf_b", (3, 16, 1024), BF),
    ("gf_out", (4, 4, 1024), F32),
    ("gf_in", (4, 4, 1024), F32),
    ("turned", (8, 128, 512), BF),
    ("scores", (9, 512, 512), F32),
    ("sums", (512, 128), F32),
    ("query_low", (2, 512, 128), BF),
    ("grad_low", (2, 512, 128), BF),
    ("out_turned", (2, 64, 512), F32),
    ("back_turned", (2, 64, 512), F32),
    ("centre", (2, 1, 512), F32),
    ("od", (2, 512, 128), BF),
    ("od_in", (2, 512, 128), BF),
    ("dk", (2, 4, 512, 128), BF),
    ("dk_in", (4, 512, 128), BF),
    ("dk_chip", (4, 512, 128), BF),
    ("dk_mate", (2, 512, 128), BF),
    ("dk_pass", (512, 128), BF),
    ("dk_cross", (512, 128), BF),
    ("dkv", (2, 512, 128), BF),
    ("pair_out", (512, 128), BF),
    ("joint_out", (512, 384), BF),
    ("out_cols", (4, 128, 128), BF),
    ("out_in", (4, 128, 128), BF),
    ("out_part", (4, 128, 512), BF),
    ("out_got", (4, 128, 512), BF),
    ("back_part", (4, 128, 512), BF),
    ("back_got", (4, 128, 512), BF),
    ("gj", (2, 4, 4, 16, 512), BF),
    ("gj_core", (4, 4, 16, 512), BF),
    ("gj_chip", (4, 4, 16, 512), BF),
    ("gj_a", (3, 4, 16, 512), BF),
    ("gj_line", (4, 16, 512), BF),
    ("gj_b", (3, 16, 512), BF),
    ("gj_out", (4, 4, 512), F32),
    ("gj_in", (4, 4, 512), F32),
    ("vp", (4, 4, 16, 128), F32),
    ("vp_core", (4, 16, 128), F32),
    ("vp_z", (3, 4, 16, 128), F32),
    ("vp_x", (3, 4, 16, 128), F32),
    ("vp_t", (3, 4, 16, 128), F32),
    ("gm_out", (4, 16, 512), F32),
    ("gm_in", (4, 16, 512), F32),
    ("m_rows", (16, 2048), F32),
    ("momentum", (2, 4, 4, 16, 2048), BF),
    ("gram", (512, 512), F32),
    ("gram_h", (512, 512), BF),
    ("gram_l", (512, 512), BF),
    ("poly_h", (512, 512), BF),
    ("poly_l", (512, 512), BF),
    ("temp_h", (512, 512), BF),
    ("temp_l", (512, 512), BF),
    ("u_out", (4, 4, 2048), F32),
    ("u_in", (4, 4, 2048), F32),
)

PUSHES = 192
LOADS = 16


class Box:
    pass


def attend_chunk(place, slot):
    return place.seq if slot == 0 else 7 - place.seq


def attend_score(slot, k):
    return 8 - k if slot == 0 else k


def attend_forward(r, place, slot):
    chunk = attend_chunk(place, slot)
    low = lax.broadcasted_iota(jnp.int32, (512, 128), 1) < 64
    packed = r.qo[slot].astype(F32)
    r.query_low[slot] = jnp.where(low, packed * (HD ** -0.5), 0.0).astype(BF)
    r.grad_low[slot] = jnp.where(low, 0.0, packed).astype(BF)
    out_grad = r.qo[slot].T[64:128, :].astype(F32)
    query = r.query_low[slot]
    index = 512 * chunk + lax.broadcasted_iota(jnp.int32, (1, 512), 1)
    begin = jnp.zeros((1, 512), jnp.int32)
    finish = 0
    for j in range(4):
        finish = finish + r.lengths[0, j]
        begin = jnp.where(index >= finish, finish, begin)

    def score(k, carry):
        top, total_sum = carry
        raw = dot_cols(r.kv[k], query) * LOG2_E
        key = lax.broadcasted_iota(jnp.int32, (512, 512), 0)
        allowed = (key <= index - 512 * k) & (key >= begin - 512 * k)
        raw = jnp.where(allowed, raw, masked_score)
        r.scores[attend_score(slot, k)] = raw
        higher = jnp.maximum(top, jnp.max(raw, axis=0, keepdims=True))
        part = jnp.sum(jnp.exp2(raw - higher), axis=0, keepdims=True)
        return higher, total_sum * jnp.exp2(top - higher) + part

    start = (jnp.full((1, 512), masked_score, F32), jnp.zeros((1, 512), F32))
    top, total_sum = lax.fori_loop(0, chunk + 1, score, start)
    level = top + jnp.log(total_sum) * LOG2_E

    def weigh(k, out):
        prob = jnp.exp2(r.scores[attend_score(slot, k)] - level)
        r.scores[attend_score(slot, k)] = prob
        return out + dot(r.turned[k, 64:128, :], prob.astype(BF))

    out = lax.fori_loop(0, chunk + 1, weigh, jnp.zeros((64, 512), F32))
    r.out_turned[slot] = out
    r.back_turned[slot] = jnp.zeros((64, 512), F32)
    r.centre[slot] = jnp.sum(out * out_grad, axis=0, keepdims=True)


def attend_backward(r, place, k):
    r.sums[...] = jnp.zeros_like(r.sums)
    for slot in range(2):

        @pl.when(k <= attend_chunk(place, slot))
        def _(slot=slot):
            prob = r.scores[attend_score(slot, k)]
            grad = dot_cols(r.kv[k], r.grad_low[slot])
            score_grad = (prob * (grad - r.centre[slot])).astype(BF)
            r.back_turned[slot] += dot(r.turned[k, 0:64, :], score_grad)
            r.sums[...] += dot(prob.astype(BF), r.grad_low[slot]) + dot(
                score_grad, r.query_low[slot]
            )

    return r.sums[...].astype(BF)


def attend_write(r, slot):
    both = jnp.concatenate([r.out_turned[slot], r.back_turned[slot] * (HD ** -0.5)], axis=0)
    r.od[slot] = both.T.astype(BF)


def newton(r, place):
    blocks, size = 1, 512

    def rows(i):
        return pl.ds(size * i, size)

    def diagonal(i):
        row = size * i + lax.broadcasted_iota(jnp.int32, (size, 512), 0)
        return row == lax.broadcasted_iota(jnp.int32, (size, 512), 1)

    def fill(i, trace):
        value = jnp.zeros((size, 512), F32)
        for k in range(4):
            lanes = slice(512 * k, 512 * k + 512)
            right = r.momentum[:, :, :, :, lanes].reshape(512, 512)
            value = value + dot_cols(right, right)
        r.gram[rows(i), :] = value
        return trace + jnp.sum(jnp.where(diagonal(i), value, 0.0), keepdims=True)

    trace = lax.fori_loop(0, blocks, fill, jnp.zeros((1, 1), F32))
    scale = 1.0 / (jnp.sqrt(trace) + 1e-07)

    def keep(value, i, high_ref, low_ref):
        high, small = halves(value)
        high_ref[rows(i), :] = high
        low_ref[rows(i), :] = small

    def prepare(i, _):
        value = r.gram[rows(i), :] * (scale * scale)
        r.gram[rows(i), :] = value
        keep(value, i, r.gram_h, r.gram_l)
        return 0

    lax.fori_loop(0, blocks, prepare, 0)

    def polynomial(i, _):
        square = product(r.gram_h[rows(i), :], r.gram_l[rows(i), :], r.gram_h[...], r.gram_l[...])
        value = (
            jnp.where(diagonal(i), newton_first, 0.0)
            + newton_second * r.gram[rows(i), :]
            + newton_third * square
        )
        keep(value, i, r.poly_h, r.poly_l)
        return 0

    def inner(i, _):
        value = product(r.gram_h[rows(i), :], r.gram_l[rows(i), :], r.poly_h[...], r.poly_l[...])
        keep(value, i, r.temp_h, r.temp_l)
        return 0

    def outer(i, _):
        value = product(r.temp_h[rows(i), :], r.temp_l[rows(i), :], r.poly_h[...], r.poly_l[...])
        r.gram[rows(i), :] = value
        keep(value, i, r.gram_h, r.gram_l)
        return 0

    def times(left, right_h, right_l):
        high, small = halves(left)
        return product(high, small, right_h[...], right_l[...])

    mine = pl.ds(pl.multiple_of(256 * place.c + 64 * place.a + 16 * place.b, 16), 16)
    own = None
    for sweep in range(4):
        lax.fori_loop(0, blocks, polynomial, 0)
        if sweep == 0:
            own = r.poly_h[mine, :].astype(F32) + r.poly_l[mine, :].astype(F32)
        else:
            own = times(own, r.poly_h, r.poly_l)
        if sweep < 3:
            lax.fori_loop(0, blocks, inner, 0)
            lax.fori_loop(0, blocks, outer, 0)

    def last_gram(left):
        left = times(left, r.gram_h, r.gram_l)
        left = times(left, r.poly_h, r.poly_l)
        return times(left, r.poly_h, r.poly_l)

    once = last_gram(own)
    own = newton_first * own + newton_second * once + newton_third * last_gram(once)
    return halves(own * scale)


def block_kernel(*refs):
    r = Box()
    names = list(INPUTS) + [n for n, _, _ in OUTPUTS] + [n for n, _, _ in SCRATCH]
    for name, ref in zip(names, refs):
        setattr(r, name, ref)
    place = Place()
    wire = Wire(*refs[-3:])
    z, x, c, t, d = place.z, place.x, place.c, place.t, place.d
    seq, mate, cross, head = place.seq, place.mate, place.cross, place.head
    sibling = place.sibling()

    met = greet(
        place.octet() + place.row_x() + place.row_z() + [place.at(x=cross, c=1 - c)]
    )

    load_w = [
        wire.load(r.joint, r.joint_v),
        wire.load(r.output, r.output_v),
        wire.load(r.expand, r.expand_v),
        wire.load(r.reduce, r.reduce_v),
    ]
    load_v = wire.load(r.vectors, r.vectors_v)
    load_x = wire.load(r.x, r.rows_x.at[t])
    load_c = wire.load(r.c, r.rows_c.at[t])
    load_m = [
        wire.load(r.m_joint, r.m_joint_v),
        wire.load(r.m_output, r.m_output_v),
        wire.load(r.m_expand, r.m_expand_v),
        wire.load(r.m_reduce, r.m_reduce_v),
        wire.load(r.first, r.first_v),
        wire.load(r.second, r.second_v),
    ]
    for copy in load_w:
        copy.wait()
    for k in range(4):
        for part in range(3):
            r.w_out[k, :, 128 * part : 128 * part + 128] = r.joint_v[
                :, 512 * part + 128 * k : 512 * part + 128 * k + 128
            ]
        r.w_out[k, :, 384:896] = r.output_v[...]
        r.w_out[k, :, 896:1408] = r.expand_v[:, 512 * k : 512 * k + 512]
        r.w_out[k, :, 1408:1920] = r.reduce_v[:, 512 * k : 512 * k + 512]
    load_v.wait()
    r.table[...] = jnp.zeros((128, 128), F32)
    column = lax.broadcasted_iota(jnp.int32, (128, 11), 0) - (16 * seq + 4 * t)
    own_vec = jnp.zeros((128, 11), F32)
    for j in range(4):
        own_vec = jnp.where(column == j, r.vectors_v[j : j + 1, :], own_vec)
    r.table[:, 0:11] = own_vec.astype(BF).astype(F32)
    r.v_own[...] = r.table[...].T[0:16, :]
    load_x.wait()
    load_c.wait()
    met()

    weights = trade_t(wire, place, r.w_out, r.w_in)
    octet = []
    for partner in place.octet():
        octet.append(wire.push(r.v_own, r.v_in.at[4 * c + t], partner))
    ahead, behind = ring(t, d), ring(t, -d)
    r.w_in[t] = r.w_out[t]
    r.v_in[4 * c + t] = r.v_own[...]
    arrive(weights)
    for k in range(4):
        r.w_rows[4 * k : 4 * k + 4, :] = r.w_in[k]
    keys, values = r.w_rows[:, 128:256], r.w_rows[:, 256:384]
    low16 = lax.broadcasted_iota(jnp.int32, (16, 128), 1) < 64
    r.wj[c, place.a, place.b, :, 0:128] = r.w_rows[:, 0:128].astype(BF)
    r.wj[c, place.a, place.b, :, 128:256] = jnp.where(
        low16, keys, pltpu.roll(values, 64, 1)
    ).astype(BF)
    r.wj[c, place.a, place.b, :, 256:384] = jnp.where(
        low16, pltpu.roll(keys, 64, 1), values
    ).astype(BF)
    joint_b = spread_b(wire, place, r.wj)
    x_first = wire.push(r.rows_x.at[t], r.rows_x.at[t], place.at(t=ahead))
    x_second = wire.push(r.rows_x.at[t], r.rows_x.at[t], place.at(t=behind))
    arrive(octet)
    vec = r.v_in[0]
    for k in range(1, 8):
        vec = vec + r.v_in[k]
    r.v_x[x] = vec
    vec_x = [wire.push(r.v_x.at[x], r.v_x.at[x], partner) for partner in place.row_x()]
    r.wr[c, place.a, place.b] = r.w_rows[:, 384:1920].astype(BF)
    rest_b = spread_b(wire, place, r.wr)

    half = ROT // 2
    lane = lax.rem(lax.broadcasted_iota(jnp.int32, (1, 128), 1), 64)
    frequency = jnp.zeros((1, 128), F32)
    for i in range(half):
        frequency = jnp.where(lax.rem(lane, half) == i, 10000.0 ** (-2.0 * i / ROT), frequency)
    frequency = jnp.where(lane < ROT, frequency, 0.0)

    def angles(i, _):
        index = 512 * seq + 128 * i + lax.broadcasted_iota(jnp.int32, (128, 1), 0)
        begin = jnp.zeros((128, 1), jnp.int32)
        finish = 0
        for j in range(4):
            finish = finish + r.lengths[0, j]
            begin = jnp.where(index >= finish, finish, begin)
        angle = (index - begin).astype(F32) * frequency
        r.cos[i] = jnp.cos(angle)
        r.sin[i] = jnp.sin(angle)
        return 0

    lax.fori_loop(0, 4, angles, 0)
    arrive(joint_b)
    joint_a = spread_a(wire, place, r.wj)
    arrive(vec_x)
    r.v[z] = (r.v_x[0] + r.v_x[1]) + (r.v_x[2] + r.v_x[3])
    vec_z = [wire.push(r.v.at[z], r.v.at[z], partner) for partner in place.row_z()]
    for copy in load_m:
        copy.wait()
    arrive(rest_b)
    rest_up, rest_down = ring_open(wire, place, r.wr)
    rest_swaps = [swap_part(wire, place, r.wr, 0)]
    x_first.wait_recv()
    x_third = wire.push(r.rows_x.at[behind], r.rows_x.at[behind], place.at(t=ahead))
    c_first = wire.push(r.rows_c.at[t], r.rows_c.at[t], place.at(t=ahead))
    c_second = wire.push(r.rows_c.at[t], r.rows_c.at[t], place.at(t=behind))
    arrive(joint_a)
    joint_swap = swap_cores(wire, place, r.wj)
    rest_more = ring_pass(wire, place, r.wr, rest_up, rest_down)
    arrive([joint_swap, *vec_z, x_second, x_third])
    natural(r.wj, r.w_joint, 0, 384)

    gain, shift = vec_row(r.v, 0), vec_row(r.v, 1)
    q_bias, k_bias, v_bias = r.v[t, 2:3, :], r.v[t, 3:4, :], r.v[t, 4:5, :]
    low_row = lax.broadcasted_iota(jnp.int32, (1, 128), 1) < 64
    pair_bias = (
        jnp.where(low_row, k_bias, pltpu.roll(v_bias, 64, 1)),
        jnp.where(low_row, pltpu.roll(k_bias, 64, 1), v_bias),
    )
    low = lax.broadcasted_iota(jnp.int32, (256, 128), 1) < 64

    def project(i, _):
        blocks, rows = pl.ds(2 * i, 2), pl.ds(256 * i, 256)
        normal, _rate = normalise(r.rows_x[blocks].reshape(256, 512))
        part = (normal * gain + shift).astype(BF)
        r.normed[blocks] = part.reshape(2, 128, 512)
        raw = dot(part, r.w_joint[...].reshape(512, 384))
        cosine, sine = r.cos[blocks].reshape(256, 128), r.sin[blocks].reshape(256, 128)
        r.query[rows, :] = turn(raw[:, 0:128] + q_bias, cosine, sine, 1.0)
        key_cos = jnp.where(low, cosine, 1.0)
        key_sin = jnp.where(low, sine, 0.0)
        for h in range(2):
            pair = raw[:, 128 + 128 * h : 256 + 128 * h] + pair_bias[h]
            r.kv_buf[h, rows, :] = turn(pair, key_cos, key_sin, 1.0).astype(BF)
        return 0

    lax.fori_loop(0, 2, project, 0)
    kv_cross = wire.push(r.kv_buf.at[1 - head], r.kv.at[seq], place.at(x=cross))
    kv_mate = wire.push(r.kv_buf.at[head], r.kv.at[seq], place.at(x=mate))
    kv_core = wire.push(r.kv_buf.at[head], r.kv.at[seq], sibling)
    r.kv[seq] = r.kv_buf[head]
    c_first.wait_recv()
    c_third = wire.push(r.rows_c.at[behind], r.rows_c.at[behind], place.at(t=ahead))
    rest_swaps += ring_close(wire, place, r.wr, rest_up, rest_down, rest_more)
    for k in range(4):
        lanes = slice(128 * k, 128 * k + 128)
        keys = r.m_joint_v[:, 512 + 128 * k : 640 + 128 * k]
        values = r.m_joint_v[:, 1024 + 128 * k : 1152 + 128 * k]
        r.m_own[0, :, 512 * k : 512 * k + 128] = r.m_joint_v[:, lanes]
        r.m_own[0, :, 512 * k + 128 : 512 * k + 256] = jnp.concatenate(
            [keys[:, 0:64], values[:, 0:64]], axis=1
        )
        r.m_own[0, :, 512 * k + 256 : 512 * k + 384] = jnp.concatenate(
            [keys[:, 64:128], values[:, 64:128]], axis=1
        )
        r.m_own[0, :, 512 * k + 384 : 512 * k + 512] = jnp.zeros((4, 128), F32)
        r.m_own[1, :, 512 * k : 512 * k + 128] = r.m_output_v[:, lanes]
        r.m_own[1, :, 512 * k + 128 : 512 * k + 512] = jnp.zeros((4, 384), F32)
    r.m_own[2] = r.m_expand_v[...]
    r.m_own[3] = r.m_reduce_v[...]
    arrive([c_second, c_third, *rest_swaps])
    natural(r.wr, r.w_output, 0, 512)
    natural(r.wr, r.w_expand, 512, 1024)
    natural(r.wr, r.w_reduce, 1024, 1536)
    out_rows = r.w_output[pl.ds(8 * t, 8)].reshape(128, 512)
    low = lax.broadcasted_iota(jnp.int32, (512, 128), 1) < 64
    grad = dot_cols(r.rows_c[...].reshape(512, 512), out_rows)
    query = r.query[...]
    r.q_buf[0] = jnp.where(low, query, pltpu.roll(grad, 64, 1)).astype(BF)
    r.q_buf[1] = jnp.where(low, pltpu.roll(query, 64, 1), grad).astype(BF)
    q_cross = wire.push(r.q_buf.at[1 - head], r.qo.at[1], place.at(x=cross, c=1 - c))
    early = trade_t(wire, place, r.m_own, r.m_early)
    r.qo[0] = r.q_buf[head]
    at_cross, at_mate = 2 * cross + c, 2 * mate + c
    at_far = 2 * (3 - mate) + c
    kv_cross.wait_recv()
    kv_far = wire.push(r.kv.at[at_cross], r.kv.at[at_cross], place.at(x=mate))
    kv_more = [kv_core, wire.push(r.kv.at[at_cross], r.kv.at[at_cross], sibling)]

    bias = jnp.concatenate([r.v[k, pl.ds(7 + t, 1), :] for k in range(4)], axis=1)

    def feed_forward(i, sums):
        blocks = pl.ds(2 * i, 2)
        part = r.normed[blocks].reshape(256, 512)
        wide = dot(part, r.w_expand[...].reshape(512, 512)) + bias
        square = wide * wide
        curve = jnp.tanh(0.7978845608 * (wide + 0.044715 * (square * wide)))
        r.hidden[blocks] = (0.5 * wide * (1.0 + curve)).astype(BF).reshape(2, 128, 512)
        slope = 0.5 * (1.0 + curve) + (0.5 * 0.7978845608) * wide * (1.0 - curve * curve) * (
            1.0 + (3 * 0.044715) * square
        )
        part = r.rows_c[blocks].reshape(256, 512)
        back = dot(part, r.w_reduce[...].reshape(512, 512))
        grad = (back * slope).astype(BF)
        r.pre[blocks] = grad.reshape(2, 128, 512)
        return sums + jnp.sum(grad.astype(F32), axis=0, keepdims=True)

    hidden_sum = lax.fori_loop(0, 2, feed_forward, jnp.zeros((1, 512), F32))
    kv_mate.wait_recv()
    kv_more.append(wire.push(r.kv.at[at_mate], r.kv.at[at_mate], sibling))
    for j in range(4):
        lanes = slice(128 * j, 128 * j + 128)
        expand_grad = dot_rows(
            r.normed[:, :, lanes].reshape(512, 128), r.pre[...].reshape(512, 512)
        )
        by_owner(r.gf, j, expand_grad.astype(BF), 0, 512)
        reduce_grad = dot_rows(
            r.rows_c[:, :, lanes].reshape(512, 128), r.hidden[...].reshape(512, 512)
        )
        by_owner(r.gf, j, reduce_grad.astype(BF), 512, 1024)
    gf_swap = sum_cores(wire, place, r.gf, r.gf_core)
    kv_far.wait_recv()
    kv_more.append(wire.push(r.kv.at[at_far], r.kv.at[at_far], sibling))

    arrive(early)
    r.m_early[t] = r.m_own[t]
    for k in range(4):
        r.m_old[4 * k : 4 * k + 4, :] = r.m_early[k]
    gf_swap.wait_recv()
    for a in range(4):
        r.gf_chip[a] = (r.gf[c, a].astype(F32) + r.gf_core[a].astype(F32)).astype(BF)
    gf_a = scatter_a(wire, place, r.gf_chip, r.gf_a)
    arrive(kv_more)

    for k in range(8):
        r.turned[k] = r.kv[k].T
    attend_forward(r, place, 0)
    q_cross.wait_recv()
    arrive(gf_a)
    r.gf_line[...] = total(r.gf_chip[place.a], r.gf_a).astype(BF)
    gf_b = scatter_b(wire, place, r.gf_line, r.gf_b)
    attend_forward(r, place, 1)

    far = 3 - mate
    dk_swap = []

    def chip_sum(index):
        return r.dk[c, index].astype(F32) + r.dk_in[index].astype(F32)

    for step, column in enumerate((far, mate, cross, x)):

        def key_block(p, _, column=column):
            parity = lax.rem(1 - c + p, 2)
            r.dk[parity, column] = attend_backward(r, place, 2 * column + parity)
            return 0

        lax.fori_loop(0, 2, key_block, 0)
        dk_swap.append(wire.push(r.dk.at[1 - c, column], r.dk_in.at[column], sibling))
        if step == 1:
            dk_swap[0].wait_recv()
            r.dk_chip[0] = chip_sum(far).astype(BF)
            dk_far = wire.push(r.dk_chip.at[0], r.dk_mate.at[0], place.at(x=mate))
        if step == 2:
            dk_swap[1].wait_recv()
            r.dk_chip[1] = chip_sum(mate).astype(BF)
            dk_near = wire.push(r.dk_chip.at[1], r.dk_mate.at[1], place.at(x=mate))
    attend_write(r, 1)
    od_cross = wire.push(r.od.at[1], r.od_in.at[head], place.at(x=cross, c=1 - c))
    attend_write(r, 0)
    r.od_in[head] = r.od[0]

    arrive(gf_b)
    gf_own = total(r.gf_line[place.b], r.gf_b)
    for k in range(4):
        r.gf_out[k] = gf_own[4 * k : 4 * k + 4, :]
    r.gm_out[2] = gf_own[:, 0:512]
    r.gm_out[3] = gf_own[:, 512:1024]
    gf_t = trade_t(wire, place, r.gf_out, r.gf_in)
    r.gf_in[t] = r.gf_out[t]
    low = lax.broadcasted_iota(jnp.int32, (128, 128), 1) < 64
    dk_swap[2].wait_recv()
    dk_far.wait_recv()
    r.dk_pass[...] = (chip_sum(cross) + r.dk_mate[0].astype(F32)).astype(BF)
    dk_cross = wire.push(r.dk_pass, r.dk_cross, place.at(x=cross))

    def feed_out(i, _):
        blocks = pl.ds(2 * i, 2)
        part = r.hidden[blocks].reshape(256, 512)
        r.feed[blocks] = dot_cols(part, r.w_reduce[...].reshape(512, 512)).reshape(2, 128, 512)
        part = r.pre[blocks].reshape(256, 512)
        r.row_grad[blocks] = dot_cols(part, r.w_expand[...].reshape(512, 512)).reshape(2, 128, 512)
        return 0

    lax.fori_loop(0, 2, feed_out, 0)
    od_cross.wait_recv()
    for i in range(4):
        rows = pl.ds(128 * i, 128)
        left = r.od_in[0, rows, :].astype(F32)
        right = r.od_in[1, rows, :].astype(F32)
        joined = jnp.where(low, left, pltpu.roll(right, 64, 1)).astype(BF)
        r.pair_out[rows, :] = joined
        back = jnp.where(low, pltpu.roll(left, 64, 1), right)
        r.joint_out[rows, 0:128] = turn(back, r.cos[i], r.sin[i], -1.0).astype(BF)
    for i in range(4):
        rows = pl.ds(128 * i, 128)
        out_rows = r.w_output[pl.ds(8 * t, 8)].reshape(128, 512)
        r.out_part[i] = (r.feed[i] + dot(r.pair_out[rows, :], out_rows)).astype(BF)
    for j in range(4):
        part = r.rows_c[:, :, 128 * j : 128 * j + 128].reshape(512, 128)
        r.out_cols[j] = dot_rows(r.pair_out[...], part).astype(BF)
    out_cols = trade_t(wire, place, r.out_cols, r.out_in)
    out_parts = trade_t(wire, place, r.out_part, r.out_got)
    r.out_in[t] = r.out_cols[t]
    r.out_got[t] = r.out_part[t]
    arrive([dk_swap[3], dk_near])
    r.dkv[head] = (chip_sum(x) + r.dk_mate[1].astype(F32)).astype(BF)
    dk_cross.wait_recv()
    r.dkv[1 - head] = r.dk_cross[...]
    for h in range(2):
        for i in range(4):
            rows = pl.ds(128 * i, 128)
            key_cos = jnp.where(low, r.cos[i], 1.0)
            key_sin = jnp.where(low, r.sin[i], 0.0)
            r.joint_out[rows, 128 + 128 * h : 256 + 128 * h] = turn(
                r.dkv[h, rows, :].astype(F32), key_cos, key_sin, -1.0
            ).astype(BF)
    arrive(out_cols)
    for j in range(4):
        part = r.normed[:, :, 128 * j : 128 * j + 128].reshape(512, 128)
        by_owner(r.gj, j, dot_rows(part, r.joint_out[...]).astype(BF), 0, 384)
        by_owner(r.gj, j, r.out_in[j], 384, 512)
    gj_swap = sum_cores(wire, place, r.gj, r.gj_core)

    r.vp[0] = jnp.zeros((4, 16, 128), F32)
    shift_sum = jnp.zeros((1, 512), F32)
    gain_sum = jnp.zeros((1, 512), F32)
    for i in range(4):
        rows = pl.ds(128 * i, 128)
        part = r.row_grad[i] + dot_cols(r.joint_out[rows, :], r.w_joint[...].reshape(512, 384))
        r.back_part[i] = part.astype(BF)
        normal, _rate = normalise(r.rows_x[i])
        shift_sum = shift_sum + jnp.sum(part, axis=0, keepdims=True)
        gain_sum = gain_sum + jnp.sum(part * normal, axis=0, keepdims=True)
    gj_swap.wait_recv()
    for a in range(4):
        r.gj_chip[a] = (r.gj[c, a].astype(F32) + r.gj_core[a].astype(F32)).astype(BF)
    gj_a = scatter_a(wire, place, r.gj_chip, r.gj_a)
    back_parts = trade_t(wire, place, r.back_part, r.back_got)
    r.back_got[t] = r.back_part[t]
    out_sum = jnp.sum(r.rows_c[t].astype(F32), axis=0, keepdims=True)
    joint_sum = jnp.sum(r.joint_out[...].astype(F32), axis=0, keepdims=True)
    one, two = joint_sum[:, 128:256], joint_sum[:, 256:384]
    for k in range(4):
        lanes = slice(128 * k, 128 * k + 128)
        r.vp[0, k, 0:1, :] = gain_sum[:, lanes]
        r.vp[0, k, 1:2, :] = shift_sum[:, lanes]
        r.vp[0, k, 5:6, :] = out_sum[:, lanes]
        r.vp[0, k, 6:7, :] = out_sum[:, lanes]
        r.vp[0, k, pl.ds(7 + t, 1), :] = hidden_sum[:, lanes]
    r.vp[0, t, 2:3, :] = joint_sum[:, 0:128]
    r.vp[0, t, 3:4, :] = jnp.where(low_row, one, pltpu.roll(two, 64, 1))
    r.vp[0, t, 4:5, :] = jnp.where(low_row, pltpu.roll(one, 64, 1), two)
    vp_swap = wire.push(r.vp.at[0], r.vp_core, sibling)
    arrive(gj_a)
    r.gj_line[...] = total(r.gj_chip[place.a], r.gj_a).astype(BF)
    gj_b = scatter_b(wire, place, r.gj_line, r.gj_b)
    vp_swap.wait_recv()
    r.vp[1] = r.vp[0] + r.vp_core[...]
    vp_z = [wire.push(r.vp.at[1], r.vp_z.at[k], p) for k, p in enumerate(place.row_z())]

    arrive(gj_b)
    gj_own = total(r.gj_line[place.b], r.gj_b)
    r.gm_out[0, :, 0:384] = gj_own[:, 0:384]
    r.gm_out[0, :, 384:512] = jnp.zeros((16, 128), F32)
    r.gm_out[1, :, 0:128] = gj_own[:, 384:512]
    r.gm_out[1, :, 128:512] = jnp.zeros((16, 384), F32)
    gm_t = trade_t(wire, place, r.gm_out, r.gm_in)
    r.gm_in[t] = r.gm_out[t]
    for k in range(4):
        r.gj_out[k] = gj_own[4 * k : 4 * k + 4, :]
    gj_t = trade_t(wire, place, r.gj_out, r.gj_in)
    r.gj_in[t] = r.gj_out[t]
    arrive(vp_z)
    r.vp[2] = total(r.vp[1], r.vp_z)
    vp_x = [wire.push(r.vp.at[2], r.vp_x.at[k], p) for k, p in enumerate(place.row_x())]

    arrive(gm_t)
    for k in range(4):
        lanes = slice(512 * k, 512 * k + 512)
        value = muon_beta * r.m_old[:, lanes] + r.gm_in[k]
        r.momentum[c, place.a, place.b, :, lanes] = value.astype(BF)
    m_b = spread_b(wire, place, r.momentum)

    arrive(gf_t)
    for k in range(4):
        part = r.gf_in[k]
        r.g_expand[:, 512 * k : 512 * k + 512] = part[:, 0:512]
        r.g_reduce[:, 512 * k : 512 * k + 512] = part[:, 512:1024]
    arrive(gj_t)
    for k in range(4):
        lanes = slice(128 * k, 128 * k + 128)
        part = r.gj_in[k]
        unpair(r.g_joint, part, k)
        r.g_output[:, lanes] = part[:, 384:512]
    for old, grad, new in (
        (r.m_joint_v, r.g_joint, r.n_joint),
        (r.m_output_v, r.g_output, r.n_output),
        (r.m_expand_v, r.g_expand, r.n_expand),
        (r.m_reduce_v, r.g_reduce, r.n_reduce),
    ):
        new[...] = muon_beta * old[...] + grad[...]
    arrive(vp_x)
    r.vp[3] = total(r.vp[2], r.vp_x)
    vp_t = [wire.push(r.vp.at[3], r.vp_t.at[k], p) for k, p in enumerate(place.row_t())]
    arrive(out_parts)
    arrive(back_parts)
    arrive(m_b)
    m_up, m_down = ring_open(wire, place, r.momentum)
    m_swaps = [swap_part(wire, place, r.momentum, 0)]
    m_more = ring_pass(wire, place, r.momentum, m_up, m_down)
    wide = r.rows_x[t].astype(F32)
    feed = r.out_got[0].astype(F32)
    back = r.back_got[0].astype(F32)
    for k in range(1, 4):
        feed = feed + r.out_got[k].astype(F32)
        back = back + r.back_got[k].astype(F32)
    r.block_output[...] = (wide + feed + vec_row(r.v, 5) + vec_row(r.v, 6)).astype(BF)
    normal, rate = normalise(r.rows_x[t])
    scaled = back * gain
    mean_one = jnp.mean(scaled, axis=-1, keepdims=True)
    mean_two = jnp.mean(scaled * normal, axis=-1, keepdims=True)
    r.input_grad[...] = r.rows_c[t].astype(F32) + rate * (scaled - mean_one - normal * mean_two)
    m_swaps += ring_close(wire, place, r.momentum, m_up, m_down, m_more)
    arrive(vp_t)
    r.vec_sum[...] = total(r.vp[3], r.vp_t)
    r.table[0:16, :] = r.vec_sum[z]
    r.table[...] = r.table[...].T
    vector_grad = r.table[pl.ds(pl.multiple_of(16 * seq + 4 * t, 4), 4), 0:11]
    r.vector_grad[...] = vector_grad
    first_next = beta_first * r.first_v[...] + (1.0 - beta_first) * vector_grad
    second_next = (
        beta_second * r.second_v[...] + (1.0 - beta_second) * vector_grad * vector_grad
    )
    r.second_next[...] = second_next
    first_hat = first_next / (1.0 - beta_first**STEP)
    second_hat = second_next / (1.0 - beta_second**STEP)
    r.vector_next[...] = r.vectors_v[...] - vector_rate * first_hat / (
        jnp.sqrt(second_hat) + adam_epsilon
    )
    arrive(m_swaps)

    high, small = newton(r, place)
    for k in range(4):
        lanes = slice(512 * k, 512 * k + 512)
        columns = r.momentum[:, :, :, :, lanes].reshape(512, 512)
        r.m_rows[:, lanes] = dot(high, columns) + dot(small, columns)
    for k in range(4):
        r.u_out[k] = r.m_rows[4 * k : 4 * k + 4, :]
    u_t = trade_t(wire, place, r.u_out, r.u_in)
    r.u_in[t] = r.u_out[t]
    arrive(u_t)
    for k in range(4):
        lanes = slice(128 * k, 128 * k + 128)
        unpair(r.u_joint, r.u_in[0, :, 512 * k : 512 * k + 384], k)
        r.u_output[:, lanes] = r.u_in[1, :, 512 * k : 512 * k + 128]
    for k, (old, change, new) in enumerate(
        (
            (r.joint_v, r.u_joint, r.u_joint),
            (r.output_v, r.u_output, r.u_output),
            (r.expand_v, r.u_in.at[2], r.u_expand),
            (r.reduce_v, r.u_in.at[3], r.u_reduce),
        )
    ):
        factor = muon_rate * 0.2 * math.sqrt(max(D, WIDTHS[k]))
        new[...] = old[...] * (1.0 - muon_rate * muon_decay) - factor * change[...]
    wire.drain()


def block_stage(*arrays):
    return pl.pallas_call(
        block_kernel,
        out_shape=tuple(shape(dims, dtype) for _, dims, dtype in OUTPUTS),
        in_specs=[SMEM] + [ANY] * (len(INPUTS) - 1),
        out_specs=(VMEM,) * len(OUTPUTS),
        scratch_shapes=[pltpu.VMEM(dims, dtype) for _, dims, dtype in SCRATCH]
        + [
            pltpu.SemaphoreType.DMA((PUSHES,)),
            pltpu.SemaphoreType.DMA((PUSHES,)),
            pltpu.SemaphoreType.DMA((LOADS,)),
        ],
        compiler_params=pltpu.CompilerParams(
            collective_id=1, has_side_effects=True, vmem_limit_bytes=56 << 20
        ),
        name="block",
    )(*arrays)


def write_kernel(*refs):
    count = len(OUTPUTS)
    sem = refs[-1]
    copies = []
    for k in range(count):
        copy = pltpu.make_async_copy(refs[k], refs[count + k], sem.at[k])
        copy.start()
        copies.append(copy)
    for copy in copies:
        copy.wait()


def write_stage(*arrays):
    count = len(arrays)
    return pl.pallas_call(
        write_kernel,
        out_shape=tuple(shape(a.shape, a.dtype) for a in arrays),
        in_specs=[VMEM] * count,
        out_specs=(ANY,) * count,
        scratch_shapes=[pltpu.SemaphoreType.DMA((count,))],
        name="write",
    )(*arrays)


def shards(
    block_input,
    cotangent,
    doc_lengths,
    joint_weight,
    output_weight,
    expand_weight,
    reduce_weight,
    joint_moment,
    output_moment,
    expand_moment,
    reduce_moment,
    vectors,
    first_moment,
    second_moment,
):
    results = block_stage(
        doc_lengths, block_input, cotangent, joint_weight, output_weight, expand_weight,
        reduce_weight, vectors.T, joint_moment, output_moment, expand_moment, reduce_moment,
        first_moment.T, second_moment.T,
    )
    results = write_stage(*results)
    return (*results[12:14], *results[0:12], *[part.T for part in results[14:]])


def solution(mesh):
    rows = P(("fsdp", "seq", "tensor"), None)
    columns = P(None, ("fsdp", "seq", "tensor"))
    return jax.shard_map(
        shards,
        mesh=mesh,
        in_specs=(rows, rows, P("fsdp", None)) + (rows,) * 8 + (columns,) * 3,
        out_specs=(rows,) * 14 + (columns,) * 3,
        check_vma=False,
    )
```

```python
import math

import jax
import jax.numpy as jnp
from jax import lax
from jax.experimental import pallas as pl
from jax.experimental.pallas import tpu as pltpu
from jax.sharding import PartitionSpec as P

D = 512
HEADS = 8
FF = 2048
ROT = 16
HD = 64
STEP = 10

norm_epsilon = 1e-05
masked_score = -1e30
newton_first = 3.4445
newton_second = -4.775
newton_third = 2.0315
beta_first = 0.9
beta_second = 0.95
adam_epsilon = 1e-08
vector_rate = 0.2
muon_rate = 0.25
muon_beta = 0.95
muon_decay = 0.01
LOG2_E = 1.4426950408889634

BF = jnp.bfloat16
F32 = jnp.float32
MESH = pl.DeviceIdType.MESH
VMEM = pl.BlockSpec(memory_space=pltpu.VMEM)
SMEM = pl.BlockSpec(memory_space=pltpu.SMEM)
ANY = pl.BlockSpec(memory_space=pl.ANY)
WIDTHS = (3 * D, D, FF, FF)


def shape(dims, dtype):
    return jax.ShapeDtypeStruct(dims, dtype)


class Place:
    def __init__(self):
        self.z = lax.axis_index("fsdp")
        self.seq = lax.axis_index("seq")
        self.t = lax.axis_index("tensor")
        self.x = lax.div(self.seq, 2)
        self.c = lax.rem(self.seq, 2)
        self.d = 1 - 2 * self.c
        self.a = self.c * self.x + (1 - self.c) * self.z
        self.b = self.c * self.z + (1 - self.c) * self.x
        self.mate = self.x + 1 - 2 * lax.rem(self.x, 2)
        self.cross = 3 - self.x
        self.head = lax.div(self.x, 2)

    def at(self, z=None, x=None, c=None, t=None):
        z = self.z if z is None else z
        x = self.x if x is None else x
        c = self.c if c is None else c
        t = self.t if t is None else t
        return (z, 2 * x + c, t)

    def at_a(self, a):
        c = self.c
        return self.at(z=(1 - c) * a + c * self.z, x=c * a + (1 - c) * self.x)

    def at_b(self, b):
        c = self.c
        return self.at(z=c * b + (1 - c) * self.z, x=(1 - c) * b + c * self.x)

    def at_ab(self, a, b):
        c = self.c
        return self.at(z=(1 - c) * a + c * b, x=c * a + (1 - c) * b)

    def plane(self):
        steps = [(i, j) for i in range(4) for j in range(4) if i + j > 0]
        steps.sort(key=lambda step: -min(step[0], 4 - step[0]) - min(step[1], 4 - step[1]))
        return [(ring(self.a, i), ring(self.b, j)) for i, j in steps]

    def sibling(self):
        return self.at(c=1 - self.c)

    def octet(self):
        g = 4 * self.c + self.t
        members = [lax.rem(g + k, 8) for k in range(1, 8)]
        return [self.at(c=lax.div(m, 4), t=lax.rem(m, 4)) for m in members]

    def row_x(self):
        return [self.at(x=lax.rem(self.x + k, 4)) for k in range(1, 4)]

    def row_z(self):
        return [self.at(z=lax.rem(self.z + k, 4)) for k in range(1, 4)]

    def row_t(self):
        return [self.at(t=lax.rem(self.t + k, 4)) for k in range(1, 4)]


def ring(index, step):
    return lax.rem(index + step + 4, 4)


def greet(partners):
    barrier = pltpu.get_barrier_semaphore()
    for partner in partners:
        pl.semaphore_signal(barrier, inc=1, device_id=partner, device_id_type=MESH)
    return lambda: pl.semaphore_wait(barrier, len(partners))


class Wire:
    def __init__(self, send, recv, local):
        self.send = send
        self.recv = recv
        self.local = local
        self.count = 0
        self.loads = 0
        self.open = []

    def push(self, src, dst, device):
        index = self.count
        self.count += 1
        copy = pltpu.make_async_remote_copy(
            src_ref=src,
            dst_ref=dst,
            send_sem=self.send.at[index],
            recv_sem=self.recv.at[index],
            device_id=device,
            device_id_type=MESH,
        )
        copy.start()
        self.open.append(copy)
        return copy

    def offer(self, first, source, target, sender, goal, device):
        return pltpu.make_async_remote_copy(
            src_ref=source,
            dst_ref=target,
            send_sem=self.send.at[first + goal],
            recv_sem=self.recv.at[first + sender],
            device_id=device,
            device_id_type=MESH,
        )

    def block(self, count):
        first = self.count
        self.count += count
        return first

    def load(self, src, dst):
        copy = pltpu.make_async_copy(src, dst, self.local.at[self.loads])
        self.loads += 1
        copy.start()
        return copy

    def drain(self):
        for copy in self.open:
            copy.wait_send()


def arrive(copies):
    for copy in copies:
        copy.wait_recv()


def dot(left, right):
    return jnp.dot(left, right, preferred_element_type=F32)


def dot_cols(left, right):
    return lax.dot_general(left, right, (((1,), (1,)), ((), ())), preferred_element_type=F32)


def dot_rows(left, right):
    return lax.dot_general(left, right, (((0,), (0,)), ((), ())), preferred_element_type=F32)


def turn(values, cosine, sine, sign):
    lane = lax.rem(lax.broadcasted_iota(jnp.int32, values.shape, 1), 64)
    crossed = jnp.where(lane < 8, -pltpu.roll(values, 120, 1), pltpu.roll(values, 8, 1))
    return values * cosine + crossed * (sine * sign)


def vec_row(v_ref, row):
    return jnp.concatenate([v_ref[k, row : row + 1, :] for k in range(4)], axis=1)


def normalise(rows):
    wide = rows.astype(F32)
    centred = wide - jnp.mean(wide, axis=-1, keepdims=True)
    variance = jnp.mean(centred * centred, axis=-1, keepdims=True)
    rate = lax.rsqrt(variance + norm_epsilon)
    return centred * rate, rate


def halves(values):
    high = values.astype(BF)
    return high, (values - high.astype(F32)).astype(BF)


def product(left_h, left_l, right_h, right_l):
    return dot(left_h, right_h) + (dot(left_h, right_l) + dot(left_l, right_h))


def squared(high, small):
    cross = dot(high, small)
    return dot(high, high) + (cross + cross.T)


def spread_b(wire, place, ref):
    block = ref.at[place.c, place.a, place.b]
    return [wire.push(block, block, place.at_b(ring(place.b, k))) for k in range(1, 4)]


def ring_open(wire, place, ref):
    ups, downs = {}, {}
    for p, q in ((0, 2), (1, 3), (2, 0), (3, 1)):
        block = ref.at[place.c, place.a, p]
        ups[p] = wire.push(block, block, place.at_a(ring(place.a, 1)))
        block = ref.at[place.c, place.a, q]
        downs[q] = wire.push(block, block, place.at_a(ring(place.a, -1)))
    return ups, downs


def ring_pass(wire, place, ref, ups, downs):
    more = []
    for p, q in ((0, 2), (1, 3)):
        ups[p].wait_recv()
        block = ref.at[place.c, ring(place.a, -1), p]
        more.append(wire.push(block, block, place.at_a(ring(place.a, 1))))
        downs[q].wait_recv()
        block = ref.at[place.c, ring(place.a, 1), q]
        more.append(wire.push(block, block, place.at_a(ring(place.a, -1))))
    return more


def swap_part(wire, place, ref, step):
    block = ref.at[place.c, ring(place.a, step)]
    return wire.push(block, block, place.sibling())


def ring_close(wire, place, ref, ups, downs, more):
    arrive([ups[2], ups[3]])
    swaps = [swap_part(wire, place, ref, -1)]
    arrive([downs[0], downs[1]])
    swaps.append(swap_part(wire, place, ref, 1))
    arrive(more)
    swaps.append(swap_part(wire, place, ref, 2))
    return swaps


def spread_plane(wire, place, ref):
    block = ref.at[place.c, place.a, place.b]
    return [wire.push(block, block, place.at_ab(a, b)) for a, b in place.plane()]


def scatter_plane(wire, place, ref, target):
    copies = []
    for k, (a, b) in enumerate(place.plane()):
        copies.append(wire.push(ref.at[a, b], target.at[k], place.at_ab(a, b)))
    return copies


def add_plane(first, parts):
    value = first.astype(F32)
    for k in range(15):
        value = value + parts[k].astype(F32)
    return value


def swap_cores(wire, place, ref):
    return wire.push(ref.at[place.c], ref.at[place.c], place.sibling())


def natural(source, target, start, stop):
    for z in range(4):
        for x in range(4):
            target[8 * z + 2 * x] = source[0, z, x, :, start:stop]
            target[8 * z + 2 * x + 1] = source[1, x, z, :, start:stop]


def by_owner(target, z, rows, start, stop):
    for x in range(4):
        target[0, z, x, :, start:stop] = rows[32 * x : 32 * x + 16, :]
        target[1, x, z, :, start:stop] = rows[32 * x + 16 : 32 * x + 32, :]


def sum_cores(wire, place, ref, target):
    return wire.push(ref.at[1 - place.c], target, place.sibling())


def trade_t(wire, place, source, target):
    copies = []
    for k in range(1, 4):
        goal = ring(place.t, k)
        copies.append(wire.push(source.at[goal], target.at[place.t], place.at(t=goal)))
    return copies


def total(first, parts):
    value = first.astype(F32)
    for k in range(3):
        value = value + parts[k].astype(F32)
    return value


def unpair(target, part, k):
    one, two = part[:, 128:256], part[:, 256:384]
    target[:, 128 * k : 128 * k + 128] = part[:, 0:128]
    target[:, 512 + 128 * k : 640 + 128 * k] = jnp.concatenate(
        [one[:, 0:64], two[:, 0:64]], axis=1
    )
    target[:, 1024 + 128 * k : 1152 + 128 * k] = jnp.concatenate(
        [one[:, 64:128], two[:, 64:128]], axis=1
    )


INPUTS = (
    "lengths",
    "x",
    "c",
    "joint",
    "output",
    "expand",
    "reduce",
    "vectors",
    "m_joint",
    "m_output",
    "m_expand",
    "m_reduce",
    "first",
    "second",
)

OUTPUTS = (
    ("g_joint", (4, 1536), F32),
    ("g_output", (4, 512), F32),
    ("g_expand", (4, 2048), F32),
    ("g_reduce", (4, 2048), F32),
    ("n_joint", (4, 1536), F32),
    ("n_output", (4, 512), F32),
    ("n_expand", (4, 2048), F32),
    ("n_reduce", (4, 2048), F32),
    ("u_joint", (4, 1536), F32),
    ("u_output", (4, 512), F32),
    ("u_expand", (4, 2048), F32),
    ("u_reduce", (4, 2048), F32),
    ("block_output", (128, 512), BF),
    ("input_grad", (128, 512), F32),
    ("vector_grad", (4, 11), F32),
    ("second_next", (4, 11), F32),
    ("vector_next", (4, 11), F32),
)

SCRATCH = (
    ("joint_v", (4, 1536), F32),
    ("output_v", (4, 512), F32),
    ("expand_v", (4, 2048), F32),
    ("reduce_v", (4, 2048), F32),
    ("vectors_v", (4, 11), F32),
    ("first_v", (4, 11), F32),
    ("second_v", (4, 11), F32),
    ("table", (128, 128), F32),
    ("vec_sum", (4, 16, 128), F32),
    ("m_joint_v", (4, 1536), F32),
    ("m_output_v", (4, 512), F32),
    ("m_expand_v", (4, 2048), F32),
    ("m_reduce_v", (4, 2048), F32),
    ("j_out", (4, 4, 384), F32),
    ("j_in", (4, 4, 384), F32),
    ("j_rows", (16, 384), F32),
    ("w_out", (4, 4, 1536), F32),
    ("w_in", (4, 4, 1536), F32),
    ("w_rows", (16, 1536), F32),
    ("wj", (2, 4, 4, 16, 512), BF),
    ("wr", (2, 4, 4, 16, 1536), BF),
    ("w_joint", (32, 16, 384), BF),
    ("w_output", (32, 16, 512), BF),
    ("w_expand", (32, 16, 512), BF),
    ("w_reduce", (32, 16, 512), BF),
    ("v_own", (16, 128), F32),
    ("m_own", (4, 4, 2048), F32),
    ("m_early", (4, 4, 2048), F32),
    ("m_old", (16, 2048), F32),
    ("v_in", (4, 16, 128), F32),
    ("v", (4, 16, 128), F32),
    ("rows_x", (4, 128, 512), BF),
    ("rows_c", (4, 128, 512), BF),
    ("cos", (4, 128, 128), F32),
    ("sin", (4, 128, 128), F32),
    ("normed", (4, 128, 512), BF),
    ("query", (512, 128), F32),
    ("q_buf", (2, 512, 128), BF),
    ("kv_buf", (2, 512, 128), BF),
    ("qo", (2, 512, 128), BF),
    ("kv", (8, 512, 128), BF),
    ("hidden", (4, 128, 512), BF),
    ("pre", (4, 128, 512), BF),
    ("feed", (4, 128, 512), F32),
    ("row_grad", (4, 128, 512), F32),
    ("gf", (2, 4, 4, 16, 1024), BF),
    ("gf_core", (4, 4, 16, 1024), BF),
    ("gf_chip", (4, 4, 16, 1024), BF),
    ("gf_in", (15, 16, 1024), BF),
    ("go", (2, 4, 4, 16, 128), BF),
    ("go_core", (4, 4, 16, 128), BF),
    ("go_chip", (4, 4, 16, 128), BF),
    ("go_in", (15, 16, 128), BF),
    ("early_out", (4, 4, 1152), F32),
    ("early_in", (4, 4, 1152), F32),
    ("turned", (8, 128, 512), BF),
    ("keys", (8, 512, 128), BF),
    ("scores", (9, 512, 512), F32),
    ("sums", (2, 512, 128), F32),
    ("query_low", (2, 512, 128), BF),
    ("grad_low", (2, 512, 128), BF),
    ("back_turned", (2, 64, 512), F32),
    ("centre", (2, 1, 512), F32),
    ("out_low", (2, 64, 512), BF),
    ("out_heads", (2, 64, 512), BF),
    ("back_low", (2, 64, 512), BF),
    ("back_heads", (2, 64, 512), BF),
    ("dk", (2, 4, 512, 128), BF),
    ("dk_in", (4, 512, 128), BF),
    ("dk_chip", (4, 512, 128), BF),
    ("dk_mate", (2, 512, 128), BF),
    ("dk_pass", (512, 128), BF),
    ("dk_cross", (512, 128), BF),
    ("dkv", (2, 512, 128), BF),
    ("pair_out", (128, 512), BF),
    ("joint_out", (512, 384), BF),
    ("out_cols", (4, 128, 128), BF),
    ("out_in", (4, 128, 128), BF),
    ("out_part", (4, 128, 512), BF),
    ("out_got", (4, 128, 512), BF),
    ("back_part", (4, 128, 512), BF),
    ("back_got", (4, 128, 512), BF),
    ("gj", (2, 4, 4, 16, 384), BF),
    ("gj_core", (4, 4, 16, 384), BF),
    ("gj_chip", (4, 4, 16, 384), BF),
    ("gj_in", (15, 16, 384), BF),
    ("late_out", (4, 4, 384), F32),
    ("late_in", (4, 4, 384), F32),
    ("vp", (4, 4, 16, 128), F32),
    ("vp_core", (4, 16, 128), F32),
    ("vp_z", (3, 4, 16, 128), F32),
    ("vp_x", (3, 4, 16, 128), F32),
    ("vp_t", (3, 4, 16, 128), F32),
    ("gm_out", (4, 16, 512), BF),
    ("gm_in", (4, 16, 512), BF),
    ("m_rows", (16, 2048), F32),
    ("momentum", (2, 4, 4, 16, 1536), BF),
    ("extra", (2, 4, 4, 16, 512), BF),
    ("gram", (512, 512), F32),
    ("gram_h", (512, 512), BF),
    ("gram_l", (512, 512), BF),
    ("poly_h", (512, 512), BF),
    ("poly_l", (512, 512), BF),
    ("temp_h", (512, 512), BF),
    ("temp_l", (512, 512), BF),
    ("u_rows", (4, 16, 512), F32),
    ("u_out", (4, 16, 512), BF),
    ("u_in", (4, 16, 512), BF),
    ("u_wide", (4, 4, 2048), F32),
)

PUSHES = 240
LOADS = 16


class Box:
    pass


def attend_chunk(place, slot):
    return place.seq if slot == 0 else 7 - place.seq


def attend_score(slot, k):
    return 8 - k if slot == 0 else k


def pairs(count, step, carry):
    def two(k, carry):
        return step(2 * k + 1, step(2 * k, carry))

    def one(_, carry):
        return step(count - 1, carry)

    carry = lax.fori_loop(0, lax.div(count, 2), two, carry)
    return lax.fori_loop(0, lax.rem(count, 2), one, carry)


def attend_forward(r, place, slot):
    chunk = attend_chunk(place, slot)
    low = lax.broadcasted_iota(jnp.int32, (512, 128), 1) < 64
    packed = r.qo[slot].astype(F32)
    r.query_low[slot] = jnp.where(low, packed * (HD ** -0.5), 0.0).astype(BF)
    r.grad_low[slot] = jnp.where(low, 0.0, packed).astype(BF)
    out_grad = r.qo[slot].T[64:128, :].astype(F32)
    high, small = halves(packed * (HD ** -0.5 * LOG2_E))
    high, small = high.astype(F32), small.astype(F32)
    query = jnp.where(low, high, pltpu.roll(small, 64, 1)).astype(BF)
    index = 512 * chunk + lax.broadcasted_iota(jnp.int32, (1, 512), 1)
    begin = jnp.zeros((1, 512), jnp.int32)
    finish = 0
    for j in range(4):
        finish = finish + r.lengths[0, j]
        begin = jnp.where(index >= finish, finish, begin)

    def score(k, carry, last=False):
        top, total_sum = carry
        raw = dot_cols(r.keys[k], query)
        key = lax.broadcasted_iota(jnp.int32, (512, 512), 0)
        allowed = key >= begin - 512 * k
        if last:
            allowed = allowed & (key <= lax.broadcasted_iota(jnp.int32, (512, 512), 1))
        raw = jnp.where(allowed, raw, masked_score)
        r.scores[attend_score(slot, k)] = raw
        higher = jnp.maximum(top, jnp.max(raw, axis=0, keepdims=True))
        part = jnp.sum(jnp.exp2(raw - higher), axis=0, keepdims=True)
        return higher, total_sum * jnp.exp2(top - higher) + part

    start = (jnp.full((1, 512), masked_score, F32), jnp.zeros((1, 512), F32))
    top, total_sum = score(chunk, pairs(chunk, score, start), last=True)
    level = top + jnp.log(total_sum) * LOG2_E

    def weigh(k, out):
        prob = jnp.exp2(r.scores[attend_score(slot, k)] - level)
        r.scores[attend_score(slot, k)] = prob
        return out + dot(r.turned[k, 64:128, :], prob.astype(BF))

    out = pairs(chunk + 1, weigh, jnp.zeros((64, 512), F32))
    r.out_low[slot] = out.astype(BF)
    r.back_turned[slot] = jnp.zeros((64, 512), F32)
    r.centre[slot] = jnp.sum(out * out_grad, axis=0, keepdims=True)


def attend_backward(r, place, column):
    r.sums[...] = jnp.zeros_like(r.sums)

    def both_slots(slot, _):
        chunk = (1 - slot) * place.seq + slot * (7 - place.seq)
        out_grad, query, centre = r.grad_low[slot], r.query_low[slot], r.centre[slot]

        def block(part):
            k = 2 * column + part
            prob = r.scores[(1 - slot) * (8 - k) + slot * k]
            grad = dot_cols(r.kv[k], out_grad)
            score_grad = (prob * (grad - centre)).astype(BF)
            r.sums[part] += dot(prob.astype(BF), out_grad) + dot(score_grad, query)
            return dot(r.turned[k, 0:64, :], score_grad)

        @pl.when(2 * column + 1 <= chunk)
        def _():
            r.back_turned[slot] += block(0) + block(1)

        @pl.when(2 * column == chunk)
        def _():
            r.back_turned[slot] += block(0)

        return 0

    lax.fori_loop(0, 2, both_slots, 0)
    r.dk[0, column] = r.sums[0].astype(BF)
    r.dk[1, column] = r.sums[1].astype(BF)


def newton(r, place):
    blocks, size = 1, 512

    def rows(i):
        return pl.ds(size * i, size)

    def diagonal(i):
        row = size * i + lax.broadcasted_iota(jnp.int32, (size, 512), 0)
        return row == lax.broadcasted_iota(jnp.int32, (size, 512), 1)

    def fill(i, trace):
        value = jnp.zeros((size, 512), F32)
        for k in range(3):
            lanes = slice(512 * k, 512 * k + 512)
            right = r.momentum[:, :, :, :, lanes].reshape(512, 512)
            value = value + dot_cols(right, right)
        r.gram[rows(i), :] = value

        @pl.when(place.t >= 2)
        def _():
            right = r.extra[...].reshape(512, 512)
            r.gram[rows(i), :] += dot_cols(right, right)

        value = r.gram[rows(i), :]
        return trace + jnp.sum(jnp.where(diagonal(i), value, 0.0), keepdims=True)

    trace = lax.fori_loop(0, blocks, fill, jnp.zeros((1, 1), F32))
    scale = 1.0 / (jnp.sqrt(trace) + 1e-07)

    def keep(value, i, high_ref, low_ref):
        high, small = halves(value)
        high_ref[rows(i), :] = high
        low_ref[rows(i), :] = small

    def prepare(i, _):
        value = r.gram[rows(i), :] * (scale * scale)
        r.gram[rows(i), :] = value
        keep(value, i, r.gram_h, r.gram_l)
        return 0

    lax.fori_loop(0, blocks, prepare, 0)

    def polynomial(i, _):
        square = squared(r.gram_h[...], r.gram_l[...])
        value = (
            jnp.where(diagonal(i), newton_first, 0.0)
            + newton_second * r.gram[rows(i), :]
            + newton_third * square
        )
        keep(value, i, r.poly_h, r.poly_l)
        return 0

    def inner(i, _):
        value = squared(r.poly_h[...], r.poly_l[...])
        keep(value, i, r.temp_h, r.temp_l)
        return 0

    def outer(i, _):
        value = product(r.gram_h[...], r.gram_l[...], r.temp_h[...], r.temp_l[...])
        r.gram[rows(i), :] = value
        keep(value, i, r.gram_h, r.gram_l)
        return 0

    def times(left, right_h, right_l):
        high, small = halves(left)
        return product(high, small, right_h[...], right_l[...])

    mine = pl.ds(pl.multiple_of(256 * place.c + 64 * place.a + 16 * place.b, 16), 16)
    own = None
    for sweep in range(4):
        lax.fori_loop(0, blocks, polynomial, 0)
        if sweep == 0:
            own = r.poly_h[mine, :].astype(F32) + r.poly_l[mine, :].astype(F32)
        else:
            own = times(own, r.poly_h, r.poly_l)
        if sweep < 3:
            lax.fori_loop(0, blocks, inner, 0)
            lax.fori_loop(0, blocks, outer, 0)

    def last_gram(left):
        left = times(left, r.gram_h, r.gram_l)
        left = times(left, r.poly_h, r.poly_l)
        return times(left, r.poly_h, r.poly_l)

    once = last_gram(own)
    own = newton_first * own + newton_second * once + newton_third * last_gram(once)
    return halves(own * scale)


def block_kernel(*refs):
    r = Box()
    names = list(INPUTS) + [n for n, _, _ in OUTPUTS] + [n for n, _, _ in SCRATCH]
    for name, ref in zip(names, refs):
        setattr(r, name, ref)
    place = Place()
    wire = Wire(*refs[-3:])
    z, x, c, t, d = place.z, place.x, place.c, place.t, place.d
    seq, mate, cross, head = place.seq, place.mate, place.cross, place.head
    sibling = place.sibling()

    met = greet(
        place.octet()
        + [place.at_ab(a, b) for a, b in place.plane()]
        + [place.at(x=cross, c=1 - c)]
    )

    load_w = [
        wire.load(r.joint, r.joint_v),
        wire.load(r.output, r.output_v),
        wire.load(r.expand, r.expand_v),
        wire.load(r.reduce, r.reduce_v),
    ]
    load_v = wire.load(r.vectors, r.vectors_v)
    load_x = wire.load(r.x, r.rows_x.at[t])
    load_c = wire.load(r.c, r.rows_c.at[t])
    load_m = [
        wire.load(r.m_joint, r.m_joint_v),
        wire.load(r.m_output, r.m_output_v),
        wire.load(r.m_expand, r.m_expand_v),
        wire.load(r.m_reduce, r.m_reduce_v),
        wire.load(r.first, r.first_v),
        wire.load(r.second, r.second_v),
    ]
    for copy in load_w:
        copy.wait()
    for k in range(4):
        for part in range(3):
            r.j_out[k, :, 128 * part : 128 * part + 128] = r.joint_v[
                :, 512 * part + 128 * k : 512 * part + 128 * k + 128
            ]
        r.w_out[k, :, 0:512] = r.output_v[...]
        r.w_out[k, :, 512:1024] = r.expand_v[:, 512 * k : 512 * k + 512]
        r.w_out[k, :, 1024:1536] = r.reduce_v[:, 512 * k : 512 * k + 512]
    load_v.wait()
    r.table[...] = jnp.zeros((128, 128), F32)
    column = lax.broadcasted_iota(jnp.int32, (128, 11), 0) - (16 * seq + 4 * t)
    own_vec = jnp.zeros((128, 11), F32)
    for j in range(4):
        own_vec = jnp.where(column == j, r.vectors_v[j : j + 1, :], own_vec)
    r.table[:, 0:11] = own_vec.astype(BF).astype(F32)
    r.v_own[...] = r.table[...].T[0:16, :]
    load_x.wait()
    load_c.wait()
    met()

    joint_t = trade_t(wire, place, r.j_out, r.j_in)
    for partner in place.row_t():
        joint_t.append(wire.push(r.v_own, r.v_in.at[t], partner))
    rest_t = trade_t(wire, place, r.w_out, r.w_in)
    r.j_in[t] = r.j_out[t]
    r.v_in[t] = r.v_own[...]
    r.w_in[t] = r.w_out[t]
    arrive(joint_t)
    for k in range(4):
        r.j_rows[4 * k : 4 * k + 4, :] = r.j_in[k]
    keys, values = r.j_rows[:, 128:256], r.j_rows[:, 256:384]
    low16 = lax.broadcasted_iota(jnp.int32, (16, 128), 1) < 64
    own_block = r.wj.at[c, place.a, place.b]
    own_block[:, 0:128] = r.j_rows[:, 0:128].astype(BF)
    own_block[:, 128:256] = jnp.where(low16, keys, pltpu.roll(values, 64, 1)).astype(BF)
    own_block[:, 256:384] = jnp.where(low16, pltpu.roll(keys, 64, 1), values).astype(BF)
    own_block[:, 384:512] = ((r.v_in[0] + r.v_in[1]) + (r.v_in[2] + r.v_in[3])).astype(BF)
    joint_all = spread_plane(wire, place, r.wj)
    x_rows = [wire.push(r.rows_x.at[t], r.rows_x.at[t], p) for p in place.row_t()]
    arrive(rest_t)
    for k in range(4):
        r.w_rows[4 * k : 4 * k + 4, :] = r.w_in[k]
    r.wr[c, place.a, place.b] = r.w_rows[...].astype(BF)
    rest_b = spread_b(wire, place, r.wr)

    half = ROT // 2
    lane = lax.rem(lax.broadcasted_iota(jnp.int32, (1, 128), 1), 64)
    frequency = jnp.zeros((1, 128), F32)
    for i in range(half):
        frequency = jnp.where(lax.rem(lane, half) == i, 10000.0 ** (-2.0 * i / ROT), frequency)
    frequency = jnp.where(lane < ROT, frequency, 0.0)

    def angles(i, _):
        index = 512 * seq + 128 * i + lax.broadcasted_iota(jnp.int32, (128, 1), 0)
        begin = jnp.zeros((128, 1), jnp.int32)
        finish = 0
        for j in range(4):
            finish = finish + r.lengths[0, j]
            begin = jnp.where(index >= finish, finish, begin)
        angle = (index - begin).astype(F32) * frequency
        r.cos[i] = jnp.cos(angle)
        r.sin[i] = jnp.sin(angle)
        return 0

    lax.fori_loop(0, 4, angles, 0)
    for copy in load_m:
        copy.wait()
    c_rows = [wire.push(r.rows_c.at[t], r.rows_c.at[t], p) for p in place.row_t()]
    arrive(joint_all)
    joint_swap = swap_cores(wire, place, r.wj)
    arrive(rest_b)
    rest_up, rest_down = ring_open(wire, place, r.wr)
    rest_swaps = [swap_part(wire, place, r.wr, 0)]
    arrive([joint_swap, *x_rows])
    for k in range(4):
        own_vec = jnp.zeros((16, 128), F32)
        for i in range(4):
            for part in (r.wj[0, k, i, :, 384:512], r.wj[1, i, k, :, 384:512]):
                own_vec = own_vec + part.astype(F32)
        r.v[k] = own_vec
    natural(r.wj, r.w_joint, 0, 384)

    gain, shift = vec_row(r.v, 0), vec_row(r.v, 1)
    q_bias, k_bias, v_bias = r.v[t, 2:3, :], r.v[t, 3:4, :], r.v[t, 4:5, :]
    low_row = lax.broadcasted_iota(jnp.int32, (1, 128), 1) < 64
    pair_bias = (
        jnp.where(low_row, k_bias, pltpu.roll(v_bias, 64, 1)),
        jnp.where(low_row, pltpu.roll(k_bias, 64, 1), v_bias),
    )
    low = lax.broadcasted_iota(jnp.int32, (256, 128), 1) < 64

    def project(i, _):
        blocks, rows = pl.ds(2 * i, 2), pl.ds(256 * i, 256)
        normal, _rate = normalise(r.rows_x[blocks].reshape(256, 512))
        part = (normal * gain + shift).astype(BF)
        r.normed[blocks] = part.reshape(2, 128, 512)
        raw = dot(part, r.w_joint[...].reshape(512, 384))
        cosine, sine = r.cos[blocks].reshape(256, 128), r.sin[blocks].reshape(256, 128)
        r.query[rows, :] = turn(raw[:, 0:128] + q_bias, cosine, sine, 1.0)
        key_cos = jnp.where(low, cosine, 1.0)
        key_sin = jnp.where(low, sine, 0.0)
        for h in range(2):
            pair = raw[:, 128 + 128 * h : 256 + 128 * h] + pair_bias[h]
            r.kv_buf[h, rows, :] = turn(pair, key_cos, key_sin, 1.0).astype(BF)
        return 0

    lax.fori_loop(0, 2, project, 0)
    kv_cross = wire.push(r.kv_buf.at[1 - head], r.kv.at[seq], place.at(x=cross))
    kv_mate = wire.push(r.kv_buf.at[head], r.kv.at[seq], place.at(x=mate))
    kv_core = wire.push(r.kv_buf.at[head], r.kv.at[seq], sibling)
    r.kv[seq] = r.kv_buf[head]
    rest_more = ring_pass(wire, place, r.wr, rest_up, rest_down)
    rest_swaps += ring_close(wire, place, r.wr, rest_up, rest_down, rest_more)
    for k in range(4):
        lanes = slice(128 * k, 128 * k + 128)
        keys = r.m_joint_v[:, 512 + 128 * k : 640 + 128 * k]
        values = r.m_joint_v[:, 1024 + 128 * k : 1152 + 128 * k]
        start = 384 * k
        r.m_own[0, :, start : start + 128] = r.m_joint_v[:, lanes]
        r.m_own[0, :, start + 128 : start + 256] = jnp.concatenate(
            [keys[:, 0:64], values[:, 0:64]], axis=1
        )
        r.m_own[0, :, start + 256 : start + 384] = jnp.concatenate(
            [keys[:, 64:128], values[:, 64:128]], axis=1
        )
    r.m_own[0, :, 1536:2048] = jnp.zeros((4, 512), F32)
    r.m_own[1, :, 0:512] = r.m_output_v[...]
    r.m_own[1, :, 512:2048] = jnp.zeros((4, 1536), F32)
    r.m_own[2] = r.m_expand_v[...]
    r.m_own[3] = r.m_reduce_v[...]
    at_cross, at_mate = 2 * cross + c, 2 * mate + c
    at_far = 2 * (3 - mate) + c
    kv_cross.wait_recv()
    kv_far = wire.push(r.kv.at[at_cross], r.kv.at[at_cross], place.at(x=mate))
    kv_more = [kv_core, wire.push(r.kv.at[at_cross], r.kv.at[at_cross], sibling)]
    arrive([*c_rows, *rest_swaps])
    natural(r.wr, r.w_output, 0, 512)
    natural(r.wr, r.w_expand, 512, 1024)
    natural(r.wr, r.w_reduce, 1024, 1536)
    out_rows = r.w_output[pl.ds(8 * t, 8)].reshape(128, 512)
    low = lax.broadcasted_iota(jnp.int32, (512, 128), 1) < 64
    grad = dot_cols(r.rows_c[...].reshape(512, 512), out_rows)
    query = r.query[...]
    r.q_buf[0] = jnp.where(low, query, pltpu.roll(grad, 64, 1)).astype(BF)
    r.q_buf[1] = jnp.where(low, pltpu.roll(query, 64, 1), grad).astype(BF)
    q_cross = wire.push(r.q_buf.at[1 - head], r.qo.at[1], place.at(x=cross, c=1 - c))
    early = trade_t(wire, place, r.m_own, r.m_early)
    r.qo[0] = r.q_buf[head]

    bias = jnp.concatenate([r.v[k, pl.ds(7 + t, 1), :] for k in range(4)], axis=1)

    def feed_forward(i, sums):
        blocks = pl.ds(2 * i, 2)
        part = r.normed[blocks].reshape(256, 512)
        wide = dot(part, r.w_expand[...].reshape(512, 512)) + bias
        square = wide * wide
        curve = jnp.tanh(0.7978845608 * (wide + 0.044715 * (square * wide)))
        r.hidden[blocks] = (0.5 * wide * (1.0 + curve)).astype(BF).reshape(2, 128, 512)
        slope = 0.5 * (1.0 + curve) + (0.5 * 0.7978845608) * wide * (1.0 - curve * curve) * (
            1.0 + (3 * 0.044715) * square
        )
        part = r.rows_c[blocks].reshape(256, 512)
        back = dot(part, r.w_reduce[...].reshape(512, 512))
        grad = (back * slope).astype(BF)
        r.pre[blocks] = grad.reshape(2, 128, 512)
        return sums + jnp.sum(grad.astype(F32), axis=0, keepdims=True)

    hidden_sum = lax.fori_loop(0, 2, feed_forward, jnp.zeros((1, 512), F32))
    kv_mate.wait_recv()
    kv_more.append(wire.push(r.kv.at[at_mate], r.kv.at[at_mate], sibling))
    for j in range(4):
        lanes = slice(128 * j, 128 * j + 128)
        expand_grad = dot_rows(
            r.normed[:, :, lanes].reshape(512, 128), r.pre[...].reshape(512, 512)
        )
        by_owner(r.gf, j, expand_grad.astype(BF), 0, 512)
        reduce_grad = dot_rows(
            r.rows_c[:, :, lanes].reshape(512, 128), r.hidden[...].reshape(512, 512)
        )
        by_owner(r.gf, j, reduce_grad.astype(BF), 512, 1024)
    gf_swap = sum_cores(wire, place, r.gf, r.gf_core)
    kv_far.wait_recv()
    kv_more.append(wire.push(r.kv.at[at_far], r.kv.at[at_far], sibling))

    arrive(early)
    r.m_early[t] = r.m_own[t]
    for k in range(4):
        r.m_old[4 * k : 4 * k + 4, :] = r.m_early[k]
    gf_swap.wait_recv()
    for a in range(4):
        r.gf_chip[a] = (r.gf[c, a].astype(F32) + r.gf_core[a].astype(F32)).astype(BF)
    arrive([*kv_more, q_cross])
    gf_all = scatter_plane(wire, place, r.gf_chip, r.gf_in)

    low = lax.broadcasted_iota(jnp.int32, (512, 128), 1) < 64
    for k in range(8):
        r.turned[k] = r.kv[k].T
        wide = r.kv[k].astype(F32)
        r.keys[k] = jnp.where(low, wide, pltpu.roll(wide, 64, 1)).astype(BF)
    attend_forward(r, place, 1)
    out_cross = wire.push(r.out_low.at[1], r.out_heads.at[head], place.at(x=cross, c=1 - c))
    attend_forward(r, place, 0)
    r.out_heads[head] = r.out_low[0]

    far = 3 - mate
    dk_swap = []

    def chip_sum(index):
        return r.dk[c, index].astype(F32) + r.dk_in[index].astype(F32)

    for step, column in enumerate((far, mate, cross, x)):
        attend_backward(r, place, column)
        dk_swap.append(wire.push(r.dk.at[1 - c, column], r.dk_in.at[column], sibling))
        if step == 0:
            out_cross.wait_recv()
            turned = r.out_heads[...].reshape(128, 512)
            r.pair_out[...] = turned
            out_grad = dot(turned, r.rows_c[...].reshape(512, 512)).astype(BF)
            for j in range(4):
                r.out_cols[j] = out_grad[:, 128 * j : 128 * j + 128]
            out_cols = trade_t(wire, place, r.out_cols, r.out_in)
            r.out_in[t] = r.out_cols[t]
        if step == 1:
            dk_swap[0].wait_recv()
            r.dk_chip[0] = chip_sum(far).astype(BF)
            dk_far = wire.push(r.dk_chip.at[0], r.dk_mate.at[0], place.at(x=mate))
        if step == 2:
            dk_swap[1].wait_recv()
            r.dk_chip[1] = chip_sum(mate).astype(BF)
            dk_near = wire.push(r.dk_chip.at[1], r.dk_mate.at[1], place.at(x=mate))
            arrive(out_cols)
            for j in range(4):
                by_owner(r.go, j, r.out_in[j], 0, 128)
            go_swap = sum_cores(wire, place, r.go, r.go_core)
    for slot in range(2):
        r.back_low[slot] = (r.back_turned[slot] * (HD ** -0.5)).astype(BF)
    back_cross = wire.push(r.back_low.at[1], r.back_heads.at[head], place.at(x=cross, c=1 - c))
    r.back_heads[head] = r.back_low[0]
    go_swap.wait_recv()
    for a in range(4):
        r.go_chip[a] = (r.go[c, a].astype(F32) + r.go_core[a].astype(F32)).astype(BF)
    go_all = scatter_plane(wire, place, r.go_chip, r.go_in)

    arrive([dk_swap[2], dk_far])
    r.dk_pass[...] = (chip_sum(cross) + r.dk_mate[0].astype(F32)).astype(BF)
    dk_cross = wire.push(r.dk_pass, r.dk_cross, place.at(x=cross))
    def feed_out(i, _):
        blocks = pl.ds(2 * i, 2)
        part = r.hidden[blocks].reshape(256, 512)
        r.feed[blocks] = dot_cols(part, r.w_reduce[...].reshape(512, 512)).reshape(2, 128, 512)
        part = r.pre[blocks].reshape(256, 512)
        r.row_grad[blocks] = dot_cols(part, r.w_expand[...].reshape(512, 512)).reshape(2, 128, 512)
        return 0

    lax.fori_loop(0, 2, feed_out, 0)
    out_rows = r.w_output[pl.ds(8 * t, 8)].reshape(128, 512)
    for i in range(2):
        blocks, lanes = slice(2 * i, 2 * i + 2), slice(256 * i, 256 * i + 256)
        part = r.feed[blocks].reshape(256, 512) + dot_rows(r.pair_out[:, lanes], out_rows)
        r.out_part[blocks] = part.astype(BF).reshape(2, 128, 512)
    out_parts = trade_t(wire, place, r.out_part, r.out_got)
    r.out_got[t] = r.out_part[t]
    back_cross.wait_recv()
    back = r.back_heads[...].reshape(128, 512).astype(F32).T
    cosine, sine = r.cos[...].reshape(512, 128), r.sin[...].reshape(512, 128)
    r.joint_out[:, 0:128] = turn(back, cosine, sine, -1.0).astype(BF)
    low = lax.broadcasted_iota(jnp.int32, (128, 128), 1) < 64
    arrive([dk_swap[3], dk_near])
    r.dkv[head] = (chip_sum(x) + r.dk_mate[1].astype(F32)).astype(BF)
    dk_cross.wait_recv()
    r.dkv[1 - head] = r.dk_cross[...]
    for h in range(2):
        for i in range(4):
            rows = pl.ds(128 * i, 128)
            key_cos = jnp.where(low, r.cos[i], 1.0)
            key_sin = jnp.where(low, r.sin[i], 0.0)
            r.joint_out[rows, 128 + 128 * h : 256 + 128 * h] = turn(
                r.dkv[h, rows, :].astype(F32), key_cos, key_sin, -1.0
            ).astype(BF)
    for j in range(4):
        part = r.normed[:, :, 128 * j : 128 * j + 128].reshape(512, 128)
        by_owner(r.gj, j, dot_rows(part, r.joint_out[...]).astype(BF), 0, 384)
    gj_swap = sum_cores(wire, place, r.gj, r.gj_core)

    r.vp[0] = jnp.zeros((4, 16, 128), F32)
    shift_sum = jnp.zeros((1, 512), F32)
    gain_sum = jnp.zeros((1, 512), F32)
    for i in range(4):
        rows = pl.ds(128 * i, 128)
        part = r.row_grad[i] + dot_cols(r.joint_out[rows, :], r.w_joint[...].reshape(512, 384))
        r.back_part[i] = part.astype(BF)
        normal, _rate = normalise(r.rows_x[i])
        shift_sum = shift_sum + jnp.sum(part, axis=0, keepdims=True)
        gain_sum = gain_sum + jnp.sum(part * normal, axis=0, keepdims=True)
    gj_swap.wait_recv()
    for a in range(4):
        r.gj_chip[a] = (r.gj[c, a].astype(F32) + r.gj_core[a].astype(F32)).astype(BF)
    gj_all = scatter_plane(wire, place, r.gj_chip, r.gj_in)
    back_parts = trade_t(wire, place, r.back_part, r.back_got)
    r.back_got[t] = r.back_part[t]
    out_sum = jnp.sum(r.rows_c[t].astype(F32), axis=0, keepdims=True)
    joint_sum = jnp.sum(r.joint_out[...].astype(F32), axis=0, keepdims=True)
    one, two = joint_sum[:, 128:256], joint_sum[:, 256:384]
    for k in range(4):
        lanes = slice(128 * k, 128 * k + 128)
        r.vp[0, k, 0:1, :] = gain_sum[:, lanes]
        r.vp[0, k, 1:2, :] = shift_sum[:, lanes]
        r.vp[0, k, 5:6, :] = out_sum[:, lanes]
        r.vp[0, k, 6:7, :] = out_sum[:, lanes]
        r.vp[0, k, pl.ds(7 + t, 1), :] = hidden_sum[:, lanes]
    r.vp[0, t, 2:3, :] = joint_sum[:, 0:128]
    r.vp[0, t, 3:4, :] = jnp.where(low_row, one, pltpu.roll(two, 64, 1))
    r.vp[0, t, 4:5, :] = jnp.where(low_row, pltpu.roll(one, 64, 1), two)
    vp_swap = wire.push(r.vp.at[0], r.vp_core, sibling)
    arrive(gf_all)
    gf_own = add_plane(r.gf_chip[place.a, place.b], r.gf_in)
    arrive(go_all)
    go_own = add_plane(r.go_chip[place.a, place.b], r.go_in)
    for k in range(4):
        r.early_out[k, :, 0:1024] = gf_own[4 * k : 4 * k + 4, :]
        r.early_out[k, :, 1024:1152] = go_own[4 * k : 4 * k + 4, :]
    r.gm_out[1, :, 0:128] = go_own.astype(BF)
    r.gm_out[2] = gf_own[:, 0:512].astype(BF)
    r.gm_out[3] = gf_own[:, 512:1024].astype(BF)
    gm_first = wire.block(4)
    gm_widths = (384, 128, 512, 512)

    def to_newton(w, sender):
        lanes = slice(0, gm_widths[w])
        return wire.offer(
            gm_first, r.gm_out.at[w, :, lanes], r.gm_in.at[sender, :, lanes], sender, w,
            place.at(t=w),
        )

    def send_newton(w):
        @pl.when(t != w)
        def _():
            to_newton(w, t).start()

        @pl.when(t == w)
        def _():
            r.gm_in[w, :, 0 : gm_widths[w]] = r.gm_out[w, :, 0 : gm_widths[w]]

    for w in (1, 2, 3):
        send_newton(w)
    early_t = trade_t(wire, place, r.early_out, r.early_in)
    r.early_in[t] = r.early_out[t]

    vp_swap.wait_recv()
    r.vp[1] = r.vp[0] + r.vp_core[...]
    vp_z = [wire.push(r.vp.at[1], r.vp_z.at[k], p) for k, p in enumerate(place.row_z())]

    arrive(gj_all)
    gj_own = add_plane(r.gj_chip[place.a, place.b], r.gj_in)
    r.gm_out[0, :, 0:384] = gj_own.astype(BF)
    send_newton(0)
    for k in range(4):
        r.late_out[k] = gj_own[4 * k : 4 * k + 4, :]
    late_t = trade_t(wire, place, r.late_out, r.late_in)
    r.late_in[t] = r.late_out[t]
    arrive(vp_z)
    r.vp[2] = total(r.vp[1], r.vp_z)
    vp_x = [wire.push(r.vp.at[2], r.vp_x.at[k], p) for k, p in enumerate(place.row_x())]

    for w in range(4):

        @pl.when(t == w)
        def _(w=w):
            width = gm_widths[w]
            for sender in range(4):
                if sender != w:
                    to_newton(w, sender).wait_recv()
            for k in range(4):
                lanes = slice(width * k, width * k + width)
                value = muon_beta * r.m_old[:, lanes] + r.gm_in[k, :, 0:width].astype(F32)
                if width * k < 1536:
                    r.momentum[c, place.a, place.b, :, lanes] = value.astype(BF)
                else:
                    r.extra[c, place.a, place.b] = value.astype(BF)
            if w == 1:
                r.momentum[c, place.a, place.b, :, 512:1536] = jnp.zeros((16, 1024), BF)

    m_b = spread_b(wire, place, r.momentum)

    extra_first = wire.block(16)

    def extra_copies():
        block = r.extra.at[c, place.a, place.b]
        copies = []
        for k, (a, b) in enumerate(place.plane()):
            copies.append(
                wire.offer(extra_first, block, block, k, k, place.at_ab(a, b))
            )
        return copies

    def extra_swap():
        block = r.extra.at[c]
        return wire.offer(extra_first, block, block, 15, 15, sibling)

    @pl.when(t >= 2)
    def _():
        for copy in extra_copies():
            copy.start()

    arrive(early_t)
    for k in range(4):
        part = r.early_in[k]
        r.g_expand[:, 512 * k : 512 * k + 512] = part[:, 0:512]
        r.g_reduce[:, 512 * k : 512 * k + 512] = part[:, 512:1024]
        r.g_output[:, 128 * k : 128 * k + 128] = part[:, 1024:1152]
    arrive(late_t)
    for k in range(4):
        unpair(r.g_joint, r.late_in[k], k)
    for old, grad, new in (
        (r.m_joint_v, r.g_joint, r.n_joint),
        (r.m_output_v, r.g_output, r.n_output),
        (r.m_expand_v, r.g_expand, r.n_expand),
        (r.m_reduce_v, r.g_reduce, r.n_reduce),
    ):
        new[...] = muon_beta * old[...] + grad[...]
    arrive(vp_x)
    r.vp[3] = total(r.vp[2], r.vp_x)
    vp_t = [wire.push(r.vp.at[3], r.vp_t.at[k], p) for k, p in enumerate(place.row_t())]
    arrive(out_parts)
    arrive(back_parts)
    arrive(m_b)
    m_up, m_down = ring_open(wire, place, r.momentum)
    m_swaps = [swap_part(wire, place, r.momentum, 0)]
    m_more = ring_pass(wire, place, r.momentum, m_up, m_down)
    wide = r.rows_x[t].astype(F32)
    feed = r.out_got[0].astype(F32)
    back = r.back_got[0].astype(F32)
    for k in range(1, 4):
        feed = feed + r.out_got[k].astype(F32)
        back = back + r.back_got[k].astype(F32)
    r.block_output[...] = (wide + feed + vec_row(r.v, 5) + vec_row(r.v, 6)).astype(BF)
    normal, rate = normalise(r.rows_x[t])
    scaled = back * gain
    mean_one = jnp.mean(scaled, axis=-1, keepdims=True)
    mean_two = jnp.mean(scaled * normal, axis=-1, keepdims=True)
    r.input_grad[...] = r.rows_c[t].astype(F32) + rate * (scaled - mean_one - normal * mean_two)
    m_swaps += ring_close(wire, place, r.momentum, m_up, m_down, m_more)
    arrive(vp_t)
    r.vec_sum[...] = total(r.vp[3], r.vp_t)
    r.table[0:16, :] = r.vec_sum[z]
    r.table[...] = r.table[...].T
    vector_grad = r.table[pl.ds(pl.multiple_of(16 * seq + 4 * t, 4), 4), 0:11]
    r.vector_grad[...] = vector_grad
    first_next = beta_first * r.first_v[...] + (1.0 - beta_first) * vector_grad
    second_next = (
        beta_second * r.second_v[...] + (1.0 - beta_second) * vector_grad * vector_grad
    )
    r.second_next[...] = second_next
    first_hat = first_next / (1.0 - beta_first**STEP)
    second_hat = second_next / (1.0 - beta_second**STEP)
    r.vector_next[...] = r.vectors_v[...] - vector_rate * first_hat / (
        jnp.sqrt(second_hat) + adam_epsilon
    )
    @pl.when(t >= 2)
    def _():
        for copy in extra_copies():
            copy.wait_recv()
        extra_swap().start()
        extra_swap().wait_recv()

    arrive(m_swaps)

    high, small = newton(r, place)
    for k in range(3):
        lanes = slice(512 * k, 512 * k + 512)
        columns = r.momentum[:, :, :, :, lanes].reshape(512, 512)
        r.m_rows[:, lanes] = dot(high, columns) + dot(small, columns)

    @pl.when(t >= 2)
    def _():
        columns = r.extra[...].reshape(512, 512)
        r.m_rows[:, 1536:2048] = dot(high, columns) + dot(small, columns)

    @pl.when(t < 2)
    def _():
        r.m_rows[:, 1536:2048] = jnp.zeros((16, 512), F32)

    for k in range(4):
        for p in range(4):
            r.u_rows[k, 4 * p : 4 * p + 4, :] = r.m_rows[
                4 * k : 4 * k + 4, 512 * p : 512 * p + 512
            ]
    r.u_out[...] = r.u_rows[...].astype(BF)
    u_t = trade_t(wire, place, r.u_out, r.u_in)
    r.u_in[t] = r.u_out[t]
    arrive(u_t)
    r.u_rows[...] = r.u_in[...].astype(F32)
    for k in range(4):
        for p in range(4):
            r.u_wide[k, :, 512 * p : 512 * p + 512] = r.u_rows[k, 4 * p : 4 * p + 4, :]
    for k in range(4):
        unpair(r.u_joint, r.u_wide[0, :, 384 * k : 384 * k + 384], k)
    for k, (old, change, new) in enumerate(
        (
            (r.joint_v, r.u_joint, r.u_joint),
            (r.output_v, r.u_wide.at[1, :, pl.ds(0, 512)], r.u_output),
            (r.expand_v, r.u_wide.at[2], r.u_expand),
            (r.reduce_v, r.u_wide.at[3], r.u_reduce),
        )
    ):
        factor = muon_rate * 0.2 * math.sqrt(max(D, WIDTHS[k]))
        new[...] = old[...] * (1.0 - muon_rate * muon_decay) - factor * change[...]
    wire.drain()
    for w in range(4):

        @pl.when(t != w)
        def _(w=w):
            to_newton(w, t).wait_send()

    @pl.when(t >= 2)
    def _():
        for copy in extra_copies():
            copy.wait_send()
        extra_swap().wait_send()


def block_stage(*arrays):
    return pl.pallas_call(
        block_kernel,
        out_shape=tuple(shape(dims, dtype) for _, dims, dtype in OUTPUTS),
        in_specs=[SMEM] + [ANY] * (len(INPUTS) - 1),
        out_specs=(VMEM,) * len(OUTPUTS),
        scratch_shapes=[pltpu.VMEM(dims, dtype) for _, dims, dtype in SCRATCH]
        + [
            pltpu.SemaphoreType.DMA((PUSHES,)),
            pltpu.SemaphoreType.DMA((PUSHES,)),
            pltpu.SemaphoreType.DMA((LOADS,)),
        ],
        compiler_params=pltpu.CompilerParams(
            collective_id=1, has_side_effects=True, vmem_limit_bytes=56 << 20
        ),
        name="block",
    )(*arrays)


def write_kernel(*refs):
    count = len(OUTPUTS)
    sem = refs[-1]
    copies = []
    for k in range(count):
        copy = pltpu.make_async_copy(refs[k], refs[count + k], sem.at[k])
        copy.start()
        copies.append(copy)
    for copy in copies:
        copy.wait()


def write_stage(*arrays):
    count = len(arrays)
    return pl.pallas_call(
        write_kernel,
        out_shape=tuple(shape(a.shape, a.dtype) for a in arrays),
        in_specs=[VMEM] * count,
        out_specs=(ANY,) * count,
        scratch_shapes=[pltpu.SemaphoreType.DMA((count,))],
        name="write",
    )(*arrays)


def shards(
    block_input,
    cotangent,
    doc_lengths,
    joint_weight,
    output_weight,
    expand_weight,
    reduce_weight,
    joint_moment,
    output_moment,
    expand_moment,
    reduce_moment,
    vectors,
    first_moment,
    second_moment,
):
    results = block_stage(
        doc_lengths, block_input, cotangent, joint_weight, output_weight, expand_weight,
        reduce_weight, vectors.T, joint_moment, output_moment, expand_moment, reduce_moment,
        first_moment.T, second_moment.T,
    )
    results = write_stage(*results)
    return (*results[12:14], *results[0:12], *[part.T for part in results[14:]])


def solution(mesh):
    rows = P(("fsdp", "seq", "tensor"), None)
    columns = P(None, ("fsdp", "seq", "tensor"))
    return jax.shard_map(
        shards,
        mesh=mesh,
        in_specs=(rows, rows, P("fsdp", None)) + (rows,) * 8 + (columns,) * 3,
        out_specs=(rows,) * 14 + (columns,) * 3,
        check_vma=False,
    )
```

```python
import functools
import math

import jax
import jax.numpy as jnp
from jax import lax
from jax.experimental import pallas as pl
from jax.experimental.pallas import tpu as pltpu
from jax.sharding import PartitionSpec as P

D = 512
HEADS = 8
FF = 2048
ROT = 16
HD = 64
STEP = 10

norm_epsilon = 1e-05
masked_score = -1e30
newton_first = 3.4445
newton_second = -4.775
newton_third = 2.0315
beta_first = 0.9
beta_second = 0.95
adam_epsilon = 1e-08
vector_rate = 0.2
muon_rate = 0.25
muon_beta = 0.95
muon_decay = 0.01
LOG2_E = 1.4426950408889634

BF = jnp.bfloat16
F32 = jnp.float32
MESH = pl.DeviceIdType.MESH
VMEM = pl.BlockSpec(memory_space=pltpu.VMEM)
SMEM = pl.BlockSpec(memory_space=pltpu.SMEM)
ANY = pl.BlockSpec(memory_space=pl.ANY)
WIDTHS = (3 * D, D, FF, FF)


def shape(dims, dtype):
    return jax.ShapeDtypeStruct(dims, dtype)


class Place:
    def __init__(self):
        self.z = lax.axis_index("fsdp")
        self.seq = lax.axis_index("seq")
        self.t = lax.axis_index("tensor")
        self.x = lax.div(self.seq, 2)
        self.c = lax.rem(self.seq, 2)
        self.d = 1 - 2 * self.c
        self.a = self.c * self.x + (1 - self.c) * self.z
        self.b = self.c * self.z + (1 - self.c) * self.x
        self.mate = self.x + 1 - 2 * lax.rem(self.x, 2)
        self.cross = 3 - self.x
        self.head = lax.div(self.x, 2)

    def at(self, z=None, x=None, c=None, t=None):
        z = self.z if z is None else z
        x = self.x if x is None else x
        c = self.c if c is None else c
        t = self.t if t is None else t
        return (z, 2 * x + c, t)

    def at_a(self, a):
        c = self.c
        return self.at(z=(1 - c) * a + c * self.z, x=c * a + (1 - c) * self.x)

    def at_b(self, b):
        c = self.c
        return self.at(z=c * b + (1 - c) * self.z, x=(1 - c) * b + c * self.x)

    def at_ab(self, a, b):
        c = self.c
        return self.at(z=(1 - c) * a + c * b, x=c * a + (1 - c) * b)

    def plane(self):
        steps = [(i, j) for i in range(4) for j in range(4) if i + j > 0]
        steps.sort(key=lambda step: -min(step[0], 4 - step[0]) - min(step[1], 4 - step[1]))
        return [(ring(self.a, i), ring(self.b, j)) for i, j in steps]

    def sibling(self):
        return self.at(c=1 - self.c)

    def octet(self):
        g = 4 * self.c + self.t
        members = [lax.rem(g + k, 8) for k in range(1, 8)]
        return [self.at(c=lax.div(m, 4), t=lax.rem(m, 4)) for m in members]

    def row_x(self):
        return [self.at(x=lax.rem(self.x + k, 4)) for k in range(1, 4)]

    def row_z(self):
        return [self.at(z=lax.rem(self.z + k, 4)) for k in range(1, 4)]

    def row_t(self):
        return [self.at(t=lax.rem(self.t + k, 4)) for k in range(1, 4)]


def ring(index, step):
    return lax.rem(index + step + 4, 4)


def greet(partners):
    barrier = pltpu.get_barrier_semaphore()
    for partner in partners:
        pl.semaphore_signal(barrier, inc=1, device_id=partner, device_id_type=MESH)
    return lambda: pl.semaphore_wait(barrier, len(partners))


class Wire:
    def __init__(self, send, recv, local):
        self.send = send
        self.recv = recv
        self.local = local
        self.count = 0
        self.loads = 0
        self.open = []

    def push(self, src, dst, device):
        index = self.count
        self.count += 1
        copy = pltpu.make_async_remote_copy(
            src_ref=src,
            dst_ref=dst,
            send_sem=self.send.at[index],
            recv_sem=self.recv.at[index],
            device_id=device,
            device_id_type=MESH,
        )
        copy.start()
        self.open.append(copy)
        return copy

    def offer(self, first, source, target, sender, goal, device):
        return pltpu.make_async_remote_copy(
            src_ref=source,
            dst_ref=target,
            send_sem=self.send.at[first + goal],
            recv_sem=self.recv.at[first + sender],
            device_id=device,
            device_id_type=MESH,
        )

    def block(self, count):
        first = self.count
        self.count += count
        return first

    def load(self, src, dst):
        copy = pltpu.make_async_copy(src, dst, self.local.at[self.loads])
        self.loads += 1
        copy.start()
        return copy

    def drain(self):
        for copy in self.open:
            copy.wait_send()
        self.open = []


def arrive(copies):
    for copy in copies:
        copy.wait_recv()


def dot(left, right):
    return jnp.dot(left, right, preferred_element_type=F32)


def dot_cols(left, right):
    return lax.dot_general(left, right, (((1,), (1,)), ((), ())), preferred_element_type=F32)


def dot_rows(left, right):
    return lax.dot_general(left, right, (((0,), (0,)), ((), ())), preferred_element_type=F32)


def turn(values, cosine, sine, sign):
    lane = lax.rem(lax.broadcasted_iota(jnp.int32, values.shape, 1), 64)
    crossed = jnp.where(lane < 8, -pltpu.roll(values, 120, 1), pltpu.roll(values, 8, 1))
    return values * cosine + crossed * (sine * sign)


def vec_row(v_ref, row):
    return jnp.concatenate([v_ref[k, row : row + 1, :] for k in range(4)], axis=1)


def normalise(rows):
    wide = rows.astype(F32)
    centred = wide - jnp.mean(wide, axis=-1, keepdims=True)
    variance = jnp.mean(centred * centred, axis=-1, keepdims=True)
    rate = lax.rsqrt(variance + norm_epsilon)
    return centred * rate, rate


def halves(values):
    high = values.astype(BF)
    return high, (values - high.astype(F32)).astype(BF)


def product(left_h, left_l, right_h, right_l):
    return dot(left_h, right_h) + (dot(left_h, right_l) + dot(left_l, right_h))


def squared(high, small):
    cross = dot(high, small)
    return dot(high, high) + (cross + cross.T)


def spread_b(wire, place, ref):
    block = ref.at[place.c, place.a, place.b]
    return [wire.push(block, block, place.at_b(ring(place.b, k))) for k in range(1, 4)]


class Ring:
    def __init__(self, wire, place, ref, index, at):
        self.wire = wire
        self.place = place
        self.ref = ref
        self.index = index
        self.at = at
        self.ups, self.downs = {}, {}
        for p, q in ((0, 2), (1, 3), (2, 0), (3, 1)):
            self.ups[p] = self.send(0, p, 1)
            self.downs[q] = self.send(0, q, -1)
        self.swaps = [self.swap(0)]

    def send(self, step, part, way):
        block = self.ref.at[self.place.c, ring(self.index, step), part]
        return self.wire.push(block, block, self.at(ring(self.index, way)))

    def swap(self, step):
        block = self.ref.at[self.place.c, ring(self.index, step)]
        return self.wire.push(block, block, self.place.sibling())

    def hand_on(self):
        self.more = []
        for p, q in ((0, 2), (1, 3)):
            self.ups[p].wait_recv()
            self.more.append(self.send(-1, p, 1))
            self.downs[q].wait_recv()
            self.more.append(self.send(1, q, -1))

    def close(self):
        arrive([self.ups[2], self.ups[3]])
        self.swaps.append(self.swap(-1))
        arrive([self.downs[0], self.downs[1]])
        self.swaps.append(self.swap(1))
        arrive(self.more)
        self.swaps.append(self.swap(2))


def spread_plane(wire, place, ref):
    block = ref.at[place.c, place.a, place.b]
    return [wire.push(block, block, place.at_ab(a, b)) for a, b in place.plane()]


def scatter_plane(wire, place, ref, target):
    copies = []
    for k, (a, b) in enumerate(place.plane()):
        copies.append(wire.push(ref.at[a, b], target.at[k], place.at_ab(a, b)))
    return copies


def add_plane(first, parts):
    value = first.astype(F32)
    for k in range(15):
        value = value + parts[k].astype(F32)
    return value


def swap_cores(wire, place, ref):
    return wire.push(ref.at[place.c], ref.at[place.c], place.sibling())


def natural(source, target, start, stop):
    for z in range(4):
        for x in range(4):
            target[8 * z + 2 * x] = source[0, z, x, :, start:stop]
            target[8 * z + 2 * x + 1] = source[1, x, z, :, start:stop]


def by_row(source, target, start, stop):
    for z in range(4):
        for x in range(4):
            for c in range(2):
                target[8 * z + 2 * x + c] = source[c, z, x, :, start:stop]


def by_owner(target, z, rows, start, stop):
    for x in range(4):
        target[0, z, x, :, start:stop] = rows[32 * x : 32 * x + 16, :]
        target[1, x, z, :, start:stop] = rows[32 * x + 16 : 32 * x + 32, :]


def by_core(target, z, rows, start, stop):
    for x in range(4):
        for c in range(2):
            block = rows[32 * x + 16 * c : 32 * x + 16 * c + 16, :]
            target[c, z, x, :, start:stop] = block


def sum_cores(wire, place, ref, target):
    return wire.push(ref.at[1 - place.c], target, place.sibling())


def trade_t(wire, place, source, target):
    copies = []
    for k in range(1, 4):
        goal = ring(place.t, k)
        copies.append(wire.push(source.at[goal], target.at[place.t], place.at(t=goal)))
    return copies


def total(first, parts):
    value = first.astype(F32)
    for k in range(3):
        value = value + parts[k].astype(F32)
    return value


def unpair(target, part, k):
    one, two = part[:, 128:256], part[:, 256:384]
    target[:, 128 * k : 128 * k + 128] = part[:, 0:128]
    target[:, 512 + 128 * k : 640 + 128 * k] = jnp.concatenate(
        [one[:, 0:64], two[:, 0:64]], axis=1
    )
    target[:, 1024 + 128 * k : 1152 + 128 * k] = jnp.concatenate(
        [one[:, 64:128], two[:, 64:128]], axis=1
    )


INPUTS = (
    "lengths",
    "x",
    "c",
    "joint",
    "output",
    "expand",
    "reduce",
    "vectors",
    "m_joint",
    "m_output",
    "m_expand",
    "m_reduce",
    "first",
    "second",
)

OUTPUTS = (
    ("g_joint", (4, 1536), F32),
    ("g_output", (4, 512), F32),
    ("g_expand", (4, 2048), F32),
    ("g_reduce", (4, 2048), F32),
    ("n_joint", (4, 1536), F32),
    ("n_output", (4, 512), F32),
    ("n_expand", (4, 2048), F32),
    ("n_reduce", (4, 2048), F32),
    ("u_joint", (4, 1536), F32),
    ("u_output", (4, 512), F32),
    ("u_expand", (4, 2048), F32),
    ("u_reduce", (4, 2048), F32),
    ("block_output", (128, 512), BF),
    ("input_grad", (128, 512), F32),
    ("vector_grad", (4, 11), F32),
    ("second_next", (4, 11), F32),
    ("vector_next", (4, 11), F32),
)

SCRATCH = (
    ("joint_v", (4, 1536), F32),
    ("output_v", (4, 512), F32),
    ("expand_v", (4, 2048), F32),
    ("reduce_v", (4, 2048), F32),
    ("vectors_v", (4, 11), F32),
    ("first_v", (4, 11), F32),
    ("second_v", (4, 11), F32),
    ("table", (128, 128), F32),
    ("vec_sum", (4, 16, 128), F32),
    ("m_joint_v", (4, 1536), F32),
    ("m_output_v", (4, 512), F32),
    ("m_expand_v", (4, 2048), F32),
    ("m_reduce_v", (4, 2048), F32),
    ("j_out", (4, 4, 384), F32),
    ("j_in", (4, 4, 384), F32),
    ("j_rows", (16, 384), F32),
    ("w_out", (4, 4, 1536), F32),
    ("w_in", (4, 4, 1536), F32),
    ("w_rows", (16, 1536), F32),
    ("wj", (2, 4, 4, 16, 512), BF),
    ("wr", (2, 4, 4, 16, 1536), BF),
    ("w_joint", (32, 16, 384), BF),
    ("w_output", (32, 16, 512), BF),
    ("w_expand", (32, 16, 512), BF),
    ("w_reduce", (32, 16, 512), BF),
    ("v_own", (16, 128), F32),
    ("m_own", (4, 4, 2048), F32),
    ("m_early", (4, 4, 2048), F32),
    ("m_old", (16, 2048), F32),
    ("v_in", (4, 16, 128), F32),
    ("v", (4, 16, 128), F32),
    ("rows_x", (4, 128, 512), BF),
    ("rows_c", (4, 128, 512), BF),
    ("cos", (4, 128, 128), F32),
    ("sin", (4, 128, 128), F32),
    ("normed", (4, 128, 512), BF),
    ("q_turned", (2, 128, 256), BF),
    ("q_buf", (2, 64, 512), BF),
    ("q_heads", (2, 64, 512), BF),
    ("g_buf", (2, 64, 512), BF),
    ("g_heads", (2, 64, 512), BF),
    ("kv_buf", (2, 512, 128), BF),
    ("kv", (8, 512, 128), BF),
    ("hidden", (4, 128, 512), BF),
    ("pre", (4, 128, 512), BF),
    ("feed", (4, 128, 512), F32),
    ("row_grad", (4, 128, 512), F32),
    ("gf", (2, 4, 4, 16, 1024), BF),
    ("gf_core", (4, 4, 16, 1024), BF),
    ("gf_chip", (4, 4, 16, 1024), BF),
    ("gf_z", (3, 4, 16, 1024), BF),
    ("gf_line", (4, 16, 1024), BF),
    ("gf_x", (3, 16, 1024), BF),
    ("go", (2, 4, 4, 16, 128), BF),
    ("go_core", (4, 4, 16, 128), BF),
    ("go_chip", (4, 4, 16, 128), BF),
    ("go_in", (15, 16, 128), BF),
    ("early_out", (4, 4, 1152), F32),
    ("early_in", (4, 4, 1152), F32),
    ("turned", (8, 128, 512), BF),
    ("keys", (8, 512, 128), BF),
    ("scores", (9, 512, 512), F32),
    ("sums", (8, 512, 128), F32),
    ("query_low", (2, 512, 128), BF),
    ("query_two", (2, 512, 128), BF),
    ("begin", (2, 1, 512), jnp.int32),
    ("top", (2, 1, 512), F32),
    ("total_sum", (2, 1, 512), F32),
    ("out_turned", (2, 64, 512), F32),
    ("grad_low", (2, 512, 128), BF),
    ("back_turned", (64, 512), F32),
    ("centre", (2, 1, 512), F32),
    ("out_low", (2, 64, 512), BF),
    ("out_heads", (2, 64, 512), BF),
    ("back_low", (2, 64, 512), BF),
    ("back_heads", (2, 64, 512), BF),
    ("dk", (2, 4, 512, 128), BF),
    ("dk_in", (4, 512, 128), BF),
    ("dk_chip", (4, 512, 128), BF),
    ("dk_got", (3, 512, 128), BF),
    ("dkv", (2, 512, 128), BF),
    ("pair_out", (128, 512), BF),
    ("joint_out", (512, 384), BF),
    ("out_cols", (4, 128, 128), BF),
    ("out_in", (4, 128, 128), BF),
    ("out_part", (4, 128, 512), BF),
    ("out_got", (4, 128, 512), BF),
    ("back_part", (4, 128, 512), BF),
    ("back_got", (4, 128, 512), BF),
    ("gj", (2, 4, 4, 16, 384), BF),
    ("gj_core", (4, 4, 16, 384), BF),
    ("gj_chip", (4, 4, 16, 384), BF),
    ("gj_in", (15, 16, 384), BF),
    ("late_out", (4, 4, 384), F32),
    ("late_in", (4, 4, 384), F32),
    ("vp", (4, 4, 16, 128), F32),
    ("vp_core", (4, 16, 128), F32),
    ("vp_z", (3, 4, 16, 128), F32),
    ("vp_x", (3, 4, 16, 128), F32),
    ("vp_t", (3, 4, 16, 128), F32),
    ("gm_out", (4, 16, 512), BF),
    ("gm_in", (4, 16, 512), BF),
    ("m_rows", (16, 2048), F32),
    ("momentum", (2, 4, 4, 16, 1536), BF),
    ("extra", (2, 4, 4, 16, 512), BF),
    ("gram", (512, 512), F32),
    ("gram_h", (512, 512), BF),
    ("gram_l", (512, 512), BF),
    ("poly_h", (512, 512), BF),
    ("poly_l", (512, 512), BF),
    ("temp_h", (512, 512), BF),
    ("temp_l", (512, 512), BF),
    ("own", (16, 512), F32),
    ("u_rows", (4, 16, 512), F32),
    ("u_out", (4, 16, 512), BF),
    ("u_in", (4, 16, 512), BF),
    ("u_wide", (4, 4, 2048), F32),
)

PUSHES = 240
LOADS = 16


class Box:
    pass


def attend_chunk(place, slot):
    return place.seq if slot == 0 else 7 - place.seq


def attend_score(slot, k):
    return 8 - k if slot == 0 else k


def pairs(count, step, carry):
    def two(k, carry):
        return step(2 * k + 1, step(2 * k, carry))

    def one(_, carry):
        return step(count - 1, carry)

    carry = lax.fori_loop(0, lax.div(count, 2), two, carry)
    return lax.fori_loop(0, lax.rem(count, 2), one, carry)


def attend_start(r, place):
    for slot in range(2):
        index = 512 * attend_chunk(place, slot) + lax.broadcasted_iota(jnp.int32, (1, 512), 1)
        begin = jnp.zeros((1, 512), jnp.int32)
        finish = 0
        for j in range(4):
            finish = finish + r.lengths[0, j]
            begin = jnp.where(index >= finish, finish, begin)
        r.begin[slot] = begin
        r.top[slot] = jnp.full((1, 512), masked_score, F32)
        r.total_sum[slot] = jnp.zeros((1, 512), F32)


def query_prepare(r, slot):
    wide = r.q_heads[slot].astype(F32)
    high, small = halves(wide * (HD ** -0.5 * LOG2_E))
    r.query_two[slot] = jnp.concatenate([high, small], axis=0).T
    low = (wide * (HD ** -0.5)).astype(BF)
    r.query_low[slot] = jnp.concatenate([low, jnp.zeros((64, 512), BF)], axis=0).T


def grad_prepare(r, slot):
    r.grad_low[slot] = jnp.concatenate([jnp.zeros((64, 512), BF), r.g_heads[slot]], axis=0).T


def keys_prepare(r, column):
    low = lax.broadcasted_iota(jnp.int32, (512, 128), 1) < 64
    for part in range(2):
        k = 2 * column + part
        r.turned[k] = r.kv[k].T
        wide = r.kv[k].astype(F32)
        r.keys[k] = jnp.where(low, wide, pltpu.roll(wide, 64, 1)).astype(BF)


def score_column(r, place, column, slot):
    chunk = attend_chunk(place, slot)

    def run(parts):
        top, total_sum = r.top[slot], r.total_sum[slot]
        for part, last in parts:
            k = 2 * column + part
            raw = dot_cols(r.keys[k], r.query_two[slot])
            key = lax.broadcasted_iota(jnp.int32, (512, 512), 0)
            allowed = key >= r.begin[slot] - 512 * k
            if last:
                allowed = allowed & (key <= lax.broadcasted_iota(jnp.int32, (512, 512), 1))
            raw = jnp.where(allowed, raw, masked_score)
            r.scores[attend_score(slot, k)] = raw
            higher = jnp.maximum(top, jnp.max(raw, axis=0, keepdims=True))
            total_part = jnp.sum(jnp.exp2(raw - higher), axis=0, keepdims=True)
            total_sum = total_sum * jnp.exp2(top - higher) + total_part
            top = higher
        r.top[slot] = top
        r.total_sum[slot] = total_sum

    @pl.when(2 * column + 1 < chunk)
    def _():
        run(((0, False), (1, False)))

    @pl.when(2 * column + 1 == chunk)
    def _():
        run(((0, False), (1, True)))

    @pl.when(2 * column == chunk)
    def _():
        run(((0, True),))


def weigh_values(r, place, slot):
    level = r.top[slot] + jnp.log(r.total_sum[slot]) * LOG2_E

    def weigh(k, out):
        prob = jnp.exp2(r.scores[attend_score(slot, k)] - level)
        r.scores[attend_score(slot, k)] = prob
        return out + dot(r.turned[k, 64:128, :], prob.astype(BF))

    out = pairs(attend_chunk(place, slot) + 1, weigh, jnp.zeros((64, 512), F32))
    r.out_turned[slot] = out
    r.out_low[slot] = out.astype(BF)


def backward_block(r, slot, k):
    prob = r.scores[attend_score(slot, k)]
    out_grad = r.grad_low[slot]
    grad = dot_cols(r.kv[k], out_grad)
    score_grad = (prob * (grad - r.centre[slot])).astype(BF)
    r.sums[k] += dot(prob.astype(BF), out_grad) + dot(score_grad, r.query_low[slot])
    return dot(r.turned[k, 0:64, :], score_grad)


def backward_cross(r, place):
    def step(k, back):
        return back + backward_block(r, 1, k)

    back = pairs(attend_chunk(place, 1) + 1, step, jnp.zeros((64, 512), F32))
    r.back_low[1] = (back * (HD ** -0.5)).astype(BF)


def backward_column(r, place, column):
    chunk = attend_chunk(place, 0)

    @pl.when(2 * column + 1 <= chunk)
    def _():
        r.back_turned[...] += backward_block(r, 0, 2 * column) + backward_block(
            r, 0, 2 * column + 1
        )

    @pl.when(2 * column == chunk)
    def _():
        r.back_turned[...] += backward_block(r, 0, 2 * column)

    r.dk[0, column] = r.sums[2 * column].astype(BF)
    r.dk[1, column] = r.sums[2 * column + 1].astype(BF)


def newton(r, place):
    blocks, size = 1, 512

    def rows(i):
        return pl.ds(size * i, size)

    def diagonal(i):
        row = size * i + lax.broadcasted_iota(jnp.int32, (size, 512), 0)
        return row == lax.broadcasted_iota(jnp.int32, (size, 512), 1)

    def fill(i, trace):
        value = jnp.zeros((size, 512), F32)
        for k in range(3):
            lanes = slice(512 * k, 512 * k + 512)
            right = r.momentum[:, :, :, :, lanes].reshape(512, 512)
            value = value + dot_cols(right, right)
        r.gram[rows(i), :] = value

        @pl.when(place.t >= 2)
        def _():
            right = r.extra[...].reshape(512, 512)
            r.gram[rows(i), :] += dot_cols(right, right)

        value = r.gram[rows(i), :]
        return trace + jnp.sum(jnp.where(diagonal(i), value, 0.0), keepdims=True)

    trace = lax.fori_loop(0, blocks, fill, jnp.zeros((1, 1), F32))
    scale = 1.0 / (jnp.sqrt(trace) + 1e-07)

    def keep(value, i, high_ref, low_ref):
        high, small = halves(value)
        high_ref[rows(i), :] = high
        low_ref[rows(i), :] = small

    def prepare(i, _):
        value = r.gram[rows(i), :] * (scale * scale)
        r.gram[rows(i), :] = value
        keep(value, i, r.gram_h, r.gram_l)
        return 0

    lax.fori_loop(0, blocks, prepare, 0)

    def polynomial(i, _):
        square = squared(r.gram_h[...], r.gram_l[...])
        value = (
            jnp.where(diagonal(i), newton_first, 0.0)
            + newton_second * r.gram[rows(i), :]
            + newton_third * square
        )
        keep(value, i, r.poly_h, r.poly_l)
        return 0

    def inner(i, _):
        high, small = r.poly_h[...], r.poly_l[...]
        own_h, own_l = halves(r.own[...])
        left = jnp.concatenate([high, own_h], axis=0)
        cross = dot(left, small)
        main = dot(jnp.concatenate([left, own_l], axis=0), high)
        r.own[...] = main[512:528] + (main[528:544] + cross[512:528])
        keep(main[0:512] + (cross[0:512] + cross[0:512].T), i, r.temp_h, r.temp_l)
        return 0

    def outer(i, _):
        value = product(r.gram_h[...], r.gram_l[...], r.temp_h[...], r.temp_l[...])
        r.gram[rows(i), :] = value
        keep(value, i, r.gram_h, r.gram_l)
        return 0

    def times(left, right_h, right_l):
        high, small = halves(left)
        both = dot(jnp.concatenate([high, small], axis=0), right_h[...])
        return both[0:16] + (both[16:32] + dot(high, right_l[...]))

    r.own[...] = jnp.zeros((16, 512), F32)
    mine = pl.ds(pl.multiple_of(256 * place.c + 64 * place.a + 16 * place.b, 16), 16)
    for sweep in range(4):
        lax.fori_loop(0, blocks, polynomial, 0)
        if sweep == 0:
            first = r.poly_h[mine, :].astype(F32) + r.poly_l[mine, :].astype(F32)
        lax.fori_loop(0, blocks, inner, 0)
        if sweep == 0:
            r.own[...] = first
        if sweep < 3:
            lax.fori_loop(0, blocks, outer, 0)

    def last_gram(left):
        return times(times(left, r.gram_h, r.gram_l), r.temp_h, r.temp_l)

    own = r.own[...]
    once = last_gram(own)
    own = newton_first * own + newton_second * once + newton_third * last_gram(once)
    return halves(own * scale)


def block_kernel(*refs):
    r = Box()
    names = list(INPUTS) + [n for n, _, _ in OUTPUTS] + [n for n, _, _ in SCRATCH]
    for name, ref in zip(names, refs):
        setattr(r, name, ref)
    place = Place()
    wire = Wire(*refs[-3:])
    z, x, c, t, d = place.z, place.x, place.c, place.t, place.d
    seq, mate, cross, head = place.seq, place.mate, place.cross, place.head
    sibling = place.sibling()

    met = greet(
        place.octet()
        + [place.at_ab(a, b) for a, b in place.plane()]
        + [place.at(x=cross, c=1 - c)]
    )

    load_w = [
        wire.load(r.joint, r.joint_v),
        wire.load(r.output, r.output_v),
        wire.load(r.expand, r.expand_v),
        wire.load(r.reduce, r.reduce_v),
    ]
    load_v = wire.load(r.vectors, r.vectors_v)
    load_x = wire.load(r.x, r.rows_x.at[t])
    load_c = wire.load(r.c, r.rows_c.at[t])
    load_m = [
        wire.load(r.m_joint, r.m_joint_v),
        wire.load(r.m_output, r.m_output_v),
        wire.load(r.m_expand, r.m_expand_v),
        wire.load(r.m_reduce, r.m_reduce_v),
        wire.load(r.first, r.first_v),
        wire.load(r.second, r.second_v),
    ]
    for copy in load_w:
        copy.wait()
    for k in range(4):
        for part in range(3):
            r.j_out[k, :, 128 * part : 128 * part + 128] = r.joint_v[
                :, 512 * part + 128 * k : 512 * part + 128 * k + 128
            ]
        r.w_out[k, :, 0:512] = r.output_v[...]
        r.w_out[k, :, 512:1024] = r.expand_v[:, 512 * k : 512 * k + 512]
        r.w_out[k, :, 1024:1536] = r.reduce_v[:, 512 * k : 512 * k + 512]
    load_v.wait()
    r.table[...] = jnp.zeros((128, 128), F32)
    column = lax.broadcasted_iota(jnp.int32, (128, 11), 0) - (16 * seq + 4 * t)
    own_vec = jnp.zeros((128, 11), F32)
    for j in range(4):
        own_vec = jnp.where(column == j, r.vectors_v[j : j + 1, :], own_vec)
    r.table[:, 0:11] = own_vec.astype(BF).astype(F32)
    r.v_own[...] = r.table[...].T[0:16, :]
    load_x.wait()
    load_c.wait()
    met()

    joint_t = trade_t(wire, place, r.j_out, r.j_in)
    for partner in place.row_t():
        joint_t.append(wire.push(r.v_own, r.v_in.at[t], partner))
    rest_t = trade_t(wire, place, r.w_out, r.w_in)
    x_rows = [wire.push(r.rows_x.at[t], r.rows_x.at[t], p) for p in place.row_t()]
    r.j_in[t] = r.j_out[t]
    r.v_in[t] = r.v_own[...]
    r.w_in[t] = r.w_out[t]
    arrive(joint_t)
    for k in range(4):
        r.j_rows[4 * k : 4 * k + 4, :] = r.j_in[k]
    keys, values = r.j_rows[:, 128:256], r.j_rows[:, 256:384]
    low16 = lax.broadcasted_iota(jnp.int32, (16, 128), 1) < 64
    own_block = r.wj.at[c, place.a, place.b]
    own_block[:, 0:128] = r.j_rows[:, 0:128].astype(BF)
    own_block[:, 128:256] = jnp.where(low16, keys, pltpu.roll(values, 64, 1)).astype(BF)
    own_block[:, 256:384] = jnp.where(low16, pltpu.roll(keys, 64, 1), values).astype(BF)
    own_block[:, 384:512] = ((r.v_in[0] + r.v_in[1]) + (r.v_in[2] + r.v_in[3])).astype(BF)
    joint_all = spread_plane(wire, place, r.wj)
    arrive(rest_t)
    for k in range(4):
        r.w_rows[4 * k : 4 * k + 4, :] = r.w_in[k]
    r.wr[c, z, x] = r.w_rows[...].astype(BF)
    block = r.wr.at[c, z, x]
    rest_b = [wire.push(block, block, partner) for partner in place.row_x()]

    half = ROT // 2
    lane = lax.rem(lax.broadcasted_iota(jnp.int32, (1, 128), 1), 64)
    frequency = jnp.zeros((1, 128), F32)
    for i in range(half):
        frequency = jnp.where(lax.rem(lane, half) == i, 10000.0 ** (-2.0 * i / ROT), frequency)
    frequency = jnp.where(lane < ROT, frequency, 0.0)

    def angles(i, _):
        index = 512 * seq + 128 * i + lax.broadcasted_iota(jnp.int32, (128, 1), 0)
        begin = jnp.zeros((128, 1), jnp.int32)
        finish = 0
        for j in range(4):
            finish = finish + r.lengths[0, j]
            begin = jnp.where(index >= finish, finish, begin)
        angle = (index - begin).astype(F32) * frequency
        r.cos[i] = jnp.cos(angle)
        r.sin[i] = jnp.sin(angle)
        return 0

    lax.fori_loop(0, 4, angles, 0)
    for copy in load_m:
        copy.wait()
    arrive(joint_all)
    joint_swap = swap_cores(wire, place, r.wj)
    arrive(rest_b)
    rest = Ring(wire, place, r.wr, z, lambda i: place.at(z=i))
    arrive(x_rows)
    c_rows = [wire.push(r.rows_c.at[t], r.rows_c.at[t], p) for p in place.row_t()]
    joint_swap.wait_recv()
    for k in range(4):
        own_vec = jnp.zeros((16, 128), F32)
        for i in range(4):
            for part in (r.wj[0, k, i, :, 384:512], r.wj[1, i, k, :, 384:512]):
                own_vec = own_vec + part.astype(F32)
        r.v[k] = own_vec
    natural(r.wj, r.w_joint, 0, 384)

    gain, shift = vec_row(r.v, 0), vec_row(r.v, 1)
    q_bias, k_bias, v_bias = r.v[t, 2:3, :], r.v[t, 3:4, :], r.v[t, 4:5, :]
    low_row = lax.broadcasted_iota(jnp.int32, (1, 128), 1) < 64
    pair_bias = (
        jnp.where(low_row, k_bias, pltpu.roll(v_bias, 64, 1)),
        jnp.where(low_row, pltpu.roll(k_bias, 64, 1), v_bias),
    )
    low = lax.broadcasted_iota(jnp.int32, (256, 128), 1) < 64

    def project(i, _):
        blocks, rows = pl.ds(2 * i, 2), pl.ds(256 * i, 256)
        normal, _rate = normalise(r.rows_x[blocks].reshape(256, 512))
        part = (normal * gain + shift).astype(BF)
        r.normed[blocks] = part.reshape(2, 128, 512)
        raw = dot(part, r.w_joint[...].reshape(512, 384))
        cosine, sine = r.cos[blocks].reshape(256, 128), r.sin[blocks].reshape(256, 128)
        query = turn(raw[:, 0:128] + q_bias, cosine, sine, 1.0)
        r.q_turned[i] = query.T.astype(BF)
        key_cos = jnp.where(low, cosine, 1.0)
        key_sin = jnp.where(low, sine, 0.0)
        for h in range(2):
            pair = raw[:, 128 + 128 * h : 256 + 128 * h] + pair_bias[h]
            r.kv_buf[h, rows, :] = turn(pair, key_cos, key_sin, 1.0).astype(BF)
        return 0

    lax.fori_loop(0, 2, project, 0)
    for i in range(2):
        for h in range(2):
            r.q_buf[h, :, 256 * i : 256 * i + 256] = r.q_turned[i, 64 * h : 64 * h + 64, :]
    kv_cross = []
    for i in range(2):
        rows = pl.ds(256 * i, 256)
        kv_cross.append(
            wire.push(r.kv_buf.at[1 - head, rows], r.kv.at[seq, rows], place.at(x=cross))
        )
    q_cross = wire.push(r.q_buf.at[1 - head], r.q_heads.at[1], place.at(x=cross, c=1 - c))
    kv_mate = wire.push(r.kv_buf.at[head], r.kv.at[seq], place.at(x=mate))
    kv_core = wire.push(r.kv_buf.at[head], r.kv.at[seq], sibling)
    r.kv[seq] = r.kv_buf[head]
    r.q_heads[0] = r.q_buf[head]
    attend_start(r, place)
    query_prepare(r, 0)
    r.sums[...] = jnp.zeros_like(r.sums)
    r.back_turned[...] = jnp.zeros_like(r.back_turned)
    for k in range(4):
        lanes = slice(128 * k, 128 * k + 128)
        keys = r.m_joint_v[:, 512 + 128 * k : 640 + 128 * k]
        values = r.m_joint_v[:, 1024 + 128 * k : 1152 + 128 * k]
        start = 384 * k
        r.m_own[0, :, start : start + 128] = r.m_joint_v[:, lanes]
        r.m_own[0, :, start + 128 : start + 256] = jnp.concatenate(
            [keys[:, 0:64], values[:, 0:64]], axis=1
        )
        r.m_own[0, :, start + 256 : start + 384] = jnp.concatenate(
            [keys[:, 64:128], values[:, 64:128]], axis=1
        )
    r.m_own[0, :, 1536:2048] = jnp.zeros((4, 512), F32)
    r.m_own[1, :, 0:512] = r.m_output_v[...]
    r.m_own[1, :, 512:2048] = jnp.zeros((4, 1536), F32)
    r.m_own[2] = r.m_expand_v[...]
    r.m_own[3] = r.m_reduce_v[...]
    rest.hand_on()
    kv_core.wait_recv()
    keys_prepare(r, x)
    score_column(r, place, x, 0)
    at_cross, at_mate = 2 * cross + c, 2 * mate + c
    at_far = 2 * (3 - mate) + c
    kv_far, kv_sent, far_sent = [], [], []
    for i in range(2):
        kv_cross[i].wait_recv()
        part = r.kv.at[at_cross, pl.ds(256 * i, 256)]
        kv_far.append(wire.push(part, part, place.at(x=mate)))
        kv_sent.append(wire.push(part, part, sibling))
    kv_mate.wait_recv()
    mate_sent = wire.push(r.kv.at[at_mate], r.kv.at[at_mate], sibling)
    rest.close()
    q_cross.wait_recv()
    query_prepare(r, 1)
    score_column(r, place, x, 1)
    mate_sent.wait_recv()
    keys_prepare(r, mate)
    score_column(r, place, mate, 0)
    score_column(r, place, mate, 1)
    arrive([*c_rows, *rest.swaps])
    by_row(r.wr, r.w_output, 0, 512)
    by_row(r.wr, r.w_expand, 512, 1024)
    by_row(r.wr, r.w_reduce, 1024, 1536)
    out_rows = r.w_output[pl.ds(8 * t, 8)].reshape(128, 512)
    grad = dot_cols(out_rows, r.rows_c[...].reshape(512, 512)).astype(BF)
    r.g_buf[0] = grad[0:64, :]
    r.g_buf[1] = grad[64:128, :]
    g_cross = wire.push(r.g_buf.at[1 - head], r.g_heads.at[1], place.at(x=cross, c=1 - c))
    r.g_heads[0] = r.g_buf[head]
    grad_prepare(r, 0)
    early = trade_t(wire, place, r.m_own, r.m_early)

    bias = jnp.concatenate([r.v[k, pl.ds(7 + t, 1), :] for k in range(4)], axis=1)

    def feed_forward(i, sums):
        blocks = pl.ds(2 * i, 2)
        part = r.normed[blocks].reshape(256, 512)
        wide = dot(part, r.w_expand[...].reshape(512, 512)) + bias
        square = wide * wide
        curve = jnp.tanh(0.7978845608 * (wide + 0.044715 * (square * wide)))
        r.hidden[blocks] = (0.5 * wide * (1.0 + curve)).astype(BF).reshape(2, 128, 512)
        slope = 0.5 * (1.0 + curve) + (0.5 * 0.7978845608) * wide * (1.0 - curve * curve) * (
            1.0 + (3 * 0.044715) * square
        )
        part = r.rows_c[blocks].reshape(256, 512)
        back = dot(part, r.w_reduce[...].reshape(512, 512))
        grad = (back * slope).astype(BF)
        r.pre[blocks] = grad.reshape(2, 128, 512)
        return sums + jnp.sum(grad.astype(F32), axis=0, keepdims=True)

    hidden_sum = lax.fori_loop(0, 2, feed_forward, jnp.zeros((1, 512), F32))
    for i in range(2):
        kv_far[i].wait_recv()
        part = r.kv.at[at_far, pl.ds(256 * i, 256)]
        far_sent.append(wire.push(part, part, sibling))
    for j in range(4):
        lanes = slice(128 * j, 128 * j + 128)
        expand_grad = dot_rows(
            r.normed[:, :, lanes].reshape(512, 128), r.pre[...].reshape(512, 512)
        )
        by_core(r.gf, j, expand_grad.astype(BF), 0, 512)
        reduce_grad = dot_rows(
            r.rows_c[:, :, lanes].reshape(512, 128), r.hidden[...].reshape(512, 512)
        )
        by_core(r.gf, j, reduce_grad.astype(BF), 512, 1024)
    gf_swap = sum_cores(wire, place, r.gf, r.gf_core)
    far = 3 - mate
    arrive(kv_sent)
    keys_prepare(r, cross)
    score_column(r, place, cross, 0)
    score_column(r, place, cross, 1)
    arrive(far_sent)
    keys_prepare(r, far)
    score_column(r, place, far, 0)
    score_column(r, place, far, 1)
    gf_swap.wait_recv()
    for a in range(4):
        r.gf_chip[a] = (r.gf[c, a].astype(F32) + r.gf_core[a].astype(F32)).astype(BF)
    gf_z = []
    for k in range(1, 4):
        goal = ring(z, k)
        gf_z.append(wire.push(r.gf_chip.at[goal], r.gf_z.at[k - 1], place.at(z=goal)))
    weigh_values(r, place, 1)
    out_cross = wire.push(r.out_low.at[1], r.out_heads.at[head], place.at(x=cross, c=1 - c))
    weigh_values(r, place, 0)
    r.out_heads[head] = r.out_low[0]
    g_cross.wait_recv()
    grad_prepare(r, 1)
    for slot in range(2):
        r.centre[slot] = jnp.sum(
            r.out_turned[slot] * r.g_heads[slot].astype(F32), axis=0, keepdims=True
        )

    dk_swap = []

    def chip_sum(index):
        return r.dk[c, index].astype(F32) + r.dk_in[index].astype(F32)

    dk_sent = []

    def send_column(step, column):
        dk_swap[step].wait_recv()
        r.dk_chip[step] = chip_sum(column).astype(BF)
        dk_sent.append(
            wire.push(r.dk_chip.at[step], r.dk_got.at[step], place.at(x=column))
        )

    backward_cross(r, place)
    back_cross = wire.push(r.back_low.at[1], r.back_heads.at[head], place.at(x=cross, c=1 - c))
    out_cross.wait_recv()
    turned = r.out_heads[...].reshape(128, 512)
    r.pair_out[...] = turned
    out_grad = dot(turned, r.rows_c[...].reshape(512, 512)).astype(BF)
    for j in range(4):
        r.out_cols[j] = out_grad[:, 128 * j : 128 * j + 128]
    out_cols = trade_t(wire, place, r.out_cols, r.out_in)
    r.out_in[t] = r.out_cols[t]
    columns = (far, cross, mate, x)
    for step, column in enumerate(columns):
        backward_column(r, place, column)
        dk_swap.append(wire.push(r.dk.at[1 - c, column], r.dk_in.at[column], sibling))
        if step > 0:
            send_column(step - 1, columns[step - 1])
    r.back_low[0] = (r.back_turned[...] * (HD ** -0.5)).astype(BF)
    r.back_heads[head] = r.back_low[0]
    arrive(gf_z)
    r.gf_line[...] = total(r.gf_chip[z], r.gf_z).astype(BF)
    gf_x = []
    for k in range(1, 4):
        goal = ring(x, k)
        gf_x.append(wire.push(r.gf_line.at[goal], r.gf_x.at[k - 1], place.at(x=goal)))
    arrive(out_cols)
    for j in range(4):
        by_owner(r.go, j, r.out_in[j], 0, 128)
    go_swap = sum_cores(wire, place, r.go, r.go_core)

    def feed_out(i, _):
        blocks = pl.ds(2 * i, 2)
        part = r.hidden[blocks].reshape(256, 512)
        r.feed[blocks] = dot_cols(part, r.w_reduce[...].reshape(512, 512)).reshape(2, 128, 512)
        part = r.pre[blocks].reshape(256, 512)
        r.row_grad[blocks] = dot_cols(part, r.w_expand[...].reshape(512, 512)).reshape(2, 128, 512)
        return 0

    lax.fori_loop(0, 2, feed_out, 0)
    go_swap.wait_recv()
    for a in range(4):
        r.go_chip[a] = (r.go[c, a].astype(F32) + r.go_core[a].astype(F32)).astype(BF)
    go_all = scatter_plane(wire, place, r.go_chip, r.go_in)
    out_rows = r.w_output[pl.ds(8 * t, 8)].reshape(128, 512)
    for i in range(2):
        blocks, lanes = slice(2 * i, 2 * i + 2), slice(256 * i, 256 * i + 256)
        part = r.feed[blocks].reshape(256, 512) + dot_rows(r.pair_out[:, lanes], out_rows)
        r.out_part[blocks] = part.astype(BF).reshape(2, 128, 512)
    out_parts = trade_t(wire, place, r.out_part, r.out_got)
    r.out_got[t] = r.out_part[t]
    back_cross.wait_recv()
    back = r.back_heads[...].reshape(128, 512).astype(F32).T
    cosine, sine = r.cos[...].reshape(512, 128), r.sin[...].reshape(512, 128)
    r.joint_out[:, 0:128] = turn(back, cosine, sine, -1.0).astype(BF)
    low = lax.broadcasted_iota(jnp.int32, (128, 128), 1) < 64
    arrive([dk_swap[3], *dk_sent])
    r.dkv[head] = (chip_sum(x) + r.dk_got[2].astype(F32)).astype(BF)
    r.dkv[1 - head] = (r.dk_got[0].astype(F32) + r.dk_got[1].astype(F32)).astype(BF)
    for h in range(2):
        for i in range(4):
            rows = pl.ds(128 * i, 128)
            key_cos = jnp.where(low, r.cos[i], 1.0)
            key_sin = jnp.where(low, r.sin[i], 0.0)
            r.joint_out[rows, 128 + 128 * h : 256 + 128 * h] = turn(
                r.dkv[h, rows, :].astype(F32), key_cos, key_sin, -1.0
            ).astype(BF)
    for j in range(4):
        part = r.normed[:, :, 128 * j : 128 * j + 128].reshape(512, 128)
        by_owner(r.gj, j, dot_rows(part, r.joint_out[...]).astype(BF), 0, 384)
    gj_swap = sum_cores(wire, place, r.gj, r.gj_core)

    r.vp[0] = jnp.zeros((4, 16, 128), F32)
    shift_sum = jnp.zeros((1, 512), F32)
    gain_sum = jnp.zeros((1, 512), F32)
    for i in range(4):
        rows = pl.ds(128 * i, 128)
        part = r.row_grad[i] + dot_cols(r.joint_out[rows, :], r.w_joint[...].reshape(512, 384))
        r.back_part[i] = part.astype(BF)
        normal, _rate = normalise(r.rows_x[i])
        shift_sum = shift_sum + jnp.sum(part, axis=0, keepdims=True)
        gain_sum = gain_sum + jnp.sum(part * normal, axis=0, keepdims=True)
    gj_swap.wait_recv()
    for a in range(4):
        r.gj_chip[a] = (r.gj[c, a].astype(F32) + r.gj_core[a].astype(F32)).astype(BF)
    gj_all = scatter_plane(wire, place, r.gj_chip, r.gj_in)
    back_parts = trade_t(wire, place, r.back_part, r.back_got)
    r.back_got[t] = r.back_part[t]
    out_sum = jnp.sum(r.rows_c[t].astype(F32), axis=0, keepdims=True)
    joint_sum = jnp.sum(r.joint_out[...].astype(F32), axis=0, keepdims=True)
    one, two = joint_sum[:, 128:256], joint_sum[:, 256:384]
    for k in range(4):
        lanes = slice(128 * k, 128 * k + 128)
        r.vp[0, k, 0:1, :] = gain_sum[:, lanes]
        r.vp[0, k, 1:2, :] = shift_sum[:, lanes]
        r.vp[0, k, 5:6, :] = out_sum[:, lanes]
        r.vp[0, k, 6:7, :] = out_sum[:, lanes]
        r.vp[0, k, pl.ds(7 + t, 1), :] = hidden_sum[:, lanes]
    r.vp[0, t, 2:3, :] = joint_sum[:, 0:128]
    r.vp[0, t, 3:4, :] = jnp.where(low_row, one, pltpu.roll(two, 64, 1))
    r.vp[0, t, 4:5, :] = jnp.where(low_row, pltpu.roll(one, 64, 1), two)
    vp_swap = wire.push(r.vp.at[0], r.vp_core, sibling)
    arrive(gf_x)
    gf_own = total(r.gf_line[x], r.gf_x)
    arrive(go_all)
    go_own = add_plane(r.go_chip[place.a, place.b], r.go_in)
    for k in range(4):
        r.early_out[k, :, 0:1024] = gf_own[4 * k : 4 * k + 4, :]
        r.early_out[k, :, 1024:1152] = go_own[4 * k : 4 * k + 4, :]
    r.gm_out[1, :, 0:128] = go_own.astype(BF)
    r.gm_out[2] = gf_own[:, 0:512].astype(BF)
    r.gm_out[3] = gf_own[:, 512:1024].astype(BF)
    gm_first = wire.block(4)
    gm_widths = (384, 128, 512, 512)

    def to_newton(w, sender):
        lanes = slice(0, gm_widths[w])
        return wire.offer(
            gm_first, r.gm_out.at[w, :, lanes], r.gm_in.at[sender, :, lanes], sender, w,
            place.at(t=w),
        )

    def send_newton(w):
        @pl.when(t != w)
        def _():
            to_newton(w, t).start()

        @pl.when(t == w)
        def _():
            r.gm_in[w, :, 0 : gm_widths[w]] = r.gm_out[w, :, 0 : gm_widths[w]]

    for w in (1, 2, 3):
        send_newton(w)
    early_t = trade_t(wire, place, r.early_out, r.early_in)
    r.early_in[t] = r.early_out[t]

    arrive(early)
    r.m_early[t] = r.m_own[t]
    for k in range(4):
        r.m_old[4 * k : 4 * k + 4, :] = r.m_early[k]
    vp_swap.wait_recv()
    r.vp[1] = r.vp[0] + r.vp_core[...]
    vp_z = [wire.push(r.vp.at[1], r.vp_z.at[k], p) for k, p in enumerate(place.row_z())]

    arrive(gj_all)
    gj_own = add_plane(r.gj_chip[place.a, place.b], r.gj_in)
    r.gm_out[0, :, 0:384] = gj_own.astype(BF)
    send_newton(0)
    for k in range(4):
        r.late_out[k] = gj_own[4 * k : 4 * k + 4, :]
    late_t = trade_t(wire, place, r.late_out, r.late_in)
    r.late_in[t] = r.late_out[t]
    arrive(vp_z)
    r.vp[2] = total(r.vp[1], r.vp_z)
    vp_x = [wire.push(r.vp.at[2], r.vp_x.at[k], p) for k, p in enumerate(place.row_x())]

    for w in range(4):

        @pl.when(t == w)
        def _(w=w):
            width = gm_widths[w]
            for sender in range(4):
                if sender != w:
                    to_newton(w, sender).wait_recv()
            for k in range(4):
                lanes = slice(width * k, width * k + width)
                value = muon_beta * r.m_old[:, lanes] + r.gm_in[k, :, 0:width].astype(F32)
                if width * k < 1536:
                    r.momentum[c, place.a, place.b, :, lanes] = value.astype(BF)
                else:
                    r.extra[c, place.a, place.b] = value.astype(BF)
            if w == 1:
                r.momentum[c, place.a, place.b, :, 512:1536] = jnp.zeros((16, 1024), BF)

    m_b = spread_b(wire, place, r.momentum)

    extra_first = wire.block(16)

    def extra_copies():
        block = r.extra.at[c, place.a, place.b]
        copies = []
        for k, (a, b) in enumerate(place.plane()):
            copies.append(
                wire.offer(extra_first, block, block, k, k, place.at_ab(a, b))
            )
        return copies

    def extra_swap():
        block = r.extra.at[c]
        return wire.offer(extra_first, block, block, 15, 15, sibling)

    @pl.when(t >= 2)
    def _():
        for copy in extra_copies():
            copy.start()

    arrive(early_t)
    for k in range(4):
        part = r.early_in[k]
        r.g_expand[:, 512 * k : 512 * k + 512] = part[:, 0:512]
        r.g_reduce[:, 512 * k : 512 * k + 512] = part[:, 512:1024]
        r.g_output[:, 128 * k : 128 * k + 128] = part[:, 1024:1152]
    arrive(late_t)
    for k in range(4):
        unpair(r.g_joint, r.late_in[k], k)
    for old, grad, new in (
        (r.m_joint_v, r.g_joint, r.n_joint),
        (r.m_output_v, r.g_output, r.n_output),
        (r.m_expand_v, r.g_expand, r.n_expand),
        (r.m_reduce_v, r.g_reduce, r.n_reduce),
    ):
        new[...] = muon_beta * old[...] + grad[...]
    arrive(vp_x)
    r.vp[3] = total(r.vp[2], r.vp_x)
    vp_t = [wire.push(r.vp.at[3], r.vp_t.at[k], p) for k, p in enumerate(place.row_t())]
    arrive(out_parts)
    arrive(back_parts)
    arrive(m_b)
    whole = Ring(wire, place, r.momentum, place.a, place.at_a)
    whole.hand_on()
    wide = r.rows_x[t].astype(F32)
    feed = r.out_got[0].astype(F32)
    back = r.back_got[0].astype(F32)
    for k in range(1, 4):
        feed = feed + r.out_got[k].astype(F32)
        back = back + r.back_got[k].astype(F32)
    r.block_output[...] = (wide + feed + vec_row(r.v, 5) + vec_row(r.v, 6)).astype(BF)
    normal, rate = normalise(r.rows_x[t])
    scaled = back * gain
    mean_one = jnp.mean(scaled, axis=-1, keepdims=True)
    mean_two = jnp.mean(scaled * normal, axis=-1, keepdims=True)
    r.input_grad[...] = r.rows_c[t].astype(F32) + rate * (scaled - mean_one - normal * mean_two)
    whole.close()
    arrive(vp_t)
    r.vec_sum[...] = total(r.vp[3], r.vp_t)
    r.table[0:16, :] = r.vec_sum[z]
    r.table[...] = r.table[...].T
    vector_grad = r.table[pl.ds(pl.multiple_of(16 * seq + 4 * t, 4), 4), 0:11]
    r.vector_grad[...] = vector_grad
    first_next = beta_first * r.first_v[...] + (1.0 - beta_first) * vector_grad
    second_next = (
        beta_second * r.second_v[...] + (1.0 - beta_second) * vector_grad * vector_grad
    )
    r.second_next[...] = second_next
    first_hat = first_next / (1.0 - beta_first**STEP)
    second_hat = second_next / (1.0 - beta_second**STEP)
    r.vector_next[...] = r.vectors_v[...] - vector_rate * first_hat / (
        jnp.sqrt(second_hat) + adam_epsilon
    )
    @pl.when(t >= 2)
    def _():
        for copy in extra_copies():
            copy.wait_recv()
        extra_swap().start()
        extra_swap().wait_recv()

    arrive(whole.swaps)

    high, small = newton(r, place)
    both = jnp.concatenate([high, small], axis=0)
    for k in range(3):
        lanes = slice(512 * k, 512 * k + 512)
        rows = dot(both, r.momentum[:, :, :, :, lanes].reshape(512, 512))
        r.m_rows[:, lanes] = rows[0:16] + rows[16:32]

    @pl.when(t >= 2)
    def _():
        rows = dot(both, r.extra[...].reshape(512, 512))
        r.m_rows[:, 1536:2048] = rows[0:16] + rows[16:32]

    @pl.when(t < 2)
    def _():
        r.m_rows[:, 1536:2048] = jnp.zeros((16, 512), F32)

    for k in range(4):
        for p in range(4):
            r.u_rows[k, 4 * p : 4 * p + 4, :] = r.m_rows[
                4 * k : 4 * k + 4, 512 * p : 512 * p + 512
            ]
    r.u_out[...] = r.u_rows[...].astype(BF)
    u_t = trade_t(wire, place, r.u_out, r.u_in)
    r.u_in[t] = r.u_out[t]
    wire.drain()
    for w in range(4):

        @pl.when(t != w)
        def _(w=w):
            to_newton(w, t).wait_send()

    @pl.when(t >= 2)
    def _():
        for copy in extra_copies():
            copy.wait_send()
        extra_swap().wait_send()

    arrive(u_t)
    r.u_rows[...] = r.u_in[...].astype(F32)
    for k in range(4):
        for p in range(4):
            r.u_wide[k, :, 512 * p : 512 * p + 512] = r.u_rows[k, 4 * p : 4 * p + 4, :]
    for k in range(4):
        unpair(r.u_joint, r.u_wide[0, :, 384 * k : 384 * k + 384], k)
    for k, (old, change, new) in enumerate(
        (
            (r.joint_v, r.u_joint, r.u_joint),
            (r.output_v, r.u_wide.at[1, :, pl.ds(0, 512)], r.u_output),
            (r.expand_v, r.u_wide.at[2], r.u_expand),
            (r.reduce_v, r.u_wide.at[3], r.u_reduce),
        )
    ):
        factor = muon_rate * 0.2 * math.sqrt(max(D, WIDTHS[k]))
        new[...] = old[...] * (1.0 - muon_rate * muon_decay) - factor * change[...]
    wire.drain()


def block_stage(*arrays):
    return pl.pallas_call(
        block_kernel,
        out_shape=tuple(shape(dims, dtype) for _, dims, dtype in OUTPUTS),
        in_specs=[SMEM] + [ANY] * (len(INPUTS) - 1),
        out_specs=(VMEM,) * len(OUTPUTS),
        scratch_shapes=[pltpu.VMEM(dims, dtype) for _, dims, dtype in SCRATCH]
        + [
            pltpu.SemaphoreType.DMA((PUSHES,)),
            pltpu.SemaphoreType.DMA((PUSHES,)),
            pltpu.SemaphoreType.DMA((LOADS,)),
        ],
        compiler_params=pltpu.CompilerParams(
            collective_id=1, has_side_effects=True, vmem_limit_bytes=56 << 20
        ),
        name="block",
    )(*arrays)


def write_kernel(*refs):
    count = len(OUTPUTS)
    sem = refs[-1]
    copies = []
    for k in range(count):
        copy = pltpu.make_async_copy(refs[k], refs[count + k], sem.at[k])
        copy.start()
        copies.append(copy)
    for copy in copies:
        copy.wait()


def write_stage(*arrays):
    count = len(arrays)
    return pl.pallas_call(
        write_kernel,
        out_shape=tuple(shape(a.shape, a.dtype) for a in arrays),
        in_specs=[VMEM] * count,
        out_specs=(ANY,) * count,
        scratch_shapes=[pltpu.SemaphoreType.DMA((count,))],
        name="write",
    )(*arrays)


def shards(
    block_input,
    cotangent,
    doc_lengths,
    joint_weight,
    output_weight,
    expand_weight,
    reduce_weight,
    joint_moment,
    output_moment,
    expand_moment,
    reduce_moment,
    vectors,
    first_moment,
    second_moment,
):
    results = block_stage(
        doc_lengths, block_input, cotangent, joint_weight, output_weight, expand_weight,
        reduce_weight, vectors.T, joint_moment, output_moment, expand_moment, reduce_moment,
        first_moment.T, second_moment.T,
    )
    results = write_stage(*results)
    return (*results[12:14], *results[0:12], *[part.T for part in results[14:]])


def solution(mesh):
    rows = P(("fsdp", "seq", "tensor"), None)
    columns = P(None, ("fsdp", "seq", "tensor"))
    return jax.shard_map(
        shards,
        mesh=mesh,
        in_specs=(rows, rows, P("fsdp", None)) + (rows,) * 8 + (columns,) * 3,
        out_specs=(rows,) * 14 + (columns,) * 3,
        check_vma=False,
    )
```

```python
import functools
import math

import jax
import jax.numpy as jnp
from jax import lax
from jax.experimental import pallas as pl
from jax.experimental.pallas import tpu as pltpu
from jax.sharding import PartitionSpec as P

D = 512
HEADS = 8
FF = 2048
ROT = 16
HD = 64
STEP = 10

norm_epsilon = 1e-05
masked_score = -1e30
newton_first = 3.4445
newton_second = -4.775
newton_third = 2.0315
beta_first = 0.9
beta_second = 0.95
adam_epsilon = 1e-08
vector_rate = 0.2
muon_rate = 0.25
muon_beta = 0.95
muon_decay = 0.01
LOG2_E = 1.4426950408889634

BF = jnp.bfloat16
F32 = jnp.float32
MESH = pl.DeviceIdType.MESH
VMEM = pl.BlockSpec(memory_space=pltpu.VMEM)
SMEM = pl.BlockSpec(memory_space=pltpu.SMEM)
ANY = pl.BlockSpec(memory_space=pl.ANY)
WIDTHS = (3 * D, D, FF, FF)


def shape(dims, dtype):
    return jax.ShapeDtypeStruct(dims, dtype)


class Place:
    def __init__(self):
        self.z = lax.axis_index("fsdp")
        self.seq = lax.axis_index("seq")
        self.t = lax.axis_index("tensor")
        self.x = lax.div(self.seq, 2)
        self.c = lax.rem(self.seq, 2)
        self.d = 1 - 2 * self.c
        self.a = self.c * self.x + (1 - self.c) * self.z
        self.b = self.c * self.z + (1 - self.c) * self.x
        self.mate = self.x + 1 - 2 * lax.rem(self.x, 2)
        self.cross = 3 - self.x
        self.head = lax.div(self.x, 2)

    def at(self, z=None, x=None, c=None, t=None):
        z = self.z if z is None else z
        x = self.x if x is None else x
        c = self.c if c is None else c
        t = self.t if t is None else t
        return (z, 2 * x + c, t)

    def at_a(self, a):
        c = self.c
        return self.at(z=(1 - c) * a + c * self.z, x=c * a + (1 - c) * self.x)

    def at_b(self, b):
        c = self.c
        return self.at(z=c * b + (1 - c) * self.z, x=(1 - c) * b + c * self.x)

    def at_ab(self, a, b):
        c = self.c
        return self.at(z=(1 - c) * a + c * b, x=c * a + (1 - c) * b)

    def plane(self):
        steps = [(i, j) for i in range(4) for j in range(4) if i + j > 0]
        steps.sort(key=lambda step: -min(step[0], 4 - step[0]) - min(step[1], 4 - step[1]))
        return [(ring(self.a, i), ring(self.b, j)) for i, j in steps]

    def sibling(self):
        return self.at(c=1 - self.c)

    def octet(self):
        g = 4 * self.c + self.t
        members = [lax.rem(g + k, 8) for k in range(1, 8)]
        return [self.at(c=lax.div(m, 4), t=lax.rem(m, 4)) for m in members]

    def row_x(self):
        return [self.at(x=lax.rem(self.x + k, 4)) for k in range(1, 4)]

    def row_z(self):
        return [self.at(z=lax.rem(self.z + k, 4)) for k in range(1, 4)]

    def row_t(self):
        return [self.at(t=lax.rem(self.t + k, 4)) for k in range(1, 4)]


def ring(index, step):
    return lax.rem(index + step + 4, 4)


def greet(partners):
    barrier = pltpu.get_barrier_semaphore()
    for partner in partners:
        pl.semaphore_signal(barrier, inc=1, device_id=partner, device_id_type=MESH)
    return lambda: pl.semaphore_wait(barrier, len(partners))


class Wire:
    def __init__(self, send, recv, local):
        self.send = send
        self.recv = recv
        self.local = local
        self.count = 0
        self.loads = 0
        self.open = []

    def push(self, src, dst, device):
        index = self.count
        self.count += 1
        copy = pltpu.make_async_remote_copy(
            src_ref=src,
            dst_ref=dst,
            send_sem=self.send.at[index],
            recv_sem=self.recv.at[index],
            device_id=device,
            device_id_type=MESH,
        )
        copy.start()
        self.open.append(copy)
        return copy

    def offer(self, first, source, target, sender, goal, device):
        return pltpu.make_async_remote_copy(
            src_ref=source,
            dst_ref=target,
            send_sem=self.send.at[first + goal],
            recv_sem=self.recv.at[first + sender],
            device_id=device,
            device_id_type=MESH,
        )

    def block(self, count):
        first = self.count
        self.count += count
        return first

    def load(self, src, dst):
        copy = pltpu.make_async_copy(src, dst, self.local.at[self.loads])
        self.loads += 1
        copy.start()
        return copy

    def drain(self):
        for copy in self.open:
            copy.wait_send()
        self.open = []


def arrive(copies):
    for copy in copies:
        copy.wait_recv()


def dot(left, right):
    return jnp.dot(left, right, preferred_element_type=F32)


def dot_cols(left, right):
    return lax.dot_general(left, right, (((1,), (1,)), ((), ())), preferred_element_type=F32)


def dot_rows(left, right):
    return lax.dot_general(left, right, (((0,), (0,)), ((), ())), preferred_element_type=F32)


def turn(values, cosine, sine, sign):
    lane = lax.rem(lax.broadcasted_iota(jnp.int32, values.shape, 1), 64)
    crossed = jnp.where(lane < 8, -pltpu.roll(values, 120, 1), pltpu.roll(values, 8, 1))
    return values * cosine + crossed * (sine * sign)


def vec_row(v_ref, row):
    return jnp.concatenate([v_ref[k, row : row + 1, :] for k in range(4)], axis=1)


def normalise(rows):
    wide = rows.astype(F32)
    centred = wide - jnp.mean(wide, axis=-1, keepdims=True)
    variance = jnp.mean(centred * centred, axis=-1, keepdims=True)
    rate = lax.rsqrt(variance + norm_epsilon)
    return centred * rate, rate


def halves(values):
    high = values.astype(BF)
    return high, (values - high.astype(F32)).astype(BF)


def product(left_h, left_l, right_h, right_l):
    return dot(left_h, right_h) + (dot(left_h, right_l) + dot(left_l, right_h))


def squared(high, small):
    cross = dot(high, small)
    return dot(high, high) + (cross + cross.T)


def spread_b(wire, place, ref):
    block = ref.at[place.c, place.a, place.b]
    return [wire.push(block, block, place.at_b(ring(place.b, k))) for k in range(1, 4)]


class Ring:
    def __init__(self, wire, place, ref, index, at):
        self.wire = wire
        self.place = place
        self.ref = ref
        self.index = index
        self.at = at
        self.ups, self.downs = {}, {}
        for p, q in ((0, 2), (1, 3), (2, 0), (3, 1)):
            self.ups[p] = self.send(0, p, 1)
            self.downs[q] = self.send(0, q, -1)
        self.swaps = [self.swap(0)]

    def send(self, step, part, way):
        block = self.ref.at[self.place.c, ring(self.index, step), part]
        return self.wire.push(block, block, self.at(ring(self.index, way)))

    def swap(self, step):
        block = self.ref.at[self.place.c, ring(self.index, step)]
        return self.wire.push(block, block, self.place.sibling())

    def hand_on(self):
        self.more = []
        for p, q in ((0, 2), (1, 3)):
            self.ups[p].wait_recv()
            self.more.append(self.send(-1, p, 1))
            self.downs[q].wait_recv()
            self.more.append(self.send(1, q, -1))

    def close(self):
        arrive([self.ups[2], self.ups[3]])
        self.swaps.append(self.swap(-1))
        arrive([self.downs[0], self.downs[1]])
        self.swaps.append(self.swap(1))
        arrive(self.more)
        self.swaps.append(self.swap(2))


def spread_plane(wire, place, ref):
    block = ref.at[place.c, place.a, place.b]
    return [wire.push(block, block, place.at_ab(a, b)) for a, b in place.plane()]


def scatter_plane(wire, place, ref, target):
    copies = []
    for k, (a, b) in enumerate(place.plane()):
        copies.append(wire.push(ref.at[a, b], target.at[k], place.at_ab(a, b)))
    return copies


def add_plane(first, parts):
    value = first.astype(F32)
    for k in range(15):
        value = value + parts[k].astype(F32)
    return value


def swap_cores(wire, place, ref):
    return wire.push(ref.at[place.c], ref.at[place.c], place.sibling())


def natural(source, target, start, stop):
    for z in range(4):
        for x in range(4):
            target[8 * z + 2 * x] = source[0, z, x, :, start:stop]
            target[8 * z + 2 * x + 1] = source[1, x, z, :, start:stop]


def by_row(source, target, start, stop):
    for z in range(4):
        for x in range(4):
            for c in range(2):
                target[8 * z + 2 * x + c] = source[c, z, x, :, start:stop]


def by_owner(target, z, rows, start, stop):
    for x in range(4):
        target[0, z, x, :, start:stop] = rows[32 * x : 32 * x + 16, :]
        target[1, x, z, :, start:stop] = rows[32 * x + 16 : 32 * x + 32, :]


def by_core(target, z, rows, start, stop):
    for x in range(4):
        for c in range(2):
            block = rows[32 * x + 16 * c : 32 * x + 16 * c + 16, :]
            target[c, z, x, :, start:stop] = block


def sum_cores(wire, place, ref, target):
    return wire.push(ref.at[1 - place.c], target, place.sibling())


def trade_t(wire, place, source, target):
    copies = []
    for k in range(1, 4):
        goal = ring(place.t, k)
        copies.append(wire.push(source.at[goal], target.at[place.t], place.at(t=goal)))
    return copies


def total(first, parts):
    value = first.astype(F32)
    for k in range(3):
        value = value + parts[k].astype(F32)
    return value


def unpair(target, part, k):
    one, two = part[:, 128:256], part[:, 256:384]
    target[:, 128 * k : 128 * k + 128] = part[:, 0:128]
    target[:, 512 + 128 * k : 640 + 128 * k] = jnp.concatenate(
        [one[:, 0:64], two[:, 0:64]], axis=1
    )
    target[:, 1024 + 128 * k : 1152 + 128 * k] = jnp.concatenate(
        [one[:, 64:128], two[:, 64:128]], axis=1
    )


INPUTS = (
    "lengths",
    "x",
    "c",
    "joint",
    "output",
    "expand",
    "reduce",
    "vectors",
    "m_joint",
    "m_output",
    "m_expand",
    "m_reduce",
    "first",
    "second",
)

OUTPUTS = (
    ("g_joint", (4, 1536), F32),
    ("g_output", (4, 512), F32),
    ("g_expand", (4, 2048), F32),
    ("g_reduce", (4, 2048), F32),
    ("n_joint", (4, 1536), F32),
    ("n_output", (4, 512), F32),
    ("n_expand", (4, 2048), F32),
    ("n_reduce", (4, 2048), F32),
    ("u_joint", (4, 1536), F32),
    ("u_output", (4, 512), F32),
    ("u_expand", (4, 2048), F32),
    ("u_reduce", (4, 2048), F32),
    ("block_output", (128, 512), BF),
    ("input_grad", (128, 512), F32),
    ("vector_grad", (4, 11), F32),
    ("second_next", (4, 11), F32),
    ("vector_next", (4, 11), F32),
)

SCRATCH = (
    ("joint_v", (4, 1536), F32),
    ("output_v", (4, 512), F32),
    ("expand_v", (4, 2048), F32),
    ("reduce_v", (4, 2048), F32),
    ("vectors_v", (4, 11), F32),
    ("first_v", (4, 11), F32),
    ("second_v", (4, 11), F32),
    ("table", (128, 128), F32),
    ("vec_sum", (4, 16, 128), F32),
    ("m_joint_v", (4, 1536), F32),
    ("m_output_v", (4, 512), F32),
    ("m_expand_v", (4, 2048), F32),
    ("m_reduce_v", (4, 2048), F32),
    ("j_out", (4, 4, 384), F32),
    ("j_in", (4, 4, 384), F32),
    ("j_rows", (16, 384), F32),
    ("w_out", (4, 4, 1536), F32),
    ("w_in", (4, 4, 1536), F32),
    ("w_rows", (16, 1536), F32),
    ("wj", (2, 4, 4, 16, 512), BF),
    ("wr", (2, 4, 4, 16, 1536), BF),
    ("w_joint", (32, 16, 384), BF),
    ("w_output", (32, 16, 512), BF),
    ("w_expand", (32, 16, 512), BF),
    ("w_reduce", (32, 16, 512), BF),
    ("v_own", (16, 128), F32),
    ("m_own", (4, 4, 2048), F32),
    ("m_early", (4, 4, 2048), F32),
    ("m_old", (16, 2048), F32),
    ("v_in", (4, 16, 128), F32),
    ("v", (4, 16, 128), F32),
    ("rows_x", (4, 128, 512), BF),
    ("rows_c", (4, 128, 512), BF),
    ("cos", (4, 128, 128), F32),
    ("sin", (4, 128, 128), F32),
    ("normed", (4, 128, 512), BF),
    ("q_turned", (2, 128, 256), BF),
    ("q_buf", (2, 64, 512), BF),
    ("q_heads", (2, 64, 512), BF),
    ("g_buf", (2, 64, 512), BF),
    ("g_heads", (2, 64, 512), BF),
    ("kv_buf", (2, 512, 128), BF),
    ("kv", (8, 512, 128), BF),
    ("hidden", (4, 128, 512), BF),
    ("pre", (4, 128, 512), BF),
    ("feed", (4, 128, 512), F32),
    ("row_grad", (4, 128, 512), F32),
    ("gf", (2, 4, 4, 16, 1024), BF),
    ("gf_core", (4, 4, 16, 1024), BF),
    ("gf_chip", (4, 4, 16, 1024), BF),
    ("gf_z", (3, 4, 16, 1024), BF),
    ("gf_line", (4, 16, 1024), BF),
    ("gf_x", (3, 16, 1024), BF),
    ("go", (2, 4, 4, 16, 128), BF),
    ("go_core", (4, 4, 16, 128), BF),
    ("go_chip", (4, 4, 16, 128), BF),
    ("go_in", (15, 16, 128), BF),
    ("early_out", (4, 4, 1152), F32),
    ("early_in", (4, 4, 1152), F32),
    ("turned", (8, 128, 512), BF),
    ("keys", (8, 512, 128), BF),
    ("scores", (9, 512, 512), F32),
    ("sums", (8, 512, 128), F32),
    ("query_low", (2, 512, 128), BF),
    ("query_two", (2, 512, 128), BF),
    ("begin", (2, 1, 512), jnp.int32),
    ("top", (2, 1, 512), F32),
    ("total_sum", (2, 1, 512), F32),
    ("out_turned", (2, 64, 512), F32),
    ("grad_low", (2, 512, 128), BF),
    ("back_turned", (64, 512), F32),
    ("centre", (2, 1, 512), F32),
    ("out_low", (2, 64, 512), BF),
    ("out_heads", (2, 64, 512), BF),
    ("back_low", (2, 64, 512), BF),
    ("back_heads", (2, 64, 512), BF),
    ("dk", (2, 4, 512, 128), BF),
    ("dk_in", (4, 512, 128), BF),
    ("dk_chip", (4, 512, 128), BF),
    ("dk_got", (3, 512, 128), BF),
    ("dkv", (2, 512, 128), BF),
    ("pair_out", (128, 512), BF),
    ("joint_out", (512, 384), BF),
    ("out_cols", (4, 128, 128), BF),
    ("out_in", (4, 128, 128), BF),
    ("out_part", (4, 128, 512), BF),
    ("out_got", (4, 128, 512), BF),
    ("back_part", (4, 128, 512), BF),
    ("back_got", (4, 128, 512), BF),
    ("gj", (2, 4, 4, 16, 384), BF),
    ("gj_core", (4, 4, 16, 384), BF),
    ("gj_chip", (4, 4, 16, 384), BF),
    ("gj_in", (15, 16, 384), BF),
    ("late_out", (4, 4, 384), F32),
    ("late_in", (4, 4, 384), F32),
    ("vp", (4, 4, 16, 128), F32),
    ("vp_core", (4, 16, 128), F32),
    ("vp_z", (3, 4, 16, 128), F32),
    ("vp_x", (3, 4, 16, 128), F32),
    ("vp_t", (3, 4, 16, 128), F32),
    ("gm_out", (4, 16, 512), BF),
    ("gm_in", (4, 16, 512), BF),
    ("m_rows", (16, 2048), F32),
    ("momentum", (2, 4, 4, 16, 1536), BF),
    ("extra", (2, 4, 4, 16, 512), BF),
    ("gram", (512, 512), F32),
    ("gram_h", (512, 512), BF),
    ("gram_l", (512, 512), BF),
    ("poly_h", (512, 512), BF),
    ("poly_l", (512, 512), BF),
    ("temp_h", (512, 512), BF),
    ("temp_l", (512, 512), BF),
    ("own", (16, 512), F32),
    ("u_rows", (4, 16, 512), F32),
    ("u_out", (4, 16, 512), BF),
    ("u_in", (4, 16, 512), BF),
    ("u_wide", (4, 4, 2048), F32),
)

PUSHES = 240
LOADS = 16


class Box:
    pass


def attend_chunk(place, slot):
    return place.seq if slot == 0 else 7 - place.seq


def attend_score(slot, k):
    return 8 - k if slot == 0 else k


def pairs(count, step, carry):
    def two(k, carry):
        return step(2 * k + 1, step(2 * k, carry))

    def one(_, carry):
        return step(count - 1, carry)

    carry = lax.fori_loop(0, lax.div(count, 2), two, carry)
    return lax.fori_loop(0, lax.rem(count, 2), one, carry)


def attend_start(r, place):
    for slot in range(2):
        index = 512 * attend_chunk(place, slot) + lax.broadcasted_iota(jnp.int32, (1, 512), 1)
        begin = jnp.zeros((1, 512), jnp.int32)
        finish = 0
        for j in range(4):
            finish = finish + r.lengths[0, j]
            begin = jnp.where(index >= finish, finish, begin)
        r.begin[slot] = begin
        r.top[slot] = jnp.full((1, 512), masked_score, F32)
        r.total_sum[slot] = jnp.zeros((1, 512), F32)


def query_prepare(r, slot):
    wide = r.q_heads[slot].astype(F32)
    high, small = halves(wide * (HD ** -0.5 * LOG2_E))
    r.query_two[slot] = jnp.concatenate([high, small], axis=0).T
    low = (wide * (HD ** -0.5)).astype(BF)
    r.query_low[slot] = jnp.concatenate([low, jnp.zeros((64, 512), BF)], axis=0).T


def grad_prepare(r, slot):
    r.grad_low[slot] = jnp.concatenate([jnp.zeros((64, 512), BF), r.g_heads[slot]], axis=0).T


def keys_prepare(r, column):
    low = lax.broadcasted_iota(jnp.int32, (512, 128), 1) < 64
    for part in range(2):
        k = 2 * column + part
        r.turned[k] = r.kv[k].T
        wide = r.kv[k].astype(F32)
        r.keys[k] = jnp.where(low, wide, pltpu.roll(wide, 64, 1)).astype(BF)


def score_column(r, place, column, slot, diagonal=False):
    chunk = attend_chunk(place, slot)

    def run(parts):
        top, total_sum = r.top[slot], r.total_sum[slot]
        for part, last in parts:
            k = 2 * column + part
            raw = dot_cols(r.keys[k], r.query_two[slot])
            key = lax.broadcasted_iota(jnp.int32, (512, 512), 0)
            allowed = key >= r.begin[slot] - 512 * k
            if last:
                allowed = allowed & (key <= lax.broadcasted_iota(jnp.int32, (512, 512), 1))
            raw = jnp.where(allowed, raw, masked_score)
            r.scores[attend_score(slot, k)] = raw
            higher = jnp.maximum(top, jnp.max(raw, axis=0, keepdims=True))
            total_part = jnp.sum(jnp.exp2(raw - higher), axis=0, keepdims=True)
            total_sum = total_sum * jnp.exp2(top - higher) + total_part
            top = higher
        r.top[slot] = top
        r.total_sum[slot] = total_sum

    if not diagonal:

        @pl.when(2 * column + 1 < chunk)
        def _():
            run(((0, False), (1, False)))

        return

    @pl.when(2 * column + 1 == chunk)
    def _():
        run(((0, False), (1, True)))

    @pl.when(2 * column == chunk)
    def _():
        run(((0, True),))


def weigh_values(r, place, slot):
    level = r.top[slot] + jnp.log(r.total_sum[slot]) * LOG2_E

    def weigh(k, out):
        prob = jnp.exp2(r.scores[attend_score(slot, k)] - level)
        r.scores[attend_score(slot, k)] = prob
        return out + dot(r.turned[k, 64:128, :], prob.astype(BF))

    out = pairs(attend_chunk(place, slot) + 1, weigh, jnp.zeros((64, 512), F32))
    r.out_turned[slot] = out
    r.out_low[slot] = out.astype(BF)


def backward_block(r, slot, k):
    prob = r.scores[attend_score(slot, k)]
    out_grad = r.grad_low[slot]
    grad = dot_cols(r.kv[k], out_grad)
    score_grad = (prob * (grad - r.centre[slot])).astype(BF)
    r.sums[k] += dot(prob.astype(BF), out_grad) + dot(score_grad, r.query_low[slot])
    return dot(r.turned[k, 0:64, :], score_grad)


def backward_cross(r, place):
    def step(k, back):
        return back + backward_block(r, 1, k)

    back = pairs(attend_chunk(place, 1) + 1, step, jnp.zeros((64, 512), F32))
    r.back_low[1] = (back * (HD ** -0.5)).astype(BF)


def backward_column(r, place, column, diagonal):
    chunk = attend_chunk(place, 0)

    @pl.when(2 * column + 1 <= chunk)
    def _():
        r.back_turned[...] += backward_block(r, 0, 2 * column) + backward_block(
            r, 0, 2 * column + 1
        )

    if diagonal:

        @pl.when(2 * column == chunk)
        def _():
            r.back_turned[...] += backward_block(r, 0, 2 * column)

    r.dk[0, column] = r.sums[2 * column].astype(BF)
    r.dk[1, column] = r.sums[2 * column + 1].astype(BF)


def newton(r, place):
    blocks, size = 1, 512

    def rows(i):
        return pl.ds(size * i, size)

    def diagonal(i):
        row = size * i + lax.broadcasted_iota(jnp.int32, (size, 512), 0)
        return row == lax.broadcasted_iota(jnp.int32, (size, 512), 1)

    def fill(i, trace):
        value = jnp.zeros((size, 512), F32)
        for k in range(3):
            lanes = slice(512 * k, 512 * k + 512)
            right = r.momentum[:, :, :, :, lanes].reshape(512, 512)
            value = value + dot_cols(right, right)
        r.gram[rows(i), :] = value

        @pl.when(place.t >= 2)
        def _():
            right = r.extra[...].reshape(512, 512)
            r.gram[rows(i), :] += dot_cols(right, right)

        value = r.gram[rows(i), :]
        return trace + jnp.sum(jnp.where(diagonal(i), value, 0.0), keepdims=True)

    trace = lax.fori_loop(0, blocks, fill, jnp.zeros((1, 1), F32))
    scale = 1.0 / (jnp.sqrt(trace) + 1e-07)

    def keep(value, i, high_ref, low_ref):
        high, small = halves(value)
        high_ref[rows(i), :] = high
        low_ref[rows(i), :] = small

    def prepare(i, _):
        value = r.gram[rows(i), :] * (scale * scale)
        r.gram[rows(i), :] = value
        keep(value, i, r.gram_h, r.gram_l)
        return 0

    lax.fori_loop(0, blocks, prepare, 0)

    def polynomial(i, _):
        square = squared(r.gram_h[...], r.gram_l[...])
        value = (
            jnp.where(diagonal(i), newton_first, 0.0)
            + newton_second * r.gram[rows(i), :]
            + newton_third * square
        )
        keep(value, i, r.poly_h, r.poly_l)
        return 0

    def inner(i, _):
        high, small = r.poly_h[...], r.poly_l[...]
        own_h, own_l = halves(r.own[...])
        left = jnp.concatenate([high, own_h], axis=0)
        cross = dot(left, small)
        main = dot(jnp.concatenate([left, own_l], axis=0), high)
        r.own[...] = main[512:528] + (main[528:544] + cross[512:528])
        keep(main[0:512] + (cross[0:512] + cross[0:512].T), i, r.temp_h, r.temp_l)
        return 0

    def outer(i, _):
        value = product(r.gram_h[...], r.gram_l[...], r.temp_h[...], r.temp_l[...])
        r.gram[rows(i), :] = value
        keep(value, i, r.gram_h, r.gram_l)
        return 0

    def times(left, right_h, right_l):
        high, small = halves(left)
        both = dot(jnp.concatenate([high, small], axis=0), right_h[...])
        return both[0:16] + (both[16:32] + dot(high, right_l[...]))

    mine = 256 * place.c + 64 * place.a + 16 * place.b
    row = lax.broadcasted_iota(jnp.int32, (16, 512), 0)
    column = lax.broadcasted_iota(jnp.int32, (16, 512), 1)
    r.own[...] = jnp.where(column - row == mine, 1.0, 0.0)

    def sweep(_, carry):
        polynomial(0, 0)
        inner(0, 0)
        outer(0, 0)
        return carry

    lax.fori_loop(0, 3, sweep, 0)
    lax.fori_loop(0, blocks, polynomial, 0)
    lax.fori_loop(0, blocks, inner, 0)

    def last_gram(left):
        return times(times(left, r.gram_h, r.gram_l), r.temp_h, r.temp_l)

    own = r.own[...]
    once = last_gram(own)
    own = newton_first * own + newton_second * once + newton_third * last_gram(once)
    return halves(own * scale)


def block_kernel(*refs):
    r = Box()
    names = list(INPUTS) + [n for n, _, _ in OUTPUTS] + [n for n, _, _ in SCRATCH]
    for name, ref in zip(names, refs):
        setattr(r, name, ref)
    place = Place()
    wire = Wire(*refs[-3:])
    z, x, c, t, d = place.z, place.x, place.c, place.t, place.d
    seq, mate, cross, head = place.seq, place.mate, place.cross, place.head
    sibling = place.sibling()

    met = greet(
        place.octet()
        + [place.at_ab(a, b) for a, b in place.plane()]
        + [place.at(x=cross, c=1 - c)]
    )

    load_w = [
        wire.load(r.joint, r.joint_v),
        wire.load(r.output, r.output_v),
        wire.load(r.expand, r.expand_v),
        wire.load(r.reduce, r.reduce_v),
    ]
    load_v = wire.load(r.vectors, r.vectors_v)
    load_x = wire.load(r.x, r.rows_x.at[t])
    load_c = wire.load(r.c, r.rows_c.at[t])
    load_m = [
        wire.load(r.m_joint, r.m_joint_v),
        wire.load(r.m_output, r.m_output_v),
        wire.load(r.m_expand, r.m_expand_v),
        wire.load(r.m_reduce, r.m_reduce_v),
        wire.load(r.first, r.first_v),
        wire.load(r.second, r.second_v),
    ]
    for copy in load_w:
        copy.wait()
    for k in range(4):
        for part in range(3):
            r.j_out[k, :, 128 * part : 128 * part + 128] = r.joint_v[
                :, 512 * part + 128 * k : 512 * part + 128 * k + 128
            ]
        r.w_out[k, :, 0:512] = r.output_v[...]
        r.w_out[k, :, 512:1024] = r.expand_v[:, 512 * k : 512 * k + 512]
        r.w_out[k, :, 1024:1536] = r.reduce_v[:, 512 * k : 512 * k + 512]
    load_v.wait()
    r.table[...] = jnp.zeros((128, 128), F32)
    column = lax.broadcasted_iota(jnp.int32, (128, 11), 0) - (16 * seq + 4 * t)
    own_vec = jnp.zeros((128, 11), F32)
    for j in range(4):
        own_vec = jnp.where(column == j, r.vectors_v[j : j + 1, :], own_vec)
    r.table[:, 0:11] = own_vec.astype(BF).astype(F32)
    r.v_own[...] = r.table[...].T[0:16, :]
    load_x.wait()
    load_c.wait()
    met()

    joint_t = trade_t(wire, place, r.j_out, r.j_in)
    for partner in place.row_t():
        joint_t.append(wire.push(r.v_own, r.v_in.at[t], partner))
    rest_t = trade_t(wire, place, r.w_out, r.w_in)
    x_rows = [wire.push(r.rows_x.at[t], r.rows_x.at[t], p) for p in place.row_t()]
    r.j_in[t] = r.j_out[t]
    r.v_in[t] = r.v_own[...]
    r.w_in[t] = r.w_out[t]
    arrive(joint_t)
    for k in range(4):
        r.j_rows[4 * k : 4 * k + 4, :] = r.j_in[k]
    keys, values = r.j_rows[:, 128:256], r.j_rows[:, 256:384]
    low16 = lax.broadcasted_iota(jnp.int32, (16, 128), 1) < 64
    own_block = r.wj.at[c, place.a, place.b]
    own_block[:, 0:128] = r.j_rows[:, 0:128].astype(BF)
    own_block[:, 128:256] = jnp.where(low16, keys, pltpu.roll(values, 64, 1)).astype(BF)
    own_block[:, 256:384] = jnp.where(low16, pltpu.roll(keys, 64, 1), values).astype(BF)
    own_block[:, 384:512] = ((r.v_in[0] + r.v_in[1]) + (r.v_in[2] + r.v_in[3])).astype(BF)
    joint_all = spread_plane(wire, place, r.wj)
    arrive(rest_t)
    for k in range(4):
        r.w_rows[4 * k : 4 * k + 4, :] = r.w_in[k]
    r.wr[c, z, x] = r.w_rows[...].astype(BF)
    block = r.wr.at[c, z, x]
    rest_b = [wire.push(block, block, partner) for partner in place.row_x()]

    half = ROT // 2
    lane = lax.rem(lax.broadcasted_iota(jnp.int32, (1, 128), 1), 64)
    frequency = jnp.zeros((1, 128), F32)
    for i in range(half):
        frequency = jnp.where(lax.rem(lane, half) == i, 10000.0 ** (-2.0 * i / ROT), frequency)
    frequency = jnp.where(lane < ROT, frequency, 0.0)

    def angles(i, _):
        index = 512 * seq + 128 * i + lax.broadcasted_iota(jnp.int32, (128, 1), 0)
        begin = jnp.zeros((128, 1), jnp.int32)
        finish = 0
        for j in range(4):
            finish = finish + r.lengths[0, j]
            begin = jnp.where(index >= finish, finish, begin)
        angle = (index - begin).astype(F32) * frequency
        r.cos[i] = jnp.cos(angle)
        r.sin[i] = jnp.sin(angle)
        return 0

    lax.fori_loop(0, 4, angles, 0)
    for copy in load_m:
        copy.wait()
    arrive(joint_all)
    joint_swap = swap_cores(wire, place, r.wj)
    arrive(rest_b)
    rest = Ring(wire, place, r.wr, z, lambda i: place.at(z=i))
    arrive(x_rows)
    c_rows = [wire.push(r.rows_c.at[t], r.rows_c.at[t], p) for p in place.row_t()]
    joint_swap.wait_recv()
    for k in range(4):
        own_vec = jnp.zeros((16, 128), F32)
        for i in range(4):
            for part in (r.wj[0, k, i, :, 384:512], r.wj[1, i, k, :, 384:512]):
                own_vec = own_vec + part.astype(F32)
        r.v[k] = own_vec
    natural(r.wj, r.w_joint, 0, 384)

    gain, shift = vec_row(r.v, 0), vec_row(r.v, 1)
    q_bias, k_bias, v_bias = r.v[t, 2:3, :], r.v[t, 3:4, :], r.v[t, 4:5, :]
    low_row = lax.broadcasted_iota(jnp.int32, (1, 128), 1) < 64
    pair_bias = (
        jnp.where(low_row, k_bias, pltpu.roll(v_bias, 64, 1)),
        jnp.where(low_row, pltpu.roll(k_bias, 64, 1), v_bias),
    )
    low = lax.broadcasted_iota(jnp.int32, (256, 128), 1) < 64

    def project(i, _):
        blocks, rows = pl.ds(2 * i, 2), pl.ds(256 * i, 256)
        normal, _rate = normalise(r.rows_x[blocks].reshape(256, 512))
        part = (normal * gain + shift).astype(BF)
        r.normed[blocks] = part.reshape(2, 128, 512)
        raw = dot(part, r.w_joint[...].reshape(512, 384))
        cosine, sine = r.cos[blocks].reshape(256, 128), r.sin[blocks].reshape(256, 128)
        query = turn(raw[:, 0:128] + q_bias, cosine, sine, 1.0)
        r.q_turned[i] = query.T.astype(BF)
        key_cos = jnp.where(low, cosine, 1.0)
        key_sin = jnp.where(low, sine, 0.0)
        for h in range(2):
            pair = raw[:, 128 + 128 * h : 256 + 128 * h] + pair_bias[h]
            r.kv_buf[h, rows, :] = turn(pair, key_cos, key_sin, 1.0).astype(BF)
        return 0

    lax.fori_loop(0, 2, project, 0)
    for i in range(2):
        for h in range(2):
            r.q_buf[h, :, 256 * i : 256 * i + 256] = r.q_turned[i, 64 * h : 64 * h + 64, :]
    kv_cross = []
    for i in range(2):
        rows = pl.ds(256 * i, 256)
        kv_cross.append(
            wire.push(r.kv_buf.at[1 - head, rows], r.kv.at[seq, rows], place.at(x=cross))
        )
    q_cross = wire.push(r.q_buf.at[1 - head], r.q_heads.at[1], place.at(x=cross, c=1 - c))
    kv_mate = wire.push(r.kv_buf.at[head], r.kv.at[seq], place.at(x=mate))
    kv_core = wire.push(r.kv_buf.at[head], r.kv.at[seq], sibling)
    r.kv[seq] = r.kv_buf[head]
    r.q_heads[0] = r.q_buf[head]
    attend_start(r, place)
    query_prepare(r, 0)
    r.sums[...] = jnp.zeros_like(r.sums)
    r.back_turned[...] = jnp.zeros_like(r.back_turned)
    for k in range(4):
        lanes = slice(128 * k, 128 * k + 128)
        keys = r.m_joint_v[:, 512 + 128 * k : 640 + 128 * k]
        values = r.m_joint_v[:, 1024 + 128 * k : 1152 + 128 * k]
        start = 384 * k
        r.m_own[0, :, start : start + 128] = r.m_joint_v[:, lanes]
        r.m_own[0, :, start + 128 : start + 256] = jnp.concatenate(
            [keys[:, 0:64], values[:, 0:64]], axis=1
        )
        r.m_own[0, :, start + 256 : start + 384] = jnp.concatenate(
            [keys[:, 64:128], values[:, 64:128]], axis=1
        )
    r.m_own[0, :, 1536:2048] = jnp.zeros((4, 512), F32)
    r.m_own[1, :, 0:512] = r.m_output_v[...]
    r.m_own[1, :, 512:2048] = jnp.zeros((4, 1536), F32)
    r.m_own[2] = r.m_expand_v[...]
    r.m_own[3] = r.m_reduce_v[...]
    rest.hand_on()
    kv_core.wait_recv()
    keys_prepare(r, x)
    score_column(r, place, x, 0, diagonal=True)
    at_cross, at_mate = 2 * cross + c, 2 * mate + c
    at_far = 2 * (3 - mate) + c
    kv_far, kv_sent, far_sent = [], [], []
    for i in range(2):
        kv_cross[i].wait_recv()
        part = r.kv.at[at_cross, pl.ds(256 * i, 256)]
        kv_far.append(wire.push(part, part, place.at(x=mate)))
        kv_sent.append(wire.push(part, part, sibling))
    kv_mate.wait_recv()
    mate_sent = wire.push(r.kv.at[at_mate], r.kv.at[at_mate], sibling)
    rest.close()
    q_cross.wait_recv()
    query_prepare(r, 1)
    score_column(r, place, x, 1)
    mate_sent.wait_recv()
    keys_prepare(r, mate)
    score_column(r, place, mate, 0)
    score_column(r, place, mate, 1)
    arrive([*c_rows, *rest.swaps])
    by_row(r.wr, r.w_output, 0, 512)
    by_row(r.wr, r.w_expand, 512, 1024)
    by_row(r.wr, r.w_reduce, 1024, 1536)
    out_rows = r.w_output[pl.ds(8 * t, 8)].reshape(128, 512)
    grad = dot_cols(out_rows, r.rows_c[...].reshape(512, 512)).astype(BF)
    r.g_buf[0] = grad[0:64, :]
    r.g_buf[1] = grad[64:128, :]
    g_cross = wire.push(r.g_buf.at[1 - head], r.g_heads.at[1], place.at(x=cross, c=1 - c))
    r.g_heads[0] = r.g_buf[head]
    grad_prepare(r, 0)
    early = trade_t(wire, place, r.m_own, r.m_early)

    bias = jnp.concatenate([r.v[k, pl.ds(7 + t, 1), :] for k in range(4)], axis=1)

    def feed_forward(i, sums):
        blocks = pl.ds(2 * i, 2)
        part = r.normed[blocks].reshape(256, 512)
        wide = dot(part, r.w_expand[...].reshape(512, 512)) + bias
        square = wide * wide
        curve = jnp.tanh(0.7978845608 * (wide + 0.044715 * (square * wide)))
        r.hidden[blocks] = (0.5 * wide * (1.0 + curve)).astype(BF).reshape(2, 128, 512)
        slope = 0.5 * (1.0 + curve) + (0.5 * 0.7978845608) * wide * (1.0 - curve * curve) * (
            1.0 + (3 * 0.044715) * square
        )
        part = r.rows_c[blocks].reshape(256, 512)
        back = dot(part, r.w_reduce[...].reshape(512, 512))
        grad = (back * slope).astype(BF)
        r.pre[blocks] = grad.reshape(2, 128, 512)
        return sums + jnp.sum(grad.astype(F32), axis=0, keepdims=True)

    hidden_sum = lax.fori_loop(0, 2, feed_forward, jnp.zeros((1, 512), F32))
    for i in range(2):
        kv_far[i].wait_recv()
        part = r.kv.at[at_far, pl.ds(256 * i, 256)]
        far_sent.append(wire.push(part, part, sibling))
    for j in range(4):
        lanes = slice(128 * j, 128 * j + 128)
        expand_grad = dot_rows(
            r.normed[:, :, lanes].reshape(512, 128), r.pre[...].reshape(512, 512)
        )
        by_core(r.gf, j, expand_grad.astype(BF), 0, 512)
        reduce_grad = dot_rows(
            r.rows_c[:, :, lanes].reshape(512, 128), r.hidden[...].reshape(512, 512)
        )
        by_core(r.gf, j, reduce_grad.astype(BF), 512, 1024)
    gf_swap = sum_cores(wire, place, r.gf, r.gf_core)
    far = 3 - mate
    arrive(kv_sent)
    keys_prepare(r, cross)
    score_column(r, place, cross, 0)
    score_column(r, place, cross, 1, diagonal=True)
    arrive(far_sent)
    keys_prepare(r, far)
    score_column(r, place, far, 0)
    score_column(r, place, far, 1)
    gf_swap.wait_recv()
    for a in range(4):
        r.gf_chip[a] = (r.gf[c, a].astype(F32) + r.gf_core[a].astype(F32)).astype(BF)
    gf_z = []
    for k in range(1, 4):
        goal = ring(z, k)
        gf_z.append(wire.push(r.gf_chip.at[goal], r.gf_z.at[k - 1], place.at(z=goal)))
    weigh_values(r, place, 1)
    out_cross = wire.push(r.out_low.at[1], r.out_heads.at[head], place.at(x=cross, c=1 - c))
    weigh_values(r, place, 0)
    r.out_heads[head] = r.out_low[0]
    g_cross.wait_recv()
    grad_prepare(r, 1)
    for slot in range(2):
        r.centre[slot] = jnp.sum(
            r.out_turned[slot] * r.g_heads[slot].astype(F32), axis=0, keepdims=True
        )

    dk_swap = []

    def chip_sum(index):
        return r.dk[c, index].astype(F32) + r.dk_in[index].astype(F32)

    dk_sent = []

    def send_column(step, column):
        dk_swap[step].wait_recv()
        r.dk_chip[step] = chip_sum(column).astype(BF)
        dk_sent.append(
            wire.push(r.dk_chip.at[step], r.dk_got.at[step], place.at(x=column))
        )

    backward_cross(r, place)
    back_cross = wire.push(r.back_low.at[1], r.back_heads.at[head], place.at(x=cross, c=1 - c))
    out_cross.wait_recv()
    turned = r.out_heads[...].reshape(128, 512)
    r.pair_out[...] = turned
    out_grad = dot(turned, r.rows_c[...].reshape(512, 512)).astype(BF)
    for j in range(4):
        r.out_cols[j] = out_grad[:, 128 * j : 128 * j + 128]
    out_cols = trade_t(wire, place, r.out_cols, r.out_in)
    r.out_in[t] = r.out_cols[t]
    columns = (far, cross, mate, x)
    for step, column in enumerate(columns):
        backward_column(r, place, column, diagonal=step == 3)
        dk_swap.append(wire.push(r.dk.at[1 - c, column], r.dk_in.at[column], sibling))
        if step > 0:
            send_column(step - 1, columns[step - 1])
    r.back_low[0] = (r.back_turned[...] * (HD ** -0.5)).astype(BF)
    r.back_heads[head] = r.back_low[0]
    arrive(gf_z)
    r.gf_line[...] = total(r.gf_chip[z], r.gf_z).astype(BF)
    gf_x = []
    for k in range(1, 4):
        goal = ring(x, k)
        gf_x.append(wire.push(r.gf_line.at[goal], r.gf_x.at[k - 1], place.at(x=goal)))
    arrive(out_cols)
    for j in range(4):
        by_owner(r.go, j, r.out_in[j], 0, 128)
    go_swap = sum_cores(wire, place, r.go, r.go_core)

    def feed_out(i, _):
        blocks = pl.ds(2 * i, 2)
        part = r.hidden[blocks].reshape(256, 512)
        r.feed[blocks] = dot_cols(part, r.w_reduce[...].reshape(512, 512)).reshape(2, 128, 512)
        part = r.pre[blocks].reshape(256, 512)
        r.row_grad[blocks] = dot_cols(part, r.w_expand[...].reshape(512, 512)).reshape(2, 128, 512)
        return 0

    lax.fori_loop(0, 2, feed_out, 0)
    go_swap.wait_recv()
    for a in range(4):
        r.go_chip[a] = (r.go[c, a].astype(F32) + r.go_core[a].astype(F32)).astype(BF)
    go_all = scatter_plane(wire, place, r.go_chip, r.go_in)
    out_rows = r.w_output[pl.ds(8 * t, 8)].reshape(128, 512)
    for i in range(2):
        blocks, lanes = slice(2 * i, 2 * i + 2), slice(256 * i, 256 * i + 256)
        part = r.feed[blocks].reshape(256, 512) + dot_rows(r.pair_out[:, lanes], out_rows)
        r.out_part[blocks] = part.astype(BF).reshape(2, 128, 512)
    out_parts = trade_t(wire, place, r.out_part, r.out_got)
    r.out_got[t] = r.out_part[t]
    back_cross.wait_recv()
    back = r.back_heads[...].reshape(128, 512).astype(F32).T
    cosine, sine = r.cos[...].reshape(512, 128), r.sin[...].reshape(512, 128)
    r.joint_out[:, 0:128] = turn(back, cosine, sine, -1.0).astype(BF)
    low = lax.broadcasted_iota(jnp.int32, (128, 128), 1) < 64
    arrive([dk_swap[3], *dk_sent])
    r.dkv[head] = (chip_sum(x) + r.dk_got[2].astype(F32)).astype(BF)
    r.dkv[1 - head] = (r.dk_got[0].astype(F32) + r.dk_got[1].astype(F32)).astype(BF)
    for h in range(2):
        for i in range(4):
            rows = pl.ds(128 * i, 128)
            key_cos = jnp.where(low, r.cos[i], 1.0)
            key_sin = jnp.where(low, r.sin[i], 0.0)
            r.joint_out[rows, 128 + 128 * h : 256 + 128 * h] = turn(
                r.dkv[h, rows, :].astype(F32), key_cos, key_sin, -1.0
            ).astype(BF)
    for j in range(4):
        part = r.normed[:, :, 128 * j : 128 * j + 128].reshape(512, 128)
        by_owner(r.gj, j, dot_rows(part, r.joint_out[...]).astype(BF), 0, 384)
    gj_swap = sum_cores(wire, place, r.gj, r.gj_core)

    r.vp[0] = jnp.zeros((4, 16, 128), F32)
    shift_sum = jnp.zeros((1, 512), F32)
    gain_sum = jnp.zeros((1, 512), F32)
    for i in range(4):
        rows = pl.ds(128 * i, 128)
        part = r.row_grad[i] + dot_cols(r.joint_out[rows, :], r.w_joint[...].reshape(512, 384))
        r.back_part[i] = part.astype(BF)
        normal, _rate = normalise(r.rows_x[i])
        shift_sum = shift_sum + jnp.sum(part, axis=0, keepdims=True)
        gain_sum = gain_sum + jnp.sum(part * normal, axis=0, keepdims=True)
    gj_swap.wait_recv()
    for a in range(4):
        r.gj_chip[a] = (r.gj[c, a].astype(F32) + r.gj_core[a].astype(F32)).astype(BF)
    gj_all = scatter_plane(wire, place, r.gj_chip, r.gj_in)
    back_parts = trade_t(wire, place, r.back_part, r.back_got)
    r.back_got[t] = r.back_part[t]
    out_sum = jnp.sum(r.rows_c[t].astype(F32), axis=0, keepdims=True)
    joint_sum = jnp.sum(r.joint_out[...].astype(F32), axis=0, keepdims=True)
    one, two = joint_sum[:, 128:256], joint_sum[:, 256:384]
    for k in range(4):
        lanes = slice(128 * k, 128 * k + 128)
        r.vp[0, k, 0:1, :] = gain_sum[:, lanes]
        r.vp[0, k, 1:2, :] = shift_sum[:, lanes]
        r.vp[0, k, 5:6, :] = out_sum[:, lanes]
        r.vp[0, k, 6:7, :] = out_sum[:, lanes]
        r.vp[0, k, pl.ds(7 + t, 1), :] = hidden_sum[:, lanes]
    r.vp[0, t, 2:3, :] = joint_sum[:, 0:128]
    r.vp[0, t, 3:4, :] = jnp.where(low_row, one, pltpu.roll(two, 64, 1))
    r.vp[0, t, 4:5, :] = jnp.where(low_row, pltpu.roll(one, 64, 1), two)
    vp_swap = wire.push(r.vp.at[0], r.vp_core, sibling)
    arrive(gf_x)
    gf_own = total(r.gf_line[x], r.gf_x)
    arrive(go_all)
    go_own = add_plane(r.go_chip[place.a, place.b], r.go_in)
    for k in range(4):
        r.early_out[k, :, 0:1024] = gf_own[4 * k : 4 * k + 4, :]
        r.early_out[k, :, 1024:1152] = go_own[4 * k : 4 * k + 4, :]
    r.gm_out[1, :, 0:128] = go_own.astype(BF)
    r.gm_out[2] = gf_own[:, 0:512].astype(BF)
    r.gm_out[3] = gf_own[:, 512:1024].astype(BF)
    gm_first = wire.block(4)
    gm_widths = (384, 128, 512, 512)

    def to_newton(w, sender):
        lanes = slice(0, gm_widths[w])
        return wire.offer(
            gm_first, r.gm_out.at[w, :, lanes], r.gm_in.at[sender, :, lanes], sender, w,
            place.at(t=w),
        )

    def send_newton(w):
        @pl.when(t != w)
        def _():
            to_newton(w, t).start()

        @pl.when(t == w)
        def _():
            r.gm_in[w, :, 0 : gm_widths[w]] = r.gm_out[w, :, 0 : gm_widths[w]]

    for w in (1, 2, 3):
        send_newton(w)
    early_t = trade_t(wire, place, r.early_out, r.early_in)
    r.early_in[t] = r.early_out[t]

    arrive(early)
    r.m_early[t] = r.m_own[t]
    for k in range(4):
        r.m_old[4 * k : 4 * k + 4, :] = r.m_early[k]
    vp_swap.wait_recv()
    r.vp[1] = r.vp[0] + r.vp_core[...]
    vp_z = [wire.push(r.vp.at[1], r.vp_z.at[k], p) for k, p in enumerate(place.row_z())]

    arrive(gj_all)
    gj_own = add_plane(r.gj_chip[place.a, place.b], r.gj_in)
    r.gm_out[0, :, 0:384] = gj_own.astype(BF)
    send_newton(0)
    for k in range(4):
        r.late_out[k] = gj_own[4 * k : 4 * k + 4, :]
    late_t = trade_t(wire, place, r.late_out, r.late_in)
    r.late_in[t] = r.late_out[t]
    arrive(vp_z)
    r.vp[2] = total(r.vp[1], r.vp_z)
    vp_x = [wire.push(r.vp.at[2], r.vp_x.at[k], p) for k, p in enumerate(place.row_x())]

    for w in range(4):

        @pl.when(t == w)
        def _(w=w):
            width = gm_widths[w]
            for sender in range(4):
                if sender != w:
                    to_newton(w, sender).wait_recv()
            for k in range(4):
                lanes = slice(width * k, width * k + width)
                value = muon_beta * r.m_old[:, lanes] + r.gm_in[k, :, 0:width].astype(F32)
                if width * k < 1536:
                    r.momentum[c, place.a, place.b, :, lanes] = value.astype(BF)
                else:
                    r.extra[c, place.a, place.b] = value.astype(BF)
            if w == 1:
                r.momentum[c, place.a, place.b, :, 512:1536] = jnp.zeros((16, 1024), BF)

    m_b = spread_b(wire, place, r.momentum)

    extra_first = wire.block(16)

    def extra_copies():
        block = r.extra.at[c, place.a, place.b]
        copies = []
        for k, (a, b) in enumerate(place.plane()):
            copies.append(
                wire.offer(extra_first, block, block, k, k, place.at_ab(a, b))
            )
        return copies

    def extra_swap():
        block = r.extra.at[c]
        return wire.offer(extra_first, block, block, 15, 15, sibling)

    @pl.when(t >= 2)
    def _():
        for copy in extra_copies():
            copy.start()

    arrive(early_t)
    for k in range(4):
        part = r.early_in[k]
        r.g_expand[:, 512 * k : 512 * k + 512] = part[:, 0:512]
        r.g_reduce[:, 512 * k : 512 * k + 512] = part[:, 512:1024]
        r.g_output[:, 128 * k : 128 * k + 128] = part[:, 1024:1152]
    arrive(late_t)
    for k in range(4):
        unpair(r.g_joint, r.late_in[k], k)
    for old, grad, new in (
        (r.m_joint_v, r.g_joint, r.n_joint),
        (r.m_output_v, r.g_output, r.n_output),
        (r.m_expand_v, r.g_expand, r.n_expand),
        (r.m_reduce_v, r.g_reduce, r.n_reduce),
    ):
        new[...] = muon_beta * old[...] + grad[...]
    arrive(vp_x)
    r.vp[3] = total(r.vp[2], r.vp_x)
    vp_t = [wire.push(r.vp.at[3], r.vp_t.at[k], p) for k, p in enumerate(place.row_t())]
    arrive(out_parts)
    arrive(back_parts)
    arrive(m_b)
    whole = Ring(wire, place, r.momentum, place.a, place.at_a)
    whole.hand_on()
    wide = r.rows_x[t].astype(F32)
    feed = r.out_got[0].astype(F32)
    back = r.back_got[0].astype(F32)
    for k in range(1, 4):
        feed = feed + r.out_got[k].astype(F32)
        back = back + r.back_got[k].astype(F32)
    r.block_output[...] = (wide + feed + vec_row(r.v, 5) + vec_row(r.v, 6)).astype(BF)
    normal, rate = normalise(r.rows_x[t])
    scaled = back * gain
    mean_one = jnp.mean(scaled, axis=-1, keepdims=True)
    mean_two = jnp.mean(scaled * normal, axis=-1, keepdims=True)
    r.input_grad[...] = r.rows_c[t].astype(F32) + rate * (scaled - mean_one - normal * mean_two)
    whole.close()
    arrive(vp_t)
    r.vec_sum[...] = total(r.vp[3], r.vp_t)
    r.table[0:16, :] = r.vec_sum[z]
    r.table[...] = r.table[...].T
    vector_grad = r.table[pl.ds(pl.multiple_of(16 * seq + 4 * t, 4), 4), 0:11]
    r.vector_grad[...] = vector_grad
    first_next = beta_first * r.first_v[...] + (1.0 - beta_first) * vector_grad
    second_next = (
        beta_second * r.second_v[...] + (1.0 - beta_second) * vector_grad * vector_grad
    )
    r.second_next[...] = second_next
    first_hat = first_next / (1.0 - beta_first**STEP)
    second_hat = second_next / (1.0 - beta_second**STEP)
    r.vector_next[...] = r.vectors_v[...] - vector_rate * first_hat / (
        jnp.sqrt(second_hat) + adam_epsilon
    )
    @pl.when(t >= 2)
    def _():
        for copy in extra_copies():
            copy.wait_recv()
        extra_swap().start()
        extra_swap().wait_recv()

    arrive(whole.swaps)

    high, small = newton(r, place)
    both = jnp.concatenate([high, small], axis=0)
    for k in range(3):
        lanes = slice(512 * k, 512 * k + 512)
        rows = dot(both, r.momentum[:, :, :, :, lanes].reshape(512, 512))
        r.m_rows[:, lanes] = rows[0:16] + rows[16:32]

    @pl.when(t >= 2)
    def _():
        rows = dot(both, r.extra[...].reshape(512, 512))
        r.m_rows[:, 1536:2048] = rows[0:16] + rows[16:32]

    @pl.when(t < 2)
    def _():
        r.m_rows[:, 1536:2048] = jnp.zeros((16, 512), F32)

    for k in range(4):
        for p in range(4):
            r.u_rows[k, 4 * p : 4 * p + 4, :] = r.m_rows[
                4 * k : 4 * k + 4, 512 * p : 512 * p + 512
            ]
    r.u_out[...] = r.u_rows[...].astype(BF)
    u_t = trade_t(wire, place, r.u_out, r.u_in)
    r.u_in[t] = r.u_out[t]
    wire.drain()
    for w in range(4):

        @pl.when(t != w)
        def _(w=w):
            to_newton(w, t).wait_send()

    @pl.when(t >= 2)
    def _():
        for copy in extra_copies():
            copy.wait_send()
        extra_swap().wait_send()

    arrive(u_t)
    r.u_rows[...] = r.u_in[...].astype(F32)
    for k in range(4):
        for p in range(4):
            r.u_wide[k, :, 512 * p : 512 * p + 512] = r.u_rows[k, 4 * p : 4 * p + 4, :]
    for k in range(4):
        unpair(r.u_joint, r.u_wide[0, :, 384 * k : 384 * k + 384], k)
    for k, (old, change, new) in enumerate(
        (
            (r.joint_v, r.u_joint, r.u_joint),
            (r.output_v, r.u_wide.at[1, :, pl.ds(0, 512)], r.u_output),
            (r.expand_v, r.u_wide.at[2], r.u_expand),
            (r.reduce_v, r.u_wide.at[3], r.u_reduce),
        )
    ):
        factor = muon_rate * 0.2 * math.sqrt(max(D, WIDTHS[k]))
        new[...] = old[...] * (1.0 - muon_rate * muon_decay) - factor * change[...]
    wire.drain()


def block_stage(*arrays):
    return pl.pallas_call(
        block_kernel,
        out_shape=tuple(shape(dims, dtype) for _, dims, dtype in OUTPUTS),
        in_specs=[SMEM] + [ANY] * (len(INPUTS) - 1),
        out_specs=(VMEM,) * len(OUTPUTS),
        scratch_shapes=[pltpu.VMEM(dims, dtype) for _, dims, dtype in SCRATCH]
        + [
            pltpu.SemaphoreType.DMA((PUSHES,)),
            pltpu.SemaphoreType.DMA((PUSHES,)),
            pltpu.SemaphoreType.DMA((LOADS,)),
        ],
        compiler_params=pltpu.CompilerParams(
            collective_id=1, has_side_effects=True, vmem_limit_bytes=56 << 20
        ),
        name="block",
    )(*arrays)


def write_kernel(*refs):
    count = len(OUTPUTS)
    sem = refs[-1]
    copies = []
    for k in range(count):
        copy = pltpu.make_async_copy(refs[k], refs[count + k], sem.at[k])
        copy.start()
        copies.append(copy)
    for copy in copies:
        copy.wait()


def write_stage(*arrays):
    count = len(arrays)
    return pl.pallas_call(
        write_kernel,
        out_shape=tuple(shape(a.shape, a.dtype) for a in arrays),
        in_specs=[VMEM] * count,
        out_specs=(ANY,) * count,
        scratch_shapes=[pltpu.SemaphoreType.DMA((count,))],
        name="write",
    )(*arrays)


def shards(
    block_input,
    cotangent,
    doc_lengths,
    joint_weight,
    output_weight,
    expand_weight,
    reduce_weight,
    joint_moment,
    output_moment,
    expand_moment,
    reduce_moment,
    vectors,
    first_moment,
    second_moment,
):
    results = block_stage(
        doc_lengths, block_input, cotangent, joint_weight, output_weight, expand_weight,
        reduce_weight, vectors.T, joint_moment, output_moment, expand_moment, reduce_moment,
        first_moment.T, second_moment.T,
    )
    results = write_stage(*results)
    return (*results[12:14], *results[0:12], *[part.T for part in results[14:]])


def solution(mesh):
    rows = P(("fsdp", "seq", "tensor"), None)
    columns = P(None, ("fsdp", "seq", "tensor"))
    return jax.shard_map(
        shards,
        mesh=mesh,
        in_specs=(rows, rows, P("fsdp", None)) + (rows,) * 8 + (columns,) * 3,
        out_specs=(rows,) * 14 + (columns,) * 3,
        check_vma=False,
    )
```

```python
import functools
import math

import jax
import jax.numpy as jnp
from jax import lax
from jax.experimental import pallas as pl
from jax.experimental.pallas import tpu as pltpu
from jax.sharding import PartitionSpec as P

D = 512
HEADS = 8
FF = 2048
ROT = 16
HD = 64
STEP = 10

norm_epsilon = 1e-05
masked_score = -1e30
newton_first = 3.4445
newton_second = -4.775
newton_third = 2.0315
beta_first = 0.9
beta_second = 0.95
adam_epsilon = 1e-08
vector_rate = 0.2
muon_rate = 0.25
muon_beta = 0.95
muon_decay = 0.01
LOG2_E = 1.4426950408889634

BF = jnp.bfloat16
F32 = jnp.float32
MESH = pl.DeviceIdType.MESH
VMEM = pl.BlockSpec(memory_space=pltpu.VMEM)
SMEM = pl.BlockSpec(memory_space=pltpu.SMEM)
ANY = pl.BlockSpec(memory_space=pl.ANY)
WIDTHS = (3 * D, D, FF, FF)


def shape(dims, dtype):
    return jax.ShapeDtypeStruct(dims, dtype)


class Place:
    def __init__(self):
        self.z = lax.axis_index("fsdp")
        self.seq = lax.axis_index("seq")
        self.t = lax.axis_index("tensor")
        self.x = lax.div(self.seq, 2)
        self.c = lax.rem(self.seq, 2)
        self.d = 1 - 2 * self.c
        self.a = self.c * self.x + (1 - self.c) * self.z
        self.b = self.c * self.z + (1 - self.c) * self.x
        self.mate = self.x + 1 - 2 * lax.rem(self.x, 2)
        self.cross = 3 - self.x
        self.head = lax.div(self.x, 2)

    def at(self, z=None, x=None, c=None, t=None):
        z = self.z if z is None else z
        x = self.x if x is None else x
        c = self.c if c is None else c
        t = self.t if t is None else t
        return (z, 2 * x + c, t)

    def at_a(self, a):
        c = self.c
        return self.at(z=(1 - c) * a + c * self.z, x=c * a + (1 - c) * self.x)

    def at_b(self, b):
        c = self.c
        return self.at(z=c * b + (1 - c) * self.z, x=(1 - c) * b + c * self.x)

    def at_ab(self, a, b):
        c = self.c
        return self.at(z=(1 - c) * a + c * b, x=c * a + (1 - c) * b)

    def plane(self):
        steps = [(i, j) for i in range(4) for j in range(4) if i + j > 0]
        steps.sort(key=lambda step: -min(step[0], 4 - step[0]) - min(step[1], 4 - step[1]))
        return [(ring(self.a, i), ring(self.b, j)) for i, j in steps]

    def sibling(self):
        return self.at(c=1 - self.c)

    def octet(self):
        g = 4 * self.c + self.t
        members = [lax.rem(g + k, 8) for k in range(1, 8)]
        return [self.at(c=lax.div(m, 4), t=lax.rem(m, 4)) for m in members]

    def row_x(self):
        return [self.at(x=lax.rem(self.x + k, 4)) for k in range(1, 4)]

    def row_z(self):
        return [self.at(z=lax.rem(self.z + k, 4)) for k in range(1, 4)]

    def row_t(self):
        return [self.at(t=lax.rem(self.t + k, 4)) for k in range(1, 4)]


def ring(index, step):
    return lax.rem(index + step + 4, 4)


def greet(partners):
    barrier = pltpu.get_barrier_semaphore()
    for partner in partners:
        pl.semaphore_signal(barrier, inc=1, device_id=partner, device_id_type=MESH)
    return lambda: pl.semaphore_wait(barrier, len(partners))


class Wire:
    def __init__(self, send, recv, local):
        self.send = send
        self.recv = recv
        self.local = local
        self.count = 0
        self.loads = 0
        self.open = []

    def push(self, src, dst, device):
        index = self.count
        self.count += 1
        copy = pltpu.make_async_remote_copy(
            src_ref=src,
            dst_ref=dst,
            send_sem=self.send.at[index],
            recv_sem=self.recv.at[index],
            device_id=device,
            device_id_type=MESH,
        )
        copy.start()
        self.open.append(copy)
        return copy

    def offer(self, first, source, target, sender, goal, device):
        return pltpu.make_async_remote_copy(
            src_ref=source,
            dst_ref=target,
            send_sem=self.send.at[first + goal],
            recv_sem=self.recv.at[first + sender],
            device_id=device,
            device_id_type=MESH,
        )

    def block(self, count):
        first = self.count
        self.count += count
        return first

    def load(self, src, dst):
        copy = pltpu.make_async_copy(src, dst, self.local.at[self.loads])
        self.loads += 1
        copy.start()
        return copy

    def drain(self):
        for copy in self.open:
            copy.wait_send()
        self.open = []


def arrive(copies):
    for copy in copies:
        copy.wait_recv()


def dot(left, right):
    return jnp.dot(left, right, preferred_element_type=F32)


def dot_cols(left, right):
    return lax.dot_general(left, right, (((1,), (1,)), ((), ())), preferred_element_type=F32)


def dot_rows(left, right):
    return lax.dot_general(left, right, (((0,), (0,)), ((), ())), preferred_element_type=F32)


def turn(values, cosine, sine, sign):
    lane = lax.rem(lax.broadcasted_iota(jnp.int32, values.shape, 1), 64)
    crossed = jnp.where(lane < 8, -pltpu.roll(values, 120, 1), pltpu.roll(values, 8, 1))
    return values * cosine + crossed * (sine * sign)


def vec_row(v_ref, row):
    return jnp.concatenate([v_ref[k, row : row + 1, :] for k in range(4)], axis=1)


def normalise(rows):
    wide = rows.astype(F32)
    centred = wide - jnp.mean(wide, axis=-1, keepdims=True)
    variance = jnp.mean(centred * centred, axis=-1, keepdims=True)
    rate = lax.rsqrt(variance + norm_epsilon)
    return centred * rate, rate


def halves(values):
    high = values.astype(BF)
    return high, (values - high.astype(F32)).astype(BF)


def product(left_h, left_l, right_h, right_l):
    return dot(left_h, right_h) + (dot(left_h, right_l) + dot(left_l, right_h))


def squared(high, small):
    cross = dot(high, small)
    return dot(high, high) + (cross + cross.T)


def spread_b(wire, place, ref):
    block = ref.at[place.c, place.a, place.b]
    return [wire.push(block, block, place.at_b(ring(place.b, k))) for k in range(1, 4)]


class Ring:
    def __init__(self, wire, place, ref, index, at):
        self.wire = wire
        self.place = place
        self.ref = ref
        self.index = index
        self.at = at
        self.ups, self.downs = {}, {}
        for p, q in ((0, 2), (1, 3), (2, 0), (3, 1)):
            self.ups[p] = self.send(0, p, 1)
            self.downs[q] = self.send(0, q, -1)
        self.swaps = [self.swap(0)]

    def send(self, step, part, way):
        block = self.ref.at[self.place.c, ring(self.index, step), part]
        return self.wire.push(block, block, self.at(ring(self.index, way)))

    def swap(self, step):
        block = self.ref.at[self.place.c, ring(self.index, step)]
        return self.wire.push(block, block, self.place.sibling())

    def hand_on(self):
        self.more = []
        for p, q in ((0, 2), (1, 3)):
            self.ups[p].wait_recv()
            self.more.append(self.send(-1, p, 1))
            self.downs[q].wait_recv()
            self.more.append(self.send(1, q, -1))

    def close(self):
        arrive([self.ups[2], self.ups[3]])
        self.swaps.append(self.swap(-1))
        arrive([self.downs[0], self.downs[1]])
        self.swaps.append(self.swap(1))
        arrive(self.more)
        self.swaps.append(self.swap(2))


def spread_plane(wire, place, ref):
    block = ref.at[place.c, place.a, place.b]
    return [wire.push(block, block, place.at_ab(a, b)) for a, b in place.plane()]


def scatter_plane(wire, place, ref, target):
    copies = []
    for k, (a, b) in enumerate(place.plane()):
        copies.append(wire.push(ref.at[a, b], target.at[k], place.at_ab(a, b)))
    return copies


def add_plane(first, parts):
    value = first.astype(F32)
    for k in range(15):
        value = value + parts[k].astype(F32)
    return value


def swap_cores(wire, place, ref):
    return wire.push(ref.at[place.c], ref.at[place.c], place.sibling())


def natural(source, target, start, stop):
    for z in range(4):
        for x in range(4):
            target[8 * z + 2 * x] = source[0, z, x, :, start:stop]
            target[8 * z + 2 * x + 1] = source[1, x, z, :, start:stop]


def by_row(source, target, start, stop):
    for z in range(4):
        for x in range(4):
            for c in range(2):
                target[8 * z + 2 * x + c] = source[c, z, x, :, start:stop]


def by_owner(target, z, rows, start, stop):
    for x in range(4):
        target[0, z, x, :, start:stop] = rows[32 * x : 32 * x + 16, :]
        target[1, x, z, :, start:stop] = rows[32 * x + 16 : 32 * x + 32, :]


def by_core(target, z, rows, start, stop):
    for x in range(4):
        for c in range(2):
            block = rows[32 * x + 16 * c : 32 * x + 16 * c + 16, :]
            target[c, z, x, :, start:stop] = block


def sum_cores(wire, place, ref, target):
    return wire.push(ref.at[1 - place.c], target, place.sibling())


def trade_t(wire, place, source, target):
    copies = []
    for k in range(1, 4):
        goal = ring(place.t, k)
        copies.append(wire.push(source.at[goal], target.at[place.t], place.at(t=goal)))
    return copies


def total(first, parts):
    value = first.astype(F32)
    for k in range(3):
        value = value + parts[k].astype(F32)
    return value


def unpair(target, part, k):
    one, two = part[:, 128:256], part[:, 256:384]
    target[:, 128 * k : 128 * k + 128] = part[:, 0:128]
    target[:, 512 + 128 * k : 640 + 128 * k] = jnp.concatenate(
        [one[:, 0:64], two[:, 0:64]], axis=1
    )
    target[:, 1024 + 128 * k : 1152 + 128 * k] = jnp.concatenate(
        [one[:, 64:128], two[:, 64:128]], axis=1
    )


INPUTS = (
    "lengths",
    "x",
    "c",
    "joint",
    "output",
    "expand",
    "reduce",
    "vectors",
    "m_joint",
    "m_output",
    "m_expand",
    "m_reduce",
    "first",
    "second",
)

OUTPUTS = (
    ("g_joint", (4, 1536), F32),
    ("g_output", (4, 512), F32),
    ("g_expand", (4, 2048), F32),
    ("g_reduce", (4, 2048), F32),
    ("n_joint", (4, 1536), F32),
    ("n_output", (4, 512), F32),
    ("n_expand", (4, 2048), F32),
    ("n_reduce", (4, 2048), F32),
    ("u_joint", (4, 1536), F32),
    ("u_output", (4, 512), F32),
    ("u_expand", (4, 2048), F32),
    ("u_reduce", (4, 2048), F32),
    ("block_output", (128, 512), BF),
    ("input_grad", (128, 512), F32),
    ("vector_grad", (4, 11), F32),
    ("second_next", (4, 11), F32),
    ("vector_next", (4, 11), F32),
)

SCRATCH = (
    ("joint_v", (4, 1536), F32),
    ("output_v", (4, 512), F32),
    ("expand_v", (4, 2048), F32),
    ("reduce_v", (4, 2048), F32),
    ("vectors_v", (4, 11), F32),
    ("first_v", (4, 11), F32),
    ("second_v", (4, 11), F32),
    ("table", (128, 128), F32),
    ("vec_sum", (4, 16, 128), F32),
    ("m_joint_v", (4, 1536), F32),
    ("m_output_v", (4, 512), F32),
    ("m_expand_v", (4, 2048), F32),
    ("m_reduce_v", (4, 2048), F32),
    ("j_out", (4, 4, 384), F32),
    ("j_in", (4, 4, 384), F32),
    ("j_rows", (16, 384), F32),
    ("w_out", (4, 4, 1536), F32),
    ("w_in", (4, 4, 1536), F32),
    ("w_rows", (16, 1536), F32),
    ("wj", (2, 4, 4, 16, 512), BF),
    ("wr", (2, 4, 4, 16, 1536), BF),
    ("w_joint", (32, 16, 384), BF),
    ("w_output", (32, 16, 512), BF),
    ("w_expand", (32, 16, 512), BF),
    ("w_reduce", (32, 16, 512), BF),
    ("v_own", (16, 128), F32),
    ("m_own", (4, 4, 2048), F32),
    ("m_early", (4, 4, 2048), F32),
    ("m_old", (16, 2048), F32),
    ("v_in", (4, 16, 128), F32),
    ("v", (4, 16, 128), F32),
    ("rows_x", (4, 128, 512), BF),
    ("rows_c", (4, 128, 512), BF),
    ("cos", (4, 128, 128), F32),
    ("sin", (4, 128, 128), F32),
    ("normed", (4, 128, 512), BF),
    ("q_turned", (2, 128, 256), BF),
    ("q_buf", (2, 64, 512), BF),
    ("q_heads", (2, 64, 512), BF),
    ("g_buf", (2, 64, 512), BF),
    ("g_heads", (2, 64, 512), BF),
    ("kv_buf", (2, 512, 128), BF),
    ("kv", (8, 512, 128), BF),
    ("hidden", (4, 128, 512), BF),
    ("pre", (4, 128, 512), BF),
    ("feed", (4, 128, 512), F32),
    ("row_grad", (4, 128, 512), F32),
    ("gf", (2, 4, 4, 16, 1024), BF),
    ("gf_core", (4, 4, 16, 1024), BF),
    ("gf_chip", (4, 4, 16, 1024), BF),
    ("gf_z", (3, 4, 16, 1024), BF),
    ("gf_line", (4, 16, 1024), BF),
    ("gf_x", (3, 16, 1024), BF),
    ("go", (2, 4, 4, 16, 128), BF),
    ("go_core", (4, 4, 16, 128), BF),
    ("go_chip", (4, 4, 16, 128), BF),
    ("go_in", (15, 16, 128), BF),
    ("early_out", (4, 4, 1152), F32),
    ("early_in", (4, 4, 1152), F32),
    ("turned", (8, 128, 512), BF),
    ("keys", (8, 512, 128), BF),
    ("scores", (9, 512, 512), F32),
    ("sums", (8, 512, 128), F32),
    ("query_low", (2, 512, 128), BF),
    ("query_two", (2, 512, 128), BF),
    ("begin", (2, 1, 512), jnp.int32),
    ("top", (2, 1, 512), F32),
    ("total_sum", (2, 1, 512), F32),
    ("out_turned", (2, 64, 512), F32),
    ("grad_low", (2, 512, 128), BF),
    ("back_turned", (64, 512), F32),
    ("centre", (2, 1, 512), F32),
    ("out_low", (2, 64, 512), BF),
    ("out_heads", (2, 64, 512), BF),
    ("back_low", (2, 64, 512), BF),
    ("back_heads", (2, 64, 512), BF),
    ("dk", (2, 4, 512, 128), BF),
    ("dk_in", (4, 512, 128), BF),
    ("dk_chip", (4, 512, 128), BF),
    ("dk_got", (3, 512, 128), BF),
    ("dkv", (2, 512, 128), BF),
    ("pair_out", (128, 512), BF),
    ("joint_out", (512, 384), BF),
    ("out_cols", (4, 128, 128), BF),
    ("out_in", (4, 128, 128), BF),
    ("out_part", (4, 128, 512), BF),
    ("out_got", (4, 128, 512), BF),
    ("back_part", (4, 128, 512), BF),
    ("back_got", (4, 128, 512), BF),
    ("gj", (2, 4, 4, 16, 384), BF),
    ("gj_core", (4, 4, 16, 384), BF),
    ("gj_chip", (4, 4, 16, 384), BF),
    ("gj_in", (15, 16, 384), BF),
    ("late_out", (4, 4, 384), F32),
    ("late_in", (4, 4, 384), F32),
    ("vp", (4, 4, 16, 128), F32),
    ("vp_core", (4, 16, 128), F32),
    ("vp_z", (3, 4, 16, 128), F32),
    ("vp_x", (3, 4, 16, 128), F32),
    ("vp_t", (3, 4, 16, 128), F32),
    ("gm_out", (4, 16, 512), BF),
    ("gm_in", (4, 16, 512), BF),
    ("m_rows", (16, 2048), F32),
    ("momentum", (2, 4, 4, 16, 1536), BF),
    ("extra", (2, 4, 4, 16, 512), BF),
    ("gram", (512, 512), F32),
    ("gram_h", (512, 512), BF),
    ("gram_l", (512, 512), BF),
    ("poly_h", (512, 512), BF),
    ("poly_l", (512, 512), BF),
    ("temp_h", (512, 512), BF),
    ("temp_l", (512, 512), BF),
    ("own", (16, 512), F32),
    ("u_rows", (4, 16, 512), F32),
    ("u_out", (4, 16, 512), BF),
    ("u_in", (4, 16, 512), BF),
    ("u_wide", (4, 4, 2048), F32),
)

PUSHES = 240
LOADS = 16


class Box:
    pass


def attend_chunk(place, slot):
    return place.seq if slot == 0 else 7 - place.seq


def attend_score(slot, k):
    return 8 - k if slot == 0 else k


def pairs(count, step, carry):
    def two(k, carry):
        return step(2 * k + 1, step(2 * k, carry))

    def one(_, carry):
        return step(count - 1, carry)

    carry = lax.fori_loop(0, lax.div(count, 2), two, carry)
    return lax.fori_loop(0, lax.rem(count, 2), one, carry)


def attend_start(r, place):
    for slot in range(2):
        index = 512 * attend_chunk(place, slot) + lax.broadcasted_iota(jnp.int32, (1, 512), 1)
        begin = jnp.zeros((1, 512), jnp.int32)
        finish = 0
        for j in range(4):
            finish = finish + r.lengths[0, j]
            begin = jnp.where(index >= finish, finish, begin)
        r.begin[slot] = begin
        r.top[slot] = jnp.full((1, 512), masked_score, F32)
        r.total_sum[slot] = jnp.zeros((1, 512), F32)


def query_prepare(r, slot):
    wide = r.q_heads[slot].astype(F32)
    high, small = halves(wide * (HD ** -0.5 * LOG2_E))
    r.query_two[slot] = jnp.concatenate([high, small], axis=0).T
    low = (wide * (HD ** -0.5)).astype(BF)
    r.query_low[slot] = jnp.concatenate([low, jnp.zeros((64, 512), BF)], axis=0).T


def grad_prepare(r, slot):
    r.grad_low[slot] = jnp.concatenate([jnp.zeros((64, 512), BF), r.g_heads[slot]], axis=0).T


def keys_prepare(r, column):
    low = lax.broadcasted_iota(jnp.int32, (512, 128), 1) < 64
    for part in range(2):
        k = 2 * column + part
        r.turned[k] = r.kv[k].T
        wide = r.kv[k].astype(F32)
        r.keys[k] = jnp.where(low, wide, pltpu.roll(wide, 64, 1)).astype(BF)


def score_column(r, place, column, slot, diagonal=False):
    chunk = attend_chunk(place, slot)

    def run(parts):
        top, total_sum = r.top[slot], r.total_sum[slot]
        for part, last in parts:
            k = 2 * column + part
            raw = dot_cols(r.keys[k], r.query_two[slot])
            key = lax.broadcasted_iota(jnp.int32, (512, 512), 0)
            allowed = key >= r.begin[slot] - 512 * k
            if last:
                allowed = allowed & (key <= lax.broadcasted_iota(jnp.int32, (512, 512), 1))
            raw = jnp.where(allowed, raw, masked_score)
            r.scores[attend_score(slot, k)] = raw
            higher = jnp.maximum(top, jnp.max(raw, axis=0, keepdims=True))
            total_part = jnp.sum(jnp.exp2(raw - higher), axis=0, keepdims=True)
            total_sum = total_sum * jnp.exp2(top - higher) + total_part
            top = higher
        r.top[slot] = top
        r.total_sum[slot] = total_sum

    if not diagonal:

        @pl.when(2 * column + 1 < chunk)
        def _():
            run(((0, False), (1, False)))

        return

    @pl.when(2 * column + 1 == chunk)
    def _():
        run(((0, False), (1, True)))

    @pl.when(2 * column == chunk)
    def _():
        run(((0, True),))


def weigh_values(r, place, slot):
    level = r.top[slot] + jnp.log(r.total_sum[slot]) * LOG2_E

    def weigh(k, out):
        prob = jnp.exp2(r.scores[attend_score(slot, k)] - level)
        r.scores[attend_score(slot, k)] = prob
        return out + dot(r.turned[k, 64:128, :], prob.astype(BF))

    out = pairs(attend_chunk(place, slot) + 1, weigh, jnp.zeros((64, 512), F32))
    r.out_turned[slot] = out
    r.out_low[slot] = out.astype(BF)


def backward_block(r, slot, k):
    prob = r.scores[attend_score(slot, k)]
    out_grad = r.grad_low[slot]
    grad = dot_cols(r.kv[k], out_grad)
    score_grad = (prob * (grad - r.centre[slot])).astype(BF)
    r.sums[k] += dot(prob.astype(BF), out_grad) + dot(score_grad, r.query_low[slot])
    return dot(r.turned[k, 0:64, :], score_grad)


def backward_cross(r, place):
    def step(k, back):
        return back + backward_block(r, 1, k)

    back = pairs(attend_chunk(place, 1) + 1, step, jnp.zeros((64, 512), F32))
    r.back_low[1] = (back * (HD ** -0.5)).astype(BF)


def backward_column(r, place, column, diagonal):
    chunk = attend_chunk(place, 0)

    @pl.when(2 * column + 1 <= chunk)
    def _():
        r.back_turned[...] += backward_block(r, 0, 2 * column) + backward_block(
            r, 0, 2 * column + 1
        )

    if diagonal:

        @pl.when(2 * column == chunk)
        def _():
            r.back_turned[...] += backward_block(r, 0, 2 * column)

    r.dk[0, column] = r.sums[2 * column].astype(BF)
    r.dk[1, column] = r.sums[2 * column + 1].astype(BF)


def newton(r, place):
    blocks, size = 1, 512

    def rows(i):
        return pl.ds(size * i, size)

    def diagonal(i):
        row = size * i + lax.broadcasted_iota(jnp.int32, (size, 512), 0)
        return row == lax.broadcasted_iota(jnp.int32, (size, 512), 1)

    def fill(i, trace):
        value = r.gram[...]
        for k in range(3):
            lanes = slice(512 * k, 512 * k + 512)
            right = r.momentum[:, :, :, :, lanes].reshape(512, 512)
            value = value + dot_cols(right, right)
        r.gram[...] = value
        return trace + jnp.sum(jnp.where(diagonal(i), value, 0.0), keepdims=True)

    trace = lax.fori_loop(0, blocks, fill, jnp.zeros((1, 1), F32))
    scale = 1.0 / (jnp.sqrt(trace) + 1e-07)

    def keep(value, i, high_ref, low_ref):
        high, small = halves(value)
        high_ref[rows(i), :] = high
        low_ref[rows(i), :] = small

    def prepare(i, _):
        value = r.gram[rows(i), :] * (scale * scale)
        r.gram[rows(i), :] = value
        keep(value, i, r.gram_h, r.gram_l)
        return 0

    lax.fori_loop(0, blocks, prepare, 0)

    def polynomial(i, _):
        square = squared(r.gram_h[...], r.gram_l[...])
        value = (
            jnp.where(diagonal(i), newton_first, 0.0)
            + newton_second * r.gram[rows(i), :]
            + newton_third * square
        )
        keep(value, i, r.poly_h, r.poly_l)
        return 0

    def inner(i, _):
        high, small = r.poly_h[...], r.poly_l[...]
        own_h, own_l = halves(r.own[...])
        left = jnp.concatenate([high, own_h], axis=0)
        cross = dot(left, small)
        main = dot(jnp.concatenate([left, own_l], axis=0), high)
        r.own[...] = main[512:528] + (main[528:544] + cross[512:528])
        keep(main[0:512] + (cross[0:512] + cross[0:512].T), i, r.temp_h, r.temp_l)
        return 0

    def outer(i, _):
        value = product(r.gram_h[...], r.gram_l[...], r.temp_h[...], r.temp_l[...])
        r.gram[rows(i), :] = value
        keep(value, i, r.gram_h, r.gram_l)
        return 0

    def times(left, right_h, right_l):
        high, small = halves(left)
        both = dot(jnp.concatenate([high, small], axis=0), right_h[...])
        return both[0:16] + (both[16:32] + dot(high, right_l[...]))

    mine = 256 * place.c + 64 * place.a + 16 * place.b
    row = lax.broadcasted_iota(jnp.int32, (16, 512), 0)
    column = lax.broadcasted_iota(jnp.int32, (16, 512), 1)
    r.own[...] = jnp.where(column - row == mine, 1.0, 0.0)

    def sweep(_, carry):
        polynomial(0, 0)
        inner(0, 0)
        outer(0, 0)
        return carry

    lax.fori_loop(0, 3, sweep, 0)
    lax.fori_loop(0, blocks, polynomial, 0)
    lax.fori_loop(0, blocks, inner, 0)

    def last_gram(left):
        return times(times(left, r.gram_h, r.gram_l), r.temp_h, r.temp_l)

    own = r.own[...]
    once = last_gram(own)
    own = newton_first * own + newton_second * once + newton_third * last_gram(once)
    return halves(own * scale)


def block_kernel(*refs):
    r = Box()
    names = list(INPUTS) + [n for n, _, _ in OUTPUTS] + [n for n, _, _ in SCRATCH]
    for name, ref in zip(names, refs):
        setattr(r, name, ref)
    place = Place()
    wire = Wire(*refs[-3:])
    z, x, c, t, d = place.z, place.x, place.c, place.t, place.d
    seq, mate, cross, head = place.seq, place.mate, place.cross, place.head
    sibling = place.sibling()

    met = greet(
        place.octet()
        + [place.at_ab(a, b) for a, b in place.plane()]
        + [place.at(x=cross, c=1 - c)]
    )

    load_w = [
        wire.load(r.joint, r.joint_v),
        wire.load(r.output, r.output_v),
        wire.load(r.expand, r.expand_v),
        wire.load(r.reduce, r.reduce_v),
    ]
    load_v = wire.load(r.vectors, r.vectors_v)
    load_x = wire.load(r.x, r.rows_x.at[t])
    load_c = wire.load(r.c, r.rows_c.at[t])
    load_m = [
        wire.load(r.m_joint, r.m_joint_v),
        wire.load(r.m_output, r.m_output_v),
        wire.load(r.m_expand, r.m_expand_v),
        wire.load(r.m_reduce, r.m_reduce_v),
        wire.load(r.first, r.first_v),
        wire.load(r.second, r.second_v),
    ]
    load_w[0].wait()
    for k in range(4):
        for part in range(3):
            r.j_out[k, :, 128 * part : 128 * part + 128] = r.joint_v[
                :, 512 * part + 128 * k : 512 * part + 128 * k + 128
            ]
    load_v.wait()
    r.table[...] = jnp.zeros((128, 128), F32)
    column = lax.broadcasted_iota(jnp.int32, (128, 11), 0) - (16 * seq + 4 * t)
    own_vec = jnp.zeros((128, 11), F32)
    for j in range(4):
        own_vec = jnp.where(column == j, r.vectors_v[j : j + 1, :], own_vec)
    r.table[:, 0:11] = own_vec.astype(BF).astype(F32)
    r.v_own[...] = r.table[...].T[0:16, :]
    met()

    joint_t = trade_t(wire, place, r.j_out, r.j_in)
    for partner in place.row_t():
        joint_t.append(wire.push(r.v_own, r.v_in.at[t], partner))
    for copy in load_w[1:]:
        copy.wait()
    for k in range(4):
        r.w_out[k, :, 0:512] = r.output_v[...]
        r.w_out[k, :, 512:1024] = r.expand_v[:, 512 * k : 512 * k + 512]
        r.w_out[k, :, 1024:1536] = r.reduce_v[:, 512 * k : 512 * k + 512]
    rest_t = trade_t(wire, place, r.w_out, r.w_in)
    load_x.wait()
    load_c.wait()
    x_rows = [wire.push(r.rows_x.at[t], r.rows_x.at[t], p) for p in place.row_t()]
    r.j_in[t] = r.j_out[t]
    r.v_in[t] = r.v_own[...]
    r.w_in[t] = r.w_out[t]
    arrive(joint_t)
    for k in range(4):
        r.j_rows[4 * k : 4 * k + 4, :] = r.j_in[k]
    keys, values = r.j_rows[:, 128:256], r.j_rows[:, 256:384]
    low16 = lax.broadcasted_iota(jnp.int32, (16, 128), 1) < 64
    own_block = r.wj.at[c, place.a, place.b]
    own_block[:, 0:128] = r.j_rows[:, 0:128].astype(BF)
    own_block[:, 128:256] = jnp.where(low16, keys, pltpu.roll(values, 64, 1)).astype(BF)
    own_block[:, 256:384] = jnp.where(low16, pltpu.roll(keys, 64, 1), values).astype(BF)
    own_block[:, 384:512] = ((r.v_in[0] + r.v_in[1]) + (r.v_in[2] + r.v_in[3])).astype(BF)
    joint_all = spread_plane(wire, place, r.wj)
    arrive(rest_t)
    for k in range(4):
        r.w_rows[4 * k : 4 * k + 4, :] = r.w_in[k]
    r.wr[c, z, x] = r.w_rows[...].astype(BF)
    block = r.wr.at[c, z, x]
    rest_b = [wire.push(block, block, partner) for partner in place.row_x()]

    half = ROT // 2
    lane = lax.rem(lax.broadcasted_iota(jnp.int32, (1, 128), 1), 64)
    frequency = jnp.zeros((1, 128), F32)
    for i in range(half):
        frequency = jnp.where(lax.rem(lane, half) == i, 10000.0 ** (-2.0 * i / ROT), frequency)
    frequency = jnp.where(lane < ROT, frequency, 0.0)

    def angles(i, _):
        index = 512 * seq + 128 * i + lax.broadcasted_iota(jnp.int32, (128, 1), 0)
        begin = jnp.zeros((128, 1), jnp.int32)
        finish = 0
        for j in range(4):
            finish = finish + r.lengths[0, j]
            begin = jnp.where(index >= finish, finish, begin)
        angle = (index - begin).astype(F32) * frequency
        r.cos[i] = jnp.cos(angle)
        r.sin[i] = jnp.sin(angle)
        return 0

    lax.fori_loop(0, 4, angles, 0)
    for copy in load_m:
        copy.wait()
    arrive(joint_all)
    joint_swap = swap_cores(wire, place, r.wj)
    arrive(rest_b)
    c_rows = [wire.push(r.rows_c.at[t], r.rows_c.at[t], p) for p in place.row_t()]
    rest = Ring(wire, place, r.wr, z, lambda i: place.at(z=i))
    arrive(x_rows)
    joint_swap.wait_recv()
    for k in range(4):
        own_vec = jnp.zeros((16, 128), F32)
        for i in range(4):
            for part in (r.wj[0, k, i, :, 384:512], r.wj[1, i, k, :, 384:512]):
                own_vec = own_vec + part.astype(F32)
        r.v[k] = own_vec
    natural(r.wj, r.w_joint, 0, 384)

    gain, shift = vec_row(r.v, 0), vec_row(r.v, 1)
    q_bias, k_bias, v_bias = r.v[t, 2:3, :], r.v[t, 3:4, :], r.v[t, 4:5, :]
    low_row = lax.broadcasted_iota(jnp.int32, (1, 128), 1) < 64
    pair_bias = (
        jnp.where(low_row, k_bias, pltpu.roll(v_bias, 64, 1)),
        jnp.where(low_row, pltpu.roll(k_bias, 64, 1), v_bias),
    )
    low = lax.broadcasted_iota(jnp.int32, (256, 128), 1) < 64

    def project(i, _):
        blocks, rows = pl.ds(2 * i, 2), pl.ds(256 * i, 256)
        normal, _rate = normalise(r.rows_x[blocks].reshape(256, 512))
        part = (normal * gain + shift).astype(BF)
        r.normed[blocks] = part.reshape(2, 128, 512)
        raw = dot(part, r.w_joint[...].reshape(512, 384))
        cosine, sine = r.cos[blocks].reshape(256, 128), r.sin[blocks].reshape(256, 128)
        query = turn(raw[:, 0:128] + q_bias, cosine, sine, 1.0)
        r.q_turned[i] = query.T.astype(BF)
        key_cos = jnp.where(low, cosine, 1.0)
        key_sin = jnp.where(low, sine, 0.0)
        for h in range(2):
            pair = raw[:, 128 + 128 * h : 256 + 128 * h] + pair_bias[h]
            r.kv_buf[h, rows, :] = turn(pair, key_cos, key_sin, 1.0).astype(BF)
        return 0

    lax.fori_loop(0, 2, project, 0)
    for i in range(2):
        for h in range(2):
            r.q_buf[h, :, 256 * i : 256 * i + 256] = r.q_turned[i, 64 * h : 64 * h + 64, :]
    kv_cross = []
    for i in range(2):
        rows = pl.ds(256 * i, 256)
        kv_cross.append(
            wire.push(r.kv_buf.at[1 - head, rows], r.kv.at[seq, rows], place.at(x=cross))
        )
    q_cross = wire.push(r.q_buf.at[1 - head], r.q_heads.at[1], place.at(x=cross, c=1 - c))
    kv_mate = wire.push(r.kv_buf.at[head], r.kv.at[seq], place.at(x=mate))
    kv_core = wire.push(r.kv_buf.at[head], r.kv.at[seq], sibling)
    r.kv[seq] = r.kv_buf[head]
    r.q_heads[0] = r.q_buf[head]
    attend_start(r, place)
    query_prepare(r, 0)
    r.sums[...] = jnp.zeros_like(r.sums)
    r.back_turned[...] = jnp.zeros_like(r.back_turned)
    for k in range(4):
        lanes = slice(128 * k, 128 * k + 128)
        keys = r.m_joint_v[:, 512 + 128 * k : 640 + 128 * k]
        values = r.m_joint_v[:, 1024 + 128 * k : 1152 + 128 * k]
        start = 384 * k
        r.m_own[0, :, start : start + 128] = r.m_joint_v[:, lanes]
        r.m_own[0, :, start + 128 : start + 256] = jnp.concatenate(
            [keys[:, 0:64], values[:, 0:64]], axis=1
        )
        r.m_own[0, :, start + 256 : start + 384] = jnp.concatenate(
            [keys[:, 64:128], values[:, 64:128]], axis=1
        )
    r.m_own[0, :, 1536:2048] = jnp.zeros((4, 512), F32)
    r.m_own[1, :, 0:512] = r.m_output_v[...]
    r.m_own[1, :, 512:2048] = jnp.zeros((4, 1536), F32)
    r.m_own[2] = r.m_expand_v[...]
    r.m_own[3] = r.m_reduce_v[...]
    rest.hand_on()
    kv_core.wait_recv()
    keys_prepare(r, x)
    score_column(r, place, x, 0, diagonal=True)
    at_cross, at_mate = 2 * cross + c, 2 * mate + c
    at_far = 2 * (3 - mate) + c
    kv_far, kv_sent, far_sent = [], [], []
    for i in range(2):
        kv_cross[i].wait_recv()
        part = r.kv.at[at_cross, pl.ds(256 * i, 256)]
        kv_far.append(wire.push(part, part, place.at(x=mate)))
        kv_sent.append(wire.push(part, part, sibling))
    kv_mate.wait_recv()
    mate_sent = wire.push(r.kv.at[at_mate], r.kv.at[at_mate], sibling)
    rest.close()
    q_cross.wait_recv()
    query_prepare(r, 1)
    score_column(r, place, x, 1)
    mate_sent.wait_recv()
    keys_prepare(r, mate)
    score_column(r, place, mate, 0)
    score_column(r, place, mate, 1)
    arrive([*c_rows, *rest.swaps])
    by_row(r.wr, r.w_output, 0, 512)
    by_row(r.wr, r.w_expand, 512, 1024)
    by_row(r.wr, r.w_reduce, 1024, 1536)
    out_rows = r.w_output[pl.ds(8 * t, 8)].reshape(128, 512)
    grad = dot_cols(out_rows, r.rows_c[...].reshape(512, 512)).astype(BF)
    r.g_buf[0] = grad[0:64, :]
    r.g_buf[1] = grad[64:128, :]
    g_cross = wire.push(r.g_buf.at[1 - head], r.g_heads.at[1], place.at(x=cross, c=1 - c))
    r.g_heads[0] = r.g_buf[head]
    grad_prepare(r, 0)
    early = trade_t(wire, place, r.m_own, r.m_early)

    bias = jnp.concatenate([r.v[k, pl.ds(7 + t, 1), :] for k in range(4)], axis=1)

    def feed_forward(i, sums):
        blocks = pl.ds(2 * i, 2)
        part = r.normed[blocks].reshape(256, 512)
        wide = dot(part, r.w_expand[...].reshape(512, 512)) + bias
        square = wide * wide
        curve = jnp.tanh(0.7978845608 * (wide + 0.044715 * (square * wide)))
        r.hidden[blocks] = (0.5 * wide * (1.0 + curve)).astype(BF).reshape(2, 128, 512)
        slope = 0.5 * (1.0 + curve) + (0.5 * 0.7978845608) * wide * (1.0 - curve * curve) * (
            1.0 + (3 * 0.044715) * square
        )
        part = r.rows_c[blocks].reshape(256, 512)
        back = dot(part, r.w_reduce[...].reshape(512, 512))
        grad = (back * slope).astype(BF)
        r.pre[blocks] = grad.reshape(2, 128, 512)
        return sums + jnp.sum(grad.astype(F32), axis=0, keepdims=True)

    hidden_sum = lax.fori_loop(0, 2, feed_forward, jnp.zeros((1, 512), F32))
    for i in range(2):
        kv_far[i].wait_recv()
        part = r.kv.at[at_far, pl.ds(256 * i, 256)]
        far_sent.append(wire.push(part, part, sibling))
    for j in range(4):
        lanes = slice(128 * j, 128 * j + 128)
        expand_grad = dot_rows(
            r.normed[:, :, lanes].reshape(512, 128), r.pre[...].reshape(512, 512)
        )
        by_core(r.gf, j, expand_grad.astype(BF), 0, 512)
        reduce_grad = dot_rows(
            r.rows_c[:, :, lanes].reshape(512, 128), r.hidden[...].reshape(512, 512)
        )
        by_core(r.gf, j, reduce_grad.astype(BF), 512, 1024)
    gf_swap = sum_cores(wire, place, r.gf, r.gf_core)
    far = 3 - mate
    arrive(kv_sent)
    keys_prepare(r, cross)
    score_column(r, place, cross, 0)
    score_column(r, place, cross, 1, diagonal=True)
    arrive(far_sent)
    keys_prepare(r, far)
    score_column(r, place, far, 0)
    score_column(r, place, far, 1)
    gf_swap.wait_recv()
    for a in range(4):
        r.gf_chip[a] = (r.gf[c, a].astype(F32) + r.gf_core[a].astype(F32)).astype(BF)
    gf_z = []
    for k in range(1, 4):
        goal = ring(z, k)
        gf_z.append(wire.push(r.gf_chip.at[goal], r.gf_z.at[k - 1], place.at(z=goal)))
    weigh_values(r, place, 1)
    out_cross = wire.push(r.out_low.at[1], r.out_heads.at[head], place.at(x=cross, c=1 - c))
    weigh_values(r, place, 0)
    r.out_heads[head] = r.out_low[0]
    g_cross.wait_recv()
    grad_prepare(r, 1)
    for slot in range(2):
        r.centre[slot] = jnp.sum(
            r.out_turned[slot] * r.g_heads[slot].astype(F32), axis=0, keepdims=True
        )

    dk_swap = []

    def chip_sum(index):
        return r.dk[c, index].astype(F32) + r.dk_in[index].astype(F32)

    dk_sent = []

    def send_column(step, column):
        dk_swap[step].wait_recv()
        r.dk_chip[step] = chip_sum(column).astype(BF)
        dk_sent.append(
            wire.push(r.dk_chip.at[step], r.dk_got.at[step], place.at(x=column))
        )

    backward_cross(r, place)
    back_cross = wire.push(r.back_low.at[1], r.back_heads.at[head], place.at(x=cross, c=1 - c))
    out_cross.wait_recv()
    turned = r.out_heads[...].reshape(128, 512)
    r.pair_out[...] = turned
    out_grad = dot(turned, r.rows_c[...].reshape(512, 512)).astype(BF)
    for j in range(4):
        r.out_cols[j] = out_grad[:, 128 * j : 128 * j + 128]
    out_cols = trade_t(wire, place, r.out_cols, r.out_in)
    r.out_in[t] = r.out_cols[t]
    columns = (far, cross, mate, x)
    for step, column in enumerate(columns):
        backward_column(r, place, column, diagonal=step == 3)
        dk_swap.append(wire.push(r.dk.at[1 - c, column], r.dk_in.at[column], sibling))
        if step > 0:
            send_column(step - 1, columns[step - 1])
    r.back_low[0] = (r.back_turned[...] * (HD ** -0.5)).astype(BF)
    r.back_heads[head] = r.back_low[0]
    arrive(gf_z)
    r.gf_line[...] = total(r.gf_chip[z], r.gf_z).astype(BF)
    gf_x = []
    for k in range(1, 4):
        goal = ring(x, k)
        gf_x.append(wire.push(r.gf_line.at[goal], r.gf_x.at[k - 1], place.at(x=goal)))
    arrive(out_cols)
    for j in range(4):
        by_owner(r.go, j, r.out_in[j], 0, 128)
    go_swap = sum_cores(wire, place, r.go, r.go_core)

    def feed_out(i, _):
        blocks = pl.ds(2 * i, 2)
        part = r.hidden[blocks].reshape(256, 512)
        r.feed[blocks] = dot_cols(part, r.w_reduce[...].reshape(512, 512)).reshape(2, 128, 512)
        part = r.pre[blocks].reshape(256, 512)
        r.row_grad[blocks] = dot_cols(part, r.w_expand[...].reshape(512, 512)).reshape(2, 128, 512)
        return 0

    lax.fori_loop(0, 2, feed_out, 0)
    go_swap.wait_recv()
    for a in range(4):
        r.go_chip[a] = (r.go[c, a].astype(F32) + r.go_core[a].astype(F32)).astype(BF)
    go_all = scatter_plane(wire, place, r.go_chip, r.go_in)
    out_rows = r.w_output[pl.ds(8 * t, 8)].reshape(128, 512)
    for i in range(2):
        blocks, lanes = slice(2 * i, 2 * i + 2), slice(256 * i, 256 * i + 256)
        part = r.feed[blocks].reshape(256, 512) + dot_rows(r.pair_out[:, lanes], out_rows)
        r.out_part[blocks] = part.astype(BF).reshape(2, 128, 512)
    out_parts = trade_t(wire, place, r.out_part, r.out_got)
    r.out_got[t] = r.out_part[t]
    back_cross.wait_recv()
    back = r.back_heads[...].reshape(128, 512).astype(F32).T
    cosine, sine = r.cos[...].reshape(512, 128), r.sin[...].reshape(512, 128)
    r.joint_out[:, 0:128] = turn(back, cosine, sine, -1.0).astype(BF)
    low = lax.broadcasted_iota(jnp.int32, (128, 128), 1) < 64
    arrive([dk_swap[3], *dk_sent])
    r.dkv[head] = (chip_sum(x) + r.dk_got[2].astype(F32)).astype(BF)
    r.dkv[1 - head] = (r.dk_got[0].astype(F32) + r.dk_got[1].astype(F32)).astype(BF)
    for h in range(2):
        for i in range(4):
            rows = pl.ds(128 * i, 128)
            key_cos = jnp.where(low, r.cos[i], 1.0)
            key_sin = jnp.where(low, r.sin[i], 0.0)
            r.joint_out[rows, 128 + 128 * h : 256 + 128 * h] = turn(
                r.dkv[h, rows, :].astype(F32), key_cos, key_sin, -1.0
            ).astype(BF)
    for j in range(4):
        part = r.normed[:, :, 128 * j : 128 * j + 128].reshape(512, 128)
        by_owner(r.gj, j, dot_rows(part, r.joint_out[...]).astype(BF), 0, 384)
    gj_swap = sum_cores(wire, place, r.gj, r.gj_core)

    r.vp[0] = jnp.zeros((4, 16, 128), F32)
    shift_sum = jnp.zeros((1, 512), F32)
    gain_sum = jnp.zeros((1, 512), F32)
    for i in range(4):
        rows = pl.ds(128 * i, 128)
        part = r.row_grad[i] + dot_cols(r.joint_out[rows, :], r.w_joint[...].reshape(512, 384))
        r.back_part[i] = part.astype(BF)
        normal, _rate = normalise(r.rows_x[i])
        shift_sum = shift_sum + jnp.sum(part, axis=0, keepdims=True)
        gain_sum = gain_sum + jnp.sum(part * normal, axis=0, keepdims=True)
    gj_swap.wait_recv()
    for a in range(4):
        r.gj_chip[a] = (r.gj[c, a].astype(F32) + r.gj_core[a].astype(F32)).astype(BF)
    gj_all = scatter_plane(wire, place, r.gj_chip, r.gj_in)
    back_parts = trade_t(wire, place, r.back_part, r.back_got)
    r.back_got[t] = r.back_part[t]
    out_sum = jnp.sum(r.rows_c[t].astype(F32), axis=0, keepdims=True)
    joint_sum = jnp.sum(r.joint_out[...].astype(F32), axis=0, keepdims=True)
    one, two = joint_sum[:, 128:256], joint_sum[:, 256:384]
    for k in range(4):
        lanes = slice(128 * k, 128 * k + 128)
        r.vp[0, k, 0:1, :] = gain_sum[:, lanes]
        r.vp[0, k, 1:2, :] = shift_sum[:, lanes]
        r.vp[0, k, 5:6, :] = out_sum[:, lanes]
        r.vp[0, k, 6:7, :] = out_sum[:, lanes]
        r.vp[0, k, pl.ds(7 + t, 1), :] = hidden_sum[:, lanes]
    r.vp[0, t, 2:3, :] = joint_sum[:, 0:128]
    r.vp[0, t, 3:4, :] = jnp.where(low_row, one, pltpu.roll(two, 64, 1))
    r.vp[0, t, 4:5, :] = jnp.where(low_row, pltpu.roll(one, 64, 1), two)
    vp_swap = wire.push(r.vp.at[0], r.vp_core, sibling)
    arrive(gf_x)
    gf_own = total(r.gf_line[x], r.gf_x)
    arrive(go_all)
    go_own = add_plane(r.go_chip[place.a, place.b], r.go_in)
    for k in range(4):
        r.early_out[k, :, 0:1024] = gf_own[4 * k : 4 * k + 4, :]
        r.early_out[k, :, 1024:1152] = go_own[4 * k : 4 * k + 4, :]
    r.gm_out[1, :, 0:128] = go_own.astype(BF)
    r.gm_out[2] = gf_own[:, 0:512].astype(BF)
    r.gm_out[3] = gf_own[:, 512:1024].astype(BF)
    gm_first = wire.block(4)
    gm_widths = (384, 128, 512, 512)

    def to_newton(w, sender):
        lanes = slice(0, gm_widths[w])
        return wire.offer(
            gm_first, r.gm_out.at[w, :, lanes], r.gm_in.at[sender, :, lanes], sender, w,
            place.at(t=w),
        )

    def send_newton(w):
        @pl.when(t != w)
        def _():
            to_newton(w, t).start()

        @pl.when(t == w)
        def _():
            r.gm_in[w, :, 0 : gm_widths[w]] = r.gm_out[w, :, 0 : gm_widths[w]]

    for w in (1, 2, 3):
        send_newton(w)
    early_t = trade_t(wire, place, r.early_out, r.early_in)
    r.early_in[t] = r.early_out[t]

    arrive(early)
    r.m_early[t] = r.m_own[t]
    for k in range(4):
        r.m_old[4 * k : 4 * k + 4, :] = r.m_early[k]
    vp_swap.wait_recv()
    r.vp[1] = r.vp[0] + r.vp_core[...]
    vp_z = [wire.push(r.vp.at[1], r.vp_z.at[k], p) for k, p in enumerate(place.row_z())]

    arrive(gj_all)
    gj_own = add_plane(r.gj_chip[place.a, place.b], r.gj_in)
    r.gm_out[0, :, 0:384] = gj_own.astype(BF)
    send_newton(0)
    for k in range(4):
        r.late_out[k] = gj_own[4 * k : 4 * k + 4, :]
    late_t = trade_t(wire, place, r.late_out, r.late_in)
    r.late_in[t] = r.late_out[t]
    arrive(vp_z)
    r.vp[2] = total(r.vp[1], r.vp_z)
    vp_x = [wire.push(r.vp.at[2], r.vp_x.at[k], p) for k, p in enumerate(place.row_x())]

    for w in range(4):

        @pl.when(t == w)
        def _(w=w):
            width = gm_widths[w]
            for sender in range(4):
                if sender != w:
                    to_newton(w, sender).wait_recv()
            for k in range(4):
                lanes = slice(width * k, width * k + width)
                value = muon_beta * r.m_old[:, lanes] + r.gm_in[k, :, 0:width].astype(F32)
                if width * k < 1536:
                    r.momentum[c, place.a, place.b, :, lanes] = value.astype(BF)
                else:
                    r.extra[c, place.a, place.b] = value.astype(BF)
            if w == 1:
                r.momentum[c, place.a, place.b, :, 512:1536] = jnp.zeros((16, 1024), BF)

    m_b = spread_b(wire, place, r.momentum)

    extra_first = wire.block(7)

    def extra_line():
        block = r.extra.at[c, place.a, place.b]
        return [
            wire.offer(extra_first, block, block, k, k, place.at_b(ring(place.b, k)))
            for k in range(1, 4)
        ]

    def extra_lines():
        block = r.extra.at[c, place.a]
        return [
            wire.offer(extra_first, block, block, 3 + k, 3 + k, place.at_a(ring(place.a, k)))
            for k in range(1, 4)
        ]

    def extra_swap():
        block = r.extra.at[c]
        return wire.offer(extra_first, block, block, 0, 0, sibling)

    @pl.when(t >= 2)
    def _():
        for copy in extra_line():
            copy.start()

    arrive(m_b)
    whole = Ring(wire, place, r.momentum, place.a, place.at_a)

    @pl.when(t >= 2)
    def _():
        for copy in extra_line():
            copy.wait_recv()
        for copy in extra_lines():
            copy.start()

    arrive(early_t)
    for k in range(4):
        part = r.early_in[k]
        r.g_expand[:, 512 * k : 512 * k + 512] = part[:, 0:512]
        r.g_reduce[:, 512 * k : 512 * k + 512] = part[:, 512:1024]
        r.g_output[:, 128 * k : 128 * k + 128] = part[:, 1024:1152]
    arrive(late_t)
    for k in range(4):
        unpair(r.g_joint, r.late_in[k], k)
    for old, grad, new in (
        (r.m_joint_v, r.g_joint, r.n_joint),
        (r.m_output_v, r.g_output, r.n_output),
        (r.m_expand_v, r.g_expand, r.n_expand),
        (r.m_reduce_v, r.g_reduce, r.n_reduce),
    ):
        new[...] = muon_beta * old[...] + grad[...]
    arrive(vp_x)
    r.vp[3] = total(r.vp[2], r.vp_x)
    vp_t = [wire.push(r.vp.at[3], r.vp_t.at[k], p) for k, p in enumerate(place.row_t())]
    arrive(out_parts)
    arrive(back_parts)
    wide = r.rows_x[t].astype(F32)
    feed = r.out_got[0].astype(F32)
    back = r.back_got[0].astype(F32)
    for k in range(1, 4):
        feed = feed + r.out_got[k].astype(F32)
        back = back + r.back_got[k].astype(F32)
    r.block_output[...] = (wide + feed + vec_row(r.v, 5) + vec_row(r.v, 6)).astype(BF)
    normal, rate = normalise(r.rows_x[t])
    scaled = back * gain
    mean_one = jnp.mean(scaled, axis=-1, keepdims=True)
    mean_two = jnp.mean(scaled * normal, axis=-1, keepdims=True)
    r.input_grad[...] = r.rows_c[t].astype(F32) + rate * (scaled - mean_one - normal * mean_two)
    whole.hand_on()

    @pl.when(t >= 2)
    def _():
        for copy in extra_lines():
            copy.wait_recv()
        extra_swap().start()

    whole.close()
    arrive(vp_t)
    r.vec_sum[...] = total(r.vp[3], r.vp_t)
    r.table[0:16, :] = r.vec_sum[z]
    r.table[...] = r.table[...].T
    vector_grad = r.table[pl.ds(pl.multiple_of(16 * seq + 4 * t, 4), 4), 0:11]
    r.vector_grad[...] = vector_grad
    first_next = beta_first * r.first_v[...] + (1.0 - beta_first) * vector_grad
    second_next = (
        beta_second * r.second_v[...] + (1.0 - beta_second) * vector_grad * vector_grad
    )
    r.second_next[...] = second_next
    first_hat = first_next / (1.0 - beta_first**STEP)
    second_hat = second_next / (1.0 - beta_second**STEP)
    r.vector_next[...] = r.vectors_v[...] - vector_rate * first_hat / (
        jnp.sqrt(second_hat) + adam_epsilon
    )
    @pl.when(t >= 2)
    def _():
        extra_swap().wait_recv()
        columns = r.extra[...].reshape(512, 512)
        r.gram[...] = dot_cols(columns, columns)

    @pl.when(t < 2)
    def _():
        r.gram[...] = jnp.zeros((512, 512), F32)

    arrive(whole.swaps)

    high, small = newton(r, place)
    both = jnp.concatenate([high, small], axis=0)
    for k in range(3):
        lanes = slice(512 * k, 512 * k + 512)
        rows = dot(both, r.momentum[:, :, :, :, lanes].reshape(512, 512))
        r.m_rows[:, lanes] = rows[0:16] + rows[16:32]

    @pl.when(t >= 2)
    def _():
        rows = dot(both, r.extra[...].reshape(512, 512))
        r.m_rows[:, 1536:2048] = rows[0:16] + rows[16:32]

    @pl.when(t < 2)
    def _():
        r.m_rows[:, 1536:2048] = jnp.zeros((16, 512), F32)

    for k in range(4):
        for p in range(4):
            r.u_rows[k, 4 * p : 4 * p + 4, :] = r.m_rows[
                4 * k : 4 * k + 4, 512 * p : 512 * p + 512
            ]
    r.u_out[...] = r.u_rows[...].astype(BF)
    u_t = trade_t(wire, place, r.u_out, r.u_in)
    r.u_in[t] = r.u_out[t]
    wire.drain()
    for w in range(4):

        @pl.when(t != w)
        def _(w=w):
            to_newton(w, t).wait_send()

    @pl.when(t >= 2)
    def _():
        for copy in extra_line() + extra_lines():
            copy.wait_send()
        extra_swap().wait_send()

    arrive(u_t)
    r.u_rows[...] = r.u_in[...].astype(F32)
    for k in range(4):
        for p in range(4):
            r.u_wide[k, :, 512 * p : 512 * p + 512] = r.u_rows[k, 4 * p : 4 * p + 4, :]
    for k in range(4):
        unpair(r.u_joint, r.u_wide[0, :, 384 * k : 384 * k + 384], k)
    for k, (old, change, new) in enumerate(
        (
            (r.joint_v, r.u_joint, r.u_joint),
            (r.output_v, r.u_wide.at[1, :, pl.ds(0, 512)], r.u_output),
            (r.expand_v, r.u_wide.at[2], r.u_expand),
            (r.reduce_v, r.u_wide.at[3], r.u_reduce),
        )
    ):
        factor = muon_rate * 0.2 * math.sqrt(max(D, WIDTHS[k]))
        new[...] = old[...] * (1.0 - muon_rate * muon_decay) - factor * change[...]
    wire.drain()


def block_stage(*arrays):
    return pl.pallas_call(
        block_kernel,
        out_shape=tuple(shape(dims, dtype) for _, dims, dtype in OUTPUTS),
        in_specs=[SMEM] + [ANY] * (len(INPUTS) - 1),
        out_specs=(VMEM,) * len(OUTPUTS),
        scratch_shapes=[pltpu.VMEM(dims, dtype) for _, dims, dtype in SCRATCH]
        + [
            pltpu.SemaphoreType.DMA((PUSHES,)),
            pltpu.SemaphoreType.DMA((PUSHES,)),
            pltpu.SemaphoreType.DMA((LOADS,)),
        ],
        compiler_params=pltpu.CompilerParams(
            collective_id=1, has_side_effects=True, vmem_limit_bytes=56 << 20
        ),
        name="block",
    )(*arrays)


def write_kernel(*refs):
    count = len(OUTPUTS)
    sem = refs[-1]
    copies = []
    for k in range(count):
        copy = pltpu.make_async_copy(refs[k], refs[count + k], sem.at[k])
        copy.start()
        copies.append(copy)
    for copy in copies:
        copy.wait()


def write_stage(*arrays):
    count = len(arrays)
    return pl.pallas_call(
        write_kernel,
        out_shape=tuple(shape(a.shape, a.dtype) for a in arrays),
        in_specs=[VMEM] * count,
        out_specs=(ANY,) * count,
        scratch_shapes=[pltpu.SemaphoreType.DMA((count,))],
        name="write",
    )(*arrays)


def shards(
    block_input,
    cotangent,
    doc_lengths,
    joint_weight,
    output_weight,
    expand_weight,
    reduce_weight,
    joint_moment,
    output_moment,
    expand_moment,
    reduce_moment,
    vectors,
    first_moment,
    second_moment,
):
    results = block_stage(
        doc_lengths, block_input, cotangent, joint_weight, output_weight, expand_weight,
        reduce_weight, vectors.T, joint_moment, output_moment, expand_moment, reduce_moment,
        first_moment.T, second_moment.T,
    )
    results = write_stage(*results)
    return (*results[12:14], *results[0:12], *[part.T for part in results[14:]])


def solution(mesh):
    rows = P(("fsdp", "seq", "tensor"), None)
    columns = P(None, ("fsdp", "seq", "tensor"))
    return jax.shard_map(
        shards,
        mesh=mesh,
        in_specs=(rows, rows, P("fsdp", None)) + (rows,) * 8 + (columns,) * 3,
        out_specs=(rows,) * 14 + (columns,) * 3,
        check_vma=False,
    )
```

```python
import functools
import math

import jax
import jax.numpy as jnp
from jax import lax
from jax.experimental import pallas as pl
from jax.experimental.pallas import tpu as pltpu
from jax.sharding import PartitionSpec as P

D = 512
HEADS = 8
FF = 2048
ROT = 16
HD = 64
STEP = 10

norm_epsilon = 1e-05
masked_score = -1e30
newton_first = 3.4445
newton_second = -4.775
newton_third = 2.0315
beta_first = 0.9
beta_second = 0.95
adam_epsilon = 1e-08
vector_rate = 0.2
muon_rate = 0.25
muon_beta = 0.95
muon_decay = 0.01
LOG2_E = 1.4426950408889634

BF = jnp.bfloat16
F32 = jnp.float32
MESH = pl.DeviceIdType.MESH
VMEM = pl.BlockSpec(memory_space=pltpu.VMEM)
SMEM = pl.BlockSpec(memory_space=pltpu.SMEM)
ANY = pl.BlockSpec(memory_space=pl.ANY)
WIDTHS = (3 * D, D, FF, FF)


def shape(dims, dtype):
    return jax.ShapeDtypeStruct(dims, dtype)


class Place:
    def __init__(self):
        self.z = lax.axis_index("fsdp")
        self.seq = lax.axis_index("seq")
        self.t = lax.axis_index("tensor")
        self.x = lax.div(self.seq, 2)
        self.c = lax.rem(self.seq, 2)
        self.d = 1 - 2 * self.c
        self.a = self.c * self.x + (1 - self.c) * self.z
        self.b = self.c * self.z + (1 - self.c) * self.x
        self.mate = self.x + 1 - 2 * lax.rem(self.x, 2)
        self.cross = 3 - self.x
        self.head = lax.div(self.x, 2)

    def at(self, z=None, x=None, c=None, t=None):
        z = self.z if z is None else z
        x = self.x if x is None else x
        c = self.c if c is None else c
        t = self.t if t is None else t
        return (z, 2 * x + c, t)

    def at_a(self, a):
        c = self.c
        return self.at(z=(1 - c) * a + c * self.z, x=c * a + (1 - c) * self.x)

    def at_b(self, b):
        c = self.c
        return self.at(z=c * b + (1 - c) * self.z, x=(1 - c) * b + c * self.x)

    def at_ab(self, a, b):
        c = self.c
        return self.at(z=(1 - c) * a + c * b, x=c * a + (1 - c) * b)

    def plane(self):
        steps = [(i, j) for i in range(4) for j in range(4) if i + j > 0]
        steps.sort(key=lambda step: -min(step[0], 4 - step[0]) - min(step[1], 4 - step[1]))
        return [(ring(self.a, i), ring(self.b, j)) for i, j in steps]

    def sibling(self):
        return self.at(c=1 - self.c)

    def octet(self):
        g = 4 * self.c + self.t
        members = [lax.rem(g + k, 8) for k in range(1, 8)]
        return [self.at(c=lax.div(m, 4), t=lax.rem(m, 4)) for m in members]

    def row_x(self):
        return [self.at(x=lax.rem(self.x + k, 4)) for k in range(1, 4)]

    def row_z(self):
        return [self.at(z=lax.rem(self.z + k, 4)) for k in range(1, 4)]

    def row_t(self):
        return [self.at(t=lax.rem(self.t + k, 4)) for k in range(1, 4)]


def ring(index, step):
    return lax.rem(index + step + 4, 4)


def greet(partners):
    barrier = pltpu.get_barrier_semaphore()
    for partner in partners:
        pl.semaphore_signal(barrier, inc=1, device_id=partner, device_id_type=MESH)
    return lambda: pl.semaphore_wait(barrier, len(partners))


class Wire:
    def __init__(self, send, recv, local):
        self.send = send
        self.recv = recv
        self.local = local
        self.count = 0
        self.loads = 0
        self.open = []

    def push(self, src, dst, device):
        index = self.count
        self.count += 1
        copy = pltpu.make_async_remote_copy(
            src_ref=src,
            dst_ref=dst,
            send_sem=self.send.at[index],
            recv_sem=self.recv.at[index],
            device_id=device,
            device_id_type=MESH,
        )
        copy.start()
        self.open.append(copy)
        return copy

    def offer(self, first, source, target, sender, goal, device):
        return pltpu.make_async_remote_copy(
            src_ref=source,
            dst_ref=target,
            send_sem=self.send.at[first + goal],
            recv_sem=self.recv.at[first + sender],
            device_id=device,
            device_id_type=MESH,
        )

    def block(self, count):
        first = self.count
        self.count += count
        return first

    def load(self, src, dst):
        copy = pltpu.make_async_copy(src, dst, self.local.at[self.loads])
        self.loads += 1
        copy.start()
        return copy

    def drain(self):
        for copy in self.open:
            copy.wait_send()
        self.open = []


def arrive(copies):
    for copy in copies:
        copy.wait_recv()


def dot(left, right):
    return jnp.dot(left, right, preferred_element_type=F32)


def dot_cols(left, right):
    return lax.dot_general(left, right, (((1,), (1,)), ((), ())), preferred_element_type=F32)


def dot_rows(left, right):
    return lax.dot_general(left, right, (((0,), (0,)), ((), ())), preferred_element_type=F32)


def turn(values, cosine, sine, sign):
    lane = lax.rem(lax.broadcasted_iota(jnp.int32, values.shape, 1), 64)
    crossed = jnp.where(lane < 8, -pltpu.roll(values, 120, 1), pltpu.roll(values, 8, 1))
    return values * cosine + crossed * (sine * sign)


def vec_row(v_ref, row):
    return jnp.concatenate([v_ref[k, row : row + 1, :] for k in range(4)], axis=1)


def normalise(rows):
    wide = rows.astype(F32)
    centred = wide - jnp.mean(wide, axis=-1, keepdims=True)
    variance = jnp.mean(centred * centred, axis=-1, keepdims=True)
    rate = lax.rsqrt(variance + norm_epsilon)
    return centred * rate, rate


def halves(values):
    high = values.astype(BF)
    return high, (values - high.astype(F32)).astype(BF)


def product(left_h, left_l, right_h, right_l):
    return dot(left_h, right_h) + (dot(left_h, right_l) + dot(left_l, right_h))


def squared(high, small):
    cross = dot(high, small)
    return dot(high, high) + (cross + cross.T)


def spread_b(wire, place, ref):
    block = ref.at[place.c, place.a, place.b]
    return [wire.push(block, block, place.at_b(ring(place.b, k))) for k in range(1, 4)]


class Ring:
    def __init__(self, wire, place, ref, index, at):
        self.wire = wire
        self.place = place
        self.ref = ref
        self.index = index
        self.at = at
        self.ups, self.downs = {}, {}
        for p, q in ((0, 2), (1, 3), (2, 0), (3, 1)):
            self.ups[p] = self.send(0, p, 1)
            self.downs[q] = self.send(0, q, -1)
        self.swaps = [self.swap(0)]

    def send(self, step, part, way):
        block = self.ref.at[self.place.c, ring(self.index, step), part]
        return self.wire.push(block, block, self.at(ring(self.index, way)))

    def swap(self, step):
        block = self.ref.at[self.place.c, ring(self.index, step)]
        return self.wire.push(block, block, self.place.sibling())

    def hand_on(self):
        self.more = []
        for p, q in ((0, 2), (1, 3)):
            self.ups[p].wait_recv()
            self.more.append(self.send(-1, p, 1))
            self.downs[q].wait_recv()
            self.more.append(self.send(1, q, -1))

    def close(self):
        arrive([self.ups[2], self.ups[3]])
        self.swaps.append(self.swap(-1))
        arrive([self.downs[0], self.downs[1]])
        self.swaps.append(self.swap(1))
        arrive(self.more)
        self.swaps.append(self.swap(2))


def spread_plane(wire, place, ref):
    block = ref.at[place.c, place.a, place.b]
    return [wire.push(block, block, place.at_ab(a, b)) for a, b in place.plane()]


def scatter_plane(wire, place, ref, target):
    copies = []
    for k, (a, b) in enumerate(place.plane()):
        copies.append(wire.push(ref.at[a, b], target.at[k], place.at_ab(a, b)))
    return copies


def add_plane(first, parts):
    value = first.astype(F32)
    for k in range(15):
        value = value + parts[k].astype(F32)
    return value


def swap_cores(wire, place, ref):
    return wire.push(ref.at[place.c], ref.at[place.c], place.sibling())


def natural(source, target, start, stop):
    for z in range(4):
        for x in range(4):
            target[8 * z + 2 * x] = source[0, z, x, :, start:stop]
            target[8 * z + 2 * x + 1] = source[1, x, z, :, start:stop]


def by_row(source, target, start, stop):
    for z in range(4):
        for x in range(4):
            for c in range(2):
                target[8 * z + 2 * x + c] = source[c, z, x, :, start:stop]


def by_owner(target, z, rows, start, stop):
    for x in range(4):
        target[0, z, x, :, start:stop] = rows[32 * x : 32 * x + 16, :]
        target[1, x, z, :, start:stop] = rows[32 * x + 16 : 32 * x + 32, :]


def by_core(target, z, rows, start, stop):
    for x in range(4):
        for c in range(2):
            block = rows[32 * x + 16 * c : 32 * x + 16 * c + 16, :]
            target[c, z, x, :, start:stop] = block


def sum_cores(wire, place, ref, target):
    return wire.push(ref.at[1 - place.c], target, place.sibling())


def trade_t(wire, place, source, target):
    copies = []
    for k in range(1, 4):
        goal = ring(place.t, k)
        copies.append(wire.push(source.at[goal], target.at[place.t], place.at(t=goal)))
    return copies


def total(first, parts):
    value = first.astype(F32)
    for k in range(3):
        value = value + parts[k].astype(F32)
    return value


def unpair(target, part, k):
    one, two = part[:, 128:256], part[:, 256:384]
    target[:, 128 * k : 128 * k + 128] = part[:, 0:128]
    target[:, 512 + 128 * k : 640 + 128 * k] = jnp.concatenate(
        [one[:, 0:64], two[:, 0:64]], axis=1
    )
    target[:, 1024 + 128 * k : 1152 + 128 * k] = jnp.concatenate(
        [one[:, 64:128], two[:, 64:128]], axis=1
    )


INPUTS = (
    "lengths",
    "x",
    "c",
    "joint",
    "output",
    "expand",
    "reduce",
    "vectors",
    "m_joint",
    "m_output",
    "m_expand",
    "m_reduce",
    "first",
    "second",
)

OUTPUTS = (
    ("g_joint", (4, 1536), F32),
    ("g_output", (4, 512), F32),
    ("g_expand", (4, 2048), F32),
    ("g_reduce", (4, 2048), F32),
    ("n_joint", (4, 1536), F32),
    ("n_output", (4, 512), F32),
    ("n_expand", (4, 2048), F32),
    ("n_reduce", (4, 2048), F32),
    ("u_joint", (4, 1536), F32),
    ("u_output", (4, 512), F32),
    ("u_expand", (4, 2048), F32),
    ("u_reduce", (4, 2048), F32),
    ("block_output", (128, 512), BF),
    ("input_grad", (128, 512), F32),
    ("vector_grad", (4, 11), F32),
    ("second_next", (4, 11), F32),
    ("vector_next", (4, 11), F32),
)

SCRATCH = (
    ("joint_v", (4, 1536), F32),
    ("output_v", (4, 512), F32),
    ("expand_v", (4, 2048), F32),
    ("reduce_v", (4, 2048), F32),
    ("vectors_v", (4, 11), F32),
    ("first_v", (4, 11), F32),
    ("second_v", (4, 11), F32),
    ("table", (128, 128), F32),
    ("vec_sum", (4, 16, 128), F32),
    ("m_joint_v", (4, 1536), F32),
    ("m_output_v", (4, 512), F32),
    ("m_expand_v", (4, 2048), F32),
    ("m_reduce_v", (4, 2048), F32),
    ("j_out", (4, 4, 384), F32),
    ("j_in", (4, 4, 384), F32),
    ("j_rows", (16, 384), F32),
    ("w_out", (4, 4, 1536), F32),
    ("w_in", (4, 4, 1536), F32),
    ("w_rows", (16, 1536), F32),
    ("wj", (2, 4, 4, 16, 512), BF),
    ("wr", (2, 4, 4, 16, 1536), BF),
    ("w_joint", (32, 16, 384), BF),
    ("w_output", (32, 16, 512), BF),
    ("w_expand", (32, 16, 512), BF),
    ("w_reduce", (32, 16, 512), BF),
    ("v_own", (16, 128), F32),
    ("m_own", (4, 4, 2048), F32),
    ("m_early", (4, 4, 2048), F32),
    ("m_old", (16, 2048), F32),
    ("v_in", (4, 16, 128), F32),
    ("v", (4, 16, 128), F32),
    ("rows_x", (4, 128, 512), BF),
    ("rows_c", (4, 128, 512), BF),
    ("cos", (4, 128, 128), F32),
    ("sin", (4, 128, 128), F32),
    ("normed", (4, 128, 512), BF),
    ("q_turned", (2, 128, 256), BF),
    ("q_buf", (2, 64, 512), BF),
    ("q_heads", (2, 64, 512), BF),
    ("g_buf", (2, 64, 512), BF),
    ("g_heads", (2, 64, 512), BF),
    ("kv_buf", (2, 512, 128), BF),
    ("kv", (8, 512, 128), BF),
    ("hidden", (4, 128, 512), BF),
    ("pre", (4, 128, 512), BF),
    ("feed", (4, 128, 512), F32),
    ("row_grad", (4, 128, 512), F32),
    ("gf", (2, 4, 4, 16, 1024), BF),
    ("gf_core", (4, 4, 16, 1024), BF),
    ("gf_chip", (4, 4, 16, 1024), BF),
    ("gf_z", (3, 4, 16, 1024), BF),
    ("gf_line", (4, 16, 1024), BF),
    ("gf_x", (3, 16, 1024), BF),
    ("go", (2, 4, 4, 16, 128), BF),
    ("go_core", (4, 4, 16, 128), BF),
    ("go_chip", (4, 4, 16, 128), BF),
    ("go_in", (15, 16, 128), BF),
    ("early_out", (4, 4, 1152), F32),
    ("early_in", (4, 4, 1152), F32),
    ("turned", (8, 128, 512), BF),
    ("keys", (8, 512, 128), BF),
    ("scores", (9, 512, 512), F32),
    ("sums", (8, 512, 128), F32),
    ("query_low", (2, 512, 128), BF),
    ("query_two", (2, 512, 128), BF),
    ("begin", (2, 1, 512), jnp.int32),
    ("top", (2, 1, 512), F32),
    ("total_sum", (2, 1, 512), F32),
    ("out_turned", (2, 64, 512), F32),
    ("grad_low", (2, 512, 128), BF),
    ("back_turned", (64, 512), F32),
    ("centre", (2, 1, 512), F32),
    ("out_low", (2, 64, 512), BF),
    ("out_heads", (2, 64, 512), BF),
    ("back_low", (2, 64, 512), BF),
    ("back_heads", (2, 64, 512), BF),
    ("dk", (2, 4, 512, 128), BF),
    ("dk_in", (4, 512, 128), BF),
    ("dk_chip", (4, 512, 128), BF),
    ("dk_got", (3, 512, 128), BF),
    ("dkv", (2, 512, 128), BF),
    ("pair_out", (128, 512), BF),
    ("joint_out", (512, 384), BF),
    ("out_cols", (4, 128, 128), BF),
    ("out_in", (4, 128, 128), BF),
    ("out_part", (4, 128, 512), BF),
    ("out_got", (4, 128, 512), BF),
    ("back_part", (4, 128, 512), BF),
    ("back_got", (4, 128, 512), BF),
    ("gj", (2, 4, 4, 16, 384), BF),
    ("gj_core", (4, 4, 16, 384), BF),
    ("gj_chip", (4, 4, 16, 384), BF),
    ("gj_in", (15, 16, 384), BF),
    ("late_out", (4, 4, 384), F32),
    ("late_in", (4, 4, 384), F32),
    ("vp", (4, 4, 16, 128), F32),
    ("vp_core", (4, 16, 128), F32),
    ("vp_z", (3, 4, 16, 128), F32),
    ("vp_x", (3, 4, 16, 128), F32),
    ("vp_t", (3, 4, 16, 128), F32),
    ("gm_out", (4, 16, 512), BF),
    ("gm_in", (4, 16, 512), BF),
    ("m_rows", (16, 2048), F32),
    ("momentum", (2, 4, 4, 16, 1536), BF),
    ("extra", (2, 4, 4, 16, 512), BF),
    ("gram", (512, 512), F32),
    ("gram_h", (512, 512), BF),
    ("gram_l", (512, 512), BF),
    ("poly_h", (512, 512), BF),
    ("poly_l", (512, 512), BF),
    ("temp_h", (512, 512), BF),
    ("temp_l", (512, 512), BF),
    ("own", (16, 512), F32),
    ("u_rows", (4, 16, 512), F32),
    ("u_out", (4, 16, 512), BF),
    ("u_in", (4, 16, 512), BF),
    ("u_wide", (4, 4, 2048), F32),
)

PUSHES = 240
LOADS = 16


class Box:
    pass


def attend_chunk(place, slot):
    return place.seq if slot == 0 else 7 - place.seq


def attend_score(slot, k):
    return 8 - k if slot == 0 else k


def pairs(count, step, carry):
    def two(k, carry):
        return step(2 * k + 1, step(2 * k, carry))

    def one(_, carry):
        return step(count - 1, carry)

    carry = lax.fori_loop(0, lax.div(count, 2), two, carry)
    return lax.fori_loop(0, lax.rem(count, 2), one, carry)


def attend_start(r, place):
    for slot in range(2):
        index = 512 * attend_chunk(place, slot) + lax.broadcasted_iota(jnp.int32, (1, 512), 1)
        begin = jnp.zeros((1, 512), jnp.int32)
        finish = 0
        for j in range(4):
            finish = finish + r.lengths[0, j]
            begin = jnp.where(index >= finish, finish, begin)
        r.begin[slot] = begin
        r.top[slot] = jnp.full((1, 512), masked_score, F32)
        r.total_sum[slot] = jnp.zeros((1, 512), F32)


def query_prepare(r, slot):
    wide = r.q_heads[slot].astype(F32)
    high, small = halves(wide * (HD ** -0.5 * LOG2_E))
    r.query_two[slot] = jnp.concatenate([high, small], axis=0).T
    low = (wide * (HD ** -0.5)).astype(BF)
    r.query_low[slot] = jnp.concatenate([low, jnp.zeros((64, 512), BF)], axis=0).T


def grad_prepare(r, slot):
    r.grad_low[slot] = jnp.concatenate([jnp.zeros((64, 512), BF), r.g_heads[slot]], axis=0).T


def keys_prepare(r, column):
    low = lax.broadcasted_iota(jnp.int32, (512, 128), 1) < 64
    for part in range(2):
        k = 2 * column + part
        r.turned[k] = r.kv[k].T
        wide = r.kv[k].astype(F32)
        r.keys[k] = jnp.where(low, wide, pltpu.roll(wide, 64, 1)).astype(BF)


def score_column(r, place, column, slot, diagonal=False):
    chunk = attend_chunk(place, slot)

    def run(parts):
        top, total_sum = r.top[slot], r.total_sum[slot]
        for part, last in parts:
            k = 2 * column + part
            raw = dot_cols(r.keys[k], r.query_two[slot])
            key = lax.broadcasted_iota(jnp.int32, (512, 512), 0)
            allowed = key >= r.begin[slot] - 512 * k
            if last:
                allowed = allowed & (key <= lax.broadcasted_iota(jnp.int32, (512, 512), 1))
            raw = jnp.where(allowed, raw, masked_score)
            r.scores[attend_score(slot, k)] = raw
            higher = jnp.maximum(top, jnp.max(raw, axis=0, keepdims=True))
            total_part = jnp.sum(jnp.exp2(raw - higher), axis=0, keepdims=True)
            total_sum = total_sum * jnp.exp2(top - higher) + total_part
            top = higher
        r.top[slot] = top
        r.total_sum[slot] = total_sum

    if not diagonal:

        @pl.when(2 * column + 1 < chunk)
        def _():
            run(((0, False), (1, False)))

        return

    @pl.when(2 * column + 1 == chunk)
    def _():
        run(((0, False), (1, True)))

    @pl.when(2 * column == chunk)
    def _():
        run(((0, True),))


def weigh_values(r, place, slot):
    level = r.top[slot] + jnp.log(r.total_sum[slot]) * LOG2_E

    def weigh(k, out):
        prob = jnp.exp2(r.scores[attend_score(slot, k)] - level)
        r.scores[attend_score(slot, k)] = prob
        return out + dot(r.turned[k, 64:128, :], prob.astype(BF))

    out = pairs(attend_chunk(place, slot) + 1, weigh, jnp.zeros((64, 512), F32))
    r.out_turned[slot] = out
    r.out_low[slot] = out.astype(BF)


def backward_block(r, slot, k):
    prob = r.scores[attend_score(slot, k)]
    out_grad = r.grad_low[slot]
    grad = dot_cols(r.kv[k], out_grad)
    score_grad = (prob * (grad - r.centre[slot])).astype(BF)
    r.sums[k] += dot(prob.astype(BF), out_grad) + dot(score_grad, r.query_low[slot])
    return dot(r.turned[k, 0:64, :], score_grad)


def backward_cross(r, place):
    def step(k, back):
        return back + backward_block(r, 1, k)

    back = pairs(attend_chunk(place, 1) + 1, step, jnp.zeros((64, 512), F32))
    r.back_low[1] = (back * (HD ** -0.5)).astype(BF)


def backward_column(r, place, column, diagonal):
    chunk = attend_chunk(place, 0)

    @pl.when(2 * column + 1 <= chunk)
    def _():
        r.back_turned[...] += backward_block(r, 0, 2 * column) + backward_block(
            r, 0, 2 * column + 1
        )

    if diagonal:

        @pl.when(2 * column == chunk)
        def _():
            r.back_turned[...] += backward_block(r, 0, 2 * column)

    r.dk[0, column] = r.sums[2 * column].astype(BF)
    r.dk[1, column] = r.sums[2 * column + 1].astype(BF)


def newton(r, place):
    blocks, size = 1, 512

    def rows(i):
        return pl.ds(size * i, size)

    def diagonal(i):
        row = size * i + lax.broadcasted_iota(jnp.int32, (size, 512), 0)
        return row == lax.broadcasted_iota(jnp.int32, (size, 512), 1)

    def fill(i, trace):
        value = r.gram[...]
        for k in range(3):
            lanes = slice(512 * k, 512 * k + 512)
            right = r.momentum[:, :, :, :, lanes].reshape(512, 512)
            value = value + dot_cols(right, right)
        r.gram[...] = value
        return trace + jnp.sum(jnp.where(diagonal(i), value, 0.0), keepdims=True)

    trace = lax.fori_loop(0, blocks, fill, jnp.zeros((1, 1), F32))
    scale = 1.0 / (jnp.sqrt(trace) + 1e-07)

    def keep(value, i, high_ref, low_ref):
        high, small = halves(value)
        high_ref[rows(i), :] = high
        low_ref[rows(i), :] = small

    def prepare(i, _):
        value = r.gram[rows(i), :] * (scale * scale)
        r.gram[rows(i), :] = value
        keep(value, i, r.gram_h, r.gram_l)
        return 0

    lax.fori_loop(0, blocks, prepare, 0)

    def polynomial(i, _):
        square = squared(r.gram_h[...], r.gram_l[...])
        value = (
            jnp.where(diagonal(i), newton_first, 0.0)
            + newton_second * r.gram[rows(i), :]
            + newton_third * square
        )
        keep(value, i, r.poly_h, r.poly_l)
        return 0

    def inner(i, _):
        high, small = r.poly_h[...], r.poly_l[...]
        own_h, own_l = halves(r.own[...])
        left = jnp.concatenate([high, own_h], axis=0)
        cross = dot(left, small)
        main = dot(jnp.concatenate([left, own_l], axis=0), high)
        r.own[...] = main[512:528] + (main[528:544] + cross[512:528])
        keep(main[0:512] + (cross[0:512] + cross[0:512].T), i, r.temp_h, r.temp_l)
        return 0

    def outer(i, _):
        value = product(r.gram_h[...], r.gram_l[...], r.temp_h[...], r.temp_l[...])
        r.gram[rows(i), :] = value
        keep(value, i, r.gram_h, r.gram_l)
        return 0

    def times(left, right_h, right_l):
        high, small = halves(left)
        both = dot(jnp.concatenate([high, small], axis=0), right_h[...])
        return both[0:16] + (both[16:32] + dot(high, right_l[...]))

    mine = 256 * place.c + 64 * place.a + 16 * place.b
    row = lax.broadcasted_iota(jnp.int32, (16, 512), 0)
    column = lax.broadcasted_iota(jnp.int32, (16, 512), 1)
    r.own[...] = jnp.where(column - row == mine, 1.0, 0.0)

    def sweep(_, carry):
        polynomial(0, 0)
        inner(0, 0)
        outer(0, 0)
        return carry

    lax.fori_loop(0, 3, sweep, 0)
    lax.fori_loop(0, blocks, polynomial, 0)
    lax.fori_loop(0, blocks, inner, 0)

    def last_gram(left):
        return times(times(left, r.gram_h, r.gram_l), r.temp_h, r.temp_l)

    own = r.own[...]
    once = last_gram(own)
    own = newton_first * own + newton_second * once + newton_third * last_gram(once)
    return halves(own * scale)


def block_kernel(*refs):
    r = Box()
    names = list(INPUTS) + [n for n, _, _ in OUTPUTS] + [n for n, _, _ in SCRATCH]
    for name, ref in zip(names, refs):
        setattr(r, name, ref)
    place = Place()
    wire = Wire(*refs[-3:])
    z, x, c, t, d = place.z, place.x, place.c, place.t, place.d
    seq, mate, cross, head = place.seq, place.mate, place.cross, place.head
    sibling = place.sibling()

    met = greet(
        place.octet()
        + [place.at_ab(a, b) for a, b in place.plane()]
        + [place.at(x=cross, c=1 - c)]
    )

    load_w = [
        wire.load(r.joint, r.joint_v),
        wire.load(r.output, r.output_v),
        wire.load(r.expand, r.expand_v),
        wire.load(r.reduce, r.reduce_v),
    ]
    load_v = wire.load(r.vectors, r.vectors_v)
    load_x = wire.load(r.x, r.rows_x.at[t])
    load_c = wire.load(r.c, r.rows_c.at[t])
    load_m = [
        wire.load(r.m_joint, r.m_joint_v),
        wire.load(r.m_output, r.m_output_v),
        wire.load(r.m_expand, r.m_expand_v),
        wire.load(r.m_reduce, r.m_reduce_v),
        wire.load(r.first, r.first_v),
        wire.load(r.second, r.second_v),
    ]
    load_w[0].wait()
    for k in range(4):
        for part in range(3):
            r.j_out[k, :, 128 * part : 128 * part + 128] = r.joint_v[
                :, 512 * part + 128 * k : 512 * part + 128 * k + 128
            ]
    load_v.wait()
    r.table[...] = jnp.zeros((128, 128), F32)
    column = lax.broadcasted_iota(jnp.int32, (128, 11), 0) - (16 * seq + 4 * t)
    own_vec = jnp.zeros((128, 11), F32)
    for j in range(4):
        own_vec = jnp.where(column == j, r.vectors_v[j : j + 1, :], own_vec)
    r.table[:, 0:11] = own_vec.astype(BF).astype(F32)
    r.v_own[...] = r.table[...].T[0:16, :]
    met()

    joint_t = trade_t(wire, place, r.j_out, r.j_in)
    for partner in place.row_t():
        joint_t.append(wire.push(r.v_own, r.v_in.at[t], partner))
    for copy in load_w[1:]:
        copy.wait()
    for k in range(4):
        r.w_out[k, :, 0:512] = r.output_v[...]
        r.w_out[k, :, 512:1024] = r.expand_v[:, 512 * k : 512 * k + 512]
        r.w_out[k, :, 1024:1536] = r.reduce_v[:, 512 * k : 512 * k + 512]
    rest_t = trade_t(wire, place, r.w_out, r.w_in)
    load_x.wait()
    load_c.wait()
    x_rows = [wire.push(r.rows_x.at[t], r.rows_x.at[t], p) for p in place.row_t()]
    r.j_in[t] = r.j_out[t]
    r.v_in[t] = r.v_own[...]
    r.w_in[t] = r.w_out[t]
    arrive(joint_t)
    for k in range(4):
        r.j_rows[4 * k : 4 * k + 4, :] = r.j_in[k]
    keys, values = r.j_rows[:, 128:256], r.j_rows[:, 256:384]
    low16 = lax.broadcasted_iota(jnp.int32, (16, 128), 1) < 64
    own_block = r.wj.at[c, place.a, place.b]
    own_block[:, 0:128] = r.j_rows[:, 0:128].astype(BF)
    own_block[:, 128:256] = jnp.where(low16, keys, pltpu.roll(values, 64, 1)).astype(BF)
    own_block[:, 256:384] = jnp.where(low16, pltpu.roll(keys, 64, 1), values).astype(BF)
    own_block[:, 384:512] = ((r.v_in[0] + r.v_in[1]) + (r.v_in[2] + r.v_in[3])).astype(BF)
    joint_all = spread_plane(wire, place, r.wj)
    arrive(rest_t)
    for k in range(4):
        r.w_rows[4 * k : 4 * k + 4, :] = r.w_in[k]
    r.wr[c, z, x] = r.w_rows[...].astype(BF)
    block = r.wr.at[c, z, x]
    rest_b = [wire.push(block, block, partner) for partner in place.row_x()]

    half = ROT // 2
    lane = lax.rem(lax.broadcasted_iota(jnp.int32, (1, 128), 1), 64)
    frequency = jnp.zeros((1, 128), F32)
    for i in range(half):
        frequency = jnp.where(lax.rem(lane, half) == i, 10000.0 ** (-2.0 * i / ROT), frequency)
    frequency = jnp.where(lane < ROT, frequency, 0.0)

    def angles(i, _):
        index = 512 * seq + 128 * i + lax.broadcasted_iota(jnp.int32, (128, 1), 0)
        begin = jnp.zeros((128, 1), jnp.int32)
        finish = 0
        for j in range(4):
            finish = finish + r.lengths[0, j]
            begin = jnp.where(index >= finish, finish, begin)
        angle = (index - begin).astype(F32) * frequency
        r.cos[i] = jnp.cos(angle)
        r.sin[i] = jnp.sin(angle)
        return 0

    lax.fori_loop(0, 4, angles, 0)
    for copy in load_m:
        copy.wait()
    arrive(joint_all)
    joint_swap = swap_cores(wire, place, r.wj)
    arrive(rest_b)
    c_rows = [wire.push(r.rows_c.at[t], r.rows_c.at[t], p) for p in place.row_t()]
    rest = Ring(wire, place, r.wr, z, lambda i: place.at(z=i))
    arrive(x_rows)
    joint_swap.wait_recv()
    for k in range(4):
        own_vec = jnp.zeros((16, 128), F32)
        for i in range(4):
            for part in (r.wj[0, k, i, :, 384:512], r.wj[1, i, k, :, 384:512]):
                own_vec = own_vec + part.astype(F32)
        r.v[k] = own_vec
    natural(r.wj, r.w_joint, 0, 384)

    gain, shift = vec_row(r.v, 0), vec_row(r.v, 1)
    q_bias, k_bias, v_bias = r.v[t, 2:3, :], r.v[t, 3:4, :], r.v[t, 4:5, :]
    low_row = lax.broadcasted_iota(jnp.int32, (1, 128), 1) < 64
    pair_bias = (
        jnp.where(low_row, k_bias, pltpu.roll(v_bias, 64, 1)),
        jnp.where(low_row, pltpu.roll(k_bias, 64, 1), v_bias),
    )
    low = lax.broadcasted_iota(jnp.int32, (256, 128), 1) < 64

    def project(i, _):
        blocks, rows = pl.ds(2 * i, 2), pl.ds(256 * i, 256)
        normal, _rate = normalise(r.rows_x[blocks].reshape(256, 512))
        part = (normal * gain + shift).astype(BF)
        r.normed[blocks] = part.reshape(2, 128, 512)
        raw = dot(part, r.w_joint[...].reshape(512, 384))
        cosine, sine = r.cos[blocks].reshape(256, 128), r.sin[blocks].reshape(256, 128)
        query = turn(raw[:, 0:128] + q_bias, cosine, sine, 1.0)
        r.q_turned[i] = query.T.astype(BF)
        key_cos = jnp.where(low, cosine, 1.0)
        key_sin = jnp.where(low, sine, 0.0)
        for h in range(2):
            pair = raw[:, 128 + 128 * h : 256 + 128 * h] + pair_bias[h]
            r.kv_buf[h, rows, :] = turn(pair, key_cos, key_sin, 1.0).astype(BF)
        return 0

    lax.fori_loop(0, 2, project, 0)
    for i in range(2):
        for h in range(2):
            r.q_buf[h, :, 256 * i : 256 * i + 256] = r.q_turned[i, 64 * h : 64 * h + 64, :]
    q_cross = wire.push(r.q_buf.at[1 - head], r.q_heads.at[1], place.at(x=cross, c=1 - c))
    kv_cross = []
    for i in range(2):
        rows = pl.ds(256 * i, 256)
        kv_cross.append(
            wire.push(r.kv_buf.at[1 - head, rows], r.kv.at[seq, rows], place.at(x=cross))
        )
    kv_mate = wire.push(r.kv_buf.at[head], r.kv.at[seq], place.at(x=mate))
    kv_core = wire.push(r.kv_buf.at[head], r.kv.at[seq], sibling)
    r.kv[seq] = r.kv_buf[head]
    r.q_heads[0] = r.q_buf[head]
    attend_start(r, place)
    query_prepare(r, 0)
    r.sums[...] = jnp.zeros_like(r.sums)
    r.back_turned[...] = jnp.zeros_like(r.back_turned)
    for k in range(4):
        lanes = slice(128 * k, 128 * k + 128)
        keys = r.m_joint_v[:, 512 + 128 * k : 640 + 128 * k]
        values = r.m_joint_v[:, 1024 + 128 * k : 1152 + 128 * k]
        start = 384 * k
        r.m_own[0, :, start : start + 128] = r.m_joint_v[:, lanes]
        r.m_own[0, :, start + 128 : start + 256] = jnp.concatenate(
            [keys[:, 0:64], values[:, 0:64]], axis=1
        )
        r.m_own[0, :, start + 256 : start + 384] = jnp.concatenate(
            [keys[:, 64:128], values[:, 64:128]], axis=1
        )
    r.m_own[0, :, 1536:2048] = jnp.zeros((4, 512), F32)
    r.m_own[1, :, 0:512] = r.m_output_v[...]
    r.m_own[1, :, 512:2048] = jnp.zeros((4, 1536), F32)
    r.m_own[2] = r.m_expand_v[...]
    r.m_own[3] = r.m_reduce_v[...]
    rest.hand_on()
    kv_core.wait_recv()
    keys_prepare(r, x)
    score_column(r, place, x, 0, diagonal=True)
    at_cross, at_mate = 2 * cross + c, 2 * mate + c
    at_far = 2 * (3 - mate) + c
    kv_far, kv_sent, far_sent = [], [], []
    for i in range(2):
        kv_cross[i].wait_recv()
        part = r.kv.at[at_cross, pl.ds(256 * i, 256)]
        kv_far.append(wire.push(part, part, place.at(x=mate)))
        kv_sent.append(wire.push(part, part, sibling))
    kv_mate.wait_recv()
    mate_sent = wire.push(r.kv.at[at_mate], r.kv.at[at_mate], sibling)
    rest.close()
    q_cross.wait_recv()
    query_prepare(r, 1)
    score_column(r, place, x, 1)
    mate_sent.wait_recv()
    keys_prepare(r, mate)
    score_column(r, place, mate, 0)
    score_column(r, place, mate, 1)
    arrive([*c_rows, *rest.swaps])
    by_row(r.wr, r.w_output, 0, 512)
    by_row(r.wr, r.w_expand, 512, 1024)
    by_row(r.wr, r.w_reduce, 1024, 1536)
    out_rows = r.w_output[pl.ds(8 * t, 8)].reshape(128, 512)
    grad = dot_cols(out_rows, r.rows_c[...].reshape(512, 512)).astype(BF)
    r.g_buf[0] = grad[0:64, :]
    r.g_buf[1] = grad[64:128, :]
    g_cross = wire.push(r.g_buf.at[1 - head], r.g_heads.at[1], place.at(x=cross, c=1 - c))
    r.g_heads[0] = r.g_buf[head]
    grad_prepare(r, 0)
    early = trade_t(wire, place, r.m_own, r.m_early)

    bias = jnp.concatenate([r.v[k, pl.ds(7 + t, 1), :] for k in range(4)], axis=1)

    def feed_forward(i, sums):
        blocks = pl.ds(2 * i, 2)
        part = r.normed[blocks].reshape(256, 512)
        wide = dot(part, r.w_expand[...].reshape(512, 512)) + bias
        square = wide * wide
        curve = jnp.tanh(0.7978845608 * (wide + 0.044715 * (square * wide)))
        r.hidden[blocks] = (0.5 * wide * (1.0 + curve)).astype(BF).reshape(2, 128, 512)
        slope = 0.5 * (1.0 + curve) + (0.5 * 0.7978845608) * wide * (1.0 - curve * curve) * (
            1.0 + (3 * 0.044715) * square
        )
        part = r.rows_c[blocks].reshape(256, 512)
        back = dot(part, r.w_reduce[...].reshape(512, 512))
        grad = (back * slope).astype(BF)
        r.pre[blocks] = grad.reshape(2, 128, 512)
        return sums + jnp.sum(grad.astype(F32), axis=0, keepdims=True)

    hidden_sum = lax.fori_loop(0, 2, feed_forward, jnp.zeros((1, 512), F32))
    for i in range(2):
        kv_far[i].wait_recv()
        part = r.kv.at[at_far, pl.ds(256 * i, 256)]
        far_sent.append(wire.push(part, part, sibling))
    for j in range(4):
        lanes = slice(128 * j, 128 * j + 128)
        expand_grad = dot_rows(
            r.normed[:, :, lanes].reshape(512, 128), r.pre[...].reshape(512, 512)
        )
        by_core(r.gf, j, expand_grad.astype(BF), 0, 512)
        reduce_grad = dot_rows(
            r.rows_c[:, :, lanes].reshape(512, 128), r.hidden[...].reshape(512, 512)
        )
        by_core(r.gf, j, reduce_grad.astype(BF), 512, 1024)
    gf_swap = sum_cores(wire, place, r.gf, r.gf_core)
    far = 3 - mate
    arrive(kv_sent)
    keys_prepare(r, cross)
    score_column(r, place, cross, 0)
    score_column(r, place, cross, 1, diagonal=True)
    arrive(far_sent)
    keys_prepare(r, far)
    score_column(r, place, far, 0)
    score_column(r, place, far, 1)
    gf_swap.wait_recv()
    for a in range(4):
        r.gf_chip[a] = (r.gf[c, a].astype(F32) + r.gf_core[a].astype(F32)).astype(BF)
    gf_z = []
    for k in range(1, 4):
        goal = ring(z, k)
        gf_z.append(wire.push(r.gf_chip.at[goal], r.gf_z.at[k - 1], place.at(z=goal)))
    weigh_values(r, place, 1)
    out_cross = wire.push(r.out_low.at[1], r.out_heads.at[head], place.at(x=cross, c=1 - c))
    weigh_values(r, place, 0)
    r.out_heads[head] = r.out_low[0]
    g_cross.wait_recv()
    grad_prepare(r, 1)
    for slot in range(2):
        r.centre[slot] = jnp.sum(
            r.out_turned[slot] * r.g_heads[slot].astype(F32), axis=0, keepdims=True
        )

    dk_swap = []

    def chip_sum(index):
        return r.dk[c, index].astype(F32) + r.dk_in[index].astype(F32)

    dk_sent = []

    def send_column(step, column):
        dk_swap[step].wait_recv()
        r.dk_chip[step] = chip_sum(column).astype(BF)
        dk_sent.append(
            wire.push(r.dk_chip.at[step], r.dk_got.at[step], place.at(x=column))
        )

    backward_cross(r, place)
    back_cross = wire.push(r.back_low.at[1], r.back_heads.at[head], place.at(x=cross, c=1 - c))
    out_cross.wait_recv()
    turned = r.out_heads[...].reshape(128, 512)
    r.pair_out[...] = turned
    out_grad = dot(turned, r.rows_c[...].reshape(512, 512)).astype(BF)
    for j in range(4):
        r.out_cols[j] = out_grad[:, 128 * j : 128 * j + 128]
    out_cols = trade_t(wire, place, r.out_cols, r.out_in)
    r.out_in[t] = r.out_cols[t]
    columns = (far, cross, mate, x)
    for step, column in enumerate(columns):
        backward_column(r, place, column, diagonal=step == 3)
        dk_swap.append(wire.push(r.dk.at[1 - c, column], r.dk_in.at[column], sibling))
        if step > 0:
            send_column(step - 1, columns[step - 1])
    r.back_low[0] = (r.back_turned[...] * (HD ** -0.5)).astype(BF)
    r.back_heads[head] = r.back_low[0]
    arrive(gf_z)
    r.gf_line[...] = total(r.gf_chip[z], r.gf_z).astype(BF)
    gf_x = []
    for k in range(1, 4):
        goal = ring(x, k)
        gf_x.append(wire.push(r.gf_line.at[goal], r.gf_x.at[k - 1], place.at(x=goal)))
    arrive(out_cols)
    for j in range(4):
        by_owner(r.go, j, r.out_in[j], 0, 128)
    go_swap = sum_cores(wire, place, r.go, r.go_core)

    def feed_out(i, _):
        blocks = pl.ds(2 * i, 2)
        part = r.hidden[blocks].reshape(256, 512)
        r.feed[blocks] = dot_cols(part, r.w_reduce[...].reshape(512, 512)).reshape(2, 128, 512)
        part = r.pre[blocks].reshape(256, 512)
        r.row_grad[blocks] = dot_cols(part, r.w_expand[...].reshape(512, 512)).reshape(2, 128, 512)
        return 0

    lax.fori_loop(0, 2, feed_out, 0)
    go_swap.wait_recv()
    for a in range(4):
        r.go_chip[a] = (r.go[c, a].astype(F32) + r.go_core[a].astype(F32)).astype(BF)
    go_all = scatter_plane(wire, place, r.go_chip, r.go_in)
    out_rows = r.w_output[pl.ds(8 * t, 8)].reshape(128, 512)
    for i in range(2):
        blocks, lanes = slice(2 * i, 2 * i + 2), slice(256 * i, 256 * i + 256)
        part = r.feed[blocks].reshape(256, 512) + dot_rows(r.pair_out[:, lanes], out_rows)
        r.out_part[blocks] = part.astype(BF).reshape(2, 128, 512)
    out_parts = trade_t(wire, place, r.out_part, r.out_got)
    r.out_got[t] = r.out_part[t]
    back_cross.wait_recv()
    back = r.back_heads[...].reshape(128, 512).astype(F32).T
    cosine, sine = r.cos[...].reshape(512, 128), r.sin[...].reshape(512, 128)
    r.joint_out[:, 0:128] = turn(back, cosine, sine, -1.0).astype(BF)
    low = lax.broadcasted_iota(jnp.int32, (128, 128), 1) < 64
    arrive([dk_swap[3], *dk_sent])
    r.dkv[head] = (chip_sum(x) + r.dk_got[2].astype(F32)).astype(BF)
    r.dkv[1 - head] = (r.dk_got[0].astype(F32) + r.dk_got[1].astype(F32)).astype(BF)
    for h in range(2):
        for i in range(4):
            rows = pl.ds(128 * i, 128)
            key_cos = jnp.where(low, r.cos[i], 1.0)
            key_sin = jnp.where(low, r.sin[i], 0.0)
            r.joint_out[rows, 128 + 128 * h : 256 + 128 * h] = turn(
                r.dkv[h, rows, :].astype(F32), key_cos, key_sin, -1.0
            ).astype(BF)
    for j in range(4):
        part = r.normed[:, :, 128 * j : 128 * j + 128].reshape(512, 128)
        by_owner(r.gj, j, dot_rows(part, r.joint_out[...]).astype(BF), 0, 384)
    gj_swap = sum_cores(wire, place, r.gj, r.gj_core)

    r.vp[0] = jnp.zeros((4, 16, 128), F32)
    shift_sum = jnp.zeros((1, 512), F32)
    gain_sum = jnp.zeros((1, 512), F32)
    for i in range(4):
        rows = pl.ds(128 * i, 128)
        part = r.row_grad[i] + dot_cols(r.joint_out[rows, :], r.w_joint[...].reshape(512, 384))
        r.back_part[i] = part.astype(BF)
        normal, _rate = normalise(r.rows_x[i])
        shift_sum = shift_sum + jnp.sum(part, axis=0, keepdims=True)
        gain_sum = gain_sum + jnp.sum(part * normal, axis=0, keepdims=True)
    gj_swap.wait_recv()
    for a in range(4):
        r.gj_chip[a] = (r.gj[c, a].astype(F32) + r.gj_core[a].astype(F32)).astype(BF)
    gj_all = scatter_plane(wire, place, r.gj_chip, r.gj_in)
    back_parts = trade_t(wire, place, r.back_part, r.back_got)
    r.back_got[t] = r.back_part[t]
    out_sum = jnp.sum(r.rows_c[t].astype(F32), axis=0, keepdims=True)
    joint_sum = jnp.sum(r.joint_out[...].astype(F32), axis=0, keepdims=True)
    one, two = joint_sum[:, 128:256], joint_sum[:, 256:384]
    for k in range(4):
        lanes = slice(128 * k, 128 * k + 128)
        r.vp[0, k, 0:1, :] = gain_sum[:, lanes]
        r.vp[0, k, 1:2, :] = shift_sum[:, lanes]
        r.vp[0, k, 5:6, :] = out_sum[:, lanes]
        r.vp[0, k, 6:7, :] = out_sum[:, lanes]
        r.vp[0, k, pl.ds(7 + t, 1), :] = hidden_sum[:, lanes]
    r.vp[0, t, 2:3, :] = joint_sum[:, 0:128]
    r.vp[0, t, 3:4, :] = jnp.where(low_row, one, pltpu.roll(two, 64, 1))
    r.vp[0, t, 4:5, :] = jnp.where(low_row, pltpu.roll(one, 64, 1), two)
    vp_swap = wire.push(r.vp.at[0], r.vp_core, sibling)
    arrive(gf_x)
    gf_own = total(r.gf_line[x], r.gf_x)
    arrive(go_all)
    go_own = add_plane(r.go_chip[place.a, place.b], r.go_in)
    for k in range(4):
        r.early_out[k, :, 0:1024] = gf_own[4 * k : 4 * k + 4, :]
        r.early_out[k, :, 1024:1152] = go_own[4 * k : 4 * k + 4, :]
    r.gm_out[1, :, 0:128] = go_own.astype(BF)
    r.gm_out[2] = gf_own[:, 0:512].astype(BF)
    r.gm_out[3] = gf_own[:, 512:1024].astype(BF)
    gm_first = wire.block(4)
    gm_widths = (384, 128, 512, 512)

    def to_newton(w, sender):
        lanes = slice(0, gm_widths[w])
        return wire.offer(
            gm_first, r.gm_out.at[w, :, lanes], r.gm_in.at[sender, :, lanes], sender, w,
            place.at(t=w),
        )

    def send_newton(w):
        @pl.when(t != w)
        def _():
            to_newton(w, t).start()

        @pl.when(t == w)
        def _():
            r.gm_in[w, :, 0 : gm_widths[w]] = r.gm_out[w, :, 0 : gm_widths[w]]

    for w in (1, 2, 3):
        send_newton(w)
    early_t = trade_t(wire, place, r.early_out, r.early_in)
    r.early_in[t] = r.early_out[t]

    arrive(early)
    r.m_early[t] = r.m_own[t]
    for k in range(4):
        r.m_old[4 * k : 4 * k + 4, :] = r.m_early[k]
    vp_swap.wait_recv()
    r.vp[1] = r.vp[0] + r.vp_core[...]
    vp_z = [wire.push(r.vp.at[1], r.vp_z.at[k], p) for k, p in enumerate(place.row_z())]

    arrive(gj_all)
    gj_own = add_plane(r.gj_chip[place.a, place.b], r.gj_in)
    r.gm_out[0, :, 0:384] = gj_own.astype(BF)
    send_newton(0)
    for k in range(4):
        r.late_out[k] = gj_own[4 * k : 4 * k + 4, :]
    late_t = trade_t(wire, place, r.late_out, r.late_in)
    r.late_in[t] = r.late_out[t]
    arrive(vp_z)
    r.vp[2] = total(r.vp[1], r.vp_z)
    vp_x = [wire.push(r.vp.at[2], r.vp_x.at[k], p) for k, p in enumerate(place.row_x())]

    for w in range(4):

        @pl.when(t == w)
        def _(w=w):
            width = gm_widths[w]
            for sender in range(4):
                if sender != w:
                    to_newton(w, sender).wait_recv()
            for k in range(4):
                lanes = slice(width * k, width * k + width)
                value = muon_beta * r.m_old[:, lanes] + r.gm_in[k, :, 0:width].astype(F32)
                if width * k < 1536:
                    r.momentum[c, place.a, place.b, :, lanes] = value.astype(BF)
                else:
                    r.extra[c, place.a, place.b] = value.astype(BF)
            if w == 1:
                r.momentum[c, place.a, place.b, :, 512:1536] = jnp.zeros((16, 1024), BF)

    m_b = spread_b(wire, place, r.momentum)

    extra_first = wire.block(7)

    def extra_line():
        block = r.extra.at[c, place.a, place.b]
        return [
            wire.offer(extra_first, block, block, k, k, place.at_b(ring(place.b, k)))
            for k in range(1, 4)
        ]

    def extra_lines():
        block = r.extra.at[c, place.a]
        return [
            wire.offer(extra_first, block, block, 3 + k, 3 + k, place.at_a(ring(place.a, k)))
            for k in range(1, 4)
        ]

    def extra_swap():
        block = r.extra.at[c]
        return wire.offer(extra_first, block, block, 0, 0, sibling)

    @pl.when(t >= 2)
    def _():
        for copy in extra_line():
            copy.start()

    arrive(m_b)
    whole = Ring(wire, place, r.momentum, place.a, place.at_a)

    @pl.when(t >= 2)
    def _():
        for copy in extra_line():
            copy.wait_recv()
        for copy in extra_lines():
            copy.start()

    arrive(early_t)
    for k in range(4):
        part = r.early_in[k]
        r.g_expand[:, 512 * k : 512 * k + 512] = part[:, 0:512]
        r.g_reduce[:, 512 * k : 512 * k + 512] = part[:, 512:1024]
        r.g_output[:, 128 * k : 128 * k + 128] = part[:, 1024:1152]
    arrive(late_t)
    for k in range(4):
        unpair(r.g_joint, r.late_in[k], k)
    for old, grad, new in (
        (r.m_joint_v, r.g_joint, r.n_joint),
        (r.m_output_v, r.g_output, r.n_output),
        (r.m_expand_v, r.g_expand, r.n_expand),
        (r.m_reduce_v, r.g_reduce, r.n_reduce),
    ):
        new[...] = muon_beta * old[...] + grad[...]
    arrive(vp_x)
    r.vp[3] = total(r.vp[2], r.vp_x)
    vp_t = [wire.push(r.vp.at[3], r.vp_t.at[k], p) for k, p in enumerate(place.row_t())]
    arrive(out_parts)
    arrive(back_parts)
    wide = r.rows_x[t].astype(F32)
    feed = r.out_got[0].astype(F32)
    back = r.back_got[0].astype(F32)
    for k in range(1, 4):
        feed = feed + r.out_got[k].astype(F32)
        back = back + r.back_got[k].astype(F32)
    r.block_output[...] = (wide + feed + vec_row(r.v, 5) + vec_row(r.v, 6)).astype(BF)
    normal, rate = normalise(r.rows_x[t])
    scaled = back * gain
    mean_one = jnp.mean(scaled, axis=-1, keepdims=True)
    mean_two = jnp.mean(scaled * normal, axis=-1, keepdims=True)
    r.input_grad[...] = r.rows_c[t].astype(F32) + rate * (scaled - mean_one - normal * mean_two)
    whole.hand_on()

    @pl.when(t >= 2)
    def _():
        for copy in extra_lines():
            copy.wait_recv()
        extra_swap().start()

    whole.close()
    arrive(vp_t)
    r.vec_sum[...] = total(r.vp[3], r.vp_t)
    r.table[0:16, :] = r.vec_sum[z]
    r.table[...] = r.table[...].T
    vector_grad = r.table[pl.ds(pl.multiple_of(16 * seq + 4 * t, 4), 4), 0:11]
    r.vector_grad[...] = vector_grad
    first_next = beta_first * r.first_v[...] + (1.0 - beta_first) * vector_grad
    second_next = (
        beta_second * r.second_v[...] + (1.0 - beta_second) * vector_grad * vector_grad
    )
    r.second_next[...] = second_next
    first_hat = first_next / (1.0 - beta_first**STEP)
    second_hat = second_next / (1.0 - beta_second**STEP)
    r.vector_next[...] = r.vectors_v[...] - vector_rate * first_hat / (
        jnp.sqrt(second_hat) + adam_epsilon
    )
    @pl.when(t >= 2)
    def _():
        extra_swap().wait_recv()
        columns = r.extra[...].reshape(512, 512)
        r.gram[...] = dot_cols(columns, columns)

    @pl.when(t < 2)
    def _():
        r.gram[...] = jnp.zeros((512, 512), F32)

    arrive(whole.swaps)

    high, small = newton(r, place)
    both = jnp.concatenate([high, small], axis=0)
    for k in range(3):
        lanes = slice(512 * k, 512 * k + 512)
        rows = dot(both, r.momentum[:, :, :, :, lanes].reshape(512, 512))
        r.m_rows[:, lanes] = rows[0:16] + rows[16:32]

    @pl.when(t >= 2)
    def _():
        rows = dot(both, r.extra[...].reshape(512, 512))
        r.m_rows[:, 1536:2048] = rows[0:16] + rows[16:32]

    @pl.when(t < 2)
    def _():
        r.m_rows[:, 1536:2048] = jnp.zeros((16, 512), F32)

    for k in range(4):
        for p in range(4):
            r.u_rows[k, 4 * p : 4 * p + 4, :] = r.m_rows[
                4 * k : 4 * k + 4, 512 * p : 512 * p + 512
            ]
    r.u_out[...] = r.u_rows[...].astype(BF)
    u_t = trade_t(wire, place, r.u_out, r.u_in)
    r.u_in[t] = r.u_out[t]
    wire.drain()
    for w in range(4):

        @pl.when(t != w)
        def _(w=w):
            to_newton(w, t).wait_send()

    @pl.when(t >= 2)
    def _():
        for copy in extra_line() + extra_lines():
            copy.wait_send()
        extra_swap().wait_send()

    arrive(u_t)
    r.u_rows[...] = r.u_in[...].astype(F32)
    for k in range(4):
        for p in range(4):
            r.u_wide[k, :, 512 * p : 512 * p + 512] = r.u_rows[k, 4 * p : 4 * p + 4, :]
    for k in range(4):
        unpair(r.u_joint, r.u_wide[0, :, 384 * k : 384 * k + 384], k)
    for k, (old, change, new) in enumerate(
        (
            (r.joint_v, r.u_joint, r.u_joint),
            (r.output_v, r.u_wide.at[1, :, pl.ds(0, 512)], r.u_output),
            (r.expand_v, r.u_wide.at[2], r.u_expand),
            (r.reduce_v, r.u_wide.at[3], r.u_reduce),
        )
    ):
        factor = muon_rate * 0.2 * math.sqrt(max(D, WIDTHS[k]))
        new[...] = old[...] * (1.0 - muon_rate * muon_decay) - factor * change[...]
    wire.drain()


def block_stage(*arrays):
    return pl.pallas_call(
        block_kernel,
        out_shape=tuple(shape(dims, dtype) for _, dims, dtype in OUTPUTS),
        in_specs=[SMEM] + [ANY] * (len(INPUTS) - 1),
        out_specs=(VMEM,) * len(OUTPUTS),
        scratch_shapes=[pltpu.VMEM(dims, dtype) for _, dims, dtype in SCRATCH]
        + [
            pltpu.SemaphoreType.DMA((PUSHES,)),
            pltpu.SemaphoreType.DMA((PUSHES,)),
            pltpu.SemaphoreType.DMA((LOADS,)),
        ],
        compiler_params=pltpu.CompilerParams(
            collective_id=1, has_side_effects=True, vmem_limit_bytes=56 << 20
        ),
        name="block",
    )(*arrays)


def write_kernel(*refs):
    count = len(OUTPUTS)
    sem = refs[-1]
    copies = []
    for k in range(count):
        copy = pltpu.make_async_copy(refs[k], refs[count + k], sem.at[k])
        copy.start()
        copies.append(copy)
    for copy in copies:
        copy.wait()


def write_stage(*arrays):
    count = len(arrays)
    return pl.pallas_call(
        write_kernel,
        out_shape=tuple(shape(a.shape, a.dtype) for a in arrays),
        in_specs=[VMEM] * count,
        out_specs=(ANY,) * count,
        scratch_shapes=[pltpu.SemaphoreType.DMA((count,))],
        name="write",
    )(*arrays)


def shards(
    block_input,
    cotangent,
    doc_lengths,
    joint_weight,
    output_weight,
    expand_weight,
    reduce_weight,
    joint_moment,
    output_moment,
    expand_moment,
    reduce_moment,
    vectors,
    first_moment,
    second_moment,
):
    results = block_stage(
        doc_lengths, block_input, cotangent, joint_weight, output_weight, expand_weight,
        reduce_weight, vectors.T, joint_moment, output_moment, expand_moment, reduce_moment,
        first_moment.T, second_moment.T,
    )
    results = write_stage(*results)
    return (*results[12:14], *results[0:12], *[part.T for part in results[14:]])


def solution(mesh):
    rows = P(("fsdp", "seq", "tensor"), None)
    columns = P(None, ("fsdp", "seq", "tensor"))
    return jax.shard_map(
        shards,
        mesh=mesh,
        in_specs=(rows, rows, P("fsdp", None)) + (rows,) * 8 + (columns,) * 3,
        out_specs=(rows,) * 14 + (columns,) * 3,
        check_vma=False,
    )
```

```python
import functools
import math

import jax
import jax.numpy as jnp
from jax import lax
from jax.experimental import pallas as pl
from jax.experimental.pallas import tpu as pltpu
from jax.sharding import PartitionSpec as P

D = 512
HEADS = 8
FF = 2048
ROT = 16
HD = 64
STEP = 10

norm_epsilon = 1e-05
masked_score = -1e30
newton_first = 3.4445
newton_second = -4.775
newton_third = 2.0315
beta_first = 0.9
beta_second = 0.95
adam_epsilon = 1e-08
vector_rate = 0.2
muon_rate = 0.25
muon_beta = 0.95
muon_decay = 0.01
LOG2_E = 1.4426950408889634

BF = jnp.bfloat16
F32 = jnp.float32
MESH = pl.DeviceIdType.MESH
VMEM = pl.BlockSpec(memory_space=pltpu.VMEM)
SMEM = pl.BlockSpec(memory_space=pltpu.SMEM)
ANY = pl.BlockSpec(memory_space=pl.ANY)
WIDTHS = (3 * D, D, FF, FF)


def shape(dims, dtype):
    return jax.ShapeDtypeStruct(dims, dtype)


class Place:
    def __init__(self):
        self.z = lax.axis_index("fsdp")
        self.seq = lax.axis_index("seq")
        self.t = lax.axis_index("tensor")
        self.x = lax.div(self.seq, 2)
        self.c = lax.rem(self.seq, 2)
        self.d = 1 - 2 * self.c
        self.a = self.c * self.x + (1 - self.c) * self.z
        self.b = self.c * self.z + (1 - self.c) * self.x
        self.mate = self.x + 1 - 2 * lax.rem(self.x, 2)
        self.cross = 3 - self.x
        self.head = lax.div(self.x, 2)

    def at(self, z=None, x=None, c=None, t=None):
        z = self.z if z is None else z
        x = self.x if x is None else x
        c = self.c if c is None else c
        t = self.t if t is None else t
        return (z, 2 * x + c, t)

    def at_a(self, a):
        c = self.c
        return self.at(z=(1 - c) * a + c * self.z, x=c * a + (1 - c) * self.x)

    def at_b(self, b):
        c = self.c
        return self.at(z=c * b + (1 - c) * self.z, x=(1 - c) * b + c * self.x)

    def at_ab(self, a, b):
        c = self.c
        return self.at(z=(1 - c) * a + c * b, x=c * a + (1 - c) * b)

    def plane(self):
        steps = [(i, j) for i in range(4) for j in range(4) if i + j > 0]
        steps.sort(key=lambda step: -min(step[0], 4 - step[0]) - min(step[1], 4 - step[1]))
        return [(ring(self.a, i), ring(self.b, j)) for i, j in steps]

    def sibling(self):
        return self.at(c=1 - self.c)

    def octet(self):
        g = 4 * self.c + self.t
        members = [lax.rem(g + k, 8) for k in range(1, 8)]
        return [self.at(c=lax.div(m, 4), t=lax.rem(m, 4)) for m in members]

    def row_x(self):
        return [self.at(x=lax.rem(self.x + k, 4)) for k in range(1, 4)]

    def row_z(self):
        return [self.at(z=lax.rem(self.z + k, 4)) for k in range(1, 4)]

    def row_t(self):
        return [self.at(t=lax.rem(self.t + k, 4)) for k in range(1, 4)]


def ring(index, step):
    return lax.rem(index + step + 4, 4)


def greet(partners):
    barrier = pltpu.get_barrier_semaphore()
    for partner in partners:
        pl.semaphore_signal(barrier, inc=1, device_id=partner, device_id_type=MESH)
    return lambda: pl.semaphore_wait(barrier, len(partners))


class Wire:
    def __init__(self, send, recv, local):
        self.send = send
        self.recv = recv
        self.local = local
        self.count = 0
        self.loads = 0
        self.open = []

    def push(self, src, dst, device):
        index = self.count
        self.count += 1
        copy = pltpu.make_async_remote_copy(
            src_ref=src,
            dst_ref=dst,
            send_sem=self.send.at[index],
            recv_sem=self.recv.at[index],
            device_id=device,
            device_id_type=MESH,
        )
        copy.start()
        self.open.append(copy)
        return copy

    def offer(self, first, source, target, sender, goal, device):
        return pltpu.make_async_remote_copy(
            src_ref=source,
            dst_ref=target,
            send_sem=self.send.at[first + goal],
            recv_sem=self.recv.at[first + sender],
            device_id=device,
            device_id_type=MESH,
        )

    def block(self, count):
        first = self.count
        self.count += count
        return first

    def load(self, src, dst):
        copy = pltpu.make_async_copy(src, dst, self.local.at[self.loads])
        self.loads += 1
        copy.start()
        return copy

    def drain(self):
        for copy in self.open:
            copy.wait_send()
        self.open = []


def arrive(copies):
    for copy in copies:
        copy.wait_recv()


def dot(left, right):
    return jnp.dot(left, right, preferred_element_type=F32)


def dot_cols(left, right):
    return lax.dot_general(left, right, (((1,), (1,)), ((), ())), preferred_element_type=F32)


def dot_rows(left, right):
    return lax.dot_general(left, right, (((0,), (0,)), ((), ())), preferred_element_type=F32)


def turn(values, cosine, sine, sign):
    lane = lax.rem(lax.broadcasted_iota(jnp.int32, values.shape, 1), 64)
    crossed = jnp.where(lane < 8, -pltpu.roll(values, 120, 1), pltpu.roll(values, 8, 1))
    return values * cosine + crossed * (sine * sign)


def vec_row(v_ref, row):
    return jnp.concatenate([v_ref[k, row : row + 1, :] for k in range(4)], axis=1)


def normalise(rows):
    wide = rows.astype(F32)
    centred = wide - jnp.mean(wide, axis=-1, keepdims=True)
    variance = jnp.mean(centred * centred, axis=-1, keepdims=True)
    rate = lax.rsqrt(variance + norm_epsilon)
    return centred * rate, rate


def halves(values):
    high = values.astype(BF)
    return high, (values - high.astype(F32)).astype(BF)


def product(left_h, left_l, right_h, right_l):
    return dot(left_h, right_h) + (dot(left_h, right_l) + dot(left_l, right_h))


def squared(high, small):
    cross = dot(high, small)
    return dot(high, high) + (cross + cross.T)


def spread_b(wire, place, ref):
    block = ref.at[place.c, place.a, place.b]
    return [wire.push(block, block, place.at_b(ring(place.b, k))) for k in range(1, 4)]


class Ring:
    def __init__(self, wire, place, ref, index, at):
        self.wire = wire
        self.place = place
        self.ref = ref
        self.index = index
        self.at = at
        self.ups, self.downs = {}, {}
        for p, q in ((0, 2), (1, 3), (2, 0), (3, 1)):
            self.ups[p] = self.send(0, p, 1)
            self.downs[q] = self.send(0, q, -1)
        self.swaps = [self.swap(0)]

    def send(self, step, part, way):
        block = self.ref.at[self.place.c, ring(self.index, step), part]
        return self.wire.push(block, block, self.at(ring(self.index, way)))

    def swap(self, step):
        block = self.ref.at[self.place.c, ring(self.index, step)]
        return self.wire.push(block, block, self.place.sibling())

    def hand_on(self):
        self.more = []
        for p, q in ((0, 2), (1, 3)):
            self.ups[p].wait_recv()
            self.more.append(self.send(-1, p, 1))
            self.downs[q].wait_recv()
            self.more.append(self.send(1, q, -1))

    def close(self):
        arrive([self.ups[2], self.ups[3]])
        self.swaps.append(self.swap(-1))
        arrive([self.downs[0], self.downs[1]])
        self.swaps.append(self.swap(1))
        arrive(self.more)
        self.swaps.append(self.swap(2))


def spread_plane(wire, place, ref):
    block = ref.at[place.c, place.a, place.b]
    return [wire.push(block, block, place.at_ab(a, b)) for a, b in place.plane()]


def scatter_plane(wire, place, ref, target):
    copies = []
    for k, (a, b) in enumerate(place.plane()):
        copies.append(wire.push(ref.at[a, b], target.at[k], place.at_ab(a, b)))
    return copies


def add_plane(first, parts):
    value = first.astype(F32)
    for k in range(15):
        value = value + parts[k].astype(F32)
    return value


def swap_cores(wire, place, ref):
    return wire.push(ref.at[place.c], ref.at[place.c], place.sibling())


def natural(source, target, start, stop):
    for z in range(4):
        for x in range(4):
            target[8 * z + 2 * x] = source[0, z, x, :, start:stop]
            target[8 * z + 2 * x + 1] = source[1, x, z, :, start:stop]


def by_row(source, target, start, stop):
    for z in range(4):
        for x in range(4):
            for c in range(2):
                target[8 * z + 2 * x + c] = source[c, z, x, :, start:stop]


def by_owner(target, z, rows, start, stop):
    for x in range(4):
        target[0, z, x, :, start:stop] = rows[32 * x : 32 * x + 16, :]
        target[1, x, z, :, start:stop] = rows[32 * x + 16 : 32 * x + 32, :]


def by_core(target, z, rows, start, stop):
    for x in range(4):
        for c in range(2):
            block = rows[32 * x + 16 * c : 32 * x + 16 * c + 16, :]
            target[c, z, x, :, start:stop] = block


def sum_cores(wire, place, ref, target):
    return wire.push(ref.at[1 - place.c], target, place.sibling())


def trade_t(wire, place, source, target):
    copies = []
    for k in range(1, 4):
        goal = ring(place.t, k)
        copies.append(wire.push(source.at[goal], target.at[place.t], place.at(t=goal)))
    return copies


def total(first, parts):
    value = first.astype(F32)
    for k in range(3):
        value = value + parts[k].astype(F32)
    return value


def unpair(target, part, k):
    one, two = part[:, 128:256], part[:, 256:384]
    target[:, 128 * k : 128 * k + 128] = part[:, 0:128]
    target[:, 512 + 128 * k : 640 + 128 * k] = jnp.concatenate(
        [one[:, 0:64], two[:, 0:64]], axis=1
    )
    target[:, 1024 + 128 * k : 1152 + 128 * k] = jnp.concatenate(
        [one[:, 64:128], two[:, 64:128]], axis=1
    )


INPUTS = (
    "lengths",
    "x",
    "c",
    "joint",
    "output",
    "expand",
    "reduce",
    "vectors",
    "m_joint",
    "m_output",
    "m_expand",
    "m_reduce",
    "first",
    "second",
)

OUTPUTS = (
    ("g_joint", (4, 1536), F32),
    ("g_output", (4, 512), F32),
    ("g_expand", (4, 2048), F32),
    ("g_reduce", (4, 2048), F32),
    ("n_joint", (4, 1536), F32),
    ("n_output", (4, 512), F32),
    ("n_expand", (4, 2048), F32),
    ("n_reduce", (4, 2048), F32),
    ("u_joint", (4, 1536), F32),
    ("u_output", (4, 512), F32),
    ("u_expand", (4, 2048), F32),
    ("u_reduce", (4, 2048), F32),
    ("block_output", (128, 512), BF),
    ("input_grad", (128, 512), F32),
    ("vector_grad", (4, 11), F32),
    ("second_next", (4, 11), F32),
    ("vector_next", (4, 11), F32),
)

SCRATCH = (
    ("joint_v", (4, 1536), F32),
    ("output_v", (4, 512), F32),
    ("expand_v", (4, 2048), F32),
    ("reduce_v", (4, 2048), F32),
    ("vectors_v", (4, 11), F32),
    ("first_v", (4, 11), F32),
    ("second_v", (4, 11), F32),
    ("table", (128, 128), F32),
    ("vec_sum", (4, 16, 128), F32),
    ("m_joint_v", (4, 1536), F32),
    ("m_output_v", (4, 512), F32),
    ("m_expand_v", (4, 2048), F32),
    ("m_reduce_v", (4, 2048), F32),
    ("j_out", (4, 4, 384), F32),
    ("j_in", (4, 4, 384), F32),
    ("j_rows", (16, 384), F32),
    ("w_out", (4, 4, 1536), F32),
    ("w_in", (4, 4, 1536), F32),
    ("w_rows", (16, 1536), F32),
    ("wj", (2, 4, 4, 16, 512), BF),
    ("wr", (2, 4, 4, 16, 1536), BF),
    ("w_joint", (32, 16, 384), BF),
    ("w_output", (32, 16, 512), BF),
    ("w_expand", (32, 16, 512), BF),
    ("w_reduce", (32, 16, 512), BF),
    ("v_own", (16, 128), F32),
    ("m_own", (4, 4, 2048), F32),
    ("m_early", (4, 4, 2048), F32),
    ("m_old", (16, 2048), F32),
    ("v_in", (4, 16, 128), F32),
    ("v", (4, 16, 128), F32),
    ("rows_x", (4, 128, 512), BF),
    ("rows_c", (4, 128, 512), BF),
    ("cos", (4, 128, 128), F32),
    ("sin", (4, 128, 128), F32),
    ("normed", (4, 128, 512), BF),
    ("q_turned", (2, 128, 256), BF),
    ("q_buf", (2, 64, 512), BF),
    ("q_heads", (2, 64, 512), BF),
    ("g_buf", (2, 64, 512), BF),
    ("g_heads", (2, 64, 512), BF),
    ("kv_buf", (2, 512, 128), BF),
    ("kv", (8, 512, 128), BF),
    ("hidden", (4, 128, 512), BF),
    ("pre", (4, 128, 512), BF),
    ("feed", (4, 128, 512), F32),
    ("row_grad", (4, 128, 512), F32),
    ("gf", (2, 4, 4, 16, 1024), BF),
    ("gf_core", (4, 4, 16, 1024), BF),
    ("gf_chip", (4, 4, 16, 1024), BF),
    ("gf_z", (3, 4, 16, 1024), BF),
    ("gf_line", (4, 16, 1024), BF),
    ("gf_x", (3, 16, 1024), BF),
    ("go", (2, 4, 4, 16, 128), BF),
    ("go_core", (4, 4, 16, 128), BF),
    ("go_chip", (4, 4, 16, 128), BF),
    ("go_in", (15, 16, 128), BF),
    ("early_out", (4, 4, 1152), F32),
    ("early_in", (4, 4, 1152), F32),
    ("turned", (8, 128, 512), BF),
    ("keys", (8, 512, 128), BF),
    ("scores", (9, 512, 512), F32),
    ("sums", (8, 512, 128), F32),
    ("query_low", (2, 512, 128), BF),
    ("query_two", (2, 512, 128), BF),
    ("begin", (2, 1, 512), jnp.int32),
    ("top", (2, 1, 512), F32),
    ("total_sum", (2, 1, 512), F32),
    ("out_turned", (2, 64, 512), F32),
    ("grad_low", (2, 512, 128), BF),
    ("back_turned", (64, 512), F32),
    ("centre", (2, 1, 512), F32),
    ("out_low", (2, 64, 512), BF),
    ("out_heads", (2, 64, 512), BF),
    ("back_low", (2, 64, 512), BF),
    ("back_heads", (2, 64, 512), BF),
    ("dk", (2, 4, 512, 128), BF),
    ("dk_in", (4, 512, 128), BF),
    ("dk_chip", (4, 512, 128), BF),
    ("dk_got", (3, 512, 128), BF),
    ("dkv", (2, 512, 128), BF),
    ("pair_out", (128, 512), BF),
    ("joint_out", (512, 384), BF),
    ("out_cols", (4, 128, 128), BF),
    ("out_in", (4, 128, 128), BF),
    ("out_part", (4, 128, 512), BF),
    ("out_got", (4, 128, 512), BF),
    ("back_part", (4, 128, 512), BF),
    ("back_got", (4, 128, 512), BF),
    ("gj", (2, 4, 4, 16, 384), BF),
    ("gj_core", (4, 4, 16, 384), BF),
    ("gj_chip", (4, 4, 16, 384), BF),
    ("gj_in", (15, 16, 384), BF),
    ("late_out", (4, 4, 384), F32),
    ("late_in", (4, 4, 384), F32),
    ("vp", (4, 4, 16, 128), F32),
    ("vp_core", (4, 16, 128), F32),
    ("vp_z", (3, 4, 16, 128), F32),
    ("vp_x", (3, 4, 16, 128), F32),
    ("vp_t", (3, 4, 16, 128), F32),
    ("gm_out", (4, 16, 512), BF),
    ("gm_in", (4, 16, 512), BF),
    ("m_rows", (16, 2048), F32),
    ("momentum", (2, 4, 4, 16, 1536), BF),
    ("extra", (2, 4, 4, 16, 512), BF),
    ("gram", (512, 512), F32),
    ("gram_h", (512, 512), BF),
    ("gram_l", (512, 512), BF),
    ("poly_h", (512, 512), BF),
    ("poly_l", (512, 512), BF),
    ("temp_h", (512, 512), BF),
    ("temp_l", (512, 512), BF),
    ("own", (16, 512), F32),
    ("u_rows", (4, 16, 512), F32),
    ("u_out", (4, 16, 512), BF),
    ("u_in", (4, 16, 512), BF),
    ("u_wide", (4, 4, 2048), F32),
)

PUSHES = 240
LOADS = 16


class Box:
    pass


def attend_chunk(place, slot):
    return place.seq if slot == 0 else 7 - place.seq


def attend_score(slot, k):
    return 8 - k if slot == 0 else k


def pairs(count, step, carry):
    def two(k, carry):
        return step(2 * k + 1, step(2 * k, carry))

    def one(_, carry):
        return step(count - 1, carry)

    carry = lax.fori_loop(0, lax.div(count, 2), two, carry)
    return lax.fori_loop(0, lax.rem(count, 2), one, carry)


def attend_start(r, place):
    for slot in range(2):
        index = 512 * attend_chunk(place, slot) + lax.broadcasted_iota(jnp.int32, (1, 512), 1)
        begin = jnp.zeros((1, 512), jnp.int32)
        finish = 0
        for j in range(4):
            finish = finish + r.lengths[0, j]
            begin = jnp.where(index >= finish, finish, begin)
        r.begin[slot] = begin
        r.top[slot] = jnp.full((1, 512), masked_score, F32)
        r.total_sum[slot] = jnp.zeros((1, 512), F32)


def query_prepare(r, slot):
    wide = r.q_heads[slot].astype(F32)
    high, small = halves(wide * (HD ** -0.5 * LOG2_E))
    r.query_two[slot] = jnp.concatenate([high, small], axis=0).T
    low = (wide * (HD ** -0.5)).astype(BF)
    r.query_low[slot] = jnp.concatenate([low, jnp.zeros((64, 512), BF)], axis=0).T


def grad_prepare(r, slot):
    r.grad_low[slot] = jnp.concatenate([jnp.zeros((64, 512), BF), r.g_heads[slot]], axis=0).T


def keys_prepare(r, column):
    low = lax.broadcasted_iota(jnp.int32, (512, 128), 1) < 64
    for part in range(2):
        k = 2 * column + part
        r.turned[k] = r.kv[k].T
        wide = r.kv[k].astype(F32)
        r.keys[k] = jnp.where(low, wide, pltpu.roll(wide, 64, 1)).astype(BF)


def score_column(r, place, column, slot, diagonal=False):
    chunk = attend_chunk(place, slot)

    def run(parts):
        top, total_sum = r.top[slot], r.total_sum[slot]
        for part, last in parts:
            k = 2 * column + part
            raw = dot_cols(r.keys[k], r.query_two[slot])
            key = lax.broadcasted_iota(jnp.int32, (512, 512), 0)
            allowed = key >= r.begin[slot] - 512 * k
            if last:
                allowed = allowed & (key <= lax.broadcasted_iota(jnp.int32, (512, 512), 1))
            raw = jnp.where(allowed, raw, masked_score)
            r.scores[attend_score(slot, k)] = raw
            higher = jnp.maximum(top, jnp.max(raw, axis=0, keepdims=True))
            total_part = jnp.sum(jnp.exp2(raw - higher), axis=0, keepdims=True)
            total_sum = total_sum * jnp.exp2(top - higher) + total_part
            top = higher
        r.top[slot] = top
        r.total_sum[slot] = total_sum

    if not diagonal:

        @pl.when(2 * column + 1 < chunk)
        def _():
            run(((0, False), (1, False)))

        return

    @pl.when(2 * column + 1 == chunk)
    def _():
        run(((0, False), (1, True)))

    @pl.when(2 * column == chunk)
    def _():
        run(((0, True),))


def weigh_values(r, place, slot):
    level = r.top[slot] + jnp.log(r.total_sum[slot]) * LOG2_E

    def weigh(k, out):
        prob = jnp.exp2(r.scores[attend_score(slot, k)] - level)
        r.scores[attend_score(slot, k)] = prob
        return out + dot(r.turned[k, 64:128, :], prob.astype(BF))

    out = pairs(attend_chunk(place, slot) + 1, weigh, jnp.zeros((64, 512), F32))
    r.out_turned[slot] = out
    r.out_low[slot] = out.astype(BF)


def backward_block(r, slot, k):
    prob = r.scores[attend_score(slot, k)]
    out_grad = r.grad_low[slot]
    grad = dot_cols(r.kv[k], out_grad)
    score_grad = (prob * (grad - r.centre[slot])).astype(BF)
    r.sums[k] += dot(prob.astype(BF), out_grad) + dot(score_grad, r.query_low[slot])
    return dot(r.turned[k, 0:64, :], score_grad)


def backward_cross(r, place):
    def step(k, back):
        return back + backward_block(r, 1, k)

    back = pairs(attend_chunk(place, 1) + 1, step, jnp.zeros((64, 512), F32))
    r.back_low[1] = (back * (HD ** -0.5)).astype(BF)


def backward_column(r, place, column, diagonal):
    chunk = attend_chunk(place, 0)

    @pl.when(2 * column + 1 <= chunk)
    def _():
        r.back_turned[...] += backward_block(r, 0, 2 * column) + backward_block(
            r, 0, 2 * column + 1
        )

    if diagonal:

        @pl.when(2 * column == chunk)
        def _():
            r.back_turned[...] += backward_block(r, 0, 2 * column)

    r.dk[0, column] = r.sums[2 * column].astype(BF)
    r.dk[1, column] = r.sums[2 * column + 1].astype(BF)


def newton(r, place):
    blocks, size = 1, 512

    def rows(i):
        return pl.ds(size * i, size)

    def diagonal(i):
        row = size * i + lax.broadcasted_iota(jnp.int32, (size, 512), 0)
        return row == lax.broadcasted_iota(jnp.int32, (size, 512), 1)

    def fill(i, trace):
        value = r.gram[...]
        for k in range(3):
            lanes = slice(512 * k, 512 * k + 512)
            right = r.momentum[:, :, :, :, lanes].reshape(512, 512)
            value = value + dot_cols(right, right)
        r.gram[...] = value
        return trace + jnp.sum(jnp.where(diagonal(i), value, 0.0), keepdims=True)

    trace = lax.fori_loop(0, blocks, fill, jnp.zeros((1, 1), F32))
    scale = 1.0 / (jnp.sqrt(trace) + 1e-07)

    def keep(value, i, high_ref, low_ref):
        high, small = halves(value)
        high_ref[rows(i), :] = high
        low_ref[rows(i), :] = small

    def prepare(i, _):
        value = r.gram[rows(i), :] * (scale * scale)
        r.gram[rows(i), :] = value
        keep(value, i, r.gram_h, r.gram_l)
        return 0

    lax.fori_loop(0, blocks, prepare, 0)

    def polynomial(i, _):
        square = squared(r.gram_h[...], r.gram_l[...])
        value = (
            jnp.where(diagonal(i), newton_first, 0.0)
            + newton_second * r.gram[rows(i), :]
            + newton_third * square
        )
        keep(value, i, r.poly_h, r.poly_l)
        return 0

    def inner(i, _):
        high, small = r.poly_h[...], r.poly_l[...]
        own_h, own_l = halves(r.own[...])
        left = jnp.concatenate([high, own_h], axis=0)
        cross = dot(left, small)
        main = dot(jnp.concatenate([left, own_l], axis=0), high)
        r.own[...] = main[512:528] + (main[528:544] + cross[512:528])
        keep(main[0:512] + (cross[0:512] + cross[0:512].T), i, r.temp_h, r.temp_l)
        return 0

    def outer(i, _):
        value = product(r.gram_h[...], r.gram_l[...], r.temp_h[...], r.temp_l[...])
        r.gram[rows(i), :] = value
        keep(value, i, r.gram_h, r.gram_l)
        return 0

    def times(left, right_h, right_l):
        high, small = halves(left)
        both = dot(jnp.concatenate([high, small], axis=0), right_h[...])
        return both[0:16] + (both[16:32] + dot(high, right_l[...]))

    mine = 256 * place.c + 64 * place.a + 16 * place.b
    row = lax.broadcasted_iota(jnp.int32, (16, 512), 0)
    column = lax.broadcasted_iota(jnp.int32, (16, 512), 1)
    r.own[...] = jnp.where(column - row == mine, 1.0, 0.0)

    def sweep(_, carry):
        polynomial(0, 0)
        inner(0, 0)
        outer(0, 0)
        return carry

    lax.fori_loop(0, 3, sweep, 0)
    lax.fori_loop(0, blocks, polynomial, 0)
    lax.fori_loop(0, blocks, inner, 0)

    def last_gram(left):
        return times(times(left, r.gram_h, r.gram_l), r.temp_h, r.temp_l)

    own = r.own[...]
    once = last_gram(own)
    own = newton_first * own + newton_second * once + newton_third * last_gram(once)
    return halves(own * scale)


def block_kernel(*refs):
    r = Box()
    names = list(INPUTS) + [n for n, _, _ in OUTPUTS] + [n for n, _, _ in SCRATCH]
    for name, ref in zip(names, refs):
        setattr(r, name, ref)
    place = Place()
    wire = Wire(*refs[-3:])
    z, x, c, t, d = place.z, place.x, place.c, place.t, place.d
    seq, mate, cross, head = place.seq, place.mate, place.cross, place.head
    sibling = place.sibling()

    met = greet(
        place.octet()
        + [place.at_ab(a, b) for a, b in place.plane()]
        + [place.at(x=cross, c=1 - c)]
    )

    load_w = [
        wire.load(r.joint, r.joint_v),
        wire.load(r.output, r.output_v),
        wire.load(r.expand, r.expand_v),
        wire.load(r.reduce, r.reduce_v),
    ]
    load_v = wire.load(r.vectors, r.vectors_v)
    load_x = wire.load(r.x, r.rows_x.at[t])
    load_c = wire.load(r.c, r.rows_c.at[t])
    load_m = [
        wire.load(r.m_joint, r.m_joint_v),
        wire.load(r.m_output, r.m_output_v),
        wire.load(r.m_expand, r.m_expand_v),
        wire.load(r.m_reduce, r.m_reduce_v),
        wire.load(r.first, r.first_v),
        wire.load(r.second, r.second_v),
    ]
    load_w[0].wait()
    for k in range(4):
        for part in range(3):
            r.j_out[k, :, 128 * part : 128 * part + 128] = r.joint_v[
                :, 512 * part + 128 * k : 512 * part + 128 * k + 128
            ]
    load_v.wait()
    r.table[...] = jnp.zeros((128, 128), F32)
    column = lax.broadcasted_iota(jnp.int32, (128, 11), 0) - (16 * seq + 4 * t)
    own_vec = jnp.zeros((128, 11), F32)
    for j in range(4):
        own_vec = jnp.where(column == j, r.vectors_v[j : j + 1, :], own_vec)
    r.table[:, 0:11] = own_vec.astype(BF).astype(F32)
    r.v_own[...] = r.table[...].T[0:16, :]
    met()

    joint_t = trade_t(wire, place, r.j_out, r.j_in)
    for partner in place.row_t():
        joint_t.append(wire.push(r.v_own, r.v_in.at[t], partner))
    for copy in load_w[1:]:
        copy.wait()
    for k in range(4):
        r.w_out[k, :, 0:512] = r.output_v[...]
        r.w_out[k, :, 512:1024] = r.expand_v[:, 512 * k : 512 * k + 512]
        r.w_out[k, :, 1024:1536] = r.reduce_v[:, 512 * k : 512 * k + 512]
    rest_t = trade_t(wire, place, r.w_out, r.w_in)
    load_x.wait()
    load_c.wait()
    x_rows = [wire.push(r.rows_x.at[t], r.rows_x.at[t], p) for p in place.row_t()]
    r.j_in[t] = r.j_out[t]
    r.v_in[t] = r.v_own[...]
    r.w_in[t] = r.w_out[t]
    arrive(joint_t)
    for k in range(4):
        r.j_rows[4 * k : 4 * k + 4, :] = r.j_in[k]
    keys, values = r.j_rows[:, 128:256], r.j_rows[:, 256:384]
    low16 = lax.broadcasted_iota(jnp.int32, (16, 128), 1) < 64
    own_block = r.wj.at[c, place.a, place.b]
    own_block[:, 0:128] = r.j_rows[:, 0:128].astype(BF)
    own_block[:, 128:256] = jnp.where(low16, keys, pltpu.roll(values, 64, 1)).astype(BF)
    own_block[:, 256:384] = jnp.where(low16, pltpu.roll(keys, 64, 1), values).astype(BF)
    own_block[:, 384:512] = ((r.v_in[0] + r.v_in[1]) + (r.v_in[2] + r.v_in[3])).astype(BF)
    joint_all = spread_plane(wire, place, r.wj)
    arrive(rest_t)
    for k in range(4):
        r.w_rows[4 * k : 4 * k + 4, :] = r.w_in[k]
    r.wr[c, z, x] = r.w_rows[...].astype(BF)
    block = r.wr.at[c, z, x]
    rest_b = [wire.push(block, block, partner) for partner in place.row_x()]

    half = ROT // 2
    lane = lax.rem(lax.broadcasted_iota(jnp.int32, (1, 128), 1), 64)
    frequency = jnp.zeros((1, 128), F32)
    for i in range(half):
        frequency = jnp.where(lax.rem(lane, half) == i, 10000.0 ** (-2.0 * i / ROT), frequency)
    frequency = jnp.where(lane < ROT, frequency, 0.0)

    def angles(i, _):
        index = 512 * seq + 128 * i + lax.broadcasted_iota(jnp.int32, (128, 1), 0)
        begin = jnp.zeros((128, 1), jnp.int32)
        finish = 0
        for j in range(4):
            finish = finish + r.lengths[0, j]
            begin = jnp.where(index >= finish, finish, begin)
        angle = (index - begin).astype(F32) * frequency
        r.cos[i] = jnp.cos(angle)
        r.sin[i] = jnp.sin(angle)
        return 0

    lax.fori_loop(0, 4, angles, 0)
    for copy in load_m:
        copy.wait()
    arrive(joint_all)
    joint_swap = swap_cores(wire, place, r.wj)
    arrive(rest_b)
    c_rows = [wire.push(r.rows_c.at[t], r.rows_c.at[t], p) for p in place.row_t()]
    rest = Ring(wire, place, r.wr, z, lambda i: place.at(z=i))
    arrive(x_rows)
    joint_swap.wait_recv()
    for k in range(4):
        own_vec = jnp.zeros((16, 128), F32)
        for i in range(4):
            for part in (r.wj[0, k, i, :, 384:512], r.wj[1, i, k, :, 384:512]):
                own_vec = own_vec + part.astype(F32)
        r.v[k] = own_vec
    natural(r.wj, r.w_joint, 0, 384)

    gain, shift = vec_row(r.v, 0), vec_row(r.v, 1)
    q_bias, k_bias, v_bias = r.v[t, 2:3, :], r.v[t, 3:4, :], r.v[t, 4:5, :]
    low_row = lax.broadcasted_iota(jnp.int32, (1, 128), 1) < 64
    pair_bias = (
        jnp.where(low_row, k_bias, pltpu.roll(v_bias, 64, 1)),
        jnp.where(low_row, pltpu.roll(k_bias, 64, 1), v_bias),
    )
    low = lax.broadcasted_iota(jnp.int32, (256, 128), 1) < 64

    def project(i, _):
        blocks, rows = pl.ds(2 * i, 2), pl.ds(256 * i, 256)
        normal, _rate = normalise(r.rows_x[blocks].reshape(256, 512))
        part = (normal * gain + shift).astype(BF)
        r.normed[blocks] = part.reshape(2, 128, 512)
        raw = dot(part, r.w_joint[...].reshape(512, 384))
        cosine, sine = r.cos[blocks].reshape(256, 128), r.sin[blocks].reshape(256, 128)
        query = turn(raw[:, 0:128] + q_bias, cosine, sine, 1.0)
        r.q_turned[i] = query.T.astype(BF)
        key_cos = jnp.where(low, cosine, 1.0)
        key_sin = jnp.where(low, sine, 0.0)
        for h in range(2):
            pair = raw[:, 128 + 128 * h : 256 + 128 * h] + pair_bias[h]
            r.kv_buf[h, rows, :] = turn(pair, key_cos, key_sin, 1.0).astype(BF)
        return 0

    lax.fori_loop(0, 2, project, 0)
    for i in range(2):
        for h in range(2):
            r.q_buf[h, :, 256 * i : 256 * i + 256] = r.q_turned[i, 64 * h : 64 * h + 64, :]
    q_cross = wire.push(r.q_buf.at[1 - head], r.q_heads.at[1], place.at(x=cross, c=1 - c))
    kv_cross = []
    for i in range(2):
        rows = pl.ds(256 * i, 256)
        kv_cross.append(
            wire.push(r.kv_buf.at[1 - head, rows], r.kv.at[seq, rows], place.at(x=cross))
        )
    kv_mate = wire.push(r.kv_buf.at[head], r.kv.at[seq], place.at(x=mate))
    kv_core = wire.push(r.kv_buf.at[head], r.kv.at[seq], sibling)
    r.kv[seq] = r.kv_buf[head]
    r.q_heads[0] = r.q_buf[head]
    attend_start(r, place)
    query_prepare(r, 0)
    r.sums[...] = jnp.zeros_like(r.sums)
    r.back_turned[...] = jnp.zeros_like(r.back_turned)
    for k in range(4):
        lanes = slice(128 * k, 128 * k + 128)
        keys = r.m_joint_v[:, 512 + 128 * k : 640 + 128 * k]
        values = r.m_joint_v[:, 1024 + 128 * k : 1152 + 128 * k]
        start = 384 * k
        r.m_own[0, :, start : start + 128] = r.m_joint_v[:, lanes]
        r.m_own[0, :, start + 128 : start + 256] = jnp.concatenate(
            [keys[:, 0:64], values[:, 0:64]], axis=1
        )
        r.m_own[0, :, start + 256 : start + 384] = jnp.concatenate(
            [keys[:, 64:128], values[:, 64:128]], axis=1
        )
    r.m_own[0, :, 1536:2048] = jnp.zeros((4, 512), F32)
    r.m_own[1, :, 0:512] = r.m_output_v[...]
    r.m_own[1, :, 512:2048] = jnp.zeros((4, 1536), F32)
    r.m_own[2] = r.m_expand_v[...]
    r.m_own[3] = r.m_reduce_v[...]
    rest.hand_on()
    kv_core.wait_recv()
    keys_prepare(r, x)
    score_column(r, place, x, 0, diagonal=True)
    at_cross, at_mate = 2 * cross + c, 2 * mate + c
    at_far = 2 * (3 - mate) + c
    kv_far, kv_sent, far_sent = [], [], []
    for i in range(2):
        kv_cross[i].wait_recv()
        part = r.kv.at[at_cross, pl.ds(256 * i, 256)]
        kv_far.append(wire.push(part, part, place.at(x=mate)))
        kv_sent.append(wire.push(part, part, sibling))
    kv_mate.wait_recv()
    mate_sent = wire.push(r.kv.at[at_mate], r.kv.at[at_mate], sibling)
    rest.close()
    q_cross.wait_recv()
    query_prepare(r, 1)
    score_column(r, place, x, 1)
    mate_sent.wait_recv()
    keys_prepare(r, mate)
    score_column(r, place, mate, 0)
    score_column(r, place, mate, 1)
    arrive([*c_rows, *rest.swaps])
    by_row(r.wr, r.w_output, 0, 512)
    by_row(r.wr, r.w_expand, 512, 1024)
    by_row(r.wr, r.w_reduce, 1024, 1536)
    out_rows = r.w_output[pl.ds(8 * t, 8)].reshape(128, 512)
    grad = dot_cols(out_rows, r.rows_c[...].reshape(512, 512)).astype(BF)
    r.g_buf[0] = grad[0:64, :]
    r.g_buf[1] = grad[64:128, :]
    g_cross = wire.push(r.g_buf.at[1 - head], r.g_heads.at[1], place.at(x=cross, c=1 - c))
    r.g_heads[0] = r.g_buf[head]
    grad_prepare(r, 0)
    early = trade_t(wire, place, r.m_own, r.m_early)

    bias = jnp.concatenate([r.v[k, pl.ds(7 + t, 1), :] for k in range(4)], axis=1)

    def feed_forward(i, sums):
        blocks = pl.ds(2 * i, 2)
        part = r.normed[blocks].reshape(256, 512)
        wide = dot(part, r.w_expand[...].reshape(512, 512)) + bias
        square = wide * wide
        curve = jnp.tanh(0.7978845608 * (wide + 0.044715 * (square * wide)))
        r.hidden[blocks] = (0.5 * wide * (1.0 + curve)).astype(BF).reshape(2, 128, 512)
        slope = 0.5 * (1.0 + curve) + (0.5 * 0.7978845608) * wide * (1.0 - curve * curve) * (
            1.0 + (3 * 0.044715) * square
        )
        part = r.rows_c[blocks].reshape(256, 512)
        back = dot(part, r.w_reduce[...].reshape(512, 512))
        grad = (back * slope).astype(BF)
        r.pre[blocks] = grad.reshape(2, 128, 512)
        return sums + jnp.sum(grad.astype(F32), axis=0, keepdims=True)

    hidden_sum = lax.fori_loop(0, 2, feed_forward, jnp.zeros((1, 512), F32))
    for i in range(2):
        kv_far[i].wait_recv()
        part = r.kv.at[at_far, pl.ds(256 * i, 256)]
        far_sent.append(wire.push(part, part, sibling))
    for j in range(4):
        lanes = slice(128 * j, 128 * j + 128)
        expand_grad = dot_rows(
            r.normed[:, :, lanes].reshape(512, 128), r.pre[...].reshape(512, 512)
        )
        by_core(r.gf, j, expand_grad.astype(BF), 0, 512)
        reduce_grad = dot_rows(
            r.rows_c[:, :, lanes].reshape(512, 128), r.hidden[...].reshape(512, 512)
        )
        by_core(r.gf, j, reduce_grad.astype(BF), 512, 1024)
    gf_swap = sum_cores(wire, place, r.gf, r.gf_core)
    far = 3 - mate
    arrive(kv_sent)
    keys_prepare(r, cross)
    score_column(r, place, cross, 0)
    score_column(r, place, cross, 1, diagonal=True)
    arrive(far_sent)
    keys_prepare(r, far)
    score_column(r, place, far, 0)
    score_column(r, place, far, 1)
    gf_swap.wait_recv()
    for a in range(4):
        r.gf_chip[a] = (r.gf[c, a].astype(F32) + r.gf_core[a].astype(F32)).astype(BF)
    gf_z = []
    for k in range(1, 4):
        goal = ring(z, k)
        gf_z.append(wire.push(r.gf_chip.at[goal], r.gf_z.at[k - 1], place.at(z=goal)))
    weigh_values(r, place, 1)
    out_cross = wire.push(r.out_low.at[1], r.out_heads.at[head], place.at(x=cross, c=1 - c))
    weigh_values(r, place, 0)
    r.out_heads[head] = r.out_low[0]
    g_cross.wait_recv()
    grad_prepare(r, 1)
    for slot in range(2):
        r.centre[slot] = jnp.sum(
            r.out_turned[slot] * r.g_heads[slot].astype(F32), axis=0, keepdims=True
        )

    dk_swap = []

    def chip_sum(index):
        return r.dk[c, index].astype(F32) + r.dk_in[index].astype(F32)

    dk_sent = []

    def send_column(step, column):
        dk_swap[step].wait_recv()
        r.dk_chip[step] = chip_sum(column).astype(BF)
        dk_sent.append(
            wire.push(r.dk_chip.at[step], r.dk_got.at[step], place.at(x=column))
        )

    backward_cross(r, place)
    back_cross = wire.push(r.back_low.at[1], r.back_heads.at[head], place.at(x=cross, c=1 - c))
    columns = (far, cross, mate, x)
    for step, column in enumerate(columns):
        backward_column(r, place, column, diagonal=step == 3)
        dk_swap.append(wire.push(r.dk.at[1 - c, column], r.dk_in.at[column], sibling))
        if step > 0:
            send_column(step - 1, columns[step - 1])
    r.back_low[0] = (r.back_turned[...] * (HD ** -0.5)).astype(BF)
    r.back_heads[head] = r.back_low[0]
    out_cross.wait_recv()
    turned = r.out_heads[...].reshape(128, 512)
    r.pair_out[...] = turned
    out_grad = dot(turned, r.rows_c[...].reshape(512, 512)).astype(BF)
    for j in range(4):
        r.out_cols[j] = out_grad[:, 128 * j : 128 * j + 128]
    out_cols = trade_t(wire, place, r.out_cols, r.out_in)
    r.out_in[t] = r.out_cols[t]
    arrive(gf_z)
    r.gf_line[...] = total(r.gf_chip[z], r.gf_z).astype(BF)
    gf_x = []
    for k in range(1, 4):
        goal = ring(x, k)
        gf_x.append(wire.push(r.gf_line.at[goal], r.gf_x.at[k - 1], place.at(x=goal)))
    def feed_out(i, _):
        blocks = pl.ds(2 * i, 2)
        part = r.hidden[blocks].reshape(256, 512)
        r.feed[blocks] = dot_cols(part, r.w_reduce[...].reshape(512, 512)).reshape(2, 128, 512)
        part = r.pre[blocks].reshape(256, 512)
        r.row_grad[blocks] = dot_cols(part, r.w_expand[...].reshape(512, 512)).reshape(2, 128, 512)
        return 0

    lax.fori_loop(0, 2, feed_out, 0)
    out_rows = r.w_output[pl.ds(8 * t, 8)].reshape(128, 512)
    for i in range(2):
        blocks, lanes = slice(2 * i, 2 * i + 2), slice(256 * i, 256 * i + 256)
        part = r.feed[blocks].reshape(256, 512) + dot_rows(r.pair_out[:, lanes], out_rows)
        r.out_part[blocks] = part.astype(BF).reshape(2, 128, 512)
    out_parts = trade_t(wire, place, r.out_part, r.out_got)
    r.out_got[t] = r.out_part[t]
    back_cross.wait_recv()
    back = r.back_heads[...].reshape(128, 512).astype(F32).T
    cosine, sine = r.cos[...].reshape(512, 128), r.sin[...].reshape(512, 128)
    r.joint_out[:, 0:128] = turn(back, cosine, sine, -1.0).astype(BF)
    low = lax.broadcasted_iota(jnp.int32, (128, 128), 1) < 64
    arrive(out_cols)
    for j in range(4):
        by_owner(r.go, j, r.out_in[j], 0, 128)
    go_swap = sum_cores(wire, place, r.go, r.go_core)

    arrive([dk_swap[3], *dk_sent])
    r.dkv[head] = (chip_sum(x) + r.dk_got[2].astype(F32)).astype(BF)
    r.dkv[1 - head] = (r.dk_got[0].astype(F32) + r.dk_got[1].astype(F32)).astype(BF)
    for h in range(2):
        for i in range(4):
            rows = pl.ds(128 * i, 128)
            key_cos = jnp.where(low, r.cos[i], 1.0)
            key_sin = jnp.where(low, r.sin[i], 0.0)
            r.joint_out[rows, 128 + 128 * h : 256 + 128 * h] = turn(
                r.dkv[h, rows, :].astype(F32), key_cos, key_sin, -1.0
            ).astype(BF)
    for j in range(4):
        part = r.normed[:, :, 128 * j : 128 * j + 128].reshape(512, 128)
        by_owner(r.gj, j, dot_rows(part, r.joint_out[...]).astype(BF), 0, 384)
    gj_swap = sum_cores(wire, place, r.gj, r.gj_core)
    go_swap.wait_recv()
    for a in range(4):
        r.go_chip[a] = (r.go[c, a].astype(F32) + r.go_core[a].astype(F32)).astype(BF)
    go_all = scatter_plane(wire, place, r.go_chip, r.go_in)

    r.vp[0] = jnp.zeros((4, 16, 128), F32)
    shift_sum = jnp.zeros((1, 512), F32)
    gain_sum = jnp.zeros((1, 512), F32)
    for i in range(4):
        rows = pl.ds(128 * i, 128)
        part = r.row_grad[i] + dot_cols(r.joint_out[rows, :], r.w_joint[...].reshape(512, 384))
        r.back_part[i] = part.astype(BF)
        normal, _rate = normalise(r.rows_x[i])
        shift_sum = shift_sum + jnp.sum(part, axis=0, keepdims=True)
        gain_sum = gain_sum + jnp.sum(part * normal, axis=0, keepdims=True)
    gj_swap.wait_recv()
    for a in range(4):
        r.gj_chip[a] = (r.gj[c, a].astype(F32) + r.gj_core[a].astype(F32)).astype(BF)
    gj_all = scatter_plane(wire, place, r.gj_chip, r.gj_in)
    back_parts = trade_t(wire, place, r.back_part, r.back_got)
    r.back_got[t] = r.back_part[t]
    out_sum = jnp.sum(r.rows_c[t].astype(F32), axis=0, keepdims=True)
    joint_sum = jnp.sum(r.joint_out[...].astype(F32), axis=0, keepdims=True)
    one, two = joint_sum[:, 128:256], joint_sum[:, 256:384]
    for k in range(4):
        lanes = slice(128 * k, 128 * k + 128)
        r.vp[0, k, 0:1, :] = gain_sum[:, lanes]
        r.vp[0, k, 1:2, :] = shift_sum[:, lanes]
        r.vp[0, k, 5:6, :] = out_sum[:, lanes]
        r.vp[0, k, 6:7, :] = out_sum[:, lanes]
        r.vp[0, k, pl.ds(7 + t, 1), :] = hidden_sum[:, lanes]
    r.vp[0, t, 2:3, :] = joint_sum[:, 0:128]
    r.vp[0, t, 3:4, :] = jnp.where(low_row, one, pltpu.roll(two, 64, 1))
    r.vp[0, t, 4:5, :] = jnp.where(low_row, pltpu.roll(one, 64, 1), two)
    vp_swap = wire.push(r.vp.at[0], r.vp_core, sibling)
    arrive(gf_x)
    gf_own = total(r.gf_line[x], r.gf_x)
    arrive(go_all)
    go_own = add_plane(r.go_chip[place.a, place.b], r.go_in)
    for k in range(4):
        r.early_out[k, :, 0:1024] = gf_own[4 * k : 4 * k + 4, :]
        r.early_out[k, :, 1024:1152] = go_own[4 * k : 4 * k + 4, :]
    r.gm_out[1, :, 0:128] = go_own.astype(BF)
    r.gm_out[2] = gf_own[:, 0:512].astype(BF)
    r.gm_out[3] = gf_own[:, 512:1024].astype(BF)
    gm_first = wire.block(4)
    gm_widths = (384, 128, 512, 512)

    def to_newton(w, sender):
        lanes = slice(0, gm_widths[w])
        return wire.offer(
            gm_first, r.gm_out.at[w, :, lanes], r.gm_in.at[sender, :, lanes], sender, w,
            place.at(t=w),
        )

    def send_newton(w):
        @pl.when(t != w)
        def _():
            to_newton(w, t).start()

        @pl.when(t == w)
        def _():
            r.gm_in[w, :, 0 : gm_widths[w]] = r.gm_out[w, :, 0 : gm_widths[w]]

    for w in (1, 2, 3):
        send_newton(w)
    early_t = trade_t(wire, place, r.early_out, r.early_in)
    r.early_in[t] = r.early_out[t]

    arrive(early)
    r.m_early[t] = r.m_own[t]
    for k in range(4):
        r.m_old[4 * k : 4 * k + 4, :] = r.m_early[k]
    vp_swap.wait_recv()
    r.vp[1] = r.vp[0] + r.vp_core[...]
    vp_z = [wire.push(r.vp.at[1], r.vp_z.at[k], p) for k, p in enumerate(place.row_z())]

    arrive(gj_all)
    gj_own = add_plane(r.gj_chip[place.a, place.b], r.gj_in)
    r.gm_out[0, :, 0:384] = gj_own.astype(BF)
    send_newton(0)
    for k in range(4):
        r.late_out[k] = gj_own[4 * k : 4 * k + 4, :]
    late_t = trade_t(wire, place, r.late_out, r.late_in)
    r.late_in[t] = r.late_out[t]
    arrive(vp_z)
    r.vp[2] = total(r.vp[1], r.vp_z)
    vp_x = [wire.push(r.vp.at[2], r.vp_x.at[k], p) for k, p in enumerate(place.row_x())]

    for w in range(4):

        @pl.when(t == w)
        def _(w=w):
            width = gm_widths[w]
            for sender in range(4):
                if sender != w:
                    to_newton(w, sender).wait_recv()
            for k in range(4):
                lanes = slice(width * k, width * k + width)
                value = muon_beta * r.m_old[:, lanes] + r.gm_in[k, :, 0:width].astype(F32)
                if width * k < 1536:
                    r.momentum[c, place.a, place.b, :, lanes] = value.astype(BF)
                else:
                    r.extra[c, place.a, place.b] = value.astype(BF)
            if w == 1:
                r.momentum[c, place.a, place.b, :, 512:1536] = jnp.zeros((16, 1024), BF)

    m_b = spread_b(wire, place, r.momentum)

    extra_first = wire.block(7)

    def extra_line():
        block = r.extra.at[c, place.a, place.b]
        return [
            wire.offer(extra_first, block, block, k, k, place.at_b(ring(place.b, k)))
            for k in range(1, 4)
        ]

    def extra_lines():
        block = r.extra.at[c, place.a]
        return [
            wire.offer(extra_first, block, block, 3 + k, 3 + k, place.at_a(ring(place.a, k)))
            for k in range(1, 4)
        ]

    def extra_swap():
        block = r.extra.at[c]
        return wire.offer(extra_first, block, block, 0, 0, sibling)

    @pl.when(t >= 2)
    def _():
        for copy in extra_line():
            copy.start()

    arrive(m_b)
    whole = Ring(wire, place, r.momentum, place.a, place.at_a)

    @pl.when(t >= 2)
    def _():
        for copy in extra_line():
            copy.wait_recv()
        for copy in extra_lines():
            copy.start()

    arrive(early_t)
    for k in range(4):
        part = r.early_in[k]
        r.g_expand[:, 512 * k : 512 * k + 512] = part[:, 0:512]
        r.g_reduce[:, 512 * k : 512 * k + 512] = part[:, 512:1024]
        r.g_output[:, 128 * k : 128 * k + 128] = part[:, 1024:1152]
    arrive(late_t)
    for k in range(4):
        unpair(r.g_joint, r.late_in[k], k)
    for old, grad, new in (
        (r.m_joint_v, r.g_joint, r.n_joint),
        (r.m_output_v, r.g_output, r.n_output),
        (r.m_expand_v, r.g_expand, r.n_expand),
        (r.m_reduce_v, r.g_reduce, r.n_reduce),
    ):
        new[...] = muon_beta * old[...] + grad[...]
    arrive(vp_x)
    r.vp[3] = total(r.vp[2], r.vp_x)
    vp_t = [wire.push(r.vp.at[3], r.vp_t.at[k], p) for k, p in enumerate(place.row_t())]
    arrive(out_parts)
    arrive(back_parts)
    wide = r.rows_x[t].astype(F32)
    feed = r.out_got[0].astype(F32)
    back = r.back_got[0].astype(F32)
    for k in range(1, 4):
        feed = feed + r.out_got[k].astype(F32)
        back = back + r.back_got[k].astype(F32)
    r.block_output[...] = (wide + feed + vec_row(r.v, 5) + vec_row(r.v, 6)).astype(BF)
    normal, rate = normalise(r.rows_x[t])
    scaled = back * gain
    mean_one = jnp.mean(scaled, axis=-1, keepdims=True)
    mean_two = jnp.mean(scaled * normal, axis=-1, keepdims=True)
    r.input_grad[...] = r.rows_c[t].astype(F32) + rate * (scaled - mean_one - normal * mean_two)
    whole.hand_on()

    @pl.when(t >= 2)
    def _():
        for copy in extra_lines():
            copy.wait_recv()
        extra_swap().start()

    whole.close()
    arrive(vp_t)
    r.vec_sum[...] = total(r.vp[3], r.vp_t)
    r.table[0:16, :] = r.vec_sum[z]
    r.table[...] = r.table[...].T
    vector_grad = r.table[pl.ds(pl.multiple_of(16 * seq + 4 * t, 4), 4), 0:11]
    r.vector_grad[...] = vector_grad
    first_next = beta_first * r.first_v[...] + (1.0 - beta_first) * vector_grad
    second_next = (
        beta_second * r.second_v[...] + (1.0 - beta_second) * vector_grad * vector_grad
    )
    r.second_next[...] = second_next
    first_hat = first_next / (1.0 - beta_first**STEP)
    second_hat = second_next / (1.0 - beta_second**STEP)
    r.vector_next[...] = r.vectors_v[...] - vector_rate * first_hat / (
        jnp.sqrt(second_hat) + adam_epsilon
    )
    @pl.when(t >= 2)
    def _():
        extra_swap().wait_recv()
        columns = r.extra[...].reshape(512, 512)
        r.gram[...] = dot_cols(columns, columns)

    @pl.when(t < 2)
    def _():
        r.gram[...] = jnp.zeros((512, 512), F32)

    arrive(whole.swaps)

    high, small = newton(r, place)
    both = jnp.concatenate([high, small], axis=0)
    for k in range(3):
        lanes = slice(512 * k, 512 * k + 512)
        rows = dot(both, r.momentum[:, :, :, :, lanes].reshape(512, 512))
        r.m_rows[:, lanes] = rows[0:16] + rows[16:32]

    @pl.when(t >= 2)
    def _():
        rows = dot(both, r.extra[...].reshape(512, 512))
        r.m_rows[:, 1536:2048] = rows[0:16] + rows[16:32]

    @pl.when(t < 2)
    def _():
        r.m_rows[:, 1536:2048] = jnp.zeros((16, 512), F32)

    for k in range(4):
        for p in range(4):
            r.u_rows[k, 4 * p : 4 * p + 4, :] = r.m_rows[
                4 * k : 4 * k + 4, 512 * p : 512 * p + 512
            ]
    r.u_out[...] = r.u_rows[...].astype(BF)
    u_t = trade_t(wire, place, r.u_out, r.u_in)
    r.u_in[t] = r.u_out[t]
    wire.drain()
    for w in range(4):

        @pl.when(t != w)
        def _(w=w):
            to_newton(w, t).wait_send()

    @pl.when(t >= 2)
    def _():
        for copy in extra_line() + extra_lines():
            copy.wait_send()
        extra_swap().wait_send()

    arrive(u_t)
    r.u_rows[...] = r.u_in[...].astype(F32)
    for k in range(4):
        for p in range(4):
            r.u_wide[k, :, 512 * p : 512 * p + 512] = r.u_rows[k, 4 * p : 4 * p + 4, :]
    for k in range(4):
        unpair(r.u_joint, r.u_wide[0, :, 384 * k : 384 * k + 384], k)
    for k, (old, change, new) in enumerate(
        (
            (r.joint_v, r.u_joint, r.u_joint),
            (r.output_v, r.u_wide.at[1, :, pl.ds(0, 512)], r.u_output),
            (r.expand_v, r.u_wide.at[2], r.u_expand),
            (r.reduce_v, r.u_wide.at[3], r.u_reduce),
        )
    ):
        factor = muon_rate * 0.2 * math.sqrt(max(D, WIDTHS[k]))
        new[...] = old[...] * (1.0 - muon_rate * muon_decay) - factor * change[...]
    wire.drain()


def block_stage(*arrays):
    return pl.pallas_call(
        block_kernel,
        out_shape=tuple(shape(dims, dtype) for _, dims, dtype in OUTPUTS),
        in_specs=[SMEM] + [ANY] * (len(INPUTS) - 1),
        out_specs=(VMEM,) * len(OUTPUTS),
        scratch_shapes=[pltpu.VMEM(dims, dtype) for _, dims, dtype in SCRATCH]
        + [
            pltpu.SemaphoreType.DMA((PUSHES,)),
            pltpu.SemaphoreType.DMA((PUSHES,)),
            pltpu.SemaphoreType.DMA((LOADS,)),
        ],
        compiler_params=pltpu.CompilerParams(
            collective_id=1, has_side_effects=True, vmem_limit_bytes=56 << 20
        ),
        name="block",
    )(*arrays)


def write_kernel(*refs):
    count = len(OUTPUTS)
    sem = refs[-1]
    copies = []
    for k in range(count):
        copy = pltpu.make_async_copy(refs[k], refs[count + k], sem.at[k])
        copy.start()
        copies.append(copy)
    for copy in copies:
        copy.wait()


def write_stage(*arrays):
    count = len(arrays)
    return pl.pallas_call(
        write_kernel,
        out_shape=tuple(shape(a.shape, a.dtype) for a in arrays),
        in_specs=[VMEM] * count,
        out_specs=(ANY,) * count,
        scratch_shapes=[pltpu.SemaphoreType.DMA((count,))],
        name="write",
    )(*arrays)


def shards(
    block_input,
    cotangent,
    doc_lengths,
    joint_weight,
    output_weight,
    expand_weight,
    reduce_weight,
    joint_moment,
    output_moment,
    expand_moment,
    reduce_moment,
    vectors,
    first_moment,
    second_moment,
):
    results = block_stage(
        doc_lengths, block_input, cotangent, joint_weight, output_weight, expand_weight,
        reduce_weight, vectors.T, joint_moment, output_moment, expand_moment, reduce_moment,
        first_moment.T, second_moment.T,
    )
    results = write_stage(*results)
    return (*results[12:14], *results[0:12], *[part.T for part in results[14:]])


def solution(mesh):
    rows = P(("fsdp", "seq", "tensor"), None)
    columns = P(None, ("fsdp", "seq", "tensor"))
    return jax.shard_map(
        shards,
        mesh=mesh,
        in_specs=(rows, rows, P("fsdp", None)) + (rows,) * 8 + (columns,) * 3,
        out_specs=(rows,) * 14 + (columns,) * 3,
        check_vma=False,
    )
```
